32 devices in a mesh: batch: 8 (over y, x, core), shard: 4 (over z).
Axes of the slice: x: 2, y: 2, z: 4, core: 2. Of those that a mesh axis runs over, the one named last changes fastest.
Arguments:
- inputs: bfloat16 [32, 1024, 512], P(('batch', 'shard')), may hold values from -10 to 10
- cotangent: bfloat16 [32, 1024, 512], P(('batch', 'shard')), may hold values from -6 to 6
- lengths: int32 [32], P(('batch', 'shard')), may hold values from 512 to 1024, as said below
- segment_ids: int32 [32, 1024], P(('batch', 'shard')), may hold values from 0 to 7, never falling along the last dimension, each value on 1 to 512 neighbouring positions
- group_tags: int32 [32, 8], P(('batch', 'shard')), may hold values from 0 to 3
- weights: float32 [512, 6144], P('shard'), may hold values from -2 to 2
- first_moments: float32 [512, 6144], P('shard'), may hold values from -4 to 4
- second_moments: float32 [512, 6144], P('shard'), may hold values from 1 to 4
- vectors: float32 [12, 512], P(None, 'shard'), may hold values from -3 to 3
- vector_first: float32 [12, 512], P(None, 'shard'), may hold values from -16 to 16
- vector_second: float32 [12, 512], P(None, 'shard'), may hold values from 9 to 36
Outputs:
- outputs: bfloat16 [32, 1024, 512], P(('batch', 'shard'))
- input_grad: float32 [32, 1024, 512], P(('batch', 'shard'))
- grad_w: float32 [512, 6144], P('shard')
- grad_v: float32 [12, 512], P(None, 'shard')
- grad_norm: float32 [], replicated
- new_weights: float32 [512, 6144], P('shard')
- new_first: float32 [512, 6144], P('shard')
- new_second: float32 [512, 6144], P('shard')
- new_vectors: float32 [12, 512], P(None, 'shard')
- new_vector_first: float32 [12, 512], P(None, 'shard')
- new_vector_second: float32 [12, 512], P(None, 'shard')
The draws below stay inside these ranges and needn't reach their ends.
Inputs may be any that keep to these rules, and one draw needn't show every extreme that they name: `lengths`: each row's live tokens; positions at or past it are padding.
All inputs are finite; a program needn't handle non-finite values.
Results may differ from the reference program's by a relative error of at most 0.028.
The reference program's roundings to bfloat16 on the way count: a program that leaves them out, or rounds other values in their place, can miss the bound.
Values may be sent and summed in bfloat16 or wider, within the bound.
No kernel may reach another device: no remote copies, remote signals or barrier semaphores. Data moves between devices by JAX's collectives and lax.ppermute only.
A program may use at most 256 MiB of HBM per device.

```python
import math
import jax
import jax.numpy as jnp
import numpy as np
from jax import lax

D = 512
FF = 2048
HEADS = 8
HEAD_DIM = 64
SEQ = 1024
SEGS = 8
GROUPS = 4
STEP = 10
ROWS = 32
WCOLS = 6144
NVEC = 12


def draw_inputs(key, part):
    key = jax.random.fold_in(key, 11)
    key_one = jax.random.fold_in(key, 0)
    fraction = jnp.arange(D, dtype=jnp.float32) / (D - 1)
    rising = 0.6 * jnp.exp(fraction * math.log(3.0))
    jitter = jax.random.truncated_normal(key_one, -4.0, 4.0, (ROWS, SEQ, D), jnp.float32)
    return (jitter * rising[None, None, :]).astype(jnp.bfloat16)


def draw_weights(key, part):
    key = jax.random.fold_in(key, 7)
    column = jnp.arange(WCOLS)
    column_scale = jnp.where(column < 3 * D, D ** (-0.5), jnp.where(column < 4 * D, (D // 16) ** (-0.5), jnp.where(column < 4 * D + FF, D ** (-0.5), FF ** (-0.5))))
    jitter = jax.random.truncated_normal(key, -3.0, 3.0, (D, WCOLS), jnp.float32)
    return (jitter * column_scale[None, :]).astype(jnp.float32)


def draw_vectors(key, part):
    key = jax.random.fold_in(key, 13)
    key_one, key_two = jax.random.split(key)
    fraction = jnp.arange(D, dtype=jnp.float32) / (D - 1)
    rising = 0.6 * jnp.exp(fraction * math.log(3.0))
    jitter = jax.random.truncated_normal(key_one, -3.0, 3.0, (NVEC, D), jnp.float32)
    wobble = jax.random.uniform(key_two, (NVEC, D), jnp.float32, 0.85, 1.15)
    row_index = jnp.arange(NVEC)[:, None]
    is_gain = (row_index == 0) | (row_index == 2)
    return jnp.where(is_gain, rising[None, :] * wobble, 0.2 * jitter).astype(jnp.float32)


def draw_lengths(key, part):
    key = jax.random.fold_in(key, 5)
    key_one, key_two, key_three = jax.random.split(key, 3)
    ragged = jax.random.randint(key_one, (ROWS,), SEQ // 2, SEQ + 1)
    longest = jax.random.randint(key_two, (), 0, ROWS)
    shortest = (longest + 1 + jax.random.randint(key_three, (), 0, ROWS - 1)) % ROWS
    row_index = jnp.arange(ROWS)
    ragged = jnp.where(row_index == longest, SEQ, ragged)
    ragged = jnp.where(row_index == shortest, SEQ // 2, ragged)
    return ragged.astype(jnp.int32)


def with_ends(entries, stream_key, low, top_value):
    index_at = [jax.random.randint(jax.random.fold_in(stream_key, axis), (), 0, length) for axis, length in enumerate(entries.shape)]
    main_axis = entries.shape.index(max(entries.shape))
    neighbour = index_at[:main_axis] + [(index_at[main_axis] + 1) % entries.shape[main_axis]] + index_at[main_axis + 1:]
    return entries.at[tuple(index_at)].set(low).at[tuple(neighbour)].set(top_value)


def steps_of(key, shape, shards, least, largest):
    def one(axis_at, shards_of):
        heights = jax.random.uniform(jax.random.fold_in(jax.random.fold_in(key, 6), axis_at), (shards_of,), jnp.float32, least / len(shards), largest / len(shards))
        return jnp.repeat(jnp.exp(heights), shape[axis_at] // shards_of).reshape((-1,) + (1,) * (len(shape) - axis_at - 1))

    factor_of = one(*shards[0])
    for cut in shards[1:]:
        factor_of = factor_of * one(*cut)
    return factor_of


def length_profile(amount, total, limit, slope):
    portions = [(1 << 20) // math.isqrt(standing ** slope) + 1 for standing in range(2, amount + 1)]
    spare, counts = total - limit - (amount - 1), [1] * (amount - 1)
    while spare > 0:
        free = [i for i in range(amount - 1) if counts[i] < limit]
        whole, left = sum([portions[i] for i in free]), spare
        for i in free:
            addition = min(limit - counts[i], max(1, left * portions[i] // whole), spare)
            counts[i] = counts[i] + addition
            spare = spare - addition
    return np.array([limit] + counts)


def uneven(own_key, number_of, total, limit, slope):
    if number_of == 2:
        one = jax.random.randint(own_key, (), max(1, total - limit), min(limit, total - 1) + 1)
        return jnp.stack([one, total - one])
    sizes = jnp.asarray(length_profile(number_of, total, limit, slope), jnp.int32)
    twos = (number_of - 1) // 2
    giver, sink = sizes[1:1 + 2 * twos:2], sizes[2:2 + 2 * twos:2]
    margin = jnp.minimum(giver - 1, limit - sink)
    passed = jax.random.randint(jax.random.fold_in(own_key, 1), (twos,), 0, 1 << 20) % (margin + 1)
    sizes = sizes.at[1:1 + 2 * twos:2].set(giver - passed).at[2:2 + 2 * twos:2].set(sink + passed)
    return sizes[jax.random.permutation(jax.random.fold_in(own_key, 2), number_of)]


def noise(rng, dims, width, limit, cuts=(), kind=jnp.bfloat16):
    entries = width * jax.random.normal(rng, dims, jnp.float32)
    if cuts:
        entries = entries * steps_of(rng, dims, cuts, -0.22, 0.18)
    return jnp.clip(entries, -limit, limit).astype(kind)


def setup_inputs(seed: int = 0) -> dict:
    streams_of = jax.random.split(jax.random.key(seed), 12)
    return {
        "inputs": draw_inputs(jax.random.fold_in(streams_of[11], 71), 0),
        "cotangent": noise(streams_of[1], (ROWS, SEQ, D), 1.0, 6.0, ((0, 32),)),
        "lengths": draw_lengths(jax.random.fold_in(streams_of[11], 71), 0),
        "segment_ids": jax.vmap(lambda own: jnp.searchsorted(jnp.cumsum(uneven(own, SEGS, SEQ, SEQ // 2, 2)), jnp.arange(SEQ), side="right"))(jax.random.split(streams_of[3], ROWS)).reshape((ROWS, SEQ)).astype(jnp.int32),
        "group_tags": with_ends(jax.random.randint(streams_of[4], (ROWS, SEGS), 0, GROUPS), jax.random.fold_in(streams_of[4], 1), 0, GROUPS - 1).astype(jnp.int32),
        "weights": draw_weights(jax.random.fold_in(streams_of[11], 71), 0),
        "first_moments": noise(streams_of[6], (D, WCOLS), 1.0, 4.0, ((0, 4),), jnp.float32),
        "second_moments": jnp.clip(jnp.exp(math.log(4.0) - 1.3862944 * jax.random.uniform(streams_of[7], (D, WCOLS), jnp.float32) ** steps_of(streams_of[7], (D, WCOLS), ((0, 4),), -0.2, 0.2)), 1.0, 4.0),
        "vectors": draw_vectors(jax.random.fold_in(streams_of[11], 71), 0),
        "vector_first": noise(streams_of[9], (NVEC, D), 3.0, 16.0, ((1, 4),), jnp.float32),
        "vector_second": jnp.clip(jnp.exp(math.log(36.0) - 1.3862944 * jax.random.uniform(streams_of[10], (NVEC, D), jnp.float32) ** steps_of(streams_of[10], (NVEC, D), ((1, 4),), -0.2, 0.2)), 9.0, 36.0),
    }


HIGH = lax.Precision.HIGHEST
NORM_EPS = 1e-05
BETA_ONE = 0.5
BETA_TWO = 0.5
ADAM_EPS = 1e-08
DECAY = 0.01
WARMUP = 4000.0
RATE_SCALE = 150000.0

@jax.custom_vjp
def low(v):
    return lax.optimization_barrier(v.astype(jnp.bfloat16)).astype(jnp.float32)

@jax.custom_vjp
def low_back(v):
    return v

def low_keep(v):
    return (low(v), None)

def low_pass(kept, grad):
    return (grad,)

def back_keep(v):
    return (v, None)

def back_low(kept, grad):
    return (low(grad),)
low.defvjp(low_keep, low_pass)
low_back.defvjp(back_keep, back_low)

def layer_norm(signal, norm_gain, norm_shift):
    row_mean = lax.optimization_barrier(jnp.mean(signal, axis=-1, keepdims=True))
    centred = signal - row_mean
    variance = lax.optimization_barrier(jnp.mean(centred * centred, axis=-1, keepdims=True))
    return centred * lax.rsqrt(variance + NORM_EPS) * norm_gain + norm_shift

def gelu_tanh(signal):
    return 0.5 * signal * (1.0 + jnp.tanh(0.7978845608028654 * (signal + 0.044715 * signal * signal * signal)))

def adam_update(master, moment_one, moment_two, gradient):
    moment_one = BETA_ONE * moment_one + (1.0 - BETA_ONE) * gradient
    moment_two = BETA_TWO * moment_two + (1.0 - BETA_TWO) * gradient * gradient
    step_rate = RATE_SCALE * D ** (-0.5) * min(STEP ** (-0.5), STEP * WARMUP ** (-1.5))
    fixed_first = moment_one / (1.0 - BETA_ONE ** STEP)
    fixed_second = moment_two / (1.0 - BETA_TWO ** STEP)
    master = master - step_rate * (fixed_first / (jnp.sqrt(fixed_second) + ADAM_EPS) + DECAY * master)
    return (master, moment_one, moment_two)

def allowed_mask(seg_row, tag_row, length):
    tag_count = tag_row.shape[0]
    matches = seg_row[:, None] == jnp.arange(tag_count, dtype=jnp.int32)[None, :]
    token_group = lax.optimization_barrier(jnp.sum(jnp.where(matches, tag_row[None, :], 0), axis=1)).astype(jnp.int32)
    position = jnp.arange(seg_row.shape[0], dtype=jnp.int32)
    related = (seg_row[:, None] == seg_row[None, :]) | (token_group[:, None] == token_group[None, :])
    live_key = position[None, :] < length
    return related & live_key | (position[:, None] == position[None, :])

def attend_row(pieces):
    queries, key_rows, values, seg_row, tag_row, length = pieces
    allowed = allowed_mask(seg_row, tag_row, length)
    scores = jnp.einsum('qhd,khd->hqk', queries, key_rows, precision=HIGH) * (1.0 / math.sqrt(HEAD_DIM))
    scores = low_back(scores)
    scores = jnp.where(allowed[None], scores, -1e+30)
    row_top = lax.optimization_barrier(jnp.max(scores, axis=-1, keepdims=True))
    exponent = jnp.exp(scores - row_top)
    probability = low(exponent / lax.optimization_barrier(jnp.sum(exponent, axis=-1, keepdims=True)))
    return jnp.einsum('hqk,khd->qhd', probability, values, precision=HIGH)

def use_layer(signal, matrices, vector_rows, segment_ids, group_tags, lengths):
    low_signal = low(signal)
    project_bias = jnp.concatenate([vector_rows[4], jnp.zeros_like(vector_rows[4]), vector_rows[5]])
    projected = low_back(low(jnp.dot(low_signal, matrices[:, :3 * D], precision=HIGH) + project_bias))
    by_row = projected.reshape(ROWS, SEQ, 3, HEADS, HEAD_DIM)
    context = lax.map(jax.checkpoint(attend_row), (by_row[:, :, 0], by_row[:, :, 1], by_row[:, :, 2], segment_ids, group_tags, lengths))
    context = low_back(low(context.reshape(ROWS * SEQ, D)))
    attended = low_back(jnp.dot(context, matrices[:, 3 * D:4 * D], precision=HIGH) + vector_rows[6])
    middle = layer_norm(signal + attended, vector_rows[0], vector_rows[1])
    hidden_pre = low_back(jnp.dot(low(middle), matrices[:, 4 * D:4 * D + FF], precision=HIGH) + vector_rows[8:].reshape(FF))
    activation = low(gelu_tanh(hidden_pre))
    back_out = low_back(jnp.dot(activation, matrices[:, 4 * D + FF:].T, precision=HIGH) + vector_rows[7])
    return layer_norm(middle + back_out, vector_rows[2], vector_rows[3])

def reference(inputs, cotangent, lengths, segment_ids, group_tags, weights, first_moments, second_moments, vectors, vector_first, vector_second):
    matrices = low(weights)
    vector_rows = low(vectors)
    begin_acts = inputs.astype(jnp.float32).reshape(ROWS * SEQ, D)

    def forward(signal, matrix_in, vector_in):
        first_out = use_layer(signal, matrix_in, vector_in, segment_ids, group_tags, lengths)
        return use_layer(first_out, matrix_in, vector_in, segment_ids, group_tags, lengths)
    result, pull_back = jax.vjp(forward, begin_acts, matrices, vector_rows)
    grad_in, grad_w, grad_v = pull_back(cotangent.astype(jnp.float32).reshape(ROWS * SEQ, D))
    grad_norm = jnp.sqrt(jnp.sum(grad_w * grad_w) + jnp.sum(grad_v * grad_v))
    clip_limit = math.sqrt(D * WCOLS)
    factor = clip_limit / jnp.maximum(grad_norm, clip_limit)
    new_weights, new_first, new_second = adam_update(weights, first_moments, second_moments, grad_w * factor)
    new_vectors, new_vector_first, new_vector_second = adam_update(vectors, vector_first, vector_second, grad_v * factor)
    outputs = result.reshape(ROWS, SEQ, D).astype(jnp.bfloat16)
    input_grad = grad_in.reshape(ROWS, SEQ, D)
    return (outputs, input_grad, grad_w, grad_v, grad_norm, new_weights, new_first, new_second, new_vectors, new_vector_first, new_vector_second)
```

```python
import functools
import math

import jax
import jax.numpy as jnp
from jax import lax
from jax.experimental import pallas as pl
from jax.experimental.pallas import tpu as pltpu
from jax.sharding import PartitionSpec as P

D = 512
FF = 2048
HEADS = 8
HEAD_DIM = 64
STEP = 10
WCOLS = 6144

NORM_EPS = 1e-05
BETA_ONE = 0.5
BETA_TWO = 0.5
ADAM_EPS = 1e-08
DECAY = 0.01
WARMUP = 4000.0
RATE_SCALE = 150000.0

BF = jnp.bfloat16
F32 = jnp.float32
FAR = 1e30
SAFE_SCORE = 60.0
TILE = 256
VMEM_BYTES = 60 << 20


def params():
    return pltpu.CompilerParams(vmem_limit_bytes=VMEM_BYTES)


def cost(flops, bytes_accessed, transcendentals=0):
    return pl.CostEstimate(flops=int(flops), bytes_accessed=int(bytes_accessed), transcendentals=int(transcendentals))


def dg(left, right, left_dim, right_dim):
    return lax.dot_general(
        left, right, (((left_dim,), (right_dim,)), ((), ())), preferred_element_type=F32
    )


def whole(shape):
    return pl.BlockSpec(shape, lambda i: (0,) * len(shape))


def adam_update(master, moment_one, moment_two, gradient):
    moment_one = BETA_ONE * moment_one + (1.0 - BETA_ONE) * gradient
    moment_two = BETA_TWO * moment_two + (1.0 - BETA_TWO) * gradient * gradient
    step_rate = RATE_SCALE * D ** (-0.5) * min(STEP ** (-0.5), STEP * WARMUP ** (-1.5))
    fixed_first = moment_one / (1.0 - BETA_ONE**STEP)
    fixed_second = moment_two / (1.0 - BETA_TWO**STEP)
    master = master - step_rate * (
        fixed_first / (jnp.sqrt(fixed_second) + ADAM_EPS) + DECAY * master
    )
    return (master, moment_one, moment_two)


def attend_kernel(act_ref, wq_ref, wk_ref, wv_ref, bq_ref, bv_ref, kmask_ref, qmask_ref, e_ref, ctx_ref, qkv_ref, stat_ref):
    act = act_ref[...]
    tokens = act.shape[1]
    q = (dg(wq_ref[...], act, 0, 0) + bq_ref[...]).astype(BF) * jnp.asarray(HEAD_DIM**-0.5, BF)
    k = dg(wk_ref[...], act, 0, 0).astype(BF)
    v = (dg(wv_ref[...], act, 0, 0) + bv_ref[...]).astype(BF)
    qkv_ref[0] = q
    qkv_ref[1] = k
    qkv_ref[2] = v
    dead = kmask_ref[4:5, :].astype(F32)
    bound = jnp.zeros((1, 1), F32)
    selves = []
    for h in range(2):
        rows = slice(h * HEAD_DIM, (h + 1) * HEAD_DIM)
        qf, kf = q[rows].astype(F32), k[rows].astype(F32)
        selves.append(jnp.sum(qf * kf, axis=0, keepdims=True))
        q_top = jnp.max(jnp.sum(qf * qf, axis=0, keepdims=True), axis=1, keepdims=True)
        k_top = jnp.max(jnp.sum(kf * kf, axis=0, keepdims=True), axis=1, keepdims=True)
        bound = jnp.maximum(bound, q_top * k_top)
    safe = bound[0, 0] <= SAFE_SCORE * SAFE_SCORE

    def scores(h):
        rows = slice(h * HEAD_DIM, (h + 1) * HEAD_DIM)
        keys = jnp.concatenate([k[rows], kmask_ref[...]], axis=0).T
        queries = jnp.concatenate([q[rows], qmask_ref[...]], axis=0)
        return dg(keys, queries, 1, 0)

    def finish(h, e, e_self):
        rows = slice(h * HEAD_DIM, (h + 1) * HEAD_DIM)
        low_e = e.astype(BF)
        e_ref[h] = low_e
        total = jnp.sum(e, axis=0, keepdims=True) + e_self
        scale = 1.0 / total
        values = v[rows]
        mixed = dg(values, low_e, 1, 0) + values.astype(F32) * e_self.astype(BF).astype(F32)
        ctx_ref[rows, :] = (mixed * scale).astype(BF)
        stat_ref[h, 0:1, :] = scale
        stat_ref[h, 1:2, :] = e_self

    @pl.when(safe)
    def _():
        for h in range(2):
            finish(h, jnp.exp(scores(h)), jnp.exp(selves[h]) * dead)

    @pl.when(jnp.logical_not(safe))
    def _():
        for h in range(2):
            s = scores(h)
            own = jnp.where(dead > 0, selves[h], -FAR)
            top = jnp.maximum(jnp.max(s, axis=0, keepdims=True), own)
            finish(h, jnp.exp(s - top), jnp.exp(own - top) * dead)


def attend(act, w_qkv, bias_q, bias_v, kmask, qmask):
    width, tokens = act.shape
    pairs = width // (2 * HEAD_DIM)
    pair = 2 * HEAD_DIM
    heads = width // HEAD_DIM
    return pl.pallas_call(
        attend_kernel,
        name="attend",
        grid=(pairs,),
        in_specs=[
            whole((width, tokens)),
            pl.BlockSpec((width, pair), lambda i: (0, i)),
            pl.BlockSpec((width, pair), lambda i: (0, pairs + i)),
            pl.BlockSpec((width, pair), lambda i: (0, 2 * pairs + i)),
            pl.BlockSpec((pair, 1), lambda i: (i, 0)),
            pl.BlockSpec((pair, 1), lambda i: (i, 0)),
            whole((16, tokens)),
            whole((16, tokens)),
        ],
        out_specs=[
            pl.BlockSpec((2, tokens, tokens), lambda i: (i, 0, 0)),
            pl.BlockSpec((pair, tokens), lambda i: (i, 0)),
            pl.BlockSpec((3, pair, tokens), lambda i: (0, i, 0)),
            pl.BlockSpec((2, 2, tokens), lambda i: (i, 0, 0)),
        ],
        out_shape=[
            jax.ShapeDtypeStruct((heads, tokens, tokens), BF),
            jax.ShapeDtypeStruct((width, tokens), BF),
            jax.ShapeDtypeStruct((3, width, tokens), BF),
            jax.ShapeDtypeStruct((heads, 2, tokens), F32),
        ],
        compiler_params=params(),
        cost_estimate=cost(6 * width * width * tokens + 4 * width * tokens * tokens, 2 * heads * tokens * tokens, heads * tokens * tokens),
    )(act, w_qkv, w_qkv, w_qkv, bias_q, bias_v, kmask, qmask)


def attend_back_kernel(e_ref, qkv_ref, stat_ref, grad_ref, inner_ref, out_ref, ds_ref):
    for h in range(2):
        rows = slice(h * HEAD_DIM, (h + 1) * HEAD_DIM)
        q, k, v = qkv_ref[0, rows], qkv_ref[1, rows], qkv_ref[2, rows]
        grad = grad_ref[rows]
        inner = inner_ref[h]
        e_self = stat_ref[h, 1:2, :]
        grad_f = grad.astype(F32)
        ds = (e_ref[h].astype(F32) * (dg(v.T, grad, 1, 0) - inner)).astype(BF)
        ds_ref[h] = ds
        own = (e_self * (jnp.sum(grad_f * v.astype(F32), axis=0, keepdims=True) - inner)).astype(BF).astype(F32)
        scale = HEAD_DIM**-0.5
        out_ref[0, rows] = ((dg(k, ds, 1, 0) + k.astype(F32) * own) * scale).astype(BF)
        out_ref[2, rows] = (dg(grad, e_ref[h], 1, 1) + grad_f * e_self.astype(BF).astype(F32)).astype(BF)
        out_ref[1, rows] = (dg(q, ds_ref[h], 1, 1) + q.astype(F32) * own).astype(BF)


def attend_back(e, qkv, stat, grad, inner):
    heads, tokens, _ = e.shape
    width = grad.shape[0]
    pairs = heads // 2
    pair = 2 * HEAD_DIM
    return pl.pallas_call(
        attend_back_kernel,
        name="attend_back",
        grid=(pairs,),
        in_specs=[
            pl.BlockSpec((2, tokens, tokens), lambda i: (i, 0, 0)),
            pl.BlockSpec((3, pair, tokens), lambda i: (0, i, 0)),
            pl.BlockSpec((2, 2, tokens), lambda i: (i, 0, 0)),
            pl.BlockSpec((pair, tokens), lambda i: (i, 0)),
            pl.BlockSpec((2, 1, tokens), lambda i: (i, 0, 0)),
        ],
        out_specs=pl.BlockSpec((3, pair, tokens), lambda i: (0, i, 0)),
        out_shape=jax.ShapeDtypeStruct((3, width, tokens), BF),
        scratch_shapes=[pltpu.VMEM((2, tokens, tokens), BF)],
        compiler_params=params(),
        cost_estimate=cost(8 * width * tokens * tokens, 2 * heads * tokens * tokens),
    )(e, qkv, stat, grad, inner)


def normed(t):
    mean = jnp.mean(t, axis=0, keepdims=True)
    centred = t - mean
    rstd = lax.rsqrt(jnp.mean(centred * centred, axis=0, keepdims=True) + NORM_EPS)
    return centred * rstd, rstd


def normed_back(grad, unit, rstd, gain):
    scaled = grad * gain
    mean = jnp.mean(scaled, axis=0, keepdims=True)
    along = jnp.mean(scaled * unit, axis=0, keepdims=True)
    return rstd * (scaled - mean - unit * along)


def gelu_and_slope(t):
    square = t * t
    inside = jnp.tanh(t * (0.7978845608028654 + (0.7978845608028654 * 0.044715) * square))
    half = 0.5 + 0.5 * inside
    slope = half + (t * (0.5 - 0.5 * inside * inside)) * (
        0.7978845608028654 + (3.0 * 0.7978845608028654 * 0.044715) * square
    )
    return t * half, slope


def lanes_sum(t):
    out = t[:, 0:128]
    for j in range(128, t.shape[1], 128):
        out = out + t[:, j : j + 128]
    return out


def dense_forward(signal, ctx, wo_ref, win_ref, wback_ref, col_ref, bin_ref):
    joined = signal + dg(wo_ref[...], ctx, 0, 0) + col_ref[:, 6:7]
    unit_one, rstd_one = normed(joined)
    middle = unit_one * col_ref[:, 0:1] + col_ref[:, 1:2]
    low_middle = middle.astype(BF)
    pre = dg(win_ref[...], low_middle, 0, 0) + bin_ref[...]
    gelu, slope = gelu_and_slope(pre)
    act = gelu.astype(BF)
    summed = middle + dg(wback_ref[...], act, 1, 0) + col_ref[:, 7:8]
    unit_two, rstd_two = normed(summed)
    return unit_one, rstd_one, low_middle, slope, act, unit_two, rstd_two


def dense_back(grad, unit_one, rstd_one, slope, unit_two, rstd_two, ctx, stat_ref, wo_ref, win_ref, wback_ref, col_ref,
               sums_ref, joined_ref, gctx_ref, inner_ref, dz_ref, du_ref, dattn_ref):
    sums_ref[2] += lanes_sum(grad * unit_two)
    sums_ref[3] += lanes_sum(grad)
    grad_summed = normed_back(grad, unit_two, rstd_two, col_ref[:, 2:3])
    dz = grad_summed.astype(BF)
    dz_ref[...] = dz
    du = (dg(wback_ref[...], dz, 0, 0) * slope).astype(BF)
    du_ref[...] = du
    grad_middle = grad_summed + dg(win_ref[...], du, 1, 0)
    sums_ref[0] += lanes_sum(grad_middle * unit_one)
    sums_ref[1] += lanes_sum(grad_middle)
    grad_joined = normed_back(grad_middle, unit_one, rstd_one, col_ref[:, 0:1])
    joined_ref[...] = grad_joined
    dattn = grad_joined.astype(BF)
    dattn_ref[...] = dattn
    grad_ctx = dg(wo_ref[...], dattn, 1, 0)
    for h in range(HEADS):
        rows = slice(h * HEAD_DIM, (h + 1) * HEAD_DIM)
        part = (grad_ctx[rows] * stat_ref[h, 0:1, :]).astype(BF)
        gctx_ref[rows, :] = part
        inner_ref[h] = jnp.sum(part.astype(F32) * ctx[rows].astype(F32), axis=0, keepdims=True)


def first_dense_kernel(act_ref, ctx_ref, wo_ref, win_ref, wback_ref, col_ref, bin_ref,
                       unit_one_ref, unit_two_ref, rstd_ref, low_out_ref, act_out_ref, slope_ref):
    unit_one, rstd_one, _, slope, act, unit_two, rstd_two = dense_forward(
        act_ref[...].astype(F32), ctx_ref[...], wo_ref, win_ref, wback_ref, col_ref, bin_ref)
    unit_one_ref[...] = unit_one
    unit_two_ref[...] = unit_two
    rstd_ref[0:1, :] = rstd_one
    rstd_ref[1:2, :] = rstd_two
    act_out_ref[...] = act
    slope_ref[...] = slope.astype(BF)
    low_out_ref[...] = (unit_two * col_ref[:, 2:3] + col_ref[:, 3:4]).astype(BF)


def tile(rows):
    return pl.BlockSpec((rows, TILE), lambda i: (0, i))


def heads_tile(heads, rows):
    return pl.BlockSpec((heads, rows, TILE), lambda i: (0, 0, i))


def first_dense(act, ctx, w_o, w_in, w_back, columns, bias_in):
    width, tokens = act.shape
    hidden = w_in.shape[1]
    return pl.pallas_call(
        first_dense_kernel,
        name="first_dense",
        grid=(tokens // TILE,),
        in_specs=[tile(width), tile(width), whole(w_o.shape), whole(w_in.shape), whole(w_back.shape), whole(columns.shape), whole(bias_in.shape)],
        out_specs=[tile(width), tile(width), tile(8), tile(width), tile(hidden), tile(hidden)],
        out_shape=[
            jax.ShapeDtypeStruct((width, tokens), F32),
            jax.ShapeDtypeStruct((width, tokens), F32),
            jax.ShapeDtypeStruct((8, tokens), F32),
            jax.ShapeDtypeStruct((width, tokens), BF),
            jax.ShapeDtypeStruct((hidden, tokens), BF),
            jax.ShapeDtypeStruct((hidden, tokens), BF),
        ],
        compiler_params=params(),
        cost_estimate=cost(2 * tokens * width * (width + 2 * hidden), 24 << 20, tokens * hidden),
    )(act, ctx, w_o, w_in, w_back, columns, bias_in)


def second_dense_kernel(unit_ref, ctx_ref, cot_ref, stat_ref, wo_ref, win_ref, wback_ref, col_ref, bin_ref,
                        out_ref, sums_ref, joined_ref, gctx_ref, inner_ref, mid_ref, act_ref, dz_ref, du_ref, dattn_ref):
    @pl.when(pl.program_id(0) == 0)
    def _():
        sums_ref[...] = jnp.zeros(sums_ref.shape, F32)

    ctx = ctx_ref[...]
    signal = unit_ref[...] * col_ref[:, 2:3] + col_ref[:, 3:4]
    unit_one, rstd_one, low_middle, slope, act, unit_two, rstd_two = dense_forward(
        signal, ctx, wo_ref, win_ref, wback_ref, col_ref, bin_ref)
    mid_ref[...] = low_middle
    act_ref[...] = act
    out_ref[...] = (unit_two * col_ref[:, 2:3] + col_ref[:, 3:4]).astype(BF).T
    dense_back(cot_ref[...].astype(F32), unit_one, rstd_one, slope, unit_two, rstd_two, ctx, stat_ref,
               wo_ref, win_ref, wback_ref, col_ref, sums_ref, joined_ref, gctx_ref, inner_ref, dz_ref, du_ref, dattn_ref)


def second_dense(unit, ctx, cot, stat, w_o, w_in, w_back, columns, bias_in):
    width, tokens = unit.shape
    hidden = w_in.shape[1]
    heads = stat.shape[0]
    return pl.pallas_call(
        second_dense_kernel,
        name="second_dense",
        grid=(tokens // TILE,),
        in_specs=[tile(width), tile(width), tile(width), heads_tile(heads, 2),
                  whole(w_o.shape), whole(w_in.shape), whole(w_back.shape), whole(columns.shape), whole(bias_in.shape)],
        out_specs=[pl.BlockSpec((TILE, width), lambda i: (i, 0)), whole((4, width, 128)), tile(width), tile(width), heads_tile(heads, 1),
                   tile(width), tile(hidden), tile(width), tile(hidden), tile(width)],
        out_shape=[
            jax.ShapeDtypeStruct((tokens, width), BF),
            jax.ShapeDtypeStruct((4, width, 128), F32),
            jax.ShapeDtypeStruct((width, tokens), F32),
            jax.ShapeDtypeStruct((width, tokens), BF),
            jax.ShapeDtypeStruct((heads, 1, tokens), F32),
            jax.ShapeDtypeStruct((width, tokens), BF),
            jax.ShapeDtypeStruct((hidden, tokens), BF),
            jax.ShapeDtypeStruct((width, tokens), BF),
            jax.ShapeDtypeStruct((hidden, tokens), BF),
            jax.ShapeDtypeStruct((width, tokens), BF),
        ],
        compiler_params=params(),
        cost_estimate=cost(4 * tokens * width * (width + 2 * hidden), 28 << 20, tokens * hidden),
    )(unit, ctx, cot, stat, w_o, w_in, w_back, columns, bias_in)


def first_back_kernel(prior_ref, dqkv_ref, unit_one_ref, unit_two_ref, rstd_ref, slope_ref, ctx_ref, stat_ref, sums_in_ref,
                      wqkv_ref, wo_ref, win_ref, wback_ref, col_ref,
                      sums_ref, joined_ref, gctx_ref, inner_ref, mid_ref, dz_ref, du_ref, dattn_ref):
    @pl.when(pl.program_id(0) == 0)
    def _():
        sums_ref[...] = sums_in_ref[...]

    unit_one = unit_one_ref[...]
    mid_ref[...] = (unit_one * col_ref[:, 0:1] + col_ref[:, 1:2]).astype(BF)
    grad = prior_ref[...] + dg(wqkv_ref[...], dqkv_ref[...], 1, 0)
    dense_back(grad, unit_one, rstd_ref[0:1, :], slope_ref[...].astype(F32), unit_two_ref[...], rstd_ref[1:2, :], ctx_ref[...], stat_ref,
               wo_ref, win_ref, wback_ref, col_ref, sums_ref, joined_ref, gctx_ref, inner_ref, dz_ref, du_ref, dattn_ref)


def first_back(prior, dqkv, unit_one, unit_two, rstd, slope, ctx, stat, sums, w_qkv, w_o, w_in, w_back, columns):
    width, tokens = prior.shape
    hidden = w_in.shape[1]
    heads = stat.shape[0]
    return pl.pallas_call(
        first_back_kernel,
        name="first_back",
        grid=(tokens // TILE,),
        in_specs=[tile(width), tile(3 * width), tile(width), tile(width), tile(8), tile(hidden), tile(width), heads_tile(heads, 2), whole(sums.shape),
                  whole(w_qkv.shape), whole(w_o.shape), whole(w_in.shape), whole(w_back.shape), whole(columns.shape)],
        out_specs=[whole((4, width, 128)), tile(width), tile(width), heads_tile(heads, 1), tile(width), tile(width), tile(hidden), tile(width)],
        out_shape=[
            jax.ShapeDtypeStruct((4, width, 128), F32),
            jax.ShapeDtypeStruct((width, tokens), F32),
            jax.ShapeDtypeStruct((width, tokens), BF),
            jax.ShapeDtypeStruct((heads, 1, tokens), F32),
            jax.ShapeDtypeStruct((width, tokens), BF),
            jax.ShapeDtypeStruct((width, tokens), BF),
            jax.ShapeDtypeStruct((hidden, tokens), BF),
            jax.ShapeDtypeStruct((width, tokens), BF),
        ],
        compiler_params=params(),
        cost_estimate=cost(2 * tokens * width * (4 * width + 2 * hidden), 28 << 20),
    )(prior, dqkv, unit_one, unit_two, rstd, slope, ctx, stat, sums, w_qkv, w_o, w_in, w_back, columns)


def weight_kernel(la_ref, lb_ref, ra_ref, rb_ref, out_ref, sum_ref):
    ra, rb = ra_ref[...], rb_ref[...]
    out_ref[...] = (dg(la_ref[...], ra, 1, 1) + dg(lb_ref[...], rb, 1, 1)).astype(BF)
    ones = jnp.ones((16, ra.shape[1]), BF)
    sum_ref[...] = (dg(ones, ra, 1, 1) + dg(ones, rb, 1, 1))[0:8]


def weight_grad(left_one, left_two, right_one, right_two, block):
    rows, tokens = left_one.shape
    columns = right_one.shape[0]
    return pl.pallas_call(
        weight_kernel,
        name="weight_grad",
        grid=(columns // block,),
        in_specs=[whole((rows, tokens)), whole((rows, tokens)), pl.BlockSpec((block, tokens), lambda i: (i, 0)), pl.BlockSpec((block, tokens), lambda i: (i, 0))],
        out_specs=[pl.BlockSpec((rows, block), lambda i: (0, i)), pl.BlockSpec((8, block), lambda i: (0, i))],
        out_shape=[jax.ShapeDtypeStruct((rows, columns), BF), jax.ShapeDtypeStruct((8, columns), F32)],
        compiler_params=params(),
        cost_estimate=cost(4 * rows * columns * tokens, 4 * (rows + columns) * tokens + 2 * rows * columns),
    )(left_one, left_two, right_one, right_two)


def input_kernel(joined_ref, dqkv_ref, wqkv_ref, out_ref):
    out_ref[...] = (joined_ref[...] + dg(wqkv_ref[...], dqkv_ref[...], 1, 0)).T


def input_gradient(joined, dqkv, w_qkv):
    width, tokens = joined.shape
    return pl.pallas_call(
        input_kernel,
        name="input_gradient",
        grid=(tokens // TILE,),
        in_specs=[tile(width), tile(3 * width), whole(w_qkv.shape)],
        out_specs=pl.BlockSpec((TILE, width), lambda i: (i, 0)),
        out_shape=jax.ShapeDtypeStruct((tokens, width), F32),
        compiler_params=params(),
        cost_estimate=cost(6 * width * width * tokens, 8 << 20),
    )(joined, dqkv, w_qkv)


def masks(segments, tags, length):
    tokens = segments.shape[0]
    matches = segments[None, :] == jnp.arange(tags.shape[0], dtype=jnp.int32)[:, None]
    group = jnp.sum(jnp.where(matches, tags[:, None], 0), axis=0)
    live = jnp.arange(tokens, dtype=jnp.int32) < length
    kinds = jnp.arange(16, dtype=jnp.int32)[:, None]
    same = group[None, :] == kinds
    kmask = jnp.where(kinds < 4, (same & live[None, :]).astype(F32), jnp.where(kinds == 4, (~live)[None, :].astype(F32), 0.0))
    qmask = jnp.where(kinds < 4, jnp.where(same, 0.0, -FAR), jnp.where(kinds == 4, -FAR, 0.0))
    return kmask.astype(BF), jnp.broadcast_to(qmask, (16, tokens)).astype(BF)


def on_device(inputs, cotangent, lengths, segment_ids, group_tags, weights, first_moments, second_moments, vectors, vector_first, vector_second):
    row_count, tokens, width = inputs.shape
    matrices = lax.all_gather(weights.astype(BF), "shard", axis=0, tiled=True)
    low_vectors = lax.all_gather(vectors.astype(BF), "shard", axis=1, tiled=True)
    vector_rows = low_vectors.astype(F32)
    columns = vector_rows.T
    bias_in = vector_rows[8:].reshape(FF, 1)
    w_qkv = matrices[:, : 3 * D]
    w_o = matrices[:, 3 * D : 4 * D]
    w_in = matrices[:, 4 * D : 4 * D + FF]
    w_back = matrices[:, 4 * D + FF :]
    bias_q, bias_v = columns[:, 4:5], columns[:, 5:6]
    kmask, qmask = masks(segment_ids[0], group_tags[0], lengths[0])
    act_one = inputs[0].T
    cot = cotangent[0].T

    e_one, ctx_one, qkv_one, stat_one = attend(act_one, w_qkv, bias_q, bias_v, kmask, qmask)
    unit_one, unit_two, rstd, act_two, hid_one, slope = first_dense(act_one, ctx_one, w_o, w_in, w_back, columns, bias_in)
    e_two, ctx_two, qkv_two, stat_two = attend(act_two, w_qkv, bias_q, bias_v, kmask, qmask)
    outputs, sums, joined_two, gctx_two, inner_two, mid_two, hid_two, dz_two, du_two, dattn_two = second_dense(
        unit_two, ctx_two, cot, stat_two, w_o, w_in, w_back, columns, bias_in)
    dqkv_two = attend_back(e_two, qkv_two, stat_two, gctx_two, inner_two).reshape(3 * width, tokens)
    sums, joined_one, gctx_one, inner_one, mid_one, dz_one, du_one, dattn_one = first_back(
        joined_two, dqkv_two, unit_one, unit_two, rstd, slope, ctx_one, stat_one, sums, w_qkv, w_o, w_in, w_back, columns)
    grad_in, sum_in = weight_grad(mid_one, mid_two, du_one, du_two, 512)
    grad_back, _ = weight_grad(dz_one, dz_two, hid_one, hid_two, 512)
    grad_o, sum_o = weight_grad(ctx_one, ctx_two, dattn_one, dattn_two, 512)
    dqkv_one = attend_back(e_one, qkv_one, stat_one, gctx_one, inner_one).reshape(3 * width, tokens)
    grad_qkv, sum_qkv = weight_grad(act_one, act_two, dqkv_one, dqkv_two, 512)
    input_grad = input_gradient(joined_one, dqkv_one, w_qkv)
    sum_back = jnp.sum(dz_one.astype(F32), axis=1) + jnp.sum(dz_two.astype(F32), axis=1)
    small = jnp.sum(sums, axis=2)
    vector_grad = jnp.concatenate(
        [small, sum_qkv[0:1, :width], sum_qkv[0:1, 2 * width :], sum_o[0:1], sum_back[None], sum_in[0].reshape(FF // width, width)], axis=0)
    weight_grads = jnp.concatenate([grad_qkv, grad_o, grad_in, grad_back], axis=1)

    own_weight = lax.psum_scatter(weight_grads, "shard", scatter_dimension=0, tiled=True)
    own_vector = lax.psum_scatter(vector_grad.astype(BF), "shard", scatter_dimension=1, tiled=True)
    own_weight = lax.psum(own_weight, "batch").astype(F32)
    own_vector = lax.psum(own_vector, "batch").astype(F32)
    squares = lax.psum(jnp.sum(own_weight * own_weight) + jnp.sum(own_vector * own_vector), "shard")
    grad_norm = jnp.sqrt(squares)
    clip_limit = math.sqrt(D * WCOLS)
    factor = clip_limit / jnp.maximum(grad_norm, clip_limit)
    new_weights, new_first, new_second = adam_update(weights, first_moments, second_moments, own_weight * factor)
    new_vectors, new_vector_first, new_vector_second = adam_update(vectors, vector_first, vector_second, own_vector * factor)
    return (
        outputs[None],
        input_grad[None],
        own_weight,
        own_vector,
        grad_norm,
        new_weights,
        new_first,
        new_second,
        new_vectors,
        new_vector_first,
        new_vector_second,
    )


def solution(mesh):
    rows = ("batch", "shard")
    placed = (
        P(rows, None, None),
        P(rows, None, None),
        P(rows),
        P(rows, None),
        P(rows, None),
        P("shard", None),
        P("shard", None),
        P("shard", None),
        P(None, "shard"),
        P(None, "shard"),
        P(None, "shard"),
    )
    return jax.shard_map(
        on_device,
        mesh=mesh,
        in_specs=placed,
        out_specs=(
            P(rows, None, None),
            P(rows, None, None),
            P("shard", None),
            P(None, "shard"),
            P(),
            P("shard", None),
            P("shard", None),
            P("shard", None),
            P(None, "shard"),
            P(None, "shard"),
            P(None, "shard"),
        ),
        check_vma=False,
    )
```

```python
import functools
import math

import jax
import jax.numpy as jnp
from jax import lax
from jax.experimental import pallas as pl
from jax.experimental.pallas import tpu as pltpu
from jax.sharding import PartitionSpec as P

D = 512
FF = 2048
HEADS = 8
HEAD_DIM = 64
STEP = 10
WCOLS = 6144

NORM_EPS = 1e-05
BETA_ONE = 0.5
BETA_TWO = 0.5
ADAM_EPS = 1e-08
DECAY = 0.01
WARMUP = 4000.0
RATE_SCALE = 150000.0

BF = jnp.bfloat16
F32 = jnp.float32
FAR = 1e30
SAFE_SCORE = 60.0
TILE = 256
LANES = 128
VMEM_BYTES = 60 << 20


def params():
    return pltpu.CompilerParams(vmem_limit_bytes=VMEM_BYTES)


def cost(flops, bytes_accessed, transcendentals=0):
    return pl.CostEstimate(flops=int(flops), bytes_accessed=int(bytes_accessed), transcendentals=int(transcendentals))


def dg(left, right, left_dim, right_dim):
    return lax.dot_general(
        left, right, (((left_dim,), (right_dim,)), ((), ())), preferred_element_type=F32
    )


def whole(shape):
    return pl.BlockSpec(shape, lambda i: (0,) * len(shape))


def adam_update(master, moment_one, moment_two, gradient):
    moment_one = BETA_ONE * moment_one + (1.0 - BETA_ONE) * gradient
    moment_two = BETA_TWO * moment_two + (1.0 - BETA_TWO) * gradient * gradient
    step_rate = RATE_SCALE * D ** (-0.5) * min(STEP ** (-0.5), STEP * WARMUP ** (-1.5))
    fixed_first = moment_one / (1.0 - BETA_ONE**STEP)
    fixed_second = moment_two / (1.0 - BETA_TWO**STEP)
    master = master - step_rate * (
        fixed_first / (jnp.sqrt(fixed_second) + ADAM_EPS) + DECAY * master
    )
    return (master, moment_one, moment_two)


def attend_kernel(act_ref, wq_ref, wk_ref, wv_ref, col_ref, kmask_ref, qmask_ref, e_ref, ctx_ref, qkv_ref, stat_ref):
    act = act_ref[...]
    tokens = act.shape[1]
    q = (dg(wq_ref[...], act, 0, 0) + col_ref[:, 4:5].astype(F32)).astype(BF) * jnp.asarray(HEAD_DIM**-0.5, BF)
    k = dg(wk_ref[...], act, 0, 0).astype(BF)
    v = (dg(wv_ref[...], act, 0, 0) + col_ref[:, 5:6].astype(F32)).astype(BF)
    qkv_ref[0] = q
    qkv_ref[1] = k
    qkv_ref[2] = v
    dead = kmask_ref[4:5, :].astype(F32)
    bound = jnp.zeros((1, 1), F32)
    selves = []
    for h in range(2):
        rows = slice(h * HEAD_DIM, (h + 1) * HEAD_DIM)
        qf, kf = q[rows].astype(F32), k[rows].astype(F32)
        selves.append(jnp.sum(qf * kf, axis=0, keepdims=True))
        q_top = jnp.max(jnp.sum(qf * qf, axis=0, keepdims=True), axis=1, keepdims=True)
        k_top = jnp.max(jnp.sum(kf * kf, axis=0, keepdims=True), axis=1, keepdims=True)
        bound = jnp.maximum(bound, q_top * k_top)
    safe = bound[0, 0] <= SAFE_SCORE * SAFE_SCORE

    def scores(h):
        rows = slice(h * HEAD_DIM, (h + 1) * HEAD_DIM)
        keys = jnp.concatenate([k[rows], kmask_ref[...]], axis=0).T
        queries = jnp.concatenate([q[rows], qmask_ref[...]], axis=0)
        return dg(keys, queries, 1, 0)

    def finish(h, e, e_self):
        rows = slice(h * HEAD_DIM, (h + 1) * HEAD_DIM)
        low_e = e.astype(BF)
        e_ref[h] = low_e
        total = jnp.sum(e, axis=0, keepdims=True) + e_self
        scale = 1.0 / total
        values = v[rows]
        mixed = dg(values, low_e, 1, 0) + values.astype(F32) * e_self.astype(BF).astype(F32)
        ctx_ref[rows, :] = (mixed * scale).astype(BF)
        stat_ref[h, 0:1, :] = scale
        stat_ref[h, 1:2, :] = e_self

    @pl.when(safe)
    def _():
        for h in range(2):
            finish(h, jnp.exp(scores(h)), jnp.exp(selves[h]) * dead)

    @pl.when(jnp.logical_not(safe))
    def _():
        for h in range(2):
            s = scores(h)
            own = jnp.where(dead > 0, selves[h], -FAR)
            top = jnp.maximum(jnp.max(s, axis=0, keepdims=True), own)
            finish(h, jnp.exp(s - top), jnp.exp(own - top) * dead)


def attend(act, w_qkv, kmask, qmask):
    width, tokens = act.shape
    pairs = width // (2 * HEAD_DIM)
    pair = 2 * HEAD_DIM
    heads = width // HEAD_DIM
    return pl.pallas_call(
        attend_kernel,
        name="attend",
        grid=(pairs,),
        in_specs=[
            whole((width, tokens)),
            pl.BlockSpec((width, pair), lambda i: (0, i)),
            pl.BlockSpec((width, pair), lambda i: (0, pairs + i)),
            pl.BlockSpec((width, pair), lambda i: (0, 2 * pairs + i)),
            pl.BlockSpec((pair, pair), lambda i: (i, 3 * pairs)),
            whole((16, tokens)),
            whole((16, tokens)),
        ],
        out_specs=[
            pl.BlockSpec((2, tokens, tokens), lambda i: (i, 0, 0)),
            pl.BlockSpec((pair, tokens), lambda i: (i, 0)),
            pl.BlockSpec((3, pair, tokens), lambda i: (0, i, 0)),
            pl.BlockSpec((2, 2, tokens), lambda i: (i, 0, 0)),
        ],
        out_shape=[
            jax.ShapeDtypeStruct((heads, tokens, tokens), BF),
            jax.ShapeDtypeStruct((width, tokens), BF),
            jax.ShapeDtypeStruct((3, width, tokens), BF),
            jax.ShapeDtypeStruct((heads, 2, tokens), F32),
        ],
        compiler_params=params(),
        cost_estimate=cost(6 * width * width * tokens + 4 * width * tokens * tokens, 2 * heads * tokens * tokens, heads * tokens * tokens),
    )(act, w_qkv, w_qkv, w_qkv, w_qkv, kmask, qmask)


def attend_back_kernel(e_ref, qkv_ref, stat_ref, grad_ref, inner_ref, out_ref, ds_ref):
    for h in range(2):
        rows = slice(h * HEAD_DIM, (h + 1) * HEAD_DIM)
        q, k, v = qkv_ref[0, rows], qkv_ref[1, rows], qkv_ref[2, rows]
        grad = grad_ref[rows]
        inner = inner_ref[h]
        e_self = stat_ref[h, 1:2, :]
        grad_f = grad.astype(F32)
        ds = (e_ref[h].astype(F32) * (dg(v.T, grad, 1, 0) - inner)).astype(BF)
        ds_ref[h] = ds
        own = (e_self * (jnp.sum(grad_f * v.astype(F32), axis=0, keepdims=True) - inner)).astype(BF).astype(F32)
        scale = HEAD_DIM**-0.5
        out_ref[0, rows] = ((dg(k, ds, 1, 0) + k.astype(F32) * own) * scale).astype(BF)
        out_ref[2, rows] = (dg(grad, e_ref[h], 1, 1) + grad_f * e_self.astype(BF).astype(F32)).astype(BF)
        out_ref[1, rows] = (dg(q, ds_ref[h], 1, 1) + q.astype(F32) * own).astype(BF)


def attend_back(e, qkv, stat, grad, inner):
    heads, tokens, _ = e.shape
    width = grad.shape[0]
    pairs = heads // 2
    pair = 2 * HEAD_DIM
    return pl.pallas_call(
        attend_back_kernel,
        name="attend_back",
        grid=(pairs,),
        in_specs=[
            pl.BlockSpec((2, tokens, tokens), lambda i: (i, 0, 0)),
            pl.BlockSpec((3, pair, tokens), lambda i: (0, i, 0)),
            pl.BlockSpec((2, 2, tokens), lambda i: (i, 0, 0)),
            pl.BlockSpec((pair, tokens), lambda i: (i, 0)),
            pl.BlockSpec((2, 1, tokens), lambda i: (i, 0, 0)),
        ],
        out_specs=pl.BlockSpec((3, pair, tokens), lambda i: (0, i, 0)),
        out_shape=jax.ShapeDtypeStruct((3, width, tokens), BF),
        scratch_shapes=[pltpu.VMEM((2, tokens, tokens), BF)],
        compiler_params=params(),
        cost_estimate=cost(8 * width * tokens * tokens, 2 * heads * tokens * tokens),
    )(e, qkv, stat, grad, inner)


def normed(t):
    mean = jnp.mean(t, axis=0, keepdims=True)
    centred = t - mean
    rstd = lax.rsqrt(jnp.mean(centred * centred, axis=0, keepdims=True) + NORM_EPS)
    return centred * rstd, rstd


def normed_back(grad, unit, rstd, gain):
    scaled = grad * gain
    mean = jnp.mean(scaled, axis=0, keepdims=True)
    along = jnp.mean(scaled * unit, axis=0, keepdims=True)
    return rstd * (scaled - mean - unit * along)


def gelu_and_slope(t):
    square = t * t
    inside = jnp.tanh(t * (0.7978845608028654 + (0.7978845608028654 * 0.044715) * square))
    half = 0.5 + 0.5 * inside
    slope = half + (t * (0.5 - 0.5 * inside * inside)) * (
        0.7978845608028654 + (3.0 * 0.7978845608028654 * 0.044715) * square
    )
    return t * half, slope


def lanes_sum(t):
    out = t[:, 0:128]
    for j in range(128, t.shape[1], 128):
        out = out + t[:, j : j + 128]
    return out


def column(col_ref, j):
    return col_ref[:, j : j + 1].astype(F32)


def dense_forward(signal, ctx, wo_ref, win_ref, wback_ref, col_ref, act_ref, slope_ref):
    joined = signal + dg(wo_ref[...], ctx, 0, 0) + column(col_ref, 6)
    unit_one, rstd_one = normed(joined)
    middle = unit_one * column(col_ref, 0) + column(col_ref, 1)
    low_middle = middle.astype(BF)
    width = middle.shape[0]
    summed = middle + column(col_ref, 7)
    for c in range(win_ref.shape[1] // width):
        rows = slice(c * width, (c + 1) * width)
        pre = dg(win_ref[:, rows], low_middle, 0, 0) + column(col_ref, 8 + c)
        gelu, slope = gelu_and_slope(pre)
        act = gelu.astype(BF)
        act_ref[rows, :] = act
        slope_ref[rows, :] = slope.astype(slope_ref.dtype)
        summed = summed + dg(wback_ref[:, rows], act, 1, 0)
    unit_two, rstd_two = normed(summed)
    return unit_one, rstd_one, low_middle, unit_two, rstd_two


def dense_back(grad, unit_one, rstd_one, slope_ref, unit_two, rstd_two, ctx, stat_ref, wo_ref, win_ref, wback_ref, col_ref,
               sums_ref, joined_ref, gctx_ref, inner_ref, dz_ref, du_ref, dattn_ref):
    sums_ref[2] += lanes_sum(grad * unit_two)
    sums_ref[3] += lanes_sum(grad)
    grad_summed = normed_back(grad, unit_two, rstd_two, column(col_ref, 2))
    dz = grad_summed.astype(BF)
    dz_ref[...] = dz
    sums_ref[7] += lanes_sum(dz.astype(F32))
    width = dz.shape[0]
    grad_middle = grad_summed
    for c in range(win_ref.shape[1] // width):
        rows = slice(c * width, (c + 1) * width)
        du = (dg(wback_ref[:, rows], dz, 0, 0) * slope_ref[rows, :].astype(F32)).astype(BF)
        du_ref[rows, :] = du
        sums_ref[8 + c] += lanes_sum(du.astype(F32))
        grad_middle = grad_middle + dg(win_ref[:, rows], du, 1, 0)
    sums_ref[0] += lanes_sum(grad_middle * unit_one)
    sums_ref[1] += lanes_sum(grad_middle)
    grad_joined = normed_back(grad_middle, unit_one, rstd_one, column(col_ref, 0))
    joined_ref[...] = grad_joined
    dattn = grad_joined.astype(BF)
    dattn_ref[...] = dattn
    sums_ref[6] += lanes_sum(dattn.astype(F32))
    grad_ctx = dg(wo_ref[...], dattn, 1, 0)
    for h in range(stat_ref.shape[0]):
        rows = slice(h * HEAD_DIM, (h + 1) * HEAD_DIM)
        part = (grad_ctx[rows] * stat_ref[h, 0:1, :]).astype(BF)
        gctx_ref[rows, :] = part
        inner_ref[h] = jnp.sum(part.astype(F32) * ctx[rows].astype(F32), axis=0, keepdims=True)


def tile(rows):
    return pl.BlockSpec((rows, TILE), lambda i: (0, i))


def heads_tile(heads, rows):
    return pl.BlockSpec((heads, rows, TILE), lambda i: (0, 0, i))


def rest_specs(width, hidden):
    return [
        pl.BlockSpec((width, width), lambda i: (0, 2 * hidden // width)),
        pl.BlockSpec((width, hidden), lambda i: (0, 0)),
        pl.BlockSpec((width, hidden), lambda i: (0, 1)),
    ]


def column_spec(width):
    return pl.BlockSpec((width, LANES), lambda i: (0, 3 * width // LANES))


def first_dense_kernel(signal_ref, ctx_ref, wo_ref, win_ref, wback_ref, col_ref,
                       unit_one_ref, unit_two_ref, rstd_ref, low_out_ref, act_ref, slope_ref):
    unit_one, rstd_one, _, unit_two, rstd_two = dense_forward(
        signal_ref[...].astype(F32), ctx_ref[...], wo_ref, win_ref, wback_ref, col_ref, act_ref, slope_ref)
    unit_one_ref[...] = unit_one
    unit_two_ref[...] = unit_two
    rstd_ref[0:1, :] = rstd_one
    rstd_ref[1:2, :] = rstd_two
    low_out_ref[...] = (unit_two * column(col_ref, 2) + column(col_ref, 3)).astype(BF)


def first_dense(signal, ctx, w_rest, w_first):
    width, tokens = signal.shape
    hidden = (w_rest.shape[1] - width) // 2
    return pl.pallas_call(
        first_dense_kernel,
        name="first_dense",
        grid=(tokens // TILE,),
        in_specs=[tile(width), tile(width), *rest_specs(width, hidden), column_spec(width)],
        out_specs=[tile(width), tile(width), tile(8), tile(width), tile(hidden), tile(hidden)],
        out_shape=[
            jax.ShapeDtypeStruct((width, tokens), F32),
            jax.ShapeDtypeStruct((width, tokens), F32),
            jax.ShapeDtypeStruct((8, tokens), F32),
            jax.ShapeDtypeStruct((width, tokens), BF),
            jax.ShapeDtypeStruct((hidden, tokens), BF),
            jax.ShapeDtypeStruct((hidden, tokens), BF),
        ],
        compiler_params=params(),
        cost_estimate=cost(2 * tokens * width * (width + 2 * hidden), 24 << 20, tokens * hidden),
    )(signal, ctx, w_rest, w_rest, w_rest, w_first)


def second_dense_kernel(unit_ref, ctx_ref, cot_ref, stat_ref, wo_ref, win_ref, wback_ref, col_ref,
                        out_ref, sums_ref, joined_ref, gctx_ref, inner_ref, mid_ref, act_ref, dz_ref, du_ref, dattn_ref, slope_ref):
    @pl.when(pl.program_id(0) == 0)
    def _():
        sums_ref[...] = jnp.zeros(sums_ref.shape, F32)

    ctx = ctx_ref[...]
    gain, shift = column(col_ref, 2), column(col_ref, 3)
    unit_one, rstd_one, low_middle, unit_two, rstd_two = dense_forward(
        unit_ref[...] * gain + shift, ctx, wo_ref, win_ref, wback_ref, col_ref, act_ref, slope_ref)
    mid_ref[...] = low_middle
    out_ref[...] = (unit_two * gain + shift).astype(BF).T
    dense_back(cot_ref[...].astype(F32), unit_one, rstd_one, slope_ref, unit_two, rstd_two, ctx, stat_ref,
               wo_ref, win_ref, wback_ref, col_ref, sums_ref, joined_ref, gctx_ref, inner_ref, dz_ref, du_ref, dattn_ref)


def second_dense(unit, ctx, cot, stat, w_rest, w_first):
    width, tokens = unit.shape
    hidden = (w_rest.shape[1] - width) // 2
    heads = stat.shape[0]
    return pl.pallas_call(
        second_dense_kernel,
        name="second_dense",
        grid=(tokens // TILE,),
        in_specs=[tile(width), tile(width), tile(width), heads_tile(heads, 2), *rest_specs(width, hidden), column_spec(width)],
        out_specs=[pl.BlockSpec((TILE, width), lambda i: (i, 0)), whole((12, width, LANES)), tile(width), tile(width), heads_tile(heads, 1),
                   tile(width), tile(hidden), tile(width), tile(hidden), tile(width)],
        out_shape=[
            jax.ShapeDtypeStruct((tokens, width), BF),
            jax.ShapeDtypeStruct((12, width, LANES), F32),
            jax.ShapeDtypeStruct((width, tokens), F32),
            jax.ShapeDtypeStruct((width, tokens), BF),
            jax.ShapeDtypeStruct((heads, 1, tokens), F32),
            jax.ShapeDtypeStruct((width, tokens), BF),
            jax.ShapeDtypeStruct((hidden, tokens), BF),
            jax.ShapeDtypeStruct((width, tokens), BF),
            jax.ShapeDtypeStruct((hidden, tokens), BF),
            jax.ShapeDtypeStruct((width, tokens), BF),
        ],
        scratch_shapes=[pltpu.VMEM((hidden, TILE), F32)],
        compiler_params=params(),
        cost_estimate=cost(4 * tokens * width * (width + 2 * hidden), 28 << 20, tokens * hidden),
    )(unit, ctx, cot, stat, w_rest, w_rest, w_rest, w_first)


def first_back_kernel(prior_ref, dqkv_ref, unit_one_ref, unit_two_ref, rstd_ref, slope_ref, ctx_ref, stat_ref, sums_in_ref,
                      wqkv_ref, wo_ref, win_ref, wback_ref, col_ref,
                      vec_ref, joined_ref, gctx_ref, inner_ref, mid_ref, dz_ref, du_ref, dattn_ref, sums_ref):
    step = pl.program_id(0)

    @pl.when(step == 0)
    def _():
        sums_ref[...] = sums_in_ref[...]

    unit_one = unit_one_ref[...]
    mid_ref[...] = (unit_one * column(col_ref, 0) + column(col_ref, 1)).astype(BF)
    grad = prior_ref[...] + dg(wqkv_ref[...], dqkv_ref[...], 1, 0)
    dense_back(grad, unit_one, rstd_ref[0:1, :], slope_ref, unit_two_ref[...], rstd_ref[1:2, :], ctx_ref[...], stat_ref,
               wo_ref, win_ref, wback_ref, col_ref, sums_ref, joined_ref, gctx_ref, inner_ref, dz_ref, du_ref, dattn_ref)

    @pl.when(step == pl.num_programs(0) - 1)
    def _():
        lane = lax.broadcasted_iota(jnp.int32, vec_ref.shape, 1)
        out = jnp.zeros(vec_ref.shape, F32)
        for j in (0, 1, 2, 3, 6, 7, 8, 9, 10, 11):
            out = jnp.where(lane == j, jnp.sum(sums_ref[j], axis=1, keepdims=True), out)
        vec_ref[...] = out


def first_back(prior, dqkv, unit_one, unit_two, rstd, slope, ctx, stat, sums, w_first, w_rest):
    width, tokens = prior.shape
    hidden = (w_rest.shape[1] - width) // 2
    heads = stat.shape[0]
    return pl.pallas_call(
        first_back_kernel,
        name="first_back",
        grid=(tokens // TILE,),
        in_specs=[tile(width), tile(3 * width), tile(width), tile(width), tile(8), tile(hidden), tile(width), heads_tile(heads, 2), whole(sums.shape),
                  pl.BlockSpec((width, 3 * width), lambda i: (0, 0)), *rest_specs(width, hidden), column_spec(width)],
        out_specs=[whole((width, LANES)), tile(width), tile(width), heads_tile(heads, 1), tile(width), tile(width), tile(hidden), tile(width)],
        out_shape=[
            jax.ShapeDtypeStruct((width, LANES), F32),
            jax.ShapeDtypeStruct((width, tokens), F32),
            jax.ShapeDtypeStruct((width, tokens), BF),
            jax.ShapeDtypeStruct((heads, 1, tokens), F32),
            jax.ShapeDtypeStruct((width, tokens), BF),
            jax.ShapeDtypeStruct((width, tokens), BF),
            jax.ShapeDtypeStruct((hidden, tokens), BF),
            jax.ShapeDtypeStruct((width, tokens), BF),
        ],
        scratch_shapes=[pltpu.VMEM((12, width, LANES), F32)],
        compiler_params=params(),
        cost_estimate=cost(2 * tokens * width * (4 * width + 2 * hidden), 28 << 20),
    )(prior, dqkv, unit_one, unit_two, rstd, slope, ctx, stat, sums, w_first, w_rest, w_rest, w_rest, w_first)


class Layout:
    def __init__(self, mesh_batch, mesh_shard, width):
        self.batch = mesh_batch
        self.shards = mesh_shard
        self.parts = min(mesh_batch, width // mesh_shard // 16)
        self.planes = self.parts // 2
        self.rows = width // mesh_shard // self.parts

    def swap(self, value, axis, distance):
        size = self.batch if axis == "batch" else self.shards
        return lax.ppermute(value, axis, [(i, i ^ distance) for i in range(size)])

    def place(self):
        return jnp.stack([lax.axis_index("batch") % self.parts, lax.axis_index("shard")]).astype(jnp.int32)

    def row_of(self, place_ref, c, e, d):
        block = (place_ref[1] ^ d) * self.parts + (place_ref[0] ^ (2 * e + c))
        return pl.multiple_of(block * self.rows, self.rows)

    def gather(self, mine):
        stack = jnp.concatenate([mine] + [self.swap(mine, "shard", d) for d in range(1, self.shards)], axis=0)
        plane = [stack] + [self.swap(stack, "batch", 2 * e) for e in range(1, self.planes)]
        return plane + [self.swap(s, "batch", 1) for s in plane]

    def reduce(self, keep, send):
        half = add(keep, self.swap(send, "batch", 1))
        rows = half.shape[0] // self.planes
        parts = [half[e * rows : (e + 1) * rows] for e in range(self.planes)]
        whole_plane = add(parts[0], *[self.swap(parts[e], "batch", 2 * e) for e in range(1, self.planes)])
        blocks = [whole_plane[d * self.rows : (d + 1) * self.rows] for d in range(self.shards)]
        own = add(blocks[0], *[self.swap(blocks[d], "shard", d) for d in range(1, self.shards)])
        distance = self.parts
        while distance < self.batch:
            own = add(own, self.swap(own, "batch", distance))
            distance *= 2
        return own

    def total(self, own):
        own = tree([own] + [self.swap(own, "shard", d) for d in range(1, self.shards)])
        own = tree([own] + [self.swap(own, "batch", 2 * e) for e in range(1, self.planes)])
        return own + self.swap(own, "batch", 1)

    def spread(self, own):
        plane = [own] + [self.swap(own, "batch", 2 * e) for e in range(1, self.planes)]
        other = [self.swap(s, "batch", 1) for s in plane]
        return jnp.concatenate([t for pair in zip(plane, other, strict=True) for t in pair], axis=0)


def tree(values):
    while len(values) > 1:
        values = [a + b for a, b in zip(values[::2], values[1::2], strict=True)]
    return values[0]


def add(first, *others):
    total = first.astype(F32)
    for other in others:
        total = total + other.astype(F32)
    return total.astype(BF)


def collect_kernel(layout, place_ref, *refs):
    sources, out_ref, sem = refs[:-2], refs[-2], refs[-1]
    copies = []
    for c in range(2):
        for e in range(layout.planes):
            for d in range(layout.shards):
                copies.append(pltpu.make_async_copy(
                    sources[c * layout.planes + e].at[pl.ds(d * layout.rows, layout.rows)],
                    out_ref.at[pl.ds(layout.row_of(place_ref, c, e, d), layout.rows)],
                    sem.at[len(copies)],
                ))
    for copy in copies:
        copy.start()
    for copy in copies:
        copy.wait()


def collect(layout, place, sources):
    rows = layout.rows * layout.parts * layout.shards
    columns = sources[0].shape[1]
    return pl.pallas_call(
        functools.partial(collect_kernel, layout),
        name="collect",
        in_specs=[pl.BlockSpec(memory_space=pltpu.SMEM)] + [pl.BlockSpec(memory_space=pl.ANY)] * len(sources),
        out_specs=pl.BlockSpec(memory_space=pl.ANY),
        out_shape=jax.ShapeDtypeStruct((rows, columns), BF),
        scratch_shapes=[pltpu.SemaphoreType.DMA((layout.parts * layout.shards,))],
        compiler_params=params(),
        cost_estimate=cost(0, 4 * rows * columns),
    )(place, *sources)


def in_order(layout, place_ref, source_ref, target_ref):
    at = 0
    for c in range(2):
        for e in range(layout.planes):
            for d in range(layout.shards):
                target_ref[at : at + layout.rows] = source_ref[pl.ds(layout.row_of(place_ref, c, e, d), layout.rows), :]
                at += layout.rows


def weight_kernel(layout, place_ref, la_ref, lb_ref, ra_ref, rb_ref, keep_ref, send_ref, left_ref):
    @pl.when(pl.program_id(0) == 0)
    def _():
        in_order(layout, place_ref, la_ref, left_ref.at[0])
        in_order(layout, place_ref, lb_ref, left_ref.at[1])

    out = (dg(left_ref[0], ra_ref[...], 1, 1) + dg(left_ref[1], rb_ref[...], 1, 1)).astype(BF)
    half = out.shape[0] // 2
    keep_ref[...] = out[:half]
    send_ref[...] = out[half:]


def weight_grad(layout, place, left_one, left_two, right_one, right_two, block):
    rows, tokens = left_one.shape
    columns = right_one.shape[0]
    half = jax.ShapeDtypeStruct((rows // 2, columns), BF)
    return pl.pallas_call(
        functools.partial(weight_kernel, layout),
        name="weight_grad",
        grid=(columns // block,),
        in_specs=[pl.BlockSpec(memory_space=pltpu.SMEM), whole((rows, tokens)), whole((rows, tokens)),
                  pl.BlockSpec((block, tokens), lambda i: (i, 0)), pl.BlockSpec((block, tokens), lambda i: (i, 0))],
        out_specs=[pl.BlockSpec((rows // 2, block), lambda i: (0, i))] * 2,
        out_shape=[half, half],
        scratch_shapes=[pltpu.VMEM((2, rows, tokens), BF)],
        compiler_params=params(),
        cost_estimate=cost(4 * rows * columns * tokens, 4 * (rows + columns) * tokens + 2 * rows * columns),
    )(place, left_one, left_two, right_one, right_two)


def last_back_kernel(layout, first_pair, place_ref, e_ref, qkv_ref, stat_ref, grad_ref, inner_ref, act_one_ref, act_two_ref, dqkv_two_ref, vec_in_ref,
                     out_ref, keep_ref, send_ref, vec_ref, vec_keep_ref, vec_send_ref, ds_ref, left_ref, order_ref):
    step = pl.program_id(0)

    @pl.when(step == 0)
    def _():
        in_order(layout, place_ref, act_one_ref, left_ref.at[0])
        in_order(layout, place_ref, act_two_ref, left_ref.at[1])
        vec_ref[...] = vec_in_ref[...]

    attend_back_kernel(e_ref, qkv_ref, stat_ref, grad_ref, inner_ref, out_ref, ds_ref)
    pair = out_ref.shape[1]
    for t in range(3):
        total = (dg(left_ref[0], out_ref[t], 1, 1) + dg(left_ref[1], dqkv_two_ref[t], 1, 1)).astype(BF)
        half = total.shape[0] // 2
        keep_ref[:, t * pair : (t + 1) * pair] = total[:half]
        send_ref[:, t * pair : (t + 1) * pair] = total[half:]
    rows = pl.ds(pl.multiple_of((first_pair + step) * pair, pair), pair)
    lane = lax.broadcasted_iota(jnp.int32, (pair, LANES), 1)
    vec = vec_ref[rows, :]
    for lane_at, t in ((4, 0), (5, 2)):
        both = lanes_sum(out_ref[t].astype(F32)) + lanes_sum(dqkv_two_ref[t].astype(F32))
        vec = jnp.where(lane == lane_at, jnp.sum(both, axis=1, keepdims=True), vec)
    vec_ref[rows, :] = vec

    @pl.when(step == pl.num_programs(0) - 1)
    def _():
        in_order(layout, place_ref, vec_ref, order_ref)
        half = order_ref.shape[0] // 2
        vec_keep_ref[...] = order_ref[0:half].astype(BF)
        vec_send_ref[...] = order_ref[half:].astype(BF)


def last_back(layout, place, first_pair, pairs, e, qkv, stat, grad, inner, act_one, act_two, dqkv_two, vec):
    heads, tokens, _ = e.shape
    width = grad.shape[0]
    pair = 2 * HEAD_DIM
    half = jax.ShapeDtypeStruct((width // 2, 3 * pair * pairs), BF)
    vec_half = jax.ShapeDtypeStruct((width // 2, LANES), BF)
    return pl.pallas_call(
        functools.partial(last_back_kernel, layout, first_pair),
        name="last_back",
        grid=(pairs,),
        in_specs=[
            pl.BlockSpec(memory_space=pltpu.SMEM),
            pl.BlockSpec((2, tokens, tokens), lambda i: (first_pair + i, 0, 0)),
            pl.BlockSpec((3, pair, tokens), lambda i: (0, first_pair + i, 0)),
            pl.BlockSpec((2, 2, tokens), lambda i: (first_pair + i, 0, 0)),
            pl.BlockSpec((pair, tokens), lambda i: (first_pair + i, 0)),
            pl.BlockSpec((2, 1, tokens), lambda i: (first_pair + i, 0, 0)),
            whole((width, tokens)),
            whole((width, tokens)),
            pl.BlockSpec((3, pair, tokens), lambda i: (0, first_pair + i, 0)),
            whole((width, LANES)),
        ],
        out_specs=[
            pl.BlockSpec((3, pair, tokens), lambda i: (0, i, 0)),
            pl.BlockSpec((width // 2, 3 * pair), lambda i: (0, i)),
            pl.BlockSpec((width // 2, 3 * pair), lambda i: (0, i)),
            whole((width, LANES)),
            whole((width // 2, LANES)),
            whole((width // 2, LANES)),
        ],
        out_shape=[
            jax.ShapeDtypeStruct((3, pair * pairs, tokens), BF),
            half,
            half,
            jax.ShapeDtypeStruct((width, LANES), F32),
            vec_half,
            vec_half,
        ],
        scratch_shapes=[pltpu.VMEM((2, tokens, tokens), BF), pltpu.VMEM((2, width, tokens), BF), pltpu.VMEM((width, LANES), F32)],
        compiler_params=params(),
        cost_estimate=cost(pairs * (16 * pair * tokens * tokens + 12 * width * pair * tokens), pairs * 4 * tokens * tokens + 4 * width * tokens),
    )(place, e, qkv, stat, grad, inner, act_one, act_two, dqkv_two, vec)


def input_kernel(joined_ref, *refs):
    pieces, w_ref, out_ref = refs[:-2], refs[-2], refs[-1]
    total = joined_ref[...]
    pair = 2 * HEAD_DIM
    width = total.shape[0]
    at = 0
    for piece in pieces:
        rows = piece.shape[1]
        for t in range(3):
            total = total + dg(w_ref[:, t * width + at : t * width + at + rows], piece[t], 1, 0)
        at += rows
    out_ref[...] = total.T


def input_gradient(joined, pieces, w_first):
    width, tokens = joined.shape
    return pl.pallas_call(
        input_kernel,
        name="input_gradient",
        grid=(tokens // TILE,),
        in_specs=[tile(width)] + [heads_tile(3, p.shape[1]) for p in pieces] + [pl.BlockSpec((width, 3 * width), lambda i: (0, 0))],
        out_specs=pl.BlockSpec((TILE, width), lambda i: (i, 0)),
        out_shape=jax.ShapeDtypeStruct((tokens, width), F32),
        compiler_params=params(),
        cost_estimate=cost(6 * width * width * tokens, 8 << 20),
    )(joined, *pieces, w_first)


def adam_kernel(pieces, place_ref, factor_ref, *refs):
    del place_ref
    grads = refs[: len(pieces)]
    w_ref, one_ref, two_ref, vec_ref, v_ref, vone_ref, vtwo_ref = refs[len(pieces) : len(pieces) + 7]
    gw_ref, nw_ref, none_ref, ntwo_ref, gv_ref, nv_ref, nvone_ref, nvtwo_ref, hold_ref = refs[len(pieces) + 7 :]
    factor = factor_ref[0]
    for grad_ref, spans in zip(grads, pieces, strict=True):
        for source, target, size in spans:
            to = slice(target, target + size)
            grad = grad_ref[:, source : source + size].astype(F32)
            gw_ref[:, to] = grad
            nw_ref[:, to], none_ref[:, to], ntwo_ref[:, to] = adam_update(w_ref[:, to], one_ref[:, to], two_ref[:, to], grad * factor)
    step = pl.program_id(0)
    rows = vec_ref.shape[0]
    hold_ref[pl.ds(pl.multiple_of(step * rows, rows), rows), :] = vec_ref[...].astype(F32)

    @pl.when(step == pl.num_programs(0) - 1)
    def _():
        grad = hold_ref[...].T[0 : gv_ref.shape[0], 0 : gv_ref.shape[1]]
        gv_ref[...] = grad
        nv_ref[...], nvone_ref[...], nvtwo_ref[...] = adam_update(v_ref[...], vone_ref[...], vtwo_ref[...], grad * factor)


def adam(layout, place, factor, pieces, grads, vec, weights, first, second, vectors, vector_first, vector_second):
    rows, columns = weights.shape
    block = layout.rows
    natural = pl.BlockSpec((block, columns), lambda i, place, factor: (i, 0))
    small = pl.BlockSpec(vectors.shape, lambda i, place, factor: (0, 0))

    def relative(width):
        return pl.BlockSpec((block, width), lambda i, place, factor: (i ^ place[0], 0))

    big = jax.ShapeDtypeStruct((rows, columns), F32)
    little = jax.ShapeDtypeStruct(vectors.shape, F32)
    return pl.pallas_call(
        functools.partial(adam_kernel, pieces),
        name="adam",
        grid_spec=pltpu.PrefetchScalarGridSpec(
            num_scalar_prefetch=2,
            grid=(rows // block,),
            in_specs=[relative(g.shape[1]) for g in grads] + [natural] * 3 + [relative(LANES)] + [small] * 3,
            out_specs=[natural] * 4 + [small] * 4,
            scratch_shapes=[pltpu.VMEM((LANES, LANES), F32)],
        ),
        out_shape=[big] * 4 + [little] * 4,
        compiler_params=params(),
        cost_estimate=cost(20 * rows * columns, 30 * rows * columns, rows * columns),
    )(place, factor, *grads, weights, first, second, vec, vectors, vector_first, vector_second)


def masks(segments, tags, length):
    tokens = segments.shape[0]
    matches = segments[None, :] == jnp.arange(tags.shape[0], dtype=jnp.int32)[:, None]
    group = jnp.sum(jnp.where(matches, tags[:, None], 0), axis=0)
    live = jnp.arange(tokens, dtype=jnp.int32) < length
    kinds = jnp.arange(16, dtype=jnp.int32)[:, None]
    same = group[None, :] == kinds
    kmask = jnp.where(kinds < 4, (same & live[None, :]).astype(F32), jnp.where(kinds == 4, (~live)[None, :].astype(F32), 0.0))
    qmask = jnp.where(kinds < 4, jnp.where(same, 0.0, -FAR), jnp.where(kinds == 4, -FAR, 0.0))
    return kmask.astype(BF), jnp.broadcast_to(qmask, (16, tokens)).astype(BF)


def squares(t):
    return jnp.sum(jnp.square(t.astype(F32)))


def on_device(layout, inputs, cotangent, lengths, segment_ids, group_tags, weights, first_moments, second_moments, vectors, vector_first, vector_second):
    _, tokens, width = inputs.shape
    hidden = (weights.shape[1] - 4 * width) // 2
    pair = 2 * HEAD_DIM
    place = layout.place()
    at = place[0] * layout.rows
    my_weights = lax.dynamic_slice_in_dim(weights, at, layout.rows, 0).astype(BF)
    my_vectors = lax.dynamic_slice_in_dim(jnp.pad(vectors.T, ((0, 0), (0, LANES - vectors.shape[0]))), at, layout.rows, 0).astype(BF)
    first_blocks = layout.gather(jnp.concatenate([my_weights[:, : 3 * width], my_vectors], axis=1))
    rest_blocks = layout.gather(jnp.concatenate([my_weights[:, 4 * width :], my_weights[:, 3 * width : 4 * width]], axis=1))
    kmask, qmask = masks(segment_ids[0], group_tags[0], lengths[0])
    act_one = inputs[0].T
    cot = cotangent[0].T

    w_first = collect(layout, place, first_blocks)
    e_one, ctx_one, qkv_one, stat_one = attend(act_one, w_first, kmask, qmask)
    w_rest = collect(layout, place, rest_blocks)
    unit_one, unit_two, rstd, act_two, hid_one, slope = first_dense(act_one, ctx_one, w_rest, w_first)
    e_two, ctx_two, qkv_two, stat_two = attend(act_two, w_first, kmask, qmask)
    outputs, sums, joined_two, gctx_two, inner_two, mid_two, hid_two, dz_two, du_two, dattn_two = second_dense(
        unit_two, ctx_two, cot, stat_two, w_rest, w_first)
    dqkv_two = attend_back(e_two, qkv_two, stat_two, gctx_two, inner_two)
    vec, joined_one, gctx_one, inner_one, mid_one, dz_one, du_one, dattn_one = first_back(
        joined_two, dqkv_two.reshape(3 * width, tokens), unit_one, unit_two, rstd, slope, ctx_one, stat_one, sums, w_first, w_rest)

    owned = []
    owned.append(layout.reduce(*weight_grad(layout, place, mid_one, mid_two, du_one, du_two, width)))
    owned.append(layout.reduce(*weight_grad(layout, place, dz_one, dz_two, hid_one, hid_two, width)))
    owned.append(layout.reduce(*weight_grad(layout, place, ctx_one, ctx_two, dattn_one, dattn_two, width)))
    spans = [[(0, 4 * width, hidden)], [(0, 4 * width + hidden, hidden)], [(0, 3 * width, width)]]
    pairs = width // pair
    group = pairs // 2
    dqkv = []
    for start in range(0, pairs, group):
        out, keep, send, vec, vec_keep, vec_send = last_back(
            layout, place, start, group, e_one, qkv_one, stat_one, gctx_one, inner_one, act_one, act_two, dqkv_two, vec)
        dqkv.append(out)
        spans.append([((i * 3 + t) * pair, t * width + (start + i) * pair, pair) for i in range(group) for t in range(3)])
        if start + group == pairs:
            keep, send = jnp.concatenate([keep, vec_keep], axis=1), jnp.concatenate([send, vec_send], axis=1)
        owned.append(layout.reduce(keep, send))
    grads = [layout.spread(t) for t in owned]
    vec_grad = grads[-1][:, 3 * pair * group :]
    grad_norm = jnp.sqrt(layout.total(sum(squares(t) for t in owned)))
    input_grad = input_gradient(joined_one, dqkv, w_first)
    clip_limit = math.sqrt(width * weights.shape[1])
    factor = clip_limit / jnp.maximum(grad_norm, clip_limit)
    updated = adam(layout, place, factor.reshape(1), spans, grads, vec_grad, weights, first_moments, second_moments, vectors, vector_first, vector_second)
    grad_w, new_weights, new_first, new_second, grad_v, new_vectors, new_vector_first, new_vector_second = updated
    return (
        outputs[None],
        input_grad[None],
        grad_w,
        grad_v,
        grad_norm,
        new_weights,
        new_first,
        new_second,
        new_vectors,
        new_vector_first,
        new_vector_second,
    )


def solution(mesh):
    rows = ("batch", "shard")
    placed = (
        P(rows, None, None),
        P(rows, None, None),
        P(rows),
        P(rows, None),
        P(rows, None),
        P("shard", None),
        P("shard", None),
        P("shard", None),
        P(None, "shard"),
        P(None, "shard"),
        P(None, "shard"),
    )
    return jax.shard_map(
        functools.partial(on_device, Layout(mesh.shape["batch"], mesh.shape["shard"], D)),
        mesh=mesh,
        in_specs=placed,
        out_specs=(
            P(rows, None, None),
            P(rows, None, None),
            P("shard", None),
            P(None, "shard"),
            P(),
            P("shard", None),
            P("shard", None),
            P("shard", None),
            P(None, "shard"),
            P(None, "shard"),
            P(None, "shard"),
        ),
        check_vma=False,
    )
```

```python
import functools
import math

import jax
import jax.numpy as jnp
from jax import lax
from jax.experimental import pallas as pl
from jax.experimental.pallas import tpu as pltpu
from jax.sharding import PartitionSpec as P

D = 512
FF = 2048
HEADS = 8
HEAD_DIM = 64
STEP = 10
WCOLS = 6144

NORM_EPS = 1e-05
BETA_ONE = 0.5
BETA_TWO = 0.5
ADAM_EPS = 1e-08
DECAY = 0.01
WARMUP = 4000.0
RATE_SCALE = 150000.0

BF = jnp.bfloat16
F32 = jnp.float32
FAR = 1e30
SAFE_SCORE = 60.0
TILE = 256
LANES = 128
VMEM_BYTES = 60 << 20


def params():
    return pltpu.CompilerParams(vmem_limit_bytes=VMEM_BYTES)


def cost(flops, bytes_accessed, transcendentals=0):
    return pl.CostEstimate(flops=int(flops), bytes_accessed=int(bytes_accessed), transcendentals=int(transcendentals))


def dg(left, right, left_dim, right_dim):
    return lax.dot_general(
        left, right, (((left_dim,), (right_dim,)), ((), ())), preferred_element_type=F32
    )


def whole(shape):
    return pl.BlockSpec(shape, lambda i: (0,) * len(shape))


def adam_update(master, moment_one, moment_two, gradient):
    moment_one = BETA_ONE * moment_one + (1.0 - BETA_ONE) * gradient
    moment_two = BETA_TWO * moment_two + (1.0 - BETA_TWO) * gradient * gradient
    step_rate = RATE_SCALE * D ** (-0.5) * min(STEP ** (-0.5), STEP * WARMUP ** (-1.5))
    fixed_first = moment_one / (1.0 - BETA_ONE**STEP)
    fixed_second = moment_two / (1.0 - BETA_TWO**STEP)
    master = master - step_rate * (
        fixed_first / (jnp.sqrt(fixed_second) + ADAM_EPS) + DECAY * master
    )
    return (master, moment_one, moment_two)


def attend_kernel(act_ref, wq_ref, wk_ref, wv_ref, col_ref, kmask_ref, qmask_ref, token_ref, e_ref, ctx_ref, qkv_ref, stat_ref):
    act = act_ref[...]
    tokens = act.shape[1]
    q = (dg(wq_ref[...], act, 0, 0) + col_ref[:, 4:5].astype(F32)).astype(BF) * jnp.asarray(HEAD_DIM**-0.5, BF)
    k = dg(wk_ref[...], act, 0, 0).astype(BF)
    v = (dg(wv_ref[...], act, 0, 0) + col_ref[:, 5:6].astype(F32)).astype(BF)
    qkv_ref[0] = q
    qkv_ref[1] = k
    qkv_ref[2] = v
    dead = kmask_ref[4:5, :].astype(F32)
    bound = jnp.zeros((1, 1), F32)
    selves = []
    for h in range(2):
        rows = slice(h * HEAD_DIM, (h + 1) * HEAD_DIM)
        qf, kf = q[rows].astype(F32), k[rows].astype(F32)
        selves.append(jnp.sum(qf * kf, axis=0, keepdims=True))
        q_top = jnp.max(jnp.sum(qf * qf, axis=0, keepdims=True), axis=1, keepdims=True)
        k_top = jnp.max(jnp.sum(kf * kf, axis=0, keepdims=True), axis=1, keepdims=True)
        bound = jnp.maximum(bound, q_top * k_top)
    safe = bound[0, 0] <= SAFE_SCORE * SAFE_SCORE

    def scores(h):
        rows = slice(h * HEAD_DIM, (h + 1) * HEAD_DIM)
        keys = jnp.concatenate([k[rows], kmask_ref[...]], axis=0).T
        queries = jnp.concatenate([q[rows], qmask_ref[...]], axis=0)
        return dg(keys, queries, 1, 0)

    def finish(h, e, e_self):
        rows = slice(h * HEAD_DIM, (h + 1) * HEAD_DIM)
        low_e = e.astype(BF)
        e_ref[h] = low_e
        total = jnp.sum(e, axis=0, keepdims=True) + e_self
        scale = 1.0 / total
        values = v[rows]
        mixed = dg(values, low_e, 1, 0) + values.astype(F32) * e_self.astype(BF).astype(F32)
        ctx_ref[rows, :] = (mixed * scale).astype(BF)
        stat_ref[h, 0:1, :] = scale
        stat_ref[h, 1:2, :] = e_self

    @pl.when(safe)
    def _():
        for h in range(2):
            finish(h, jnp.exp(scores(h)), jnp.exp(selves[h]) * dead)

    @pl.when(jnp.logical_not(safe))
    def _():
        for h in range(2):
            s = scores(h)
            own = jnp.where(dead > 0, selves[h], -FAR)
            top = jnp.maximum(jnp.max(s, axis=0, keepdims=True), own)
            finish(h, jnp.exp(s - top), jnp.exp(own - top) * dead)


def attend(act, w_qkv, kmask, qmask, token):
    width, tokens = act.shape
    pairs = width // (2 * HEAD_DIM)
    pair = 2 * HEAD_DIM
    heads = width // HEAD_DIM
    return pl.pallas_call(
        attend_kernel,
        name="attend",
        grid=(pairs,),
        in_specs=[
            whole((width, tokens)),
            pl.BlockSpec((width, pair), lambda i: (0, i)),
            pl.BlockSpec((width, pair), lambda i: (0, pairs + i)),
            pl.BlockSpec((width, pair), lambda i: (0, 2 * pairs + i)),
            pl.BlockSpec((pair, pair), lambda i: (i, 3 * pairs)),
            whole((16, tokens)),
            whole((16, tokens)),
            pl.BlockSpec(memory_space=pl.ANY),
        ],
        out_specs=[
            pl.BlockSpec((2, tokens, tokens), lambda i: (i, 0, 0)),
            pl.BlockSpec((pair, tokens), lambda i: (i, 0)),
            pl.BlockSpec((3, pair, tokens), lambda i: (0, i, 0)),
            pl.BlockSpec((2, 2, tokens), lambda i: (i, 0, 0)),
        ],
        out_shape=[
            jax.ShapeDtypeStruct((heads, tokens, tokens), BF),
            jax.ShapeDtypeStruct((width, tokens), BF),
            jax.ShapeDtypeStruct((3, width, tokens), BF),
            jax.ShapeDtypeStruct((heads, 2, tokens), F32),
        ],
        compiler_params=params(),
        cost_estimate=cost(6 * width * width * tokens + 4 * width * tokens * tokens, 2 * heads * tokens * tokens, heads * tokens * tokens),
    )(act, w_qkv, w_qkv, w_qkv, w_qkv, kmask, qmask, token)


def attend_back_kernel(e_ref, qkv_ref, stat_ref, grad_ref, inner_ref, out_ref, ds_ref):
    for h in range(2):
        rows = slice(h * HEAD_DIM, (h + 1) * HEAD_DIM)
        q, k, v = qkv_ref[0, rows], qkv_ref[1, rows], qkv_ref[2, rows]
        grad = grad_ref[rows]
        inner = inner_ref[h]
        e_self = stat_ref[h, 1:2, :]
        grad_f = grad.astype(F32)
        ds = (e_ref[h].astype(F32) * (dg(v.T, grad, 1, 0) - inner)).astype(BF)
        ds_ref[h] = ds
        own = (e_self * (jnp.sum(grad_f * v.astype(F32), axis=0, keepdims=True) - inner)).astype(BF).astype(F32)
        scale = HEAD_DIM**-0.5
        out_ref[0, rows] = ((dg(k, ds, 1, 0) + k.astype(F32) * own) * scale).astype(BF)
        out_ref[2, rows] = (dg(grad, e_ref[h], 1, 1) + grad_f * e_self.astype(BF).astype(F32)).astype(BF)
        out_ref[1, rows] = (dg(q, ds_ref[h], 1, 1) + q.astype(F32) * own).astype(BF)


def attend_back(e, qkv, stat, grad, inner):
    heads, tokens, _ = e.shape
    width = grad.shape[0]
    pairs = heads // 2
    pair = 2 * HEAD_DIM
    return pl.pallas_call(
        attend_back_kernel,
        name="attend_back",
        grid=(pairs,),
        in_specs=[
            pl.BlockSpec((2, tokens, tokens), lambda i: (i, 0, 0)),
            pl.BlockSpec((3, pair, tokens), lambda i: (0, i, 0)),
            pl.BlockSpec((2, 2, tokens), lambda i: (i, 0, 0)),
            pl.BlockSpec((pair, tokens), lambda i: (i, 0)),
            pl.BlockSpec((2, 1, tokens), lambda i: (i, 0, 0)),
        ],
        out_specs=pl.BlockSpec((3, pair, tokens), lambda i: (0, i, 0)),
        out_shape=jax.ShapeDtypeStruct((3, width, tokens), BF),
        scratch_shapes=[pltpu.VMEM((2, tokens, tokens), BF)],
        compiler_params=params(),
        cost_estimate=cost(8 * width * tokens * tokens, 2 * heads * tokens * tokens),
    )(e, qkv, stat, grad, inner)


def normed(t):
    mean = jnp.mean(t, axis=0, keepdims=True)
    centred = t - mean
    rstd = lax.rsqrt(jnp.mean(centred * centred, axis=0, keepdims=True) + NORM_EPS)
    return centred * rstd, rstd


def normed_back(grad, unit, rstd, gain):
    scaled = grad * gain
    mean = jnp.mean(scaled, axis=0, keepdims=True)
    along = jnp.mean(scaled * unit, axis=0, keepdims=True)
    return rstd * (scaled - mean - unit * along)


def gelu_and_slope(t):
    square = t * t
    inside = jnp.tanh(t * (0.7978845608028654 + (0.7978845608028654 * 0.044715) * square))
    half = 0.5 + 0.5 * inside
    slope = half + (t * (0.5 - 0.5 * inside * inside)) * (
        0.7978845608028654 + (3.0 * 0.7978845608028654 * 0.044715) * square
    )
    return t * half, slope


def lanes_sum(t):
    out = t[:, 0:128]
    for j in range(128, t.shape[1], 128):
        out = out + t[:, j : j + 128]
    return out


def column(col_ref, j):
    return col_ref[:, j : j + 1].astype(F32)


def dense_forward(signal, ctx, wo_ref, win_ref, wback_ref, col_ref, act_ref, slope_ref):
    joined = signal + dg(wo_ref[...], ctx, 0, 0) + column(col_ref, 6)
    unit_one, rstd_one = normed(joined)
    middle = unit_one * column(col_ref, 0) + column(col_ref, 1)
    low_middle = middle.astype(BF)
    width = middle.shape[0]
    summed = middle + column(col_ref, 7)
    for c in range(win_ref.shape[1] // width):
        rows = slice(c * width, (c + 1) * width)
        pre = dg(win_ref[:, rows], low_middle, 0, 0) + column(col_ref, 8 + c)
        gelu, slope = gelu_and_slope(pre)
        act = gelu.astype(BF)
        act_ref[rows, :] = act
        slope_ref[rows, :] = slope.astype(slope_ref.dtype)
        summed = summed + dg(wback_ref[:, rows], act, 1, 0)
    unit_two, rstd_two = normed(summed)
    return unit_one, rstd_one, low_middle, unit_two, rstd_two


def dense_back(grad, unit_one, rstd_one, slope_ref, unit_two, rstd_two, ctx, stat_ref, wo_ref, win_ref, wback_ref, col_ref,
               sums_ref, joined_ref, gctx_ref, inner_ref, dz_ref, du_ref, dattn_ref):
    sums_ref[2] += lanes_sum(grad * unit_two)
    sums_ref[3] += lanes_sum(grad)
    grad_summed = normed_back(grad, unit_two, rstd_two, column(col_ref, 2))
    dz = grad_summed.astype(BF)
    dz_ref[...] = dz
    sums_ref[7] += lanes_sum(dz.astype(F32))
    width = dz.shape[0]
    grad_middle = grad_summed
    for c in range(win_ref.shape[1] // width):
        rows = slice(c * width, (c + 1) * width)
        du = (dg(wback_ref[:, rows], dz, 0, 0) * slope_ref[rows, :].astype(F32)).astype(BF)
        du_ref[rows, :] = du
        sums_ref[8 + c] += lanes_sum(du.astype(F32))
        grad_middle = grad_middle + dg(win_ref[:, rows], du, 1, 0)
    sums_ref[0] += lanes_sum(grad_middle * unit_one)
    sums_ref[1] += lanes_sum(grad_middle)
    grad_joined = normed_back(grad_middle, unit_one, rstd_one, column(col_ref, 0))
    joined_ref[...] = grad_joined
    dattn = grad_joined.astype(BF)
    dattn_ref[...] = dattn
    sums_ref[6] += lanes_sum(dattn.astype(F32))
    grad_ctx = dg(wo_ref[...], dattn, 1, 0)
    for h in range(stat_ref.shape[0]):
        rows = slice(h * HEAD_DIM, (h + 1) * HEAD_DIM)
        part = (grad_ctx[rows] * stat_ref[h, 0:1, :]).astype(BF)
        gctx_ref[rows, :] = part
        inner_ref[h] = jnp.sum(part.astype(F32) * ctx[rows].astype(F32), axis=0, keepdims=True)


def tile(rows):
    return pl.BlockSpec((rows, TILE), lambda i: (0, i))


def heads_tile(heads, rows):
    return pl.BlockSpec((heads, rows, TILE), lambda i: (0, 0, i))


def rest_specs(width, hidden):
    return [
        pl.BlockSpec((width, width), lambda i: (0, 2 * hidden // width)),
        pl.BlockSpec((width, hidden), lambda i: (0, 0)),
        pl.BlockSpec((width, hidden), lambda i: (0, 1)),
    ]


def column_spec(width):
    return pl.BlockSpec((width, LANES), lambda i: (0, 3 * width // LANES))


def first_dense_kernel(signal_ref, ctx_ref, wo_ref, win_ref, wback_ref, col_ref,
                       unit_one_ref, unit_two_ref, rstd_ref, low_out_ref, act_ref, slope_ref):
    unit_one, rstd_one, _, unit_two, rstd_two = dense_forward(
        signal_ref[...].astype(F32), ctx_ref[...], wo_ref, win_ref, wback_ref, col_ref, act_ref, slope_ref)
    unit_one_ref[...] = unit_one
    unit_two_ref[...] = unit_two
    rstd_ref[0:1, :] = rstd_one
    rstd_ref[1:2, :] = rstd_two
    low_out_ref[...] = (unit_two * column(col_ref, 2) + column(col_ref, 3)).astype(BF)


def first_dense(signal, ctx, w_rest, w_first):
    width, tokens = signal.shape
    hidden = (w_rest.shape[1] - width) // 2
    return pl.pallas_call(
        first_dense_kernel,
        name="first_dense",
        grid=(tokens // TILE,),
        in_specs=[tile(width), tile(width), *rest_specs(width, hidden), column_spec(width)],
        out_specs=[tile(width), tile(width), tile(8), tile(width), tile(hidden), tile(hidden)],
        out_shape=[
            jax.ShapeDtypeStruct((width, tokens), F32),
            jax.ShapeDtypeStruct((width, tokens), F32),
            jax.ShapeDtypeStruct((8, tokens), F32),
            jax.ShapeDtypeStruct((width, tokens), BF),
            jax.ShapeDtypeStruct((hidden, tokens), BF),
            jax.ShapeDtypeStruct((hidden, tokens), BF),
        ],
        compiler_params=params(),
        cost_estimate=cost(2 * tokens * width * (width + 2 * hidden), 24 << 20, tokens * hidden),
    )(signal, ctx, w_rest, w_rest, w_rest, w_first)


def second_dense_kernel(unit_ref, ctx_ref, cot_ref, stat_ref, wo_ref, win_ref, wback_ref, col_ref,
                        out_ref, sums_ref, joined_ref, gctx_ref, inner_ref, mid_ref, act_ref, dz_ref, du_ref, dattn_ref, slope_ref):
    @pl.when(pl.program_id(0) == 0)
    def _():
        sums_ref[...] = jnp.zeros(sums_ref.shape, F32)

    ctx = ctx_ref[...]
    gain, shift = column(col_ref, 2), column(col_ref, 3)
    unit_one, rstd_one, low_middle, unit_two, rstd_two = dense_forward(
        unit_ref[...] * gain + shift, ctx, wo_ref, win_ref, wback_ref, col_ref, act_ref, slope_ref)
    mid_ref[...] = low_middle
    out_ref[...] = (unit_two * gain + shift).astype(BF).T
    dense_back(cot_ref[...].astype(F32), unit_one, rstd_one, slope_ref, unit_two, rstd_two, ctx, stat_ref,
               wo_ref, win_ref, wback_ref, col_ref, sums_ref, joined_ref, gctx_ref, inner_ref, dz_ref, du_ref, dattn_ref)


def second_dense(unit, ctx, cot, stat, w_rest, w_first):
    width, tokens = unit.shape
    hidden = (w_rest.shape[1] - width) // 2
    heads = stat.shape[0]
    return pl.pallas_call(
        second_dense_kernel,
        name="second_dense",
        grid=(tokens // TILE,),
        in_specs=[tile(width), tile(width), tile(width), heads_tile(heads, 2), *rest_specs(width, hidden), column_spec(width)],
        out_specs=[pl.BlockSpec((TILE, width), lambda i: (i, 0)), whole((12, width, LANES)), tile(width), tile(width), heads_tile(heads, 1),
                   tile(width), tile(hidden), tile(width), tile(hidden), tile(width)],
        out_shape=[
            jax.ShapeDtypeStruct((tokens, width), BF),
            jax.ShapeDtypeStruct((12, width, LANES), F32),
            jax.ShapeDtypeStruct((width, tokens), F32),
            jax.ShapeDtypeStruct((width, tokens), BF),
            jax.ShapeDtypeStruct((heads, 1, tokens), F32),
            jax.ShapeDtypeStruct((width, tokens), BF),
            jax.ShapeDtypeStruct((hidden, tokens), BF),
            jax.ShapeDtypeStruct((width, tokens), BF),
            jax.ShapeDtypeStruct((hidden, tokens), BF),
            jax.ShapeDtypeStruct((width, tokens), BF),
        ],
        scratch_shapes=[pltpu.VMEM((hidden, TILE), F32)],
        compiler_params=params(),
        cost_estimate=cost(4 * tokens * width * (width + 2 * hidden), 28 << 20, tokens * hidden),
    )(unit, ctx, cot, stat, w_rest, w_rest, w_rest, w_first)


def first_back_kernel(prior_ref, dqkv_ref, unit_one_ref, unit_two_ref, rstd_ref, slope_ref, ctx_ref, stat_ref, sums_in_ref,
                      wqkv_ref, wo_ref, win_ref, wback_ref, col_ref,
                      vec_ref, joined_ref, gctx_ref, inner_ref, mid_ref, dz_ref, du_ref, dattn_ref, sums_ref):
    step = pl.program_id(0)

    @pl.when(step == 0)
    def _():
        sums_ref[...] = sums_in_ref[...]

    unit_one = unit_one_ref[...]
    mid_ref[...] = (unit_one * column(col_ref, 0) + column(col_ref, 1)).astype(BF)
    grad = prior_ref[...] + dg(wqkv_ref[...], dqkv_ref[...], 1, 0)
    dense_back(grad, unit_one, rstd_ref[0:1, :], slope_ref, unit_two_ref[...], rstd_ref[1:2, :], ctx_ref[...], stat_ref,
               wo_ref, win_ref, wback_ref, col_ref, sums_ref, joined_ref, gctx_ref, inner_ref, dz_ref, du_ref, dattn_ref)

    @pl.when(step == pl.num_programs(0) - 1)
    def _():
        lane = lax.broadcasted_iota(jnp.int32, vec_ref.shape, 1)
        out = jnp.zeros(vec_ref.shape, F32)
        for j in (0, 1, 2, 3, 6, 7, 8, 9, 10, 11):
            out = jnp.where(lane == j, jnp.sum(sums_ref[j], axis=1, keepdims=True), out)
        vec_ref[...] = out


def first_back(prior, dqkv, unit_one, unit_two, rstd, slope, ctx, stat, sums, w_first, w_rest):
    width, tokens = prior.shape
    hidden = (w_rest.shape[1] - width) // 2
    heads = stat.shape[0]
    return pl.pallas_call(
        first_back_kernel,
        name="first_back",
        grid=(tokens // TILE,),
        in_specs=[tile(width), tile(3 * width), tile(width), tile(width), tile(8), tile(hidden), tile(width), heads_tile(heads, 2), whole(sums.shape),
                  pl.BlockSpec((width, 3 * width), lambda i: (0, 0)), *rest_specs(width, hidden), column_spec(width)],
        out_specs=[whole((width, LANES)), tile(width), tile(width), heads_tile(heads, 1), tile(width), tile(width), tile(hidden), tile(width)],
        out_shape=[
            jax.ShapeDtypeStruct((width, LANES), F32),
            jax.ShapeDtypeStruct((width, tokens), F32),
            jax.ShapeDtypeStruct((width, tokens), BF),
            jax.ShapeDtypeStruct((heads, 1, tokens), F32),
            jax.ShapeDtypeStruct((width, tokens), BF),
            jax.ShapeDtypeStruct((width, tokens), BF),
            jax.ShapeDtypeStruct((hidden, tokens), BF),
            jax.ShapeDtypeStruct((width, tokens), BF),
        ],
        scratch_shapes=[pltpu.VMEM((12, width, LANES), F32)],
        compiler_params=params(),
        cost_estimate=cost(2 * tokens * width * (4 * width + 2 * hidden), 28 << 20),
    )(prior, dqkv, unit_one, unit_two, rstd, slope, ctx, stat, sums, w_first, w_rest, w_rest, w_rest, w_first)


class Layout:
    def __init__(self, mesh_batch, mesh_shard, width):
        self.batch = mesh_batch
        self.shards = mesh_shard
        self.parts = min(mesh_batch, width // mesh_shard // 16)
        self.planes = self.parts // 2
        self.rows = width // mesh_shard // self.parts

    def swap(self, value, axis, distance):
        size = self.batch if axis == "batch" else self.shards
        return lax.ppermute(value, axis, [(i, i ^ distance) for i in range(size)])

    def place(self):
        return jnp.stack([lax.axis_index("batch") % self.parts, lax.axis_index("shard")]).astype(jnp.int32)

    def row_of(self, place_ref, c, e, d):
        block = (place_ref[1] ^ d) * self.parts + (place_ref[0] ^ (2 * e + c))
        return pl.multiple_of(block * self.rows, self.rows)

    def along_shards(self, mine):
        return jnp.concatenate([self.swap(mine, "shard", d) for d in range(1, self.shards)], axis=0)

    def across_plane(self, stack):
        plane = [stack] + [self.swap(stack, "batch", 2 * e) for e in range(1, self.planes)]
        return jnp.concatenate(plane, axis=0)

    def sum_cores(self, keep, send):
        return add(keep, self.swap(send, "batch", 1))

    def sum_plane(self, half):
        rows = half.shape[0] // self.planes
        parts = [half[e * rows : (e + 1) * rows] for e in range(self.planes)]
        return add(parts[0], *[self.swap(parts[e], "batch", 2 * e) for e in range(1, self.planes)])

    def sum_shards(self, plane):
        blocks = [plane[d * self.rows : (d + 1) * self.rows] for d in range(self.shards)]
        own = add(blocks[0], *[self.swap(blocks[d], "shard", d) for d in range(1, self.shards)])
        distance = self.parts
        while distance < self.batch:
            own = add(own, self.swap(own, "batch", distance))
            distance *= 2
        return own

    def total(self, own):
        own = tree([own] + [self.swap(own, "shard", d) for d in range(1, self.shards)])
        own = tree([own] + [self.swap(own, "batch", 2 * e) for e in range(1, self.planes)])
        return own + self.swap(own, "batch", 1)

    def spread(self, own):
        plane = jnp.concatenate([own] + [self.swap(own, "batch", 2 * e) for e in range(1, self.planes)], axis=0)
        return jnp.concatenate([plane, self.swap(plane, "batch", 1)], axis=0)


def tree(values):
    while len(values) > 1:
        values = [a + b for a, b in zip(values[::2], values[1::2], strict=True)]
    return values[0]


def add(first, *others):
    total = first.astype(F32)
    for other in others:
        total = total + other.astype(F32)
    return total.astype(BF)


def pick_kernel(place_ref, *refs):
    refs[-1][...] = refs[0][...].astype(BF)


def pick(layout, place, source, token):
    columns = source.shape[1]
    return pl.pallas_call(
        pick_kernel,
        name="pick",
        grid_spec=pltpu.PrefetchScalarGridSpec(
            num_scalar_prefetch=1,
            grid=(1,),
            in_specs=[pl.BlockSpec((layout.rows, columns), lambda i, place: (place[0], 0)), pl.BlockSpec(memory_space=pl.ANY)],
            out_specs=pl.BlockSpec((layout.rows, columns), lambda i, place: (0, 0)),
        ),
        out_shape=jax.ShapeDtypeStruct((layout.rows, columns), BF),
        compiler_params=params(),
        cost_estimate=cost(0, 6 * layout.rows * columns),
    )(place, source, token)


def collect_kernel(layout, place_ref, own_ref, mine_ref, theirs_ref, out_ref):
    shard_rows = layout.rows * layout.parts
    out_ref[pl.ds(pl.multiple_of(place_ref[1] * shard_rows, shard_rows), shard_rows), :] = own_ref[...].astype(BF)
    for c, source in ((0, mine_ref), (1, theirs_ref)):
        for e in range(layout.planes):
            for d in range(1, layout.shards):
                at = (e * (layout.shards - 1) + d - 1) * layout.rows
                out_ref[pl.ds(layout.row_of(place_ref, c, e, d), layout.rows), :] = source[at : at + layout.rows, :]


def collect(layout, place, own, mine, theirs, block):
    rows = layout.rows * layout.parts * layout.shards
    columns = own.shape[1]
    return pl.pallas_call(
        functools.partial(collect_kernel, layout),
        name="collect",
        grid=(columns // block,),
        in_specs=[pl.BlockSpec(memory_space=pltpu.SMEM)] + [pl.BlockSpec((t.shape[0], block), lambda i: (0, i)) for t in (own, mine, theirs)],
        out_specs=pl.BlockSpec((rows, block), lambda i: (0, i)),
        out_shape=jax.ShapeDtypeStruct((rows, columns), BF),
        compiler_params=params(),
        cost_estimate=cost(0, 4 * rows * columns),
    )(place, own, mine, theirs)


def in_order(layout, place_ref, source_ref, target_ref):
    at = 0
    for c in range(2):
        for e in range(layout.planes):
            for d in range(layout.shards):
                target_ref[at : at + layout.rows] = source_ref[pl.ds(layout.row_of(place_ref, c, e, d), layout.rows), :]
                at += layout.rows


def weight_kernel(layout, place_ref, la_ref, lb_ref, ra_ref, rb_ref, keep_ref, send_ref, left_ref):
    @pl.when(pl.program_id(0) == 0)
    def _():
        in_order(layout, place_ref, la_ref, left_ref.at[0])
        in_order(layout, place_ref, lb_ref, left_ref.at[1])

    out = (dg(left_ref[0], ra_ref[...], 1, 1) + dg(left_ref[1], rb_ref[...], 1, 1)).astype(BF)
    half = out.shape[0] // 2
    keep_ref[...] = out[:half]
    send_ref[...] = out[half:]


def weight_grad(layout, place, left_one, left_two, right_one, right_two, block):
    rows, tokens = left_one.shape
    columns = right_one.shape[0]
    half = jax.ShapeDtypeStruct((rows // 2, columns), BF)
    return pl.pallas_call(
        functools.partial(weight_kernel, layout),
        name="weight_grad",
        grid=(columns // block,),
        in_specs=[pl.BlockSpec(memory_space=pltpu.SMEM), whole((rows, tokens)), whole((rows, tokens)),
                  pl.BlockSpec((block, tokens), lambda i: (i, 0)), pl.BlockSpec((block, tokens), lambda i: (i, 0))],
        out_specs=[pl.BlockSpec((rows // 2, block), lambda i: (0, i))] * 2,
        out_shape=[half, half],
        scratch_shapes=[pltpu.VMEM((2, rows, tokens), BF)],
        compiler_params=params(),
        cost_estimate=cost(4 * rows * columns * tokens, 4 * (rows + columns) * tokens + 2 * rows * columns),
    )(place, left_one, left_two, right_one, right_two)


def last_back_kernel(layout, first_pair, given, place_ref, e_ref, qkv_ref, stat_ref, grad_ref, inner_ref, act_one_ref, act_two_ref, dqkv_two_ref, vec_in_ref, *refs):
    out_ref, keep_ref, send_ref, vec_ref, vec_keep_ref, vec_send_ref, ds_ref, left_ref, order_ref = refs[given:]
    step = pl.program_id(0)

    @pl.when(step == 0)
    def _():
        in_order(layout, place_ref, act_one_ref, left_ref.at[0])
        in_order(layout, place_ref, act_two_ref, left_ref.at[1])
        vec_ref[...] = vec_in_ref[...]

    attend_back_kernel(e_ref, qkv_ref, stat_ref, grad_ref, inner_ref, out_ref, ds_ref)
    pair = out_ref.shape[1]
    for t in range(3):
        total = (dg(left_ref[0], out_ref[t], 1, 1) + dg(left_ref[1], dqkv_two_ref[t], 1, 1)).astype(BF)
        half = total.shape[0] // 2
        keep_ref[:, t * pair : (t + 1) * pair] = total[:half]
        send_ref[:, t * pair : (t + 1) * pair] = total[half:]
    rows = pl.ds(pl.multiple_of((first_pair + step) * pair, pair), pair)
    lane = lax.broadcasted_iota(jnp.int32, (pair, LANES), 1)
    vec = vec_ref[rows, :]
    for lane_at, t in ((4, 0), (5, 2)):
        both = lanes_sum(out_ref[t].astype(F32)) + lanes_sum(dqkv_two_ref[t].astype(F32))
        vec = jnp.where(lane == lane_at, jnp.sum(both, axis=1, keepdims=True), vec)
    vec_ref[rows, :] = vec

    @pl.when(step == pl.num_programs(0) - 1)
    def _():
        in_order(layout, place_ref, vec_ref, order_ref)
        half = order_ref.shape[0] // 2
        vec_keep_ref[...] = order_ref[0:half].astype(BF)
        vec_send_ref[...] = order_ref[half:].astype(BF)


def last_back(layout, place, first_pair, pairs, e, qkv, stat, grad, inner, act_one, act_two, dqkv_two, vec, earlier, tokens_in):
    heads, tokens, _ = e.shape
    width = grad.shape[0]
    pair = 2 * HEAD_DIM
    half = jax.ShapeDtypeStruct((width // 2, 3 * width), BF)
    vec_half = jax.ShapeDtypeStruct((width // 2, LANES), BF)
    return pl.pallas_call(
        functools.partial(last_back_kernel, layout, first_pair, len(earlier) + len(tokens_in)),
        name="last_back",
        grid=(pairs,),
        in_specs=[
            pl.BlockSpec(memory_space=pltpu.SMEM),
            pl.BlockSpec((2, tokens, tokens), lambda i: (first_pair + i, 0, 0)),
            pl.BlockSpec((3, pair, tokens), lambda i: (0, first_pair + i, 0)),
            pl.BlockSpec((2, 2, tokens), lambda i: (first_pair + i, 0, 0)),
            pl.BlockSpec((pair, tokens), lambda i: (first_pair + i, 0)),
            pl.BlockSpec((2, 1, tokens), lambda i: (first_pair + i, 0, 0)),
            whole((width, tokens)),
            whole((width, tokens)),
            pl.BlockSpec((3, pair, tokens), lambda i: (0, first_pair + i, 0)),
            whole((width, LANES)),
        ] + [pl.BlockSpec(memory_space=pl.ANY)] * (len(earlier) + len(tokens_in)),
        out_specs=[
            pl.BlockSpec((3, pair, tokens), lambda i: (0, first_pair + i, 0)),
            pl.BlockSpec((width // 2, 3 * pair), lambda i: (0, first_pair + i)),
            pl.BlockSpec((width // 2, 3 * pair), lambda i: (0, first_pair + i)),
            whole((width, LANES)),
            whole((width // 2, LANES)),
            whole((width // 2, LANES)),
        ],
        out_shape=[
            jax.ShapeDtypeStruct((3, width, tokens), BF),
            half,
            half,
            jax.ShapeDtypeStruct((width, LANES), F32),
            vec_half,
            vec_half,
        ],
        input_output_aliases={10 + i: i for i in range(len(earlier))},
        scratch_shapes=[pltpu.VMEM((2, tokens, tokens), BF), pltpu.VMEM((2, width, tokens), BF), pltpu.VMEM((width, LANES), F32)],
        compiler_params=params(),
        cost_estimate=cost(pairs * (16 * pair * tokens * tokens + 12 * width * pair * tokens), pairs * 4 * tokens * tokens + 4 * width * tokens),
    )(place, e, qkv, stat, grad, inner, act_one, act_two, dqkv_two, vec, *earlier, *tokens_in)


def input_kernel(joined_ref, dqkv_ref, w_ref, *refs):
    refs[-1][...] = (joined_ref[...] + dg(w_ref[...], dqkv_ref[...], 1, 0)).T


def input_gradient(joined, dqkv, w_first, tokens_in):
    width, tokens = joined.shape
    return pl.pallas_call(
        input_kernel,
        name="input_gradient",
        grid=(tokens // TILE,),
        in_specs=[tile(width), tile(3 * width), pl.BlockSpec((width, 3 * width), lambda i: (0, 0))] + [pl.BlockSpec(memory_space=pl.ANY)] * len(tokens_in),
        out_specs=pl.BlockSpec((TILE, width), lambda i: (i, 0)),
        out_shape=jax.ShapeDtypeStruct((tokens, width), F32),
        compiler_params=params(),
        cost_estimate=cost(6 * width * width * tokens, 8 << 20),
    )(joined, dqkv, w_first, *tokens_in)


def adam_kernel(pieces, place_ref, factor_ref, *refs):
    del place_ref
    grads = refs[: len(pieces)]
    w_ref, one_ref, two_ref, vec_ref, v_ref, vone_ref, vtwo_ref = refs[len(pieces) : len(pieces) + 7]
    gw_ref, nw_ref, none_ref, ntwo_ref, gv_ref, nv_ref, nvone_ref, nvtwo_ref, hold_ref = refs[len(pieces) + 7 :]
    factor = factor_ref[0]
    for grad_ref, spans in zip(grads, pieces, strict=True):
        for source, target, size in spans:
            to = slice(target, target + size)
            grad = grad_ref[:, source : source + size].astype(F32)
            gw_ref[:, to] = grad
            nw_ref[:, to], none_ref[:, to], ntwo_ref[:, to] = adam_update(w_ref[:, to], one_ref[:, to], two_ref[:, to], grad * factor)
    step = pl.program_id(0)
    rows = vec_ref.shape[0]
    hold_ref[pl.ds(pl.multiple_of(step * rows, rows), rows), :] = vec_ref[...].astype(F32)

    @pl.when(step == pl.num_programs(0) - 1)
    def _():
        grad = hold_ref[...].T[0 : gv_ref.shape[0], 0 : gv_ref.shape[1]]
        gv_ref[...] = grad
        nv_ref[...], nvone_ref[...], nvtwo_ref[...] = adam_update(v_ref[...], vone_ref[...], vtwo_ref[...], grad * factor)


def adam(layout, place, factor, pieces, grads, vec, weights, first, second, vectors, vector_first, vector_second):
    rows, columns = weights.shape
    block = layout.rows
    natural = pl.BlockSpec((block, columns), lambda i, place, factor: (i, 0))
    small = pl.BlockSpec(vectors.shape, lambda i, place, factor: (0, 0))

    def relative(width):
        return pl.BlockSpec((block, width), lambda i, place, factor: (((i ^ place[0]) & 1) * layout.planes + ((i ^ place[0]) >> 1), 0))

    big = jax.ShapeDtypeStruct((rows, columns), F32)
    little = jax.ShapeDtypeStruct(vectors.shape, F32)
    return pl.pallas_call(
        functools.partial(adam_kernel, pieces),
        name="adam",
        grid_spec=pltpu.PrefetchScalarGridSpec(
            num_scalar_prefetch=2,
            grid=(rows // block,),
            in_specs=[relative(g.shape[1]) for g in grads] + [natural] * 3 + [relative(LANES)] + [small] * 3,
            out_specs=[natural] * 4 + [small] * 4,
            scratch_shapes=[pltpu.VMEM((LANES, LANES), F32)],
        ),
        out_shape=[big] * 4 + [little] * 4,
        compiler_params=params(),
        cost_estimate=cost(20 * rows * columns, 30 * rows * columns, rows * columns),
    )(place, factor, *grads, weights, first, second, vec, vectors, vector_first, vector_second)


def masks(segments, tags, length):
    tokens = segments.shape[0]
    matches = segments[None, :] == jnp.arange(tags.shape[0], dtype=jnp.int32)[:, None]
    group = jnp.sum(jnp.where(matches, tags[:, None], 0), axis=0)
    live = jnp.arange(tokens, dtype=jnp.int32) < length
    kinds = jnp.arange(16, dtype=jnp.int32)[:, None]
    same = group[None, :] == kinds
    kmask = jnp.where(kinds < 4, (same & live[None, :]).astype(F32), jnp.where(kinds == 4, (~live)[None, :].astype(F32), 0.0))
    qmask = jnp.where(kinds < 4, jnp.where(same, 0.0, -FAR), jnp.where(kinds == 4, -FAR, 0.0))
    return kmask.astype(BF), jnp.broadcast_to(qmask, (16, tokens)).astype(BF)


def squares(t):
    return jnp.sum(jnp.square(t.astype(F32)))


def on_device(layout, inputs, cotangent, lengths, segment_ids, group_tags, weights, first_moments, second_moments, vectors, vector_first, vector_second):
    _, tokens, width = inputs.shape
    hidden = (weights.shape[1] - 4 * width) // 2
    pair = 2 * HEAD_DIM
    place = layout.place()
    own_first = jnp.concatenate([weights[:, : 3 * width], jnp.pad(vectors.T, ((0, 0), (0, LANES - vectors.shape[0])))], axis=1)
    own_rest = jnp.concatenate([weights[:, 4 * width :], weights[:, 3 * width : 4 * width]], axis=1)
    kmask, qmask = masks(segment_ids[0], group_tags[0], lengths[0])
    act_one = inputs[0].T
    cot = cotangent[0].T

    first_z = layout.along_shards(pick(layout, place, own_first, place))
    rest_z = layout.along_shards(pick(layout, place, own_rest, first_z))
    first_mine = layout.across_plane(first_z)
    rest_mine = layout.across_plane(rest_z)
    w_first = collect(layout, place, own_first, first_mine, layout.swap(first_mine, "batch", 1), 128)
    e_one, ctx_one, qkv_one, stat_one = attend(act_one, w_first, kmask, qmask, rest_z)
    w_rest = collect(layout, place, own_rest, rest_mine, layout.swap(rest_mine, "batch", 1), 512)
    unit_one, unit_two, rstd, act_two, hid_one, slope = first_dense(act_one, ctx_one, w_rest, w_first)
    e_two, ctx_two, qkv_two, stat_two = attend(act_two, w_first, kmask, qmask, place)
    outputs, sums, joined_two, gctx_two, inner_two, mid_two, hid_two, dz_two, du_two, dattn_two = second_dense(
        unit_two, ctx_two, cot, stat_two, w_rest, w_first)
    dqkv_two = attend_back(e_two, qkv_two, stat_two, gctx_two, inner_two)
    vec, joined_one, gctx_one, inner_one, mid_one, dz_one, du_one, dattn_one = first_back(
        joined_two, dqkv_two.reshape(3 * width, tokens), unit_one, unit_two, rstd, slope, ctx_one, stat_one, sums, w_first, w_rest)

    half_in = layout.sum_cores(*weight_grad(layout, place, mid_one, mid_two, du_one, du_two, width))
    keep_back, send_back = weight_grad(layout, place, dz_one, dz_two, hid_one, hid_two, width)
    keep_o, send_o = weight_grad(layout, place, ctx_one, ctx_two, dattn_one, dattn_two, width)
    half_back = layout.sum_cores(jnp.concatenate([keep_back, keep_o], axis=1), jnp.concatenate([send_back, send_o], axis=1))
    plane_in = layout.sum_plane(half_in)
    group = width // pair // 2
    operands = (e_one, qkv_one, stat_one, gctx_one, inner_one, act_one, act_two, dqkv_two)
    dqkv, keep, send, vec, _, _ = last_back(layout, place, 0, group, *operands, vec, (), (half_in, keep_back, keep_o))
    own_in = layout.sum_shards(plane_in)
    plane_back = layout.sum_plane(half_back)
    dqkv, keep, send, vec, vec_keep, vec_send = last_back(
        layout, place, group, group, *operands, vec, (dqkv, keep, send), (plane_in, half_back))
    half_qkv = layout.sum_cores(jnp.concatenate([keep, vec_keep], axis=1), jnp.concatenate([send, vec_send], axis=1))
    plane_qkv = layout.sum_plane(half_qkv)
    own_back = layout.sum_shards(plane_back)
    input_grad = input_gradient(joined_one, dqkv.reshape(3 * width, tokens), w_first, (own_in, plane_back))
    early = jnp.concatenate([own_in, own_back], axis=1)
    own_qkv = layout.sum_shards(plane_qkv)
    grads = [layout.spread(early), layout.spread(own_qkv)]
    spans = [
        [(0, 4 * width, 2 * hidden), (2 * hidden, 3 * width, width)],
        [((i * 3 + t) * pair, t * width + i * pair, pair) for i in range(width // pair) for t in range(3)],
    ]
    vec_grad = grads[1][:, 3 * width :]
    grad_norm = jnp.sqrt(layout.total(squares(early) + squares(own_qkv)))
    clip_limit = math.sqrt(width * weights.shape[1])
    factor = clip_limit / jnp.maximum(grad_norm, clip_limit)
    updated = adam(layout, place, factor.reshape(1), spans, grads, vec_grad, weights, first_moments, second_moments, vectors, vector_first, vector_second)
    grad_w, new_weights, new_first, new_second, grad_v, new_vectors, new_vector_first, new_vector_second = updated
    return (
        outputs[None],
        input_grad[None],
        grad_w,
        grad_v,
        grad_norm,
        new_weights,
        new_first,
        new_second,
        new_vectors,
        new_vector_first,
        new_vector_second,
    )


def solution(mesh):
    rows = ("batch", "shard")
    placed = (
        P(rows, None, None),
        P(rows, None, None),
        P(rows),
        P(rows, None),
        P(rows, None),
        P("shard", None),
        P("shard", None),
        P("shard", None),
        P(None, "shard"),
        P(None, "shard"),
        P(None, "shard"),
    )
    return jax.shard_map(
        functools.partial(on_device, Layout(mesh.shape["batch"], mesh.shape["shard"], D)),
        mesh=mesh,
        in_specs=placed,
        out_specs=(
            P(rows, None, None),
            P(rows, None, None),
            P("shard", None),
            P(None, "shard"),
            P(),
            P("shard", None),
            P("shard", None),
            P("shard", None),
            P(None, "shard"),
            P(None, "shard"),
            P(None, "shard"),
        ),
        check_vma=False,
    )
```

```python
import functools
import math

import jax
import jax.numpy as jnp
from jax import lax
from jax.experimental import pallas as pl
from jax.experimental.pallas import tpu as pltpu
from jax.sharding import PartitionSpec as P

D = 512
FF = 2048
HEADS = 8
HEAD_DIM = 64
STEP = 10
WCOLS = 6144

NORM_EPS = 1e-05
BETA_ONE = 0.5
BETA_TWO = 0.5
ADAM_EPS = 1e-08
DECAY = 0.01
WARMUP = 4000.0
RATE_SCALE = 150000.0

BF = jnp.bfloat16
F32 = jnp.float32
FAR = 1e30
SAFE_SCORE = 60.0
TILE = 256
LANES = 128
SQUARES_AT = 12
VMEM_BYTES = 50 << 20


def params():
    return pltpu.CompilerParams(vmem_limit_bytes=VMEM_BYTES)


def cost(flops, bytes_accessed, transcendentals=0):
    return pl.CostEstimate(flops=int(flops) // 10, bytes_accessed=int(bytes_accessed) // 10, transcendentals=int(transcendentals) // 10)


def dg(left, right, left_dim, right_dim):
    return lax.dot_general(
        left, right, (((left_dim,), (right_dim,)), ((), ())), preferred_element_type=F32
    )


def whole(shape):
    return pl.BlockSpec(shape, lambda i: (0,) * len(shape))


def adam_update(master, moment_one, moment_two, gradient):
    moment_one = BETA_ONE * moment_one + (1.0 - BETA_ONE) * gradient
    moment_two = BETA_TWO * moment_two + (1.0 - BETA_TWO) * gradient * gradient
    step_rate = RATE_SCALE * D ** (-0.5) * min(STEP ** (-0.5), STEP * WARMUP ** (-1.5))
    fixed_first = moment_one / (1.0 - BETA_ONE**STEP)
    fixed_second = moment_two / (1.0 - BETA_TWO**STEP)
    master = master - step_rate * (
        fixed_first / (jnp.sqrt(fixed_second) + ADAM_EPS) + DECAY * master
    )
    return (master, moment_one, moment_two)


def attend_kernel(act_ref, wq_ref, wk_ref, wv_ref, col_ref, kmask_ref, qmask_ref, e_ref, ctx_ref, qkv_ref, stat_ref):
    act = act_ref[...]
    tokens = act.shape[1]
    q = (dg(wq_ref[...], act, 0, 0) + col_ref[:, 4:5].astype(F32)).astype(BF) * jnp.asarray(HEAD_DIM**-0.5, BF)
    k = dg(wk_ref[...], act, 0, 0).astype(BF)
    v = (dg(wv_ref[...], act, 0, 0) + col_ref[:, 5:6].astype(F32)).astype(BF)
    qkv_ref[0] = q
    qkv_ref[1] = k
    qkv_ref[2] = v
    dead = kmask_ref[4:5, :].astype(F32)
    bound = jnp.zeros((1, 1), F32)
    selves = []
    for h in range(2):
        rows = slice(h * HEAD_DIM, (h + 1) * HEAD_DIM)
        qf, kf = q[rows].astype(F32), k[rows].astype(F32)
        selves.append(jnp.sum(qf * kf, axis=0, keepdims=True))
        q_top = jnp.max(jnp.sum(qf * qf, axis=0, keepdims=True), axis=1, keepdims=True)
        k_top = jnp.max(jnp.sum(kf * kf, axis=0, keepdims=True), axis=1, keepdims=True)
        bound = jnp.maximum(bound, q_top * k_top)
    safe = bound[0, 0] <= SAFE_SCORE * SAFE_SCORE

    def scores(h):
        rows = slice(h * HEAD_DIM, (h + 1) * HEAD_DIM)
        keys = jnp.concatenate([k[rows], kmask_ref[...]], axis=0).T
        queries = jnp.concatenate([q[rows], qmask_ref[...]], axis=0)
        return dg(keys, queries, 1, 0)

    def finish(h, e, e_self):
        rows = slice(h * HEAD_DIM, (h + 1) * HEAD_DIM)
        low_e = e.astype(BF)
        e_ref[h] = low_e
        total = jnp.sum(e, axis=0, keepdims=True) + e_self
        scale = 1.0 / total
        values = v[rows]
        mixed = dg(values, low_e, 1, 0) + values.astype(F32) * e_self.astype(BF).astype(F32)
        ctx_ref[rows, :] = (mixed * scale).astype(BF)
        stat_ref[h, 0:1, :] = scale
        stat_ref[h, 1:2, :] = e_self

    @pl.when(safe)
    def _():
        for h in range(2):
            finish(h, jnp.exp(scores(h)), jnp.exp(selves[h]) * dead)

    @pl.when(jnp.logical_not(safe))
    def _():
        for h in range(2):
            s = scores(h)
            own = jnp.where(dead > 0, selves[h], -FAR)
            top = jnp.maximum(jnp.max(s, axis=0, keepdims=True), own)
            finish(h, jnp.exp(s - top), jnp.exp(own - top) * dead)


def attend(act, w_qkv, kmask, qmask):
    width, tokens = act.shape
    pairs = width // (2 * HEAD_DIM)
    pair = 2 * HEAD_DIM
    heads = width // HEAD_DIM
    return pl.pallas_call(
        attend_kernel,
        name="attend",
        grid=(pairs,),
        in_specs=[
            whole((width, tokens)),
            pl.BlockSpec((width, pair), lambda i: (0, i)),
            pl.BlockSpec((width, pair), lambda i: (0, pairs + i)),
            pl.BlockSpec((width, pair), lambda i: (0, 2 * pairs + i)),
            pl.BlockSpec((pair, pair), lambda i: (i, 3 * pairs)),
            whole((16, tokens)),
            whole((16, tokens)),
        ],
        out_specs=[
            pl.BlockSpec((2, tokens, tokens), lambda i: (i, 0, 0)),
            pl.BlockSpec((pair, tokens), lambda i: (i, 0)),
            pl.BlockSpec((3, pair, tokens), lambda i: (0, i, 0)),
            pl.BlockSpec((2, 2, tokens), lambda i: (i, 0, 0)),
        ],
        out_shape=[
            jax.ShapeDtypeStruct((heads, tokens, tokens), BF),
            jax.ShapeDtypeStruct((width, tokens), BF),
            jax.ShapeDtypeStruct((3, width, tokens), BF),
            jax.ShapeDtypeStruct((heads, 2, tokens), F32),
        ],
        compiler_params=params(),
        cost_estimate=cost(6 * width * width * tokens + 4 * width * tokens * tokens, 2 * heads * tokens * tokens, heads * tokens * tokens),
    )(act, w_qkv, w_qkv, w_qkv, w_qkv, kmask, qmask)


def attend_back_kernel(e_ref, qkv_ref, stat_ref, grad_ref, inner_ref, out_ref, ds_ref):
    for h in range(2):
        rows = slice(h * HEAD_DIM, (h + 1) * HEAD_DIM)
        q, k, v = qkv_ref[0, rows], qkv_ref[1, rows], qkv_ref[2, rows]
        grad = grad_ref[rows]
        inner = inner_ref[h]
        e_self = stat_ref[h, 1:2, :]
        grad_f = grad.astype(F32)
        ds = (e_ref[h].astype(F32) * (dg(v.T, grad, 1, 0) - inner)).astype(BF)
        ds_ref[h] = ds
        own = (e_self * (jnp.sum(grad_f * v.astype(F32), axis=0, keepdims=True) - inner)).astype(BF).astype(F32)
        scale = HEAD_DIM**-0.5
        out_ref[0, rows] = ((dg(k, ds, 1, 0) + k.astype(F32) * own) * scale).astype(BF)
        out_ref[2, rows] = (dg(grad, e_ref[h], 1, 1) + grad_f * e_self.astype(BF).astype(F32)).astype(BF)
        out_ref[1, rows] = (dg(q, ds_ref[h], 1, 1) + q.astype(F32) * own).astype(BF)


def attend_back(e, qkv, stat, grad, inner):
    heads, tokens, _ = e.shape
    width = grad.shape[0]
    pairs = heads // 2
    pair = 2 * HEAD_DIM
    return pl.pallas_call(
        attend_back_kernel,
        name="attend_back",
        grid=(pairs,),
        in_specs=[
            pl.BlockSpec((2, tokens, tokens), lambda i: (i, 0, 0)),
            pl.BlockSpec((3, pair, tokens), lambda i: (0, i, 0)),
            pl.BlockSpec((2, 2, tokens), lambda i: (i, 0, 0)),
            pl.BlockSpec((pair, tokens), lambda i: (i, 0)),
            pl.BlockSpec((2, 1, tokens), lambda i: (i, 0, 0)),
        ],
        out_specs=pl.BlockSpec((3, pair, tokens), lambda i: (0, i, 0)),
        out_shape=jax.ShapeDtypeStruct((3, width, tokens), BF),
        scratch_shapes=[pltpu.VMEM((2, tokens, tokens), BF)],
        compiler_params=params(),
        cost_estimate=cost(8 * width * tokens * tokens, 2 * heads * tokens * tokens),
    )(e, qkv, stat, grad, inner)


def normed(t):
    mean = jnp.mean(t, axis=0, keepdims=True)
    centred = t - mean
    rstd = lax.rsqrt(jnp.mean(centred * centred, axis=0, keepdims=True) + NORM_EPS)
    return centred * rstd, rstd


def normed_back(grad, unit, rstd, gain):
    scaled = grad * gain
    mean = jnp.mean(scaled, axis=0, keepdims=True)
    along = jnp.mean(scaled * unit, axis=0, keepdims=True)
    return rstd * (scaled - mean - unit * along)


def gelu_and_slope(t):
    square = t * t
    inside = jnp.tanh(t * (0.7978845608028654 + (0.7978845608028654 * 0.044715) * square))
    half = 0.5 + 0.5 * inside
    slope = half + (t * (0.5 - 0.5 * inside * inside)) * (
        0.7978845608028654 + (3.0 * 0.7978845608028654 * 0.044715) * square
    )
    return t * half, slope


def lanes_sum(t):
    out = t[:, 0:128]
    for j in range(128, t.shape[1], 128):
        out = out + t[:, j : j + 128]
    return out


def column(col_ref, j):
    return col_ref[:, j : j + 1].astype(F32)


def dense_forward(signal, ctx, rest_ref, col_ref, act_ref, slope_ref):
    wo_ref, win_ref, wback_ref = parts_of(rest_ref)
    joined = signal + dg(wo_ref[...], ctx, 0, 0) + column(col_ref, 6)
    unit_one, rstd_one = normed(joined)
    middle = unit_one * column(col_ref, 0) + column(col_ref, 1)
    low_middle = middle.astype(BF)
    width = middle.shape[0]
    summed = middle + column(col_ref, 7)
    for c in range(win_ref.shape[1] // width):
        rows = slice(c * width, (c + 1) * width)
        pre = dg(win_ref[:, rows], low_middle, 0, 0) + column(col_ref, 8 + c)
        gelu, slope = gelu_and_slope(pre)
        act = gelu.astype(BF)
        act_ref[rows, :] = act
        slope_ref[rows, :] = slope.astype(slope_ref.dtype)
        summed = summed + dg(wback_ref[:, rows], act, 1, 0)
    unit_two, rstd_two = normed(summed)
    return unit_one, rstd_one, low_middle, unit_two, rstd_two


def dense_back(grad, unit_one, rstd_one, slope_ref, unit_two, rstd_two, ctx, stat_ref, rest_ref, col_ref,
               sums_ref, joined_ref, gctx_ref, inner_ref, dz_ref, du_ref, dattn_ref):
    wo_ref, win_ref, wback_ref = parts_of(rest_ref)
    sums_ref[2] += lanes_sum(grad * unit_two)
    sums_ref[3] += lanes_sum(grad)
    grad_summed = normed_back(grad, unit_two, rstd_two, column(col_ref, 2))
    dz = grad_summed.astype(BF)
    dz_ref[...] = dz
    sums_ref[7] += lanes_sum(dz.astype(F32))
    width = dz.shape[0]
    grad_middle = grad_summed
    for c in range(win_ref.shape[1] // width):
        rows = slice(c * width, (c + 1) * width)
        du = (dg(wback_ref[:, rows], dz, 0, 0) * slope_ref[rows, :].astype(F32)).astype(BF)
        du_ref[rows, :] = du
        sums_ref[8 + c] += lanes_sum(du.astype(F32))
        grad_middle = grad_middle + dg(win_ref[:, rows], du, 1, 0)
    sums_ref[0] += lanes_sum(grad_middle * unit_one)
    sums_ref[1] += lanes_sum(grad_middle)
    grad_joined = normed_back(grad_middle, unit_one, rstd_one, column(col_ref, 0))
    joined_ref[...] = grad_joined
    dattn = grad_joined.astype(BF)
    dattn_ref[...] = dattn
    sums_ref[6] += lanes_sum(dattn.astype(F32))
    grad_ctx = dg(wo_ref[...], dattn, 1, 0)
    for h in range(stat_ref.shape[0]):
        rows = slice(h * HEAD_DIM, (h + 1) * HEAD_DIM)
        part = (grad_ctx[rows] * stat_ref[h, 0:1, :]).astype(BF)
        gctx_ref[rows, :] = part
        inner_ref[h] = jnp.sum(part.astype(F32) * ctx[rows].astype(F32), axis=0, keepdims=True)


def tile(rows):
    return pl.BlockSpec((rows, TILE), lambda i: (0, i))


def heads_tile(heads, rows):
    return pl.BlockSpec((heads, rows, TILE), lambda i: (0, 0, i))


def rest_spec(w_rest):
    return pl.BlockSpec(w_rest.shape, lambda i: (0, 0), pipeline_mode=pl.Buffered(1))


def parts_of(rest_ref):
    width = rest_ref.shape[0]
    hidden = (rest_ref.shape[1] - width) // 2
    return rest_ref.at[:, 0:width], rest_ref.at[:, width : width + hidden], rest_ref.at[:, width + hidden :]


def column_spec(width):
    return pl.BlockSpec((width, LANES), lambda i: (0, 3 * width // LANES))


def first_dense_kernel(signal_ref, ctx_ref, rest_ref, col_ref,
                       unit_one_ref, unit_two_ref, rstd_ref, low_out_ref, act_ref, slope_ref):
    unit_one, rstd_one, _, unit_two, rstd_two = dense_forward(
        signal_ref[...].astype(F32), ctx_ref[...], rest_ref, col_ref, act_ref, slope_ref)
    unit_one_ref[...] = unit_one
    unit_two_ref[...] = unit_two
    rstd_ref[0:1, :] = rstd_one
    rstd_ref[1:2, :] = rstd_two
    low_out_ref[...] = (unit_two * column(col_ref, 2) + column(col_ref, 3)).astype(BF)


def first_dense(signal, ctx, w_rest, w_first):
    width, tokens = signal.shape
    hidden = (w_rest.shape[1] - width) // 2
    return pl.pallas_call(
        first_dense_kernel,
        name="first_dense",
        grid=(tokens // TILE,),
        in_specs=[tile(width), tile(width), rest_spec(w_rest), column_spec(width)],
        out_specs=[tile(width), tile(width), tile(8), tile(width), tile(hidden), tile(hidden)],
        out_shape=[
            jax.ShapeDtypeStruct((width, tokens), F32),
            jax.ShapeDtypeStruct((width, tokens), F32),
            jax.ShapeDtypeStruct((8, tokens), F32),
            jax.ShapeDtypeStruct((width, tokens), BF),
            jax.ShapeDtypeStruct((hidden, tokens), BF),
            jax.ShapeDtypeStruct((hidden, tokens), BF),
        ],
        compiler_params=params(),
        cost_estimate=cost(2 * tokens * width * (width + 2 * hidden), 24 << 20, tokens * hidden),
    )(signal, ctx, w_rest, w_first)


def second_dense_kernel(unit_ref, ctx_ref, cot_ref, stat_ref, rest_ref, col_ref,
                        out_ref, sums_ref, joined_ref, gctx_ref, inner_ref, mid_ref, act_ref, dz_ref, du_ref, dattn_ref, slope_ref):
    @pl.when(pl.program_id(0) == 0)
    def _():
        sums_ref[...] = jnp.zeros(sums_ref.shape, F32)

    ctx = ctx_ref[...]
    gain, shift = column(col_ref, 2), column(col_ref, 3)
    unit_one, rstd_one, low_middle, unit_two, rstd_two = dense_forward(
        unit_ref[...] * gain + shift, ctx, rest_ref, col_ref, act_ref, slope_ref)
    mid_ref[...] = low_middle
    out_ref[...] = (unit_two * gain + shift).astype(BF).T
    dense_back(cot_ref[...].astype(F32), unit_one, rstd_one, slope_ref, unit_two, rstd_two, ctx, stat_ref,
               rest_ref, col_ref, sums_ref, joined_ref, gctx_ref, inner_ref, dz_ref, du_ref, dattn_ref)


def second_dense(unit, ctx, cot, stat, w_rest, w_first):
    width, tokens = unit.shape
    hidden = (w_rest.shape[1] - width) // 2
    heads = stat.shape[0]
    return pl.pallas_call(
        second_dense_kernel,
        name="second_dense",
        grid=(tokens // TILE,),
        in_specs=[tile(width), tile(width), tile(width), heads_tile(heads, 2), rest_spec(w_rest), column_spec(width)],
        out_specs=[pl.BlockSpec((TILE, width), lambda i: (i, 0)), whole((12, width, LANES)), tile(width), tile(width), heads_tile(heads, 1),
                   tile(width), tile(hidden), tile(width), tile(hidden), tile(width)],
        out_shape=[
            jax.ShapeDtypeStruct((tokens, width), BF),
            jax.ShapeDtypeStruct((12, width, LANES), F32),
            jax.ShapeDtypeStruct((width, tokens), F32),
            jax.ShapeDtypeStruct((width, tokens), BF),
            jax.ShapeDtypeStruct((heads, 1, tokens), F32),
            jax.ShapeDtypeStruct((width, tokens), BF),
            jax.ShapeDtypeStruct((hidden, tokens), BF),
            jax.ShapeDtypeStruct((width, tokens), BF),
            jax.ShapeDtypeStruct((hidden, tokens), BF),
            jax.ShapeDtypeStruct((width, tokens), BF),
        ],
        scratch_shapes=[pltpu.VMEM((hidden, TILE), F32)],
        compiler_params=params(),
        cost_estimate=cost(4 * tokens * width * (width + 2 * hidden), 28 << 20, tokens * hidden),
    )(unit, ctx, cot, stat, w_rest, w_first)


def first_back_kernel(prior_ref, dqkv_ref, unit_one_ref, unit_two_ref, rstd_ref, slope_ref, ctx_ref, stat_ref, sums_in_ref,
                      wqkv_ref, rest_ref, col_ref,
                      vec_ref, joined_ref, gctx_ref, inner_ref, mid_ref, dz_ref, du_ref, dattn_ref, sums_ref):
    step = pl.program_id(0)

    @pl.when(step == 0)
    def _():
        sums_ref[...] = sums_in_ref[...]

    unit_one = unit_one_ref[...]
    mid_ref[...] = (unit_one * column(col_ref, 0) + column(col_ref, 1)).astype(BF)
    grad = prior_ref[...] + dg(wqkv_ref[...], dqkv_ref[...], 1, 0)
    dense_back(grad, unit_one, rstd_ref[0:1, :], slope_ref, unit_two_ref[...], rstd_ref[1:2, :], ctx_ref[...], stat_ref,
               rest_ref, col_ref, sums_ref, joined_ref, gctx_ref, inner_ref, dz_ref, du_ref, dattn_ref)

    @pl.when(step == pl.num_programs(0) - 1)
    def _():
        lane = lax.broadcasted_iota(jnp.int32, vec_ref.shape, 1)
        out = jnp.zeros(vec_ref.shape, F32)
        for j in (0, 1, 2, 3, 6, 7, 8, 9, 10, 11):
            out = jnp.where(lane == j, jnp.sum(sums_ref[j], axis=1, keepdims=True), out)
        vec_ref[...] = out


def first_back(prior, dqkv, unit_one, unit_two, rstd, slope, ctx, stat, sums, w_first, w_rest):
    width, tokens = prior.shape
    hidden = (w_rest.shape[1] - width) // 2
    heads = stat.shape[0]
    return pl.pallas_call(
        first_back_kernel,
        name="first_back",
        grid=(tokens // TILE,),
        in_specs=[tile(width), tile(3 * width), tile(width), tile(width), tile(8), tile(hidden), tile(width), heads_tile(heads, 2), whole(sums.shape),
                  pl.BlockSpec((width, 3 * width), lambda i: (0, 0)), rest_spec(w_rest), column_spec(width)],
        out_specs=[whole((width, LANES)), tile(width), tile(width), heads_tile(heads, 1), tile(width), tile(width), tile(hidden), tile(width)],
        out_shape=[
            jax.ShapeDtypeStruct((width, LANES), F32),
            jax.ShapeDtypeStruct((width, tokens), F32),
            jax.ShapeDtypeStruct((width, tokens), BF),
            jax.ShapeDtypeStruct((heads, 1, tokens), F32),
            jax.ShapeDtypeStruct((width, tokens), BF),
            jax.ShapeDtypeStruct((width, tokens), BF),
            jax.ShapeDtypeStruct((hidden, tokens), BF),
            jax.ShapeDtypeStruct((width, tokens), BF),
        ],
        scratch_shapes=[pltpu.VMEM((12, width, LANES), F32)],
        compiler_params=params(),
        cost_estimate=cost(2 * tokens * width * (4 * width + 2 * hidden), 28 << 20),
    )(prior, dqkv, unit_one, unit_two, rstd, slope, ctx, stat, sums, w_first, w_rest, w_first)


class Layout:
    def __init__(self, mesh_batch, mesh_shard, width):
        self.batch = mesh_batch
        self.shards = mesh_shard
        self.parts = min(mesh_batch, width // mesh_shard // 16)
        self.planes = self.parts // 2
        self.rows = width // mesh_shard // self.parts

    def swap(self, value, axis, distance):
        size = self.batch if axis == "batch" else self.shards
        return lax.ppermute(value, axis, [(i, i ^ distance) for i in range(size)])

    def place(self):
        return jnp.stack([lax.axis_index("batch") % self.parts, lax.axis_index("shard")]).astype(jnp.int32)

    def row_of(self, place_ref, c, e, d):
        block = (place_ref[1] ^ d) * self.parts + (place_ref[0] ^ (2 * e + c))
        return pl.multiple_of(block * self.rows, self.rows)

    def along_shards(self, blocks):
        return [self.swap(blocks[d % len(blocks)], "shard", d) for d in range(1, self.shards)]

    def across_plane(self, blocks):
        return [self.swap(blocks[e % len(blocks)], "batch", 2 * e) for e in range(1, self.planes)]

    def across_cores(self, block):
        return self.swap(block, "batch", 1)

    def across_rest(self, own):
        distance = self.parts
        while distance < self.batch:
            own = add([own, self.swap(own, "batch", distance)])[0]
            distance *= 2
        return own


def tree(values):
    while len(values) > 1:
        values = [a + b for a, b in zip(values[::2], values[1::2], strict=True)]
    return values[0]


def whole_specs(values, tokens_in=()):
    return [whole(v.shape) for v in values] + [pl.BlockSpec(memory_space=pl.ANY)] * len(tokens_in)


def join_kernel(count, *refs):
    out_ref = refs[-1]
    at = 0
    for source in refs[:count]:
        out_ref[at : at + source.shape[0], :] = source[...]
        at += source.shape[0]


def join(blocks, tokens_in=()):
    rows, columns = sum(b.shape[0] for b in blocks), blocks[0].shape[1]
    return pl.pallas_call(
        functools.partial(join_kernel, len(blocks)),
        name="join",
        grid=(1,),
        in_specs=whole_specs(blocks, tokens_in),
        out_specs=whole((rows, columns)),
        out_shape=jax.ShapeDtypeStruct((rows, columns), BF),
        compiler_params=params(),
        cost_estimate=cost(0, 4 * rows * columns),
    )(*blocks, *tokens_in)


def add_kernel(count, outs, *refs):
    total = refs[0][...].astype(F32)
    for other in refs[1:count]:
        total = total + other[...].astype(F32)
    total = total.astype(BF)
    rows = refs[-1].shape[0]
    for i in range(outs):
        refs[i - outs][...] = total[i * rows : (i + 1) * rows]


def add(values, outs=1, tokens_in=()):
    rows, columns = values[0].shape
    part = jax.ShapeDtypeStruct((rows // outs, columns), BF)
    return pl.pallas_call(
        functools.partial(add_kernel, len(values), outs),
        name="add",
        grid=(1,),
        in_specs=whole_specs(values, tokens_in),
        out_specs=[whole(part.shape)] * outs,
        out_shape=[part] * outs,
        compiler_params=params(),
        cost_estimate=cost(len(values) * rows * columns, 2 * (len(values) + 1) * rows * columns),
    )(*values, *tokens_in)


def add_squares_kernel(count, others, *refs):
    out_ref = refs[-1]
    total = refs[0][...].astype(F32)
    for other in refs[1:count]:
        total = total + other[...].astype(F32)
    total = total.astype(BF)
    squares = jnp.sum(jnp.square(total.astype(F32)), keepdims=True)
    for other in refs[count : count + others]:
        squares = squares + jnp.sum(jnp.square(other[...].astype(F32)), keepdims=True)
    out_ref[...] = total
    high = squares.astype(BF)
    middle = (squares - high.astype(F32)).astype(BF)
    low = (squares - high.astype(F32) - middle.astype(F32)).astype(BF)
    used = total.shape[1] - LANES
    tail = total[:, used:]
    lane = lax.broadcasted_iota(jnp.int32, tail.shape, 1)
    for i, piece in enumerate((high, middle, low)):
        tail = jnp.where(lane == SQUARES_AT + i, piece.astype(F32), tail.astype(F32)).astype(BF)
    out_ref[:, used:] = tail


def add_squares(values, others):
    rows, columns = values[0].shape
    return pl.pallas_call(
        functools.partial(add_squares_kernel, len(values), len(others)),
        name="add_squares",
        grid=(1,),
        in_specs=whole_specs(list(values) + list(others)),
        out_specs=whole((rows, columns)),
        out_shape=jax.ShapeDtypeStruct((rows, columns), BF),
        compiler_params=params(),
        cost_estimate=cost(len(values) * rows * columns, 2 * (len(values) + 1) * rows * columns),
    )(*values, *others)


def shard_squares_kernel(layout, place_ref, mine_ref, theirs_ref, out_ref):
    used = mine_ref.shape[1] - LANES
    total = jnp.zeros((1, LANES), F32)
    lane = lax.broadcasted_iota(jnp.int32, (1, LANES), 1)
    riding = (lane >= SQUARES_AT) & (lane < SQUARES_AT + 3)
    for part in range(layout.parts):
        away = place_ref[0] ^ part
        at = pl.ds(pl.multiple_of((away >> 1) * layout.rows, layout.rows), layout.rows)
        mine = mine_ref[at, used:].astype(F32)[0:1]
        theirs = theirs_ref[at, used:].astype(F32)[0:1]
        total = total + jnp.where((away & 1) == 0, mine, theirs)
    total = jnp.sum(jnp.where(riding, total, 0.0), axis=1, keepdims=True)
    out_ref[...] = jnp.broadcast_to(total, out_ref.shape)


def shard_squares(layout, place, mine, theirs):
    return pl.pallas_call(
        functools.partial(shard_squares_kernel, layout),
        name="shard_squares",
        grid=(1,),
        in_specs=[pl.BlockSpec(memory_space=pltpu.SMEM)] + whole_specs((mine, theirs)),
        out_specs=whole((8, LANES)),
        out_shape=jax.ShapeDtypeStruct((8, LANES), F32),
        compiler_params=params(),
        cost_estimate=cost(0, 4 * mine.size),
    )(place, mine, theirs)


def pick_first_kernel(place_ref, w_ref, vec_ref, out_ref, columns_ref, hold_ref):
    hold_ref[...] = jnp.zeros(hold_ref.shape, F32)
    hold_ref[0 : vec_ref.shape[0], 0 : vec_ref.shape[1]] = vec_ref[...]
    hold_ref[...] = hold_ref[...].T
    columns_ref[...] = hold_ref[0 : columns_ref.shape[0], :].astype(BF)
    used = w_ref.shape[1]
    rows = out_ref.shape[0]
    out_ref[:, 0:used] = w_ref[...].astype(BF)
    out_ref[:, used:] = hold_ref[pl.ds(pl.multiple_of(place_ref[0] * rows, rows), rows), :].astype(BF)


def pick_first(layout, place, weights, vectors):
    shard_rows, columns = weights.shape
    used = columns // 4
    return pl.pallas_call(
        pick_first_kernel,
        name="pick_first",
        grid_spec=pltpu.PrefetchScalarGridSpec(
            num_scalar_prefetch=1,
            grid=(1,),
            in_specs=[pl.BlockSpec((layout.rows, used), lambda i, place: (place[0], 0)), pl.BlockSpec(vectors.shape, lambda i, place: (0, 0))],
            out_specs=[pl.BlockSpec((layout.rows, used + LANES), lambda i, place: (0, 0)), pl.BlockSpec((shard_rows, LANES), lambda i, place: (0, 0))],
            scratch_shapes=[pltpu.VMEM((LANES, LANES), F32)],
        ),
        out_shape=[jax.ShapeDtypeStruct((layout.rows, used + LANES), BF), jax.ShapeDtypeStruct((shard_rows, LANES), BF)],
        compiler_params=params(),
        cost_estimate=cost(0, 6 * layout.rows * columns),
    )(place, weights, vectors)


def pick_rest_kernel(place_ref, w_ref, *refs):
    out_ref = refs[-1]
    out_ref[...] = w_ref[:, w_ref.shape[1] - out_ref.shape[1] :].astype(BF)


def pick_rest(layout, place, weights, tokens_in):
    columns = weights.shape[1]
    return pl.pallas_call(
        pick_rest_kernel,
        name="pick_rest",
        grid_spec=pltpu.PrefetchScalarGridSpec(
            num_scalar_prefetch=1,
            grid=(1,),
            in_specs=[pl.BlockSpec((layout.rows, columns), lambda i, place: (place[0], 0))] + [pl.BlockSpec(memory_space=pl.ANY)] * len(tokens_in),
            out_specs=pl.BlockSpec((layout.rows, 3 * columns // 4), lambda i, place: (0, 0)),
        ),
        out_shape=jax.ShapeDtypeStruct((layout.rows, 3 * columns // 4), BF),
        compiler_params=params(),
        cost_estimate=cost(0, 6 * layout.rows * columns),
    )(place, weights, *tokens_in)


def put_blocks(layout, place_ref, sources, out_ref):
    for c, source in enumerate(sources):
        for e in range(layout.planes):
            for d in range(1, layout.shards):
                at = (e * (layout.shards - 1) + d - 1) * layout.rows
                out_ref[pl.ds(layout.row_of(place_ref, c, e, d), layout.rows), :] = source[at : at + layout.rows, :]


def own_rows(layout, place_ref):
    rows = layout.rows * layout.parts
    return pl.ds(pl.multiple_of(place_ref[1] * rows, rows), rows)


def collect_first_kernel(layout, place_ref, w_ref, columns_ref, mine_ref, theirs_ref, out_ref):
    put_blocks(layout, place_ref, (mine_ref, theirs_ref), out_ref)
    rows = own_rows(layout, place_ref)
    used = w_ref.shape[1]
    out_ref[rows, 0:used] = w_ref[...].astype(BF)
    out_ref[rows, used:] = columns_ref[...]


def collect_rest_kernel(layout, place_ref, w_ref, mine_ref, theirs_ref, out_ref):
    put_blocks(layout, place_ref, (mine_ref, theirs_ref), out_ref)
    out_ref[own_rows(layout, place_ref), :] = w_ref[...].astype(BF)


def collect_first(layout, place, weights, columns, mine, theirs):
    shard_rows, all_columns = weights.shape
    rows = shard_rows * layout.shards
    total = mine.shape[1]
    return pl.pallas_call(
        functools.partial(collect_first_kernel, layout),
        name="collect_first",
        grid=(1,),
        in_specs=[pl.BlockSpec(memory_space=pltpu.SMEM), pl.BlockSpec((shard_rows, all_columns // 4), lambda i: (0, 0))] + whole_specs((columns, mine, theirs)),
        out_specs=whole((rows, total)),
        out_shape=jax.ShapeDtypeStruct((rows, total), BF),
        compiler_params=params(),
        cost_estimate=cost(0, 4 * rows * total),
    )(place, weights, columns, mine, theirs)


def collect_rest(layout, place, weights, mine, theirs):
    shard_rows, all_columns = weights.shape
    rows = shard_rows * layout.shards
    total = mine.shape[1]
    block = all_columns // 4
    return pl.pallas_call(
        functools.partial(collect_rest_kernel, layout),
        name="collect_rest",
        grid=(3,),
        in_specs=[pl.BlockSpec(memory_space=pltpu.SMEM), pl.BlockSpec((shard_rows, block), lambda i: (0, i + 1))]
        + [pl.BlockSpec((t.shape[0], block), lambda i: (0, i)) for t in (mine, theirs)],
        out_specs=pl.BlockSpec((rows, block), lambda i: (0, i)),
        out_shape=jax.ShapeDtypeStruct((rows, total), BF),
        compiler_params=params(),
        cost_estimate=cost(0, 4 * rows * total),
    )(place, weights, mine, theirs)


def in_order(layout, place_ref, source_ref, target_ref):
    at = 0
    for c in range(2):
        for e in range(layout.planes):
            for d in range(layout.shards):
                target_ref[at : at + layout.rows] = source_ref[pl.ds(layout.row_of(place_ref, c, e, d), layout.rows), :]
                at += layout.rows


def weight_step(left_ref, ra_ref, rb_ref, keep_ref, send_ref):
    out = (dg(left_ref[0], ra_ref[...], 1, 1) + dg(left_ref[1], rb_ref[...], 1, 1)).astype(BF)
    half = out.shape[0] // 2
    keep_ref[...] = out[:half]
    send_ref[...] = out[half:]


def weight_in_kernel(layout, place_ref, la_ref, lb_ref, ra_ref, rb_ref, keep_ref, send_ref, left_ref):
    @pl.when(pl.program_id(0) == 0)
    def _():
        in_order(layout, place_ref, la_ref, left_ref.at[0])
        in_order(layout, place_ref, lb_ref, left_ref.at[1])

    weight_step(left_ref, ra_ref, rb_ref, keep_ref, send_ref)


def weight_back_kernel(layout, place_ref, za_ref, zb_ref, ca_ref, cb_ref, ra_ref, rb_ref, oa_ref, ob_ref, keep_ref, send_ref, left_ref):
    step = pl.program_id(0)
    last = step == pl.num_programs(0) - 1

    @pl.when(step == 0)
    def _():
        in_order(layout, place_ref, za_ref, left_ref.at[0])
        in_order(layout, place_ref, zb_ref, left_ref.at[1])

    @pl.when(last)
    def _():
        in_order(layout, place_ref, ca_ref, left_ref.at[0])
        in_order(layout, place_ref, cb_ref, left_ref.at[1])
        weight_step(left_ref, oa_ref, ob_ref, keep_ref, send_ref)

    @pl.when(jnp.logical_not(last))
    def _():
        weight_step(left_ref, ra_ref, rb_ref, keep_ref, send_ref)


def weight_call(kernel, name, layout, place, lefts, rights, tails, block):
    rows, tokens = lefts[0].shape
    steps = rights[0].shape[0] // block
    count = steps + (1 if tails else 0)
    half = jax.ShapeDtypeStruct((rows // 2, count * block), BF)
    return pl.pallas_call(
        functools.partial(kernel, layout),
        name=name,
        grid=(count,),
        in_specs=[pl.BlockSpec(memory_space=pltpu.SMEM)] + [whole((rows, tokens))] * len(lefts)
        + [pl.BlockSpec((block, tokens), lambda i: (jnp.minimum(i, steps - 1), 0))] * len(rights)
        + [whole((block, tokens))] * len(tails),
        out_specs=[pl.BlockSpec((rows // 2, block), lambda i: (0, i))] * 2,
        out_shape=[half, half],
        scratch_shapes=[pltpu.VMEM((2, rows, tokens), BF)],
        compiler_params=params(),
        cost_estimate=cost(4 * rows * count * block * tokens, 4 * (rows + count * block) * tokens),
    )(place, *lefts, *rights, *tails)


def last_back_kernel(layout, first_pair, given, place_ref, e_ref, qkv_ref, stat_ref, grad_ref, inner_ref, act_one_ref, act_two_ref, dqkv_two_ref, vec_in_ref, *refs):
    out_ref, keep_ref, send_ref, vec_ref, ds_ref, left_ref, order_ref = refs[given:]
    step = pl.program_id(0)

    @pl.when(step == 0)
    def _():
        in_order(layout, place_ref, act_one_ref, left_ref.at[0])
        in_order(layout, place_ref, act_two_ref, left_ref.at[1])
        vec_ref[...] = vec_in_ref[...]
        if first_pair:
            keep_ref[...] = refs[1][...]
            send_ref[...] = refs[2][...]

    attend_back_kernel(e_ref, qkv_ref, stat_ref, grad_ref, inner_ref, out_ref, ds_ref)
    pair = out_ref.shape[1]
    for t in range(3):
        total = (dg(left_ref[0], out_ref[t], 1, 1) + dg(left_ref[1], dqkv_two_ref[t], 1, 1)).astype(BF)
        half = total.shape[0] // 2
        columns = pl.ds(pl.multiple_of((3 * (first_pair + step) + t) * pair, pair), pair)
        keep_ref[:, columns] = total[:half]
        send_ref[:, columns] = total[half:]
    rows = pl.ds(pl.multiple_of((first_pair + step) * pair, pair), pair)
    lane = lax.broadcasted_iota(jnp.int32, (pair, LANES), 1)
    vec = vec_ref[rows, :]
    for lane_at, t in ((4, 0), (5, 2)):
        both = lanes_sum(out_ref[t].astype(F32)) + lanes_sum(dqkv_two_ref[t].astype(F32))
        vec = jnp.where(lane == lane_at, jnp.sum(both, axis=1, keepdims=True), vec)
    vec_ref[rows, :] = vec

    @pl.when(step == pl.num_programs(0) - 1)
    def _():
        in_order(layout, place_ref, vec_ref, order_ref)
        half = order_ref.shape[0] // 2
        used = keep_ref.shape[1] - LANES
        keep_ref[:, used:] = order_ref[0:half].astype(BF)
        send_ref[:, used:] = order_ref[half:].astype(BF)


def last_back(layout, place, first_pair, pairs, e, qkv, stat, grad, inner, act_one, act_two, dqkv_two, vec, earlier, tokens_in):
    heads, tokens, _ = e.shape
    width = grad.shape[0]
    pair = 2 * HEAD_DIM
    half = jax.ShapeDtypeStruct((width // 2, 3 * width + LANES), BF)
    earlier_specs = [pl.BlockSpec(memory_space=pl.ANY), whole(half.shape), whole(half.shape)] if earlier else []
    return pl.pallas_call(
        functools.partial(last_back_kernel, layout, first_pair, len(earlier) + len(tokens_in)),
        name="last_back",
        grid=(pairs,),
        in_specs=[
            pl.BlockSpec(memory_space=pltpu.SMEM),
            pl.BlockSpec((2, tokens, tokens), lambda i: (first_pair + i, 0, 0)),
            pl.BlockSpec((3, pair, tokens), lambda i: (0, first_pair + i, 0)),
            pl.BlockSpec((2, 2, tokens), lambda i: (first_pair + i, 0, 0)),
            pl.BlockSpec((pair, tokens), lambda i: (first_pair + i, 0)),
            pl.BlockSpec((2, 1, tokens), lambda i: (first_pair + i, 0, 0)),
            whole((width, tokens)),
            whole((width, tokens)),
            pl.BlockSpec((3, pair, tokens), lambda i: (0, first_pair + i, 0)),
            whole((width, LANES)),
        ] + earlier_specs + [pl.BlockSpec(memory_space=pl.ANY)] * len(tokens_in),
        out_specs=[
            pl.BlockSpec((3, pair, tokens), lambda i: (0, first_pair + i, 0)),
            whole(half.shape),
            whole(half.shape),
            whole((width, LANES)),
        ],
        out_shape=[
            jax.ShapeDtypeStruct((3, width, tokens), BF),
            half,
            half,
            jax.ShapeDtypeStruct((width, LANES), F32),
        ],
        input_output_aliases={10: 0} if earlier else {},
        scratch_shapes=[pltpu.VMEM((2, tokens, tokens), BF), pltpu.VMEM((2, width, tokens), BF), pltpu.VMEM((width, LANES), F32)],
        compiler_params=params(),
        cost_estimate=cost(pairs * (16 * pair * tokens * tokens + 12 * width * pair * tokens), pairs * 4 * tokens * tokens + 4 * width * tokens),
    )(place, e, qkv, stat, grad, inner, act_one, act_two, dqkv_two, vec, *earlier, *tokens_in)


def input_kernel(joined_ref, dqkv_ref, w_ref, *refs):
    refs[-1][...] = (joined_ref[...] + dg(w_ref[...], dqkv_ref[...], 1, 0)).T


def input_gradient(joined, dqkv, w_first, tokens_in):
    width, tokens = joined.shape
    return pl.pallas_call(
        input_kernel,
        name="input_gradient",
        grid=(tokens // TILE,),
        in_specs=[tile(width), tile(3 * width), pl.BlockSpec((width, 3 * width), lambda i: (0, 0))] + [pl.BlockSpec(memory_space=pl.ANY)] * len(tokens_in),
        out_specs=pl.BlockSpec((TILE, width), lambda i: (i, 0)),
        out_shape=jax.ShapeDtypeStruct((tokens, width), F32),
        compiler_params=params(),
        cost_estimate=cost(6 * width * width * tokens, 8 << 20),
    )(joined, dqkv, w_first, *tokens_in)


def adam_kernel(layout, pieces, place_ref, *refs):
    grads = [refs[2 * i : 2 * i + 2] for i in range(len(pieces))]
    rest = refs[2 * len(pieces) :]
    shares, rest = rest[: layout.shards], rest[layout.shards :]
    w_ref, one_ref, two_ref, v_ref, vone_ref, vtwo_ref = rest[:6]
    gw_ref, nw_ref, none_ref, ntwo_ref, gv_ref, nv_ref, nvone_ref, nvtwo_ref, norm_ref = rest[6:15]
    holds, hold_ref = rest[15:-1], rest[-1]
    norm = jnp.sqrt(tree([share[0:1, 0:1] for share in shares]))
    clip_limit = math.sqrt(D * WCOLS)
    factor = clip_limit / jnp.maximum(norm, clip_limit)
    step = pl.program_id(0)
    rows = layout.rows

    @pl.when(step == 0)
    def _():
        norm_ref[...] = jnp.broadcast_to(norm, norm_ref.shape)
        for blocks, target in zip(grads, holds, strict=True):
            for c, block in enumerate(blocks):
                for e in range(layout.planes):
                    part = place_ref[0] ^ (2 * e + c)
                    target[pl.ds(pl.multiple_of(part * rows, rows), rows), :] = block[e * rows : (e + 1) * rows, :]
        hold_ref[0 : holds[-1].shape[0], :] = holds[-1][:, holds[-1].shape[1] - LANES :].astype(F32)
        grad = hold_ref[...].T[0 : gv_ref.shape[0], 0 : gv_ref.shape[1]]
        gv_ref[...] = grad
        nv_ref[...], nvone_ref[...], nvtwo_ref[...] = adam_update(v_ref[...], vone_ref[...], vtwo_ref[...], grad * factor)

    size = w_ref.shape[0]
    at = pl.ds(pl.multiple_of(step * size, size), size)
    for held, spans in zip(holds, pieces, strict=True):
        for source, target, width in spans:
            to = slice(target, target + width)
            grad = held[at, source : source + width].astype(F32)
            gw_ref[:, to] = grad
            nw_ref[:, to], none_ref[:, to], ntwo_ref[:, to] = adam_update(w_ref[:, to], one_ref[:, to], two_ref[:, to], grad * factor)


def adam(layout, place, shares, pieces, grads, weights, first, second, vectors, vector_first, vector_second):
    rows, columns = weights.shape
    block = 16
    natural = pl.BlockSpec((block, columns), lambda i: (i, 0))
    big = jax.ShapeDtypeStruct((rows, columns), F32)
    little = jax.ShapeDtypeStruct(vectors.shape, F32)
    flat = [t for blocks in grads for t in blocks] + list(shares)
    return pl.pallas_call(
        functools.partial(adam_kernel, layout, pieces),
        name="adam",
        grid=(rows // block,),
        in_specs=[pl.BlockSpec(memory_space=pltpu.SMEM)] + whole_specs(flat) + [natural] * 3 + [whole(vectors.shape)] * 3,
        out_specs=[natural] * 4 + [whole(vectors.shape)] * 4 + [whole((1, 1))],
        out_shape=[big] * 4 + [little] * 4 + [jax.ShapeDtypeStruct((1, 1), F32)],
        scratch_shapes=[pltpu.VMEM((rows, blocks[0].shape[1]), BF) for blocks in grads] + [pltpu.VMEM((LANES, LANES), F32)],
        compiler_params=params(),
        cost_estimate=cost(20 * rows * columns, 30 * rows * columns, rows * columns),
    )(place, *flat, weights, first, second, vectors, vector_first, vector_second)


def masks(segments, tags, length):
    tokens = segments.shape[0]
    matches = segments[None, :] == jnp.arange(tags.shape[0], dtype=jnp.int32)[:, None]
    group = jnp.sum(jnp.where(matches, tags[:, None], 0), axis=0)
    live = jnp.arange(tokens, dtype=jnp.int32) < length
    kinds = jnp.arange(16, dtype=jnp.int32)[:, None]
    same = group[None, :] == kinds
    kmask = jnp.where(kinds < 4, (same & live[None, :]).astype(F32), jnp.where(kinds == 4, (~live)[None, :].astype(F32), 0.0))
    qmask = jnp.where(kinds < 4, jnp.where(same, 0.0, -FAR), jnp.where(kinds == 4, -FAR, 0.0))
    return kmask.astype(BF), jnp.broadcast_to(qmask, (16, tokens)).astype(BF)


def on_device(layout, inputs, cotangent, lengths, segment_ids, group_tags, weights, first_moments, second_moments, vectors, vector_first, vector_second):
    _, tokens, width = inputs.shape
    hidden = (weights.shape[1] - 4 * width) // 2
    pair = 2 * HEAD_DIM
    place = layout.place()
    kmask, qmask = masks(segment_ids[0], group_tags[0], lengths[0])
    act_one = inputs[0].T
    cot = cotangent[0].T

    first_part, own_columns = pick_first(layout, place, weights, vectors)
    first_z = join(layout.along_shards([first_part]))
    rest_part = pick_rest(layout, place, weights, (first_z,))
    first_mine = join([first_z] + layout.across_plane([first_z]))
    rest_z = join(layout.along_shards([rest_part]), (first_mine,))
    w_first = collect_first(layout, place, weights, own_columns, first_mine, layout.across_cores(first_mine))
    e_one, ctx_one, qkv_one, stat_one = attend(act_one, w_first, kmask, qmask)
    rest_mine = join([rest_z] + layout.across_plane([rest_z]), (ctx_one,))
    w_rest = collect_rest(layout, place, weights, rest_mine, layout.across_cores(rest_mine))
    unit_one, unit_two, rstd, act_two, hid_one, slope = first_dense(act_one, ctx_one, w_rest, w_first)
    e_two, ctx_two, qkv_two, stat_two = attend(act_two, w_first, kmask, qmask)
    outputs, sums, joined_two, gctx_two, inner_two, mid_two, hid_two, dz_two, du_two, dattn_two = second_dense(
        unit_two, ctx_two, cot, stat_two, w_rest, w_first)
    dqkv_two = attend_back(e_two, qkv_two, stat_two, gctx_two, inner_two)
    vec, joined_one, gctx_one, inner_one, mid_one, dz_one, du_one, dattn_one = first_back(
        joined_two, dqkv_two.reshape(3 * width, tokens), unit_one, unit_two, rstd, slope, ctx_one, stat_one, sums, w_first, w_rest)

    keep, send = weight_call(weight_in_kernel, "weight_in", layout, place, (mid_one, mid_two), (du_one, du_two), (), width)
    keep_back, send_back = weight_call(
        weight_back_kernel, "weight_back", layout, place, (dz_one, dz_two, ctx_one, ctx_two), (hid_one, hid_two), (dattn_one, dattn_two), width)
    half_in = add((keep, layout.across_cores(send)), layout.planes, (keep_back,))
    group = width // pair // 2
    operands = (e_one, qkv_one, stat_one, gctx_one, inner_one, act_one, act_two, dqkv_two)
    dqkv, keep, send, vec = last_back(layout, place, 0, group, *operands, vec, (), (half_in[0],))
    half_back = add((keep_back, layout.across_cores(send_back)), layout.planes, (vec,))
    plane_in = add([half_in[0]] + layout.across_plane(half_in), layout.shards, (vec,))
    dqkv, keep, send, vec = last_back(layout, place, group, group, *operands, vec, (dqkv, keep, send), (plane_in[0], half_back[0]))
    half_qkv = add((keep, layout.across_cores(send)), layout.planes)
    own_in = layout.across_rest(add([plane_in[0]] + layout.along_shards(plane_in), 1, (vec,))[0])
    plane_back = add([half_back[0]] + layout.across_plane(half_back), layout.shards, (vec,))
    input_grad = input_gradient(joined_one, dqkv.reshape(3 * width, tokens), w_first, (half_qkv[0], plane_back[0], own_in))
    plane_qkv = add([half_qkv[0]] + layout.across_plane(half_qkv), layout.shards, (input_grad,))
    own_back = layout.across_rest(add([plane_back[0]] + layout.along_shards(plane_back), 1, (input_grad,))[0])
    all_in = join([own_in] + layout.across_plane([own_in]), (plane_qkv[0],))
    all_back = join([own_back] + layout.across_plane([own_back]), (plane_qkv[0],))
    own_qkv = [plane_qkv[0]] + layout.along_shards(plane_qkv)
    if layout.parts < layout.batch:
        own_qkv = [layout.across_rest(add(own_qkv)[0])]
    own_qkv = add_squares(own_qkv, (own_in, own_back))
    all_qkv = join([own_qkv] + layout.across_plane([own_qkv]))
    grads = [(t, layout.across_cores(t)) for t in (all_in, all_back, all_qkv)]
    spans = [
        [(0, 4 * width, hidden)],
        [(0, 4 * width + hidden, hidden), (hidden, 3 * width, width)],
        [((i * 3 + t) * pair, t * width + i * pair, pair) for i in range(width // pair) for t in range(3)],
    ]
    share = shard_squares(layout, place, *grads[2])
    updated = adam(layout, place, [share] + layout.along_shards([share]), spans, grads, weights, first_moments, second_moments, vectors, vector_first, vector_second)
    grad_w, new_weights, new_first, new_second, grad_v, new_vectors, new_vector_first, new_vector_second, grad_norm = updated
    grad_norm = grad_norm.reshape(())
    return (
        outputs[None],
        input_grad[None],
        grad_w,
        grad_v,
        grad_norm,
        new_weights,
        new_first,
        new_second,
        new_vectors,
        new_vector_first,
        new_vector_second,
    )


def solution(mesh):
    rows = ("batch", "shard")
    placed = (
        P(rows, None, None),
        P(rows, None, None),
        P(rows),
        P(rows, None),
        P(rows, None),
        P("shard", None),
        P("shard", None),
        P("shard", None),
        P(None, "shard"),
        P(None, "shard"),
        P(None, "shard"),
    )
    return jax.shard_map(
        functools.partial(on_device, Layout(mesh.shape["batch"], mesh.shape["shard"], D)),
        mesh=mesh,
        in_specs=placed,
        out_specs=(
            P(rows, None, None),
            P(rows, None, None),
            P("shard", None),
            P(None, "shard"),
            P(),
            P("shard", None),
            P("shard", None),
            P("shard", None),
            P(None, "shard"),
            P(None, "shard"),
            P(None, "shard"),
        ),
        check_vma=False,
    )
```

```python
import functools
import math

import jax
import jax.numpy as jnp
from jax import lax
from jax.experimental import pallas as pl
from jax.experimental.pallas import tpu as pltpu
from jax.sharding import PartitionSpec as P

D = 512
FF = 2048
HEADS = 8
HEAD_DIM = 64
STEP = 10
WCOLS = 6144

NORM_EPS = 1e-05
BETA_ONE = 0.5
BETA_TWO = 0.5
ADAM_EPS = 1e-08
DECAY = 0.01
WARMUP = 4000.0
RATE_SCALE = 150000.0

BF = jnp.bfloat16
F32 = jnp.float32
FAR = 1e30
SAFE_SCORE = 60.0
TILE = 256
LANES = 128
SQUARES_AT = 12
COST_SCALE = 100


def params(mebibytes=50):
    return pltpu.CompilerParams(vmem_limit_bytes=mebibytes << 20)


def cost(flops, bytes_accessed, transcendentals=0):
    return pl.CostEstimate(flops=int(flops) // COST_SCALE, bytes_accessed=int(bytes_accessed) // COST_SCALE, transcendentals=int(transcendentals) // COST_SCALE)


def dg(left, right, left_dim, right_dim):
    return lax.dot_general(
        left, right, (((left_dim,), (right_dim,)), ((), ())), preferred_element_type=F32
    )


def whole(shape):
    return pl.BlockSpec(shape, lambda i: (0,) * len(shape))


def adam_update(master, moment_one, moment_two, gradient):
    moment_one = BETA_ONE * moment_one + (1.0 - BETA_ONE) * gradient
    moment_two = BETA_TWO * moment_two + (1.0 - BETA_TWO) * gradient * gradient
    step_rate = RATE_SCALE * D ** (-0.5) * min(STEP ** (-0.5), STEP * WARMUP ** (-1.5))
    fixed_first = moment_one / (1.0 - BETA_ONE**STEP)
    fixed_second = moment_two / (1.0 - BETA_TWO**STEP)
    master = master - step_rate * (
        fixed_first / (jnp.sqrt(fixed_second) + ADAM_EPS) + DECAY * master
    )
    return (master, moment_one, moment_two)


def attend_kernel(act_ref, wq_ref, wk_ref, wv_ref, col_ref, kmask_ref, qmask_ref, e_ref, ctx_ref, qkv_ref, stat_ref):
    act = act_ref[...]
    tokens = act.shape[1]
    q = (dg(wq_ref[...], act, 0, 0) + col_ref[:, 4:5].astype(F32)).astype(BF) * jnp.asarray(HEAD_DIM**-0.5, BF)
    k = dg(wk_ref[...], act, 0, 0).astype(BF)
    v = (dg(wv_ref[...], act, 0, 0) + col_ref[:, 5:6].astype(F32)).astype(BF)
    qkv_ref[0] = q
    qkv_ref[1] = k
    qkv_ref[2] = v
    dead = kmask_ref[4:5, :].astype(F32)
    bound = jnp.zeros((1, 1), F32)
    selves = []
    for h in range(2):
        rows = slice(h * HEAD_DIM, (h + 1) * HEAD_DIM)
        qf, kf = q[rows].astype(F32), k[rows].astype(F32)
        selves.append(jnp.sum(qf * kf, axis=0, keepdims=True))
        q_top = jnp.max(jnp.sum(qf * qf, axis=0, keepdims=True), axis=1, keepdims=True)
        k_top = jnp.max(jnp.sum(kf * kf, axis=0, keepdims=True), axis=1, keepdims=True)
        bound = jnp.maximum(bound, q_top * k_top)
    safe = bound[0, 0] <= SAFE_SCORE * SAFE_SCORE

    def scores(h):
        rows = slice(h * HEAD_DIM, (h + 1) * HEAD_DIM)
        keys = jnp.concatenate([k[rows], kmask_ref[...]], axis=0).T
        queries = jnp.concatenate([q[rows], qmask_ref[...]], axis=0)
        return dg(keys, queries, 1, 0)

    def finish(h, e, e_self):
        rows = slice(h * HEAD_DIM, (h + 1) * HEAD_DIM)
        low_e = e.astype(BF)
        e_ref[h] = low_e
        total = jnp.sum(e, axis=0, keepdims=True) + e_self
        scale = 1.0 / total
        values = v[rows]
        mixed = dg(values, low_e, 1, 0) + values.astype(F32) * e_self.astype(BF).astype(F32)
        ctx_ref[rows, :] = (mixed * scale).astype(BF)
        stat_ref[h, 0:1, :] = scale
        stat_ref[h, 1:2, :] = e_self

    @pl.when(safe)
    def _():
        for h in range(2):
            finish(h, jnp.exp(scores(h)), jnp.exp(selves[h]) * dead)

    @pl.when(jnp.logical_not(safe))
    def _():
        for h in range(2):
            s = scores(h)
            own = jnp.where(dead > 0, selves[h], -FAR)
            top = jnp.maximum(jnp.max(s, axis=0, keepdims=True), own)
            finish(h, jnp.exp(s - top), jnp.exp(own - top) * dead)


def attend(act, w_qkv, kmask, qmask):
    width, tokens = act.shape
    pairs = width // (2 * HEAD_DIM)
    pair = 2 * HEAD_DIM
    heads = width // HEAD_DIM
    return pl.pallas_call(
        attend_kernel,
        name="attend",
        grid=(pairs,),
        in_specs=[
            whole((width, tokens)),
            pl.BlockSpec((width, pair), lambda i: (0, i)),
            pl.BlockSpec((width, pair), lambda i: (0, pairs + i)),
            pl.BlockSpec((width, pair), lambda i: (0, 2 * pairs + i)),
            pl.BlockSpec((pair, pair), lambda i: (i, 3 * pairs)),
            whole((16, tokens)),
            whole((16, tokens)),
        ],
        out_specs=[
            pl.BlockSpec((2, tokens, tokens), lambda i: (i, 0, 0)),
            pl.BlockSpec((pair, tokens), lambda i: (i, 0)),
            pl.BlockSpec((3, pair, tokens), lambda i: (0, i, 0)),
            pl.BlockSpec((2, 2, tokens), lambda i: (i, 0, 0)),
        ],
        out_shape=[
            jax.ShapeDtypeStruct((heads, tokens, tokens), BF),
            jax.ShapeDtypeStruct((width, tokens), BF),
            jax.ShapeDtypeStruct((3, width, tokens), BF),
            jax.ShapeDtypeStruct((heads, 2, tokens), F32),
        ],
        compiler_params=params(),
        cost_estimate=cost(6 * width * width * tokens + 4 * width * tokens * tokens, 2 * heads * tokens * tokens, heads * tokens * tokens),
    )(act, w_qkv, w_qkv, w_qkv, w_qkv, kmask, qmask)


def attend_back_pair(e_ref, qkv_ref, stat_ref, grad_ref, inner_ref, out_ref, ds_ref):
    for h in range(2):
        rows = slice(h * HEAD_DIM, (h + 1) * HEAD_DIM)
        q, k, v = qkv_ref[0, rows], qkv_ref[1, rows], qkv_ref[2, rows]
        grad = grad_ref[rows]
        inner = inner_ref[h]
        e_self = stat_ref[h, 1:2, :]
        grad_f = grad.astype(F32)
        ds = (e_ref[h].astype(F32) * (dg(v.T, grad, 1, 0) - inner)).astype(BF)
        ds_ref[h] = ds
        own = (e_self * (jnp.sum(grad_f * v.astype(F32), axis=0, keepdims=True) - inner)).astype(BF).astype(F32)
        scale = HEAD_DIM**-0.5
        out_ref[0, rows] = ((dg(k, ds, 1, 0) + k.astype(F32) * own) * scale).astype(BF)
        out_ref[2, rows] = (dg(grad, e_ref[h], 1, 1) + grad_f * e_self.astype(BF).astype(F32)).astype(BF)
        out_ref[1, rows] = (dg(q, ds_ref[h], 1, 1) + q.astype(F32) * own).astype(BF)


def attend_back(e, qkv, stat, grad, inner, start=0, pairs=None):
    heads, tokens, _ = e.shape
    width = grad.shape[0]
    pair = 2 * HEAD_DIM
    pairs = pairs or heads // 2
    return pl.pallas_call(
        attend_back_pair,
        name="attend_back",
        grid=(pairs,),
        in_specs=[
            pl.BlockSpec((2, tokens, tokens), lambda i: (start + i, 0, 0)),
            pl.BlockSpec((3, pair, tokens), lambda i: (0, start + i, 0)),
            pl.BlockSpec((2, 2, tokens), lambda i: (start + i, 0, 0)),
            pl.BlockSpec((pair, tokens), lambda i: (start + i, 0)),
            pl.BlockSpec((2, 1, tokens), lambda i: (start + i, 0, 0)),
        ],
        out_specs=pl.BlockSpec((3, pair, tokens), lambda i: (0, i, 0)),
        out_shape=jax.ShapeDtypeStruct((3, pairs * pair, tokens), BF),
        scratch_shapes=[pltpu.VMEM((2, tokens, tokens), BF)],
        compiler_params=params(),
        cost_estimate=cost(8 * pairs * pair * tokens * tokens, 4 * pairs * tokens * tokens),
    )(e, qkv, stat, grad, inner)


def normed(t):
    mean = jnp.mean(t, axis=0, keepdims=True)
    centred = t - mean
    rstd = lax.rsqrt(jnp.mean(centred * centred, axis=0, keepdims=True) + NORM_EPS)
    return centred * rstd, rstd


def normed_back(grad, unit, rstd, gain):
    scaled = grad * gain
    mean = jnp.mean(scaled, axis=0, keepdims=True)
    along = jnp.mean(scaled * unit, axis=0, keepdims=True)
    return rstd * (scaled - mean - unit * along)


def gelu_and_slope(t):
    square = t * t
    inside = jnp.tanh(t * (0.7978845608028654 + (0.7978845608028654 * 0.044715) * square))
    half = 0.5 + 0.5 * inside
    slope = half + (t * (0.5 - 0.5 * inside * inside)) * (
        0.7978845608028654 + (3.0 * 0.7978845608028654 * 0.044715) * square
    )
    return t * half, slope


def lanes_sum(t):
    out = t[:, 0:128]
    for j in range(128, t.shape[1], 128):
        out = out + t[:, j : j + 128]
    return out


def column(col_ref, j):
    return col_ref[:, j : j + 1].astype(F32)


def dense_forward(signal, ctx, rest_ref, col_ref, act_ref, slope_ref):
    wo_ref, win_ref, wback_ref = parts_of(rest_ref)
    joined = signal + dg(wo_ref[...], ctx, 0, 0) + column(col_ref, 6)
    unit_one, rstd_one = normed(joined)
    middle = unit_one * column(col_ref, 0) + column(col_ref, 1)
    low_middle = middle.astype(BF)
    width = middle.shape[0]
    summed = middle + column(col_ref, 7)
    for c in range(win_ref.shape[1] // width):
        rows = slice(c * width, (c + 1) * width)
        pre = dg(win_ref[:, rows], low_middle, 0, 0) + column(col_ref, 8 + c)
        gelu, slope = gelu_and_slope(pre)
        act = gelu.astype(BF)
        act_ref[rows, :] = act
        slope_ref[rows, :] = slope.astype(slope_ref.dtype)
        summed = summed + dg(wback_ref[:, rows], act, 1, 0)
    unit_two, rstd_two = normed(summed)
    return unit_one, rstd_one, low_middle, unit_two, rstd_two


def dense_back(grad, unit_one, rstd_one, slope_ref, unit_two, rstd_two, ctx, stat_ref, rest_ref, col_ref,
               sums_ref, joined_ref, gctx_ref, inner_ref, dz_ref, du_ref, dattn_ref):
    wo_ref, win_ref, wback_ref = parts_of(rest_ref)
    sums_ref[2] += lanes_sum(grad * unit_two)
    sums_ref[3] += lanes_sum(grad)
    grad_summed = normed_back(grad, unit_two, rstd_two, column(col_ref, 2))
    dz = grad_summed.astype(BF)
    dz_ref[...] = dz
    sums_ref[7] += lanes_sum(dz.astype(F32))
    width = dz.shape[0]
    grad_middle = grad_summed
    for c in range(win_ref.shape[1] // width):
        rows = slice(c * width, (c + 1) * width)
        du = (dg(wback_ref[:, rows], dz, 0, 0) * slope_ref[rows, :].astype(F32)).astype(BF)
        du_ref[rows, :] = du
        sums_ref[8 + c] += lanes_sum(du.astype(F32))
        grad_middle = grad_middle + dg(win_ref[:, rows], du, 1, 0)
    sums_ref[0] += lanes_sum(grad_middle * unit_one)
    sums_ref[1] += lanes_sum(grad_middle)
    grad_joined = normed_back(grad_middle, unit_one, rstd_one, column(col_ref, 0))
    joined_ref[...] = grad_joined
    dattn = grad_joined.astype(BF)
    dattn_ref[...] = dattn
    sums_ref[6] += lanes_sum(dattn.astype(F32))
    grad_ctx = dg(wo_ref[...], dattn, 1, 0)
    for h in range(stat_ref.shape[0]):
        rows = slice(h * HEAD_DIM, (h + 1) * HEAD_DIM)
        part = (grad_ctx[rows] * stat_ref[h, 0:1, :]).astype(BF)
        gctx_ref[rows, :] = part
        inner_ref[h] = jnp.sum(part.astype(F32) * ctx[rows].astype(F32), axis=0, keepdims=True)


def tile(rows):
    return pl.BlockSpec((rows, TILE), lambda i: (0, i))


def heads_tile(heads, rows):
    return pl.BlockSpec((heads, rows, TILE), lambda i: (0, 0, i))


def rest_spec(w_rest):
    return pl.BlockSpec(w_rest.shape, lambda i: (0, 0), pipeline_mode=pl.Buffered(1))


def parts_of(rest_ref):
    width = rest_ref.shape[0]
    hidden = (rest_ref.shape[1] - width) // 2
    return rest_ref.at[:, 0:width], rest_ref.at[:, width : width + hidden], rest_ref.at[:, width + hidden :]


def column_spec(width):
    return pl.BlockSpec((width, LANES), lambda i: (0, 3 * width // LANES))


def first_dense_kernel(signal_ref, ctx_ref, rest_ref, col_ref,
                       unit_one_ref, unit_two_ref, rstd_ref, low_out_ref, act_ref, slope_ref):
    unit_one, rstd_one, _, unit_two, rstd_two = dense_forward(
        signal_ref[...].astype(F32), ctx_ref[...], rest_ref, col_ref, act_ref, slope_ref)
    unit_one_ref[...] = unit_one
    unit_two_ref[...] = unit_two
    rstd_ref[0:1, :] = rstd_one
    rstd_ref[1:2, :] = rstd_two
    low_out_ref[...] = (unit_two * column(col_ref, 2) + column(col_ref, 3)).astype(BF)


def first_dense(signal, ctx, w_rest, w_first):
    width, tokens = signal.shape
    hidden = (w_rest.shape[1] - width) // 2
    return pl.pallas_call(
        first_dense_kernel,
        name="first_dense",
        grid=(tokens // TILE,),
        in_specs=[tile(width), tile(width), rest_spec(w_rest), column_spec(width)],
        out_specs=[tile(width), tile(width), tile(8), tile(width), tile(hidden), tile(hidden)],
        out_shape=[
            jax.ShapeDtypeStruct((width, tokens), F32),
            jax.ShapeDtypeStruct((width, tokens), F32),
            jax.ShapeDtypeStruct((8, tokens), F32),
            jax.ShapeDtypeStruct((width, tokens), BF),
            jax.ShapeDtypeStruct((hidden, tokens), BF),
            jax.ShapeDtypeStruct((hidden, tokens), BF),
        ],
        compiler_params=params(),
        cost_estimate=cost(2 * tokens * width * (width + 2 * hidden), 24 << 20, tokens * hidden),
    )(signal, ctx, w_rest, w_first)


def second_dense_kernel(unit_ref, ctx_ref, cot_ref, stat_ref, rest_ref, col_ref,
                        out_ref, sums_ref, joined_ref, gctx_ref, inner_ref, mid_ref, act_ref, dz_ref, du_ref, dattn_ref, slope_ref):
    @pl.when(pl.program_id(0) == 0)
    def _():
        sums_ref[...] = jnp.zeros(sums_ref.shape, F32)

    ctx = ctx_ref[...]
    gain, shift = column(col_ref, 2), column(col_ref, 3)
    unit_one, rstd_one, low_middle, unit_two, rstd_two = dense_forward(
        unit_ref[...] * gain + shift, ctx, rest_ref, col_ref, act_ref, slope_ref)
    mid_ref[...] = low_middle
    out_ref[...] = (unit_two * gain + shift).astype(BF).T
    dense_back(cot_ref[...].astype(F32), unit_one, rstd_one, slope_ref, unit_two, rstd_two, ctx, stat_ref,
               rest_ref, col_ref, sums_ref, joined_ref, gctx_ref, inner_ref, dz_ref, du_ref, dattn_ref)


def second_dense(unit, ctx, cot, stat, w_rest, w_first):
    width, tokens = unit.shape
    hidden = (w_rest.shape[1] - width) // 2
    heads = stat.shape[0]
    return pl.pallas_call(
        second_dense_kernel,
        name="second_dense",
        grid=(tokens // TILE,),
        in_specs=[tile(width), tile(width), tile(width), heads_tile(heads, 2), rest_spec(w_rest), column_spec(width)],
        out_specs=[pl.BlockSpec((TILE, width), lambda i: (i, 0)), whole((12, width, LANES)), tile(width), tile(width), heads_tile(heads, 1),
                   tile(width), tile(hidden), tile(width), tile(hidden), tile(width)],
        out_shape=[
            jax.ShapeDtypeStruct((tokens, width), BF),
            jax.ShapeDtypeStruct((12, width, LANES), F32),
            jax.ShapeDtypeStruct((width, tokens), F32),
            jax.ShapeDtypeStruct((width, tokens), BF),
            jax.ShapeDtypeStruct((heads, 1, tokens), F32),
            jax.ShapeDtypeStruct((width, tokens), BF),
            jax.ShapeDtypeStruct((hidden, tokens), BF),
            jax.ShapeDtypeStruct((width, tokens), BF),
            jax.ShapeDtypeStruct((hidden, tokens), BF),
            jax.ShapeDtypeStruct((width, tokens), BF),
        ],
        scratch_shapes=[pltpu.VMEM((hidden, TILE), F32)],
        compiler_params=params(),
        cost_estimate=cost(4 * tokens * width * (width + 2 * hidden), 28 << 20, tokens * hidden),
    )(unit, ctx, cot, stat, w_rest, w_first)


def first_back_kernel(prior_ref, dqkv_ref, unit_one_ref, unit_two_ref, rstd_ref, slope_ref, ctx_ref, stat_ref, sums_in_ref,
                      wqkv_ref, rest_ref, col_ref,
                      vec_ref, joined_ref, gctx_ref, inner_ref, mid_ref, dz_ref, du_ref, dattn_ref, sums_ref):
    step = pl.program_id(0)

    @pl.when(step == 0)
    def _():
        sums_ref[...] = sums_in_ref[...]

    unit_one = unit_one_ref[...]
    mid_ref[...] = (unit_one * column(col_ref, 0) + column(col_ref, 1)).astype(BF)
    grad = prior_ref[...] + dg(wqkv_ref[...], dqkv_ref[...], 1, 0)
    dense_back(grad, unit_one, rstd_ref[0:1, :], slope_ref, unit_two_ref[...], rstd_ref[1:2, :], ctx_ref[...], stat_ref,
               rest_ref, col_ref, sums_ref, joined_ref, gctx_ref, inner_ref, dz_ref, du_ref, dattn_ref)

    @pl.when(step == pl.num_programs(0) - 1)
    def _():
        lane = lax.broadcasted_iota(jnp.int32, vec_ref.shape, 1)
        out = jnp.zeros(vec_ref.shape, F32)
        for j in (0, 1, 2, 3, 6, 7, 8, 9, 10, 11):
            out = jnp.where(lane == j, jnp.sum(sums_ref[j], axis=1, keepdims=True), out)
        vec_ref[...] = out


def first_back(prior, dqkv, unit_one, unit_two, rstd, slope, ctx, stat, sums, w_first, w_rest):
    width, tokens = prior.shape
    hidden = (w_rest.shape[1] - width) // 2
    heads = stat.shape[0]
    return pl.pallas_call(
        first_back_kernel,
        name="first_back",
        grid=(tokens // TILE,),
        in_specs=[tile(width), tile(3 * width), tile(width), tile(width), tile(8), tile(hidden), tile(width), heads_tile(heads, 2), whole(sums.shape),
                  pl.BlockSpec((width, 3 * width), lambda i: (0, 0)), rest_spec(w_rest), column_spec(width)],
        out_specs=[whole((width, LANES)), tile(width), tile(width), heads_tile(heads, 1), tile(width), tile(width), tile(hidden), tile(width)],
        out_shape=[
            jax.ShapeDtypeStruct((width, LANES), F32),
            jax.ShapeDtypeStruct((width, tokens), F32),
            jax.ShapeDtypeStruct((width, tokens), BF),
            jax.ShapeDtypeStruct((heads, 1, tokens), F32),
            jax.ShapeDtypeStruct((width, tokens), BF),
            jax.ShapeDtypeStruct((width, tokens), BF),
            jax.ShapeDtypeStruct((hidden, tokens), BF),
            jax.ShapeDtypeStruct((width, tokens), BF),
        ],
        scratch_shapes=[pltpu.VMEM((12, width, LANES), F32)],
        compiler_params=params(),
        cost_estimate=cost(2 * tokens * width * (4 * width + 2 * hidden), 28 << 20),
    )(prior, dqkv, unit_one, unit_two, rstd, slope, ctx, stat, sums, w_first, w_rest, w_first)


class Layout:
    def __init__(self, mesh_batch, mesh_shard, width):
        self.batch = mesh_batch
        self.shards = mesh_shard
        self.parts = min(mesh_batch, width // mesh_shard // 16)
        self.planes = self.parts // 2
        self.rows = width // mesh_shard // self.parts

    def swap(self, value, axis, distance):
        size = self.batch if axis == "batch" else self.shards
        return lax.ppermute(value, axis, [(i, i ^ distance) for i in range(size)])

    def place(self):
        return jnp.stack([lax.axis_index("batch") % self.parts, lax.axis_index("shard")]).astype(jnp.int32)

    def row_of(self, place_ref, c, e, d):
        block = (place_ref[1] ^ d) * self.parts + (place_ref[0] ^ (2 * e + c))
        return pl.multiple_of(block * self.rows, self.rows)

    def along_shards(self, blocks):
        return [self.swap(blocks[d % len(blocks)], "shard", d) for d in range(1, self.shards)]

    def across_plane(self, blocks):
        return [self.swap(blocks[e % len(blocks)], "batch", 2 * e) for e in range(1, self.planes)]

    def across_cores(self, block):
        return self.swap(block, "batch", 1)

    def across_rest(self, own):
        distance = self.parts
        while distance < self.batch:
            own = add([own, self.swap(own, "batch", distance)])[0]
            distance *= 2
        return own


def tree(values):
    while len(values) > 1:
        values = [a + b for a, b in zip(values[::2], values[1::2], strict=True)]
    return values[0]


def whole_specs(values, tokens_in=()):
    return [whole(v.shape) for v in values] + [pl.BlockSpec(memory_space=pl.ANY)] * len(tokens_in)


def join_kernel(count, *refs):
    out_ref = refs[-1]
    at = 0
    for source in refs[:count]:
        out_ref[at : at + source.shape[0], :] = source[...]
        at += source.shape[0]


def join(blocks, tokens_in=()):
    rows, columns = sum(b.shape[0] for b in blocks), blocks[0].shape[1]
    return pl.pallas_call(
        functools.partial(join_kernel, len(blocks)),
        name="join",
        grid=(1,),
        in_specs=whole_specs(blocks, tokens_in),
        out_specs=whole((rows, columns)),
        out_shape=jax.ShapeDtypeStruct((rows, columns), BF),
        compiler_params=params(),
        cost_estimate=cost(0, 4 * rows * columns),
    )(*blocks, *tokens_in)


def add_kernel(count, outs, *refs):
    total = refs[0][...].astype(F32)
    for other in refs[1:count]:
        total = total + other[...].astype(F32)
    total = total.astype(BF)
    rows = refs[-1].shape[0]
    for i in range(outs):
        refs[i - outs][...] = total[i * rows : (i + 1) * rows]


def add(values, outs=1, tokens_in=()):
    rows, columns = values[0].shape
    part = jax.ShapeDtypeStruct((rows // outs, columns), BF)
    return pl.pallas_call(
        functools.partial(add_kernel, len(values), outs),
        name="add",
        grid=(1,),
        in_specs=whole_specs(values, tokens_in),
        out_specs=[whole(part.shape)] * outs,
        out_shape=[part] * outs,
        compiler_params=params(),
        cost_estimate=cost(len(values) * rows * columns, 2 * (len(values) + 1) * rows * columns),
    )(*values, *tokens_in)


def add_squares_kernel(count, others, *refs):
    out_ref = refs[-1]
    total = refs[0][...].astype(F32)
    for other in refs[1:count]:
        total = total + other[...].astype(F32)
    total = total.astype(BF)
    squares = jnp.sum(jnp.square(total.astype(F32)), keepdims=True)
    for other in refs[count : count + others]:
        squares = squares + jnp.sum(jnp.square(other[...].astype(F32)), keepdims=True)
    out_ref[...] = total
    high = squares.astype(BF)
    middle = (squares - high.astype(F32)).astype(BF)
    low = (squares - high.astype(F32) - middle.astype(F32)).astype(BF)
    used = total.shape[1] - LANES
    tail = total[:, used:]
    lane = lax.broadcasted_iota(jnp.int32, tail.shape, 1)
    for i, piece in enumerate((high, middle, low)):
        tail = jnp.where(lane == SQUARES_AT + i, piece.astype(F32), tail.astype(F32)).astype(BF)
    out_ref[:, used:] = tail


def add_squares(values, others):
    rows, columns = values[0].shape
    return pl.pallas_call(
        functools.partial(add_squares_kernel, len(values), len(others)),
        name="add_squares",
        grid=(1,),
        in_specs=whole_specs(list(values) + list(others)),
        out_specs=whole((rows, columns)),
        out_shape=jax.ShapeDtypeStruct((rows, columns), BF),
        compiler_params=params(),
        cost_estimate=cost(len(values) * rows * columns, 2 * (len(values) + 1) * rows * columns),
    )(*values, *others)


def shard_squares_kernel(layout, place_ref, mine_ref, theirs_ref, out_ref):
    used = mine_ref.shape[1] - LANES
    total = jnp.zeros((1, LANES), F32)
    lane = lax.broadcasted_iota(jnp.int32, (1, LANES), 1)
    riding = (lane >= SQUARES_AT) & (lane < SQUARES_AT + 3)
    for part in range(layout.parts):
        away = place_ref[0] ^ part
        at = pl.ds(pl.multiple_of((away >> 1) * layout.rows, layout.rows), layout.rows)
        mine = mine_ref[at, used:].astype(F32)[0:1]
        theirs = theirs_ref[at, used:].astype(F32)[0:1]
        total = total + jnp.where((away & 1) == 0, mine, theirs)
    total = jnp.sum(jnp.where(riding, total, 0.0), axis=1, keepdims=True)
    out_ref[...] = jnp.broadcast_to(total, out_ref.shape)


def shard_squares(layout, place, mine, theirs):
    return pl.pallas_call(
        functools.partial(shard_squares_kernel, layout),
        name="shard_squares",
        grid=(1,),
        in_specs=[pl.BlockSpec(memory_space=pltpu.SMEM)] + whole_specs((mine, theirs)),
        out_specs=whole((8, LANES)),
        out_shape=jax.ShapeDtypeStruct((8, LANES), F32),
        compiler_params=params(),
        cost_estimate=cost(0, 4 * mine.size),
    )(place, mine, theirs)


def pick_first_kernel(place_ref, w_ref, vec_ref, out_ref, columns_ref, hold_ref):
    hold_ref[...] = jnp.zeros(hold_ref.shape, F32)
    hold_ref[0 : vec_ref.shape[0], 0 : vec_ref.shape[1]] = vec_ref[...]
    hold_ref[...] = hold_ref[...].T
    columns_ref[...] = hold_ref[0 : columns_ref.shape[0], :].astype(BF)
    used = w_ref.shape[1]
    rows = out_ref.shape[0]
    out_ref[:, 0:used] = w_ref[...].astype(BF)
    out_ref[:, used:] = hold_ref[pl.ds(pl.multiple_of(place_ref[0] * rows, rows), rows), :].astype(BF)


def pick_first(layout, place, weights, vectors):
    shard_rows, columns = weights.shape
    used = columns // 4
    return pl.pallas_call(
        pick_first_kernel,
        name="pick_first",
        grid_spec=pltpu.PrefetchScalarGridSpec(
            num_scalar_prefetch=1,
            grid=(1,),
            in_specs=[pl.BlockSpec((layout.rows, used), lambda i, place: (place[0], 0)), pl.BlockSpec(vectors.shape, lambda i, place: (0, 0))],
            out_specs=[pl.BlockSpec((layout.rows, used + LANES), lambda i, place: (0, 0)), pl.BlockSpec((shard_rows, LANES), lambda i, place: (0, 0))],
            scratch_shapes=[pltpu.VMEM((LANES, LANES), F32)],
        ),
        out_shape=[jax.ShapeDtypeStruct((layout.rows, used + LANES), BF), jax.ShapeDtypeStruct((shard_rows, LANES), BF)],
        compiler_params=params(),
        cost_estimate=cost(0, 6 * layout.rows * columns),
    )(place, weights, vectors)


def pick_rest_kernel(place_ref, w_ref, *refs):
    out_ref = refs[-1]
    out_ref[...] = w_ref[:, w_ref.shape[1] - out_ref.shape[1] :].astype(BF)


def pick_rest(layout, place, weights, tokens_in):
    columns = weights.shape[1]
    return pl.pallas_call(
        pick_rest_kernel,
        name="pick_rest",
        grid_spec=pltpu.PrefetchScalarGridSpec(
            num_scalar_prefetch=1,
            grid=(1,),
            in_specs=[pl.BlockSpec((layout.rows, columns), lambda i, place: (place[0], 0))] + [pl.BlockSpec(memory_space=pl.ANY)] * len(tokens_in),
            out_specs=pl.BlockSpec((layout.rows, 3 * columns // 4), lambda i, place: (0, 0)),
        ),
        out_shape=jax.ShapeDtypeStruct((layout.rows, 3 * columns // 4), BF),
        compiler_params=params(),
        cost_estimate=cost(0, 6 * layout.rows * columns),
    )(place, weights, *tokens_in)


def put_blocks(layout, place_ref, sources, out_ref):
    for c, source in enumerate(sources):
        for e in range(layout.planes):
            for d in range(1, layout.shards):
                at = (e * (layout.shards - 1) + d - 1) * layout.rows
                out_ref[pl.ds(layout.row_of(place_ref, c, e, d), layout.rows), :] = source[at : at + layout.rows, :]


def own_rows(layout, place_ref):
    rows = layout.rows * layout.parts
    return pl.ds(pl.multiple_of(place_ref[1] * rows, rows), rows)


def collect_first_kernel(layout, place_ref, w_ref, columns_ref, mine_ref, theirs_ref, out_ref):
    put_blocks(layout, place_ref, (mine_ref, theirs_ref), out_ref)
    rows = own_rows(layout, place_ref)
    used = w_ref.shape[1]
    out_ref[rows, 0:used] = w_ref[...].astype(BF)
    out_ref[rows, used:] = columns_ref[...]


def collect_rest_kernel(layout, place_ref, w_ref, mine_ref, theirs_ref, out_ref):
    put_blocks(layout, place_ref, (mine_ref, theirs_ref), out_ref)
    out_ref[own_rows(layout, place_ref), :] = w_ref[...].astype(BF)


def collect_first(layout, place, weights, columns, mine, theirs):
    shard_rows, all_columns = weights.shape
    rows = shard_rows * layout.shards
    total = mine.shape[1]
    return pl.pallas_call(
        functools.partial(collect_first_kernel, layout),
        name="collect_first",
        grid=(1,),
        in_specs=[pl.BlockSpec(memory_space=pltpu.SMEM), pl.BlockSpec((shard_rows, all_columns // 4), lambda i: (0, 0))] + whole_specs((columns, mine, theirs)),
        out_specs=whole((rows, total)),
        out_shape=jax.ShapeDtypeStruct((rows, total), BF),
        compiler_params=params(),
        cost_estimate=cost(0, 4 * rows * total),
    )(place, weights, columns, mine, theirs)


def collect_rest(layout, place, weights, mine, theirs):
    shard_rows, all_columns = weights.shape
    rows = shard_rows * layout.shards
    total = mine.shape[1]
    block = all_columns // 4
    return pl.pallas_call(
        functools.partial(collect_rest_kernel, layout),
        name="collect_rest",
        grid=(3,),
        in_specs=[pl.BlockSpec(memory_space=pltpu.SMEM), pl.BlockSpec((shard_rows, block), lambda i: (0, i + 1))]
        + [pl.BlockSpec((t.shape[0], block), lambda i: (0, i)) for t in (mine, theirs)],
        out_specs=pl.BlockSpec((rows, block), lambda i: (0, i)),
        out_shape=jax.ShapeDtypeStruct((rows, total), BF),
        compiler_params=params(),
        cost_estimate=cost(0, 4 * rows * total),
    )(place, weights, mine, theirs)


def in_order(layout, place_ref, source_ref, target_ref):
    at = 0
    for c in range(2):
        for e in range(layout.planes):
            for d in range(layout.shards):
                target_ref[at : at + layout.rows] = source_ref[pl.ds(layout.row_of(place_ref, c, e, d), layout.rows), :]
                at += layout.rows


def weight_step(left_ref, ra_ref, rb_ref, keep_ref, send_ref):
    out = (dg(left_ref[0], ra_ref[...], 1, 1) + dg(left_ref[1], rb_ref[...], 1, 1)).astype(BF)
    half = out.shape[0] // 2
    keep_ref[...] = out[:half]
    send_ref[...] = out[half:]


def weight_early_kernel(layout, place_ref, ma_ref, mb_ref, za_ref, zb_ref, ca_ref, cb_ref, ua_ref, ub_ref, ha_ref, hb_ref, oa_ref, ob_ref, keep_ref, send_ref, left_ref):
    step = pl.program_id(0)
    count = (pl.num_programs(0) - 1) // 2
    for at, (first_ref, second_ref) in ((0, (ma_ref, mb_ref)), (count, (za_ref, zb_ref)), (2 * count, (ca_ref, cb_ref))):
        @pl.when(step == at)
        def _(first_ref=first_ref, second_ref=second_ref):
            in_order(layout, place_ref, first_ref, left_ref.at[0])
            in_order(layout, place_ref, second_ref, left_ref.at[1])

    @pl.when(step < count)
    def _():
        weight_step(left_ref, ua_ref, ub_ref, keep_ref, send_ref)

    @pl.when((step >= count) & (step < 2 * count))
    def _():
        weight_step(left_ref, ha_ref, hb_ref, keep_ref, send_ref)

    @pl.when(step == 2 * count)
    def _():
        weight_step(left_ref, oa_ref, ob_ref, keep_ref, send_ref)


def weight_early(layout, place, lefts, hidden_grads, hidden_acts, outer):
    rows, tokens = lefts[0].shape
    block = rows
    count = hidden_grads[0].shape[0] // block
    steps = 2 * count + 1
    half = jax.ShapeDtypeStruct((rows // 2, steps * block), BF)
    once = pl.BlockSpec((rows, tokens), lambda i: (0, 0), pipeline_mode=pl.Buffered(1))
    early = pl.BlockSpec((block, tokens), lambda i: (jnp.minimum(i, count - 1), 0))
    late = pl.BlockSpec((block, tokens), lambda i: (jnp.clip(i - count, 0, count - 1), 0))
    return pl.pallas_call(
        functools.partial(weight_early_kernel, layout),
        name="weight_early",
        grid=(steps,),
        in_specs=[pl.BlockSpec(memory_space=pltpu.SMEM)] + [once] * 6 + [early] * 2 + [late] * 2 + [once] * 2,
        out_specs=[pl.BlockSpec((rows // 2, block), lambda i: (0, i))] * 2,
        out_shape=[half, half],
        scratch_shapes=[pltpu.VMEM((2, rows, tokens), BF)],
        compiler_params=params(),
        cost_estimate=cost(4 * rows * steps * block * tokens, 4 * (rows + steps * block) * tokens),
    )(place, *lefts, *hidden_grads, *hidden_acts, *outer)


def last_kernel(layout, pairs, tiles, given, place_ref, e_ref, qkv_ref, stat_ref, grad_ref, inner_ref, done_ref, joined_ref, w_ref,
                la_ref, lb_ref, rb_ref, vec_in_ref, *refs):
    keep_ref, send_ref, input_ref, ds_ref, dqkv_ref, left_ref, vec_ref, order_ref = refs[given:]
    step = pl.program_id(0)
    pair = grad_ref.shape[0]
    rows = left_ref.shape[1]
    skipped = done_ref.shape[1]

    @pl.when(step == 0)
    def _():
        dqkv_ref[:, 0:skipped] = done_ref[...]
        in_order(layout, place_ref, la_ref, left_ref.at[0])
        in_order(layout, place_ref, lb_ref, left_ref.at[1])
        vec_ref[...] = vec_in_ref[...]

    @pl.when(step < pairs)
    def _():
        at = pl.ds(pl.multiple_of(skipped + step * pair, pair), pair)
        attend_back_pair(e_ref, qkv_ref, stat_ref, grad_ref, inner_ref, dqkv_ref.at[:, at], ds_ref)

    @pl.when((step >= pairs) & (step < pairs + tiles))
    def _():
        width = joined_ref.shape[1]
        at = pl.ds(pl.multiple_of((step - pairs) * width, width), width)
        total = joined_ref[...]
        for t in range(3):
            total = total + dg(w_ref[:, t * rows : (t + 1) * rows], dqkv_ref[t, :, at], 1, 0)
        input_ref[...] = total.T

    @pl.when(step >= pairs + tiles)
    def _():
        third = step - pairs - tiles
        ra, rb = dqkv_ref[third], rb_ref[0]
        out = (dg(left_ref[0], ra, 1, 1) + dg(left_ref[1], rb, 1, 1)).astype(BF)
        half = rows // 2
        columns = pl.ds(pl.multiple_of(third * rows, rows), rows)
        keep_ref[:, columns] = out[:half]
        send_ref[:, columns] = out[half:]
        sums = jnp.sum(lanes_sum(ra.astype(F32)) + lanes_sum(rb.astype(F32)), axis=1, keepdims=True)
        lane = lax.broadcasted_iota(jnp.int32, vec_ref.shape, 1)
        wanted = ((third == 0) & (lane == 4)) | ((third == 2) & (lane == 5))
        vec_ref[...] = jnp.where(wanted, sums, vec_ref[...])

    @pl.when(step == pl.num_programs(0) - 1)
    def _():
        in_order(layout, place_ref, vec_ref, order_ref)
        half = rows // 2
        used = keep_ref.shape[1] - LANES
        keep_ref[:, used:] = order_ref[0:half].astype(BF)
        send_ref[:, used:] = order_ref[half:].astype(BF)


def last(layout, place, e, qkv, stat, grad, inner, done, skipped, joined, w_first, left_one, left_two, dqkv_two, vec, tokens_in):
    rows, tokens = left_one.shape
    pair = 2 * HEAD_DIM
    pairs = rows // pair - skipped
    tiles = tokens // TILE
    half = jax.ShapeDtypeStruct((rows // 2, 3 * rows + LANES), BF)

    def at_pair(i):
        return skipped + jnp.minimum(i, pairs - 1)

    def at_tile(i):
        return jnp.clip(i - pairs, 0, tiles - 1)

    def once(shape):
        return pl.BlockSpec(shape, lambda i: (0,) * len(shape), pipeline_mode=pl.Buffered(1))

    return pl.pallas_call(
        functools.partial(last_kernel, layout, pairs, tiles, len(tokens_in)),
        name="last",
        grid=(pairs + tiles + 3,),
        in_specs=[
            pl.BlockSpec(memory_space=pltpu.SMEM),
            pl.BlockSpec((2, tokens, tokens), lambda i: (at_pair(i), 0, 0)),
            pl.BlockSpec((3, pair, tokens), lambda i: (0, at_pair(i), 0)),
            pl.BlockSpec((2, 2, tokens), lambda i: (at_pair(i), 0, 0)),
            pl.BlockSpec((pair, tokens), lambda i: (at_pair(i), 0)),
            pl.BlockSpec((2, 1, tokens), lambda i: (at_pair(i), 0, 0)),
            once((3, skipped * pair, tokens)),
            pl.BlockSpec((rows, TILE), lambda i: (0, at_tile(i))),
            once((rows, 3 * rows)),
            once((rows, tokens)),
            once((rows, tokens)),
            pl.BlockSpec((1, rows, tokens), lambda i: (jnp.clip(i - pairs - tiles, 0, 2), 0, 0)),
            once(vec.shape),
        ] + [pl.BlockSpec(memory_space=pl.ANY)] * len(tokens_in),
        out_specs=[whole(half.shape)] * 2 + [pl.BlockSpec((TILE, rows), lambda i: (at_tile(i), 0))],
        out_shape=[half, half, jax.ShapeDtypeStruct((tokens, rows), F32)],
        scratch_shapes=[pltpu.VMEM((2, tokens, tokens), BF), pltpu.VMEM((3, rows, tokens), BF), pltpu.VMEM((2, rows, tokens), BF),
                        pltpu.VMEM(vec.shape, F32), pltpu.VMEM(vec.shape, F32)],
        compiler_params=params(),
        cost_estimate=cost(12 * rows * rows * tokens, 12 * rows * tokens),
    )(place, e, qkv, stat, grad, inner, done, joined, w_first, left_one, left_two, dqkv_two, vec, *tokens_in)


def adam_kernel(layout, pieces, place_ref, *refs):
    grads = [refs[2 * i : 2 * i + 2] for i in range(len(pieces))]
    rest = refs[2 * len(pieces) :]
    shares, rest = rest[: layout.shards], rest[layout.shards :]
    w_ref, one_ref, two_ref, v_ref, vone_ref, vtwo_ref = rest[:6]
    gw_ref, nw_ref, none_ref, ntwo_ref, gv_ref, nv_ref, nvone_ref, nvtwo_ref, norm_ref = rest[6:15]
    holds, hold_ref = rest[15:-1], rest[-1]
    norm = jnp.sqrt(tree([share[0:1, 0:1] for share in shares]))
    clip_limit = math.sqrt(D * WCOLS)
    factor = clip_limit / jnp.maximum(norm, clip_limit)
    step = pl.program_id(0)
    rows = layout.rows

    @pl.when(step == 0)
    def _():
        norm_ref[...] = jnp.broadcast_to(norm, norm_ref.shape)
        for blocks, target in zip(grads, holds, strict=True):
            for c, block in enumerate(blocks):
                for e in range(layout.planes):
                    part = place_ref[0] ^ (2 * e + c)
                    target[pl.ds(pl.multiple_of(part * rows, rows), rows), :] = block[e * rows : (e + 1) * rows, :]
        hold_ref[0 : holds[-1].shape[0], :] = holds[-1][:, holds[-1].shape[1] - LANES :].astype(F32)
        grad = hold_ref[...].T[0 : gv_ref.shape[0], 0 : gv_ref.shape[1]]
        gv_ref[...] = grad
        nv_ref[...], nvone_ref[...], nvtwo_ref[...] = adam_update(v_ref[...], vone_ref[...], vtwo_ref[...], grad * factor)

    size = w_ref.shape[0]
    at = pl.ds(pl.multiple_of(step * size, size), size)
    for held, spans in zip(holds, pieces, strict=True):
        for source, target, width in spans:
            to = slice(target, target + width)
            grad = held[at, source : source + width].astype(F32)
            gw_ref[:, to] = grad
            nw_ref[:, to], none_ref[:, to], ntwo_ref[:, to] = adam_update(w_ref[:, to], one_ref[:, to], two_ref[:, to], grad * factor)


def adam(layout, place, shares, pieces, grads, weights, first, second, vectors, vector_first, vector_second):
    rows, columns = weights.shape
    block = 16
    natural = pl.BlockSpec((block, columns), lambda i: (i, 0))
    big = jax.ShapeDtypeStruct((rows, columns), F32)
    little = jax.ShapeDtypeStruct(vectors.shape, F32)
    flat = [t for blocks in grads for t in blocks] + list(shares)
    return pl.pallas_call(
        functools.partial(adam_kernel, layout, pieces),
        name="adam",
        grid=(rows // block,),
        in_specs=[pl.BlockSpec(memory_space=pltpu.SMEM)] + whole_specs(flat) + [natural] * 3 + [whole(vectors.shape)] * 3,
        out_specs=[natural] * 4 + [whole(vectors.shape)] * 4 + [whole((1, 1))],
        out_shape=[big] * 4 + [little] * 4 + [jax.ShapeDtypeStruct((1, 1), F32)],
        scratch_shapes=[pltpu.VMEM((rows, blocks[0].shape[1]), BF) for blocks in grads] + [pltpu.VMEM((LANES, LANES), F32)],
        compiler_params=params(32),
        cost_estimate=cost(20 * rows * columns, 30 * rows * columns, rows * columns),
    )(place, *flat, weights, first, second, vectors, vector_first, vector_second)


def masks(segments, tags, length):
    tokens = segments.shape[0]
    matches = segments[None, :] == jnp.arange(tags.shape[0], dtype=jnp.int32)[:, None]
    group = jnp.sum(jnp.where(matches, tags[:, None], 0), axis=0)
    live = jnp.arange(tokens, dtype=jnp.int32) < length
    kinds = jnp.arange(16, dtype=jnp.int32)[:, None]
    same = group[None, :] == kinds
    kmask = jnp.where(kinds < 4, (same & live[None, :]).astype(F32), jnp.where(kinds == 4, (~live)[None, :].astype(F32), 0.0))
    qmask = jnp.where(kinds < 4, jnp.where(same, 0.0, -FAR), jnp.where(kinds == 4, -FAR, 0.0))
    return kmask.astype(BF), jnp.broadcast_to(qmask, (16, tokens)).astype(BF)


def on_device(layout, inputs, cotangent, lengths, segment_ids, group_tags, weights, first_moments, second_moments, vectors, vector_first, vector_second):
    _, tokens, width = inputs.shape
    hidden = (weights.shape[1] - 4 * width) // 2
    pair = 2 * HEAD_DIM
    place = layout.place()
    kmask, qmask = masks(segment_ids[0], group_tags[0], lengths[0])
    act_one = inputs[0].T
    cot = cotangent[0].T

    first_part, own_columns = pick_first(layout, place, weights, vectors)
    first_z = join(layout.along_shards([first_part]))
    rest_part = pick_rest(layout, place, weights, (first_z,))
    first_mine = join([first_z] + layout.across_plane([first_z]))
    rest_z = join(layout.along_shards([rest_part]), (first_mine,))
    w_first = collect_first(layout, place, weights, own_columns, first_mine, layout.across_cores(first_mine))
    e_one, ctx_one, qkv_one, stat_one = attend(act_one, w_first, kmask, qmask)
    rest_mine = join([rest_z] + layout.across_plane([rest_z]), (ctx_one,))
    w_rest = collect_rest(layout, place, weights, rest_mine, layout.across_cores(rest_mine))
    unit_one, unit_two, rstd, act_two, hid_one, slope = first_dense(act_one, ctx_one, w_rest, w_first)
    e_two, ctx_two, qkv_two, stat_two = attend(act_two, w_first, kmask, qmask)
    outputs, sums, joined_two, gctx_two, inner_two, mid_two, hid_two, dz_two, du_two, dattn_two = second_dense(
        unit_two, ctx_two, cot, stat_two, w_rest, w_first)
    dqkv_two = attend_back(e_two, qkv_two, stat_two, gctx_two, inner_two)
    vec, joined_one, gctx_one, inner_one, mid_one, dz_one, du_one, dattn_one = first_back(
        joined_two, dqkv_two.reshape(3 * width, tokens), unit_one, unit_two, rstd, slope, ctx_one, stat_one, sums, w_first, w_rest)

    keep, send = weight_early(layout, place, (mid_one, mid_two, dz_one, dz_two, ctx_one, ctx_two), (du_one, du_two), (hid_one, hid_two), (dattn_one, dattn_two))
    operands = (e_one, qkv_one, stat_one, gctx_one, inner_one)
    done = attend_back(*operands, 0, 1)
    half = add((keep, layout.across_cores(send)), layout.planes, (done,))
    keep, send, input_grad = last(layout, place, *operands, done, 1, joined_one, w_first, act_one, act_two, dqkv_two, vec, (half[0],))
    plane = add([half[0]] + layout.across_plane(half), layout.shards, (keep,))
    half_qkv = add((keep, layout.across_cores(join([send], (plane[0],)))), layout.planes)
    plane_qkv = add([half_qkv[0]] + layout.across_plane(half_qkv), layout.shards)
    own_early = layout.across_rest(add([plane[0]] + layout.along_shards(plane), 1, (plane_qkv[0],))[0])
    own_qkv = [plane_qkv[0]] + layout.along_shards(plane_qkv)
    if layout.parts < layout.batch:
        own_qkv = [layout.across_rest(add(own_qkv)[0])]
    own_qkv = add_squares(own_qkv, (own_early,))
    all_early = join([own_early] + layout.across_plane([own_early]), (own_qkv,))
    all_qkv = join([own_qkv] + layout.across_plane([own_qkv]))
    grads = [(t, layout.across_cores(t)) for t in (all_early, all_qkv)]
    spans = [
        [(0, 4 * width, 2 * hidden), (2 * hidden, 3 * width, width)],
        [(0, 0, 3 * width)],
    ]
    share = shard_squares(layout, place, *grads[1])
    updated = adam(layout, place, [share] + layout.along_shards([share]), spans, grads, weights, first_moments, second_moments, vectors, vector_first, vector_second)
    grad_w, new_weights, new_first, new_second, grad_v, new_vectors, new_vector_first, new_vector_second, grad_norm = updated
    grad_norm = grad_norm.reshape(())
    return (
        outputs[None],
        input_grad[None],
        grad_w,
        grad_v,
        grad_norm,
        new_weights,
        new_first,
        new_second,
        new_vectors,
        new_vector_first,
        new_vector_second,
    )


def solution(mesh):
    rows = ("batch", "shard")
    placed = (
        P(rows, None, None),
        P(rows, None, None),
        P(rows),
        P(rows, None),
        P(rows, None),
        P("shard", None),
        P("shard", None),
        P("shard", None),
        P(None, "shard"),
        P(None, "shard"),
        P(None, "shard"),
    )
    return jax.shard_map(
        functools.partial(on_device, Layout(mesh.shape["batch"], mesh.shape["shard"], D)),
        mesh=mesh,
        in_specs=placed,
        out_specs=(
            P(rows, None, None),
            P(rows, None, None),
            P("shard", None),
            P(None, "shard"),
            P(),
            P("shard", None),
            P("shard", None),
            P("shard", None),
            P(None, "shard"),
            P(None, "shard"),
            P(None, "shard"),
        ),
        check_vma=False,
    )
```

```python
import functools
import math

import jax
import jax.numpy as jnp
from jax import lax
from jax.experimental import pallas as pl
from jax.experimental.pallas import tpu as pltpu
from jax.sharding import PartitionSpec as P

D = 512
FF = 2048
HEADS = 8
HEAD_DIM = 64
STEP = 10
WCOLS = 6144

NORM_EPS = 1e-05
BETA_ONE = 0.5
BETA_TWO = 0.5
ADAM_EPS = 1e-08
DECAY = 0.01
WARMUP = 4000.0
RATE_SCALE = 150000.0

BF = jnp.bfloat16
F32 = jnp.float32
FAR = 1e30
SAFE_SCORE = 60.0
TILE = 256
WIDE_TILE = 512
LANES = 128
SQUARES_AT = 12
COST_SCALE = 100


def params(mebibytes=50):
    return pltpu.CompilerParams(vmem_limit_bytes=mebibytes << 20)


def cost(flops, bytes_accessed, transcendentals=0):
    return pl.CostEstimate(flops=int(flops) // COST_SCALE, bytes_accessed=int(bytes_accessed) // COST_SCALE, transcendentals=int(transcendentals) // COST_SCALE)


def dg(left, right, left_dim, right_dim):
    return lax.dot_general(
        left, right, (((left_dim,), (right_dim,)), ((), ())), preferred_element_type=F32
    )


def whole(shape):
    return pl.BlockSpec(shape, lambda i: (0,) * len(shape))


def adam_update(master, moment_one, moment_two, gradient):
    moment_one = BETA_ONE * moment_one + (1.0 - BETA_ONE) * gradient
    moment_two = BETA_TWO * moment_two + (1.0 - BETA_TWO) * gradient * gradient
    step_rate = RATE_SCALE * D ** (-0.5) * min(STEP ** (-0.5), STEP * WARMUP ** (-1.5))
    fixed_first = moment_one / (1.0 - BETA_ONE**STEP)
    fixed_second = moment_two / (1.0 - BETA_TWO**STEP)
    master = master - step_rate * (
        fixed_first / (jnp.sqrt(fixed_second) + ADAM_EPS) + DECAY * master
    )
    return (master, moment_one, moment_two)


def attend_kernel(act_ref, wq_ref, wk_ref, wv_ref, col_ref, kmask_ref, qmask_ref, e_ref, ctx_ref, qkv_ref, stat_ref):
    act = act_ref[...]
    tokens = act.shape[1]
    q = (dg(wq_ref[...], act, 0, 0) + col_ref[:, 4:5].astype(F32)).astype(BF) * jnp.asarray(HEAD_DIM**-0.5, BF)
    k = dg(wk_ref[...], act, 0, 0).astype(BF)
    v = (dg(wv_ref[...], act, 0, 0) + col_ref[:, 5:6].astype(F32)).astype(BF)
    qkv_ref[0] = q
    qkv_ref[1] = k
    qkv_ref[2] = v
    dead = kmask_ref[4:5, :].astype(F32)
    bound = jnp.zeros((1, 1), F32)
    selves = []
    for h in range(2):
        rows = slice(h * HEAD_DIM, (h + 1) * HEAD_DIM)
        qf, kf = q[rows].astype(F32), k[rows].astype(F32)
        selves.append(jnp.sum(qf * kf, axis=0, keepdims=True))
        q_top = jnp.max(jnp.sum(qf * qf, axis=0, keepdims=True), axis=1, keepdims=True)
        k_top = jnp.max(jnp.sum(kf * kf, axis=0, keepdims=True), axis=1, keepdims=True)
        bound = jnp.maximum(bound, q_top * k_top)
    safe = bound[0, 0] <= SAFE_SCORE * SAFE_SCORE

    def scores(h):
        rows = slice(h * HEAD_DIM, (h + 1) * HEAD_DIM)
        keys = jnp.concatenate([k[rows], kmask_ref[...]], axis=0).T
        queries = jnp.concatenate([q[rows], qmask_ref[...]], axis=0)
        return dg(keys, queries, 1, 0)

    def finish(h, e, e_self):
        rows = slice(h * HEAD_DIM, (h + 1) * HEAD_DIM)
        low_e = e.astype(BF)
        e_ref[h] = low_e
        total = jnp.sum(e, axis=0, keepdims=True) + e_self
        scale = 1.0 / total
        values = v[rows]
        mixed = dg(values, low_e, 1, 0) + values.astype(F32) * e_self.astype(BF).astype(F32)
        ctx_ref[rows, :] = (mixed * scale).astype(BF)
        stat_ref[h, 0:1, :] = scale
        stat_ref[h, 1:2, :] = e_self

    @pl.when(safe)
    def _():
        for h in range(2):
            finish(h, jnp.exp(scores(h)), jnp.exp(selves[h]) * dead)

    @pl.when(jnp.logical_not(safe))
    def _():
        for h in range(2):
            s = scores(h)
            own = jnp.where(dead > 0, selves[h], -FAR)
            top = jnp.maximum(jnp.max(s, axis=0, keepdims=True), own)
            finish(h, jnp.exp(s - top), jnp.exp(own - top) * dead)


def attend(act, w_qkv, kmask, qmask):
    width, tokens = act.shape
    pairs = width // (2 * HEAD_DIM)
    pair = 2 * HEAD_DIM
    heads = width // HEAD_DIM
    return pl.pallas_call(
        attend_kernel,
        name="attend",
        grid=(pairs,),
        in_specs=[
            whole((width, tokens)),
            pl.BlockSpec((width, pair), lambda i: (0, i)),
            pl.BlockSpec((width, pair), lambda i: (0, pairs + i)),
            pl.BlockSpec((width, pair), lambda i: (0, 2 * pairs + i)),
            pl.BlockSpec((pair, pair), lambda i: (i, 3 * pairs)),
            whole((16, tokens)),
            whole((16, tokens)),
        ],
        out_specs=[
            pl.BlockSpec((2, tokens, tokens), lambda i: (i, 0, 0)),
            pl.BlockSpec((pair, tokens), lambda i: (i, 0)),
            pl.BlockSpec((3, pair, tokens), lambda i: (0, i, 0)),
            pl.BlockSpec((2, 2, tokens), lambda i: (i, 0, 0)),
        ],
        out_shape=[
            jax.ShapeDtypeStruct((heads, tokens, tokens), BF),
            jax.ShapeDtypeStruct((width, tokens), BF),
            jax.ShapeDtypeStruct((3, width, tokens), BF),
            jax.ShapeDtypeStruct((heads, 2, tokens), F32),
        ],
        compiler_params=params(),
        cost_estimate=cost(6 * width * width * tokens + 4 * width * tokens * tokens, 2 * heads * tokens * tokens, heads * tokens * tokens),
    )(act, w_qkv, w_qkv, w_qkv, w_qkv, kmask, qmask)


def attend_back_pair(e_ref, qkv_ref, stat_ref, grad_ref, inner_ref, out_ref, ds_ref):
    for h in range(2):
        rows = slice(h * HEAD_DIM, (h + 1) * HEAD_DIM)
        q, k, v = qkv_ref[0, rows], qkv_ref[1, rows], qkv_ref[2, rows]
        grad = grad_ref[rows]
        inner = inner_ref[h]
        e_self = stat_ref[h, 1:2, :]
        grad_f = grad.astype(F32)
        ds = (e_ref[h].astype(F32) * (dg(v.T, grad, 1, 0) - inner)).astype(BF)
        ds_ref[h] = ds
        own = (e_self * (jnp.sum(grad_f * v.astype(F32), axis=0, keepdims=True) - inner)).astype(BF).astype(F32)
        scale = HEAD_DIM**-0.5
        out_ref[0, rows] = ((dg(k, ds, 1, 0) + k.astype(F32) * own) * scale).astype(BF)
        out_ref[2, rows] = (dg(e_ref[h], grad, 1, 1).T + grad_f * e_self.astype(BF).astype(F32)).astype(BF)
        out_ref[1, rows] = (dg(ds_ref[h], q, 1, 1).T + q.astype(F32) * own).astype(BF)


def attend_back(e, qkv, stat, grad, inner, start=0, pairs=None):
    heads, tokens, _ = e.shape
    width = grad.shape[0]
    pair = 2 * HEAD_DIM
    pairs = pairs or heads // 2
    return pl.pallas_call(
        attend_back_pair,
        name="attend_back",
        grid=(pairs,),
        in_specs=[
            pl.BlockSpec((2, tokens, tokens), lambda i: (start + i, 0, 0)),
            pl.BlockSpec((3, pair, tokens), lambda i: (0, start + i, 0)),
            pl.BlockSpec((2, 2, tokens), lambda i: (start + i, 0, 0)),
            pl.BlockSpec((pair, tokens), lambda i: (start + i, 0)),
            pl.BlockSpec((2, 1, tokens), lambda i: (start + i, 0, 0)),
        ],
        out_specs=pl.BlockSpec((3, pair, tokens), lambda i: (0, i, 0)),
        out_shape=jax.ShapeDtypeStruct((3, pairs * pair, tokens), BF),
        scratch_shapes=[pltpu.VMEM((2, tokens, tokens), BF)],
        compiler_params=params(),
        cost_estimate=cost(8 * pairs * pair * tokens * tokens, 4 * pairs * tokens * tokens),
    )(e, qkv, stat, grad, inner)


def normed(t):
    mean = jnp.mean(t, axis=0, keepdims=True)
    centred = t - mean
    rstd = lax.rsqrt(jnp.mean(centred * centred, axis=0, keepdims=True) + NORM_EPS)
    return centred * rstd, rstd


def normed_back(grad, unit, rstd, gain):
    scaled = grad * gain
    mean = jnp.mean(scaled, axis=0, keepdims=True)
    along = jnp.mean(scaled * unit, axis=0, keepdims=True)
    return rstd * (scaled - mean - unit * along)


def gelu_and_slope(t):
    square = t * t
    inside = jnp.tanh(t * (0.7978845608028654 + (0.7978845608028654 * 0.044715) * square))
    half = 0.5 + 0.5 * inside
    slope = half + (t * (0.5 - 0.5 * inside * inside)) * (
        0.7978845608028654 + (3.0 * 0.7978845608028654 * 0.044715) * square
    )
    return t * half, slope


def lanes_sum(t):
    out = t[:, 0:128]
    for j in range(128, t.shape[1], 128):
        out = out + t[:, j : j + 128]
    return out


def column(col_ref, j):
    return col_ref[:, j : j + 1].astype(F32)


def dense_forward(signal, ctx, rest_ref, col_ref, act_ref, slope_ref):
    wo_ref, win_ref, wback_ref = parts_of(rest_ref)
    joined = signal + dg(wo_ref[...], ctx, 0, 0) + column(col_ref, 6)
    unit_one, rstd_one = normed(joined)
    middle = unit_one * column(col_ref, 0) + column(col_ref, 1)
    low_middle = middle.astype(BF)
    width = middle.shape[0]
    summed = middle + column(col_ref, 7)
    for c in range(win_ref.shape[1] // width):
        rows = slice(c * width, (c + 1) * width)
        pre = dg(win_ref[:, rows], low_middle, 0, 0) + column(col_ref, 8 + c)
        gelu, slope = gelu_and_slope(pre)
        act = gelu.astype(BF)
        act_ref[rows, :] = act
        slope_ref[rows, :] = slope.astype(slope_ref.dtype)
        summed = summed + dg(wback_ref[:, rows], act, 1, 0)
    unit_two, rstd_two = normed(summed)
    return unit_one, rstd_one, low_middle, unit_two, rstd_two


def dense_back(grad, unit_one, rstd_one, slope_ref, unit_two, rstd_two, ctx, stat_ref, rest_ref, col_ref,
               sums_ref, joined_ref, gctx_ref, inner_ref, dz_ref, du_ref, dattn_ref):
    wo_ref, win_ref, wback_ref = parts_of(rest_ref)
    sums_ref[2] += lanes_sum(grad * unit_two)
    sums_ref[3] += lanes_sum(grad)
    grad_summed = normed_back(grad, unit_two, rstd_two, column(col_ref, 2))
    dz = grad_summed.astype(BF)
    dz_ref[...] = dz
    sums_ref[7] += lanes_sum(dz.astype(F32))
    width = dz.shape[0]
    grad_middle = grad_summed
    for c in range(win_ref.shape[1] // width):
        rows = slice(c * width, (c + 1) * width)
        du = (dg(wback_ref[:, rows], dz, 0, 0) * slope_ref[rows, :].astype(F32)).astype(BF)
        du_ref[rows, :] = du
        sums_ref[8 + c] += lanes_sum(du.astype(F32))
        grad_middle = grad_middle + dg(win_ref[:, rows], du, 1, 0)
    sums_ref[0] += lanes_sum(grad_middle * unit_one)
    sums_ref[1] += lanes_sum(grad_middle)
    grad_joined = normed_back(grad_middle, unit_one, rstd_one, column(col_ref, 0))
    joined_ref[...] = grad_joined
    dattn = grad_joined.astype(BF)
    dattn_ref[...] = dattn
    sums_ref[6] += lanes_sum(dattn.astype(F32))
    grad_ctx = dg(wo_ref[...], dattn, 1, 0)
    for h in range(stat_ref.shape[0]):
        rows = slice(h * HEAD_DIM, (h + 1) * HEAD_DIM)
        part = (grad_ctx[rows] * stat_ref[h, 0:1, :]).astype(BF)
        gctx_ref[rows, :] = part
        inner_ref[h] = jnp.sum(part.astype(F32) * ctx[rows].astype(F32), axis=0, keepdims=True)


def always(i):
    return i


def tile(rows, at=always, size=TILE):
    return pl.BlockSpec((rows, size), lambda i: (0, at(i)))


def heads_tile(heads, rows, at=always, size=TILE):
    return pl.BlockSpec((heads, rows, size), lambda i: (0, 0, at(i)))


def once(shape, *at):
    at = at or (0,) * len(shape)
    return pl.BlockSpec(shape, lambda i: at, pipeline_mode=pl.Buffered(1))


def span(step, size):
    return pl.ds(pl.multiple_of(step * size, size), size)


def rest_spec(w_rest):
    return pl.BlockSpec(w_rest.shape, lambda i: (0, 0), pipeline_mode=pl.Buffered(1))


def parts_of(rest_ref):
    width = rest_ref.shape[0]
    hidden = (rest_ref.shape[1] - width) // 2
    return rest_ref.at[:, 0:width], rest_ref.at[:, width : width + hidden], rest_ref.at[:, width + hidden :]


def column_spec(width):
    return pl.BlockSpec((width, LANES), lambda i: (0, 3 * width // LANES))


def first_dense_kernel(signal_ref, ctx_ref, rest_ref, col_ref,
                       unit_one_ref, unit_two_ref, rstd_ref, low_out_ref, act_ref, slope_ref):
    unit_one, rstd_one, _, unit_two, rstd_two = dense_forward(
        signal_ref[...].astype(F32), ctx_ref[...], rest_ref, col_ref, act_ref, slope_ref)
    unit_one_ref[...] = unit_one
    unit_two_ref[...] = unit_two
    rstd_ref[0:1, :] = rstd_one
    rstd_ref[1:2, :] = rstd_two
    low_out_ref[...] = (unit_two * column(col_ref, 2) + column(col_ref, 3)).astype(BF)


def first_half_kernel(layout, tiles, place_ref, own_ref, mine_ref, theirs_ref, signal_ref, ctx_ref, w_ref, kmask_ref, qmask_ref,
                      rest_ref, unit_one_ref, unit_two_ref, rstd_ref, low_ref, act_ref, slope_ref, e_ref, ctx_out_ref, qkv_ref, stat_ref, hold_ref):
    step = pl.program_id(0)
    width = ctx_ref.shape[0]
    pair = ctx_out_ref.shape[0]

    @pl.when(step == 0)
    def _():
        put_blocks(layout, place_ref, (mine_ref, theirs_ref), rest_ref)
        rest_ref[own_rows(layout, place_ref), :] = own_ref[:, own_ref.shape[1] - rest_ref.shape[1] :].astype(BF)

    @pl.when(step < tiles)
    def _():
        first_dense_kernel(signal_ref, ctx_ref, rest_ref, w_ref.at[:, 3 * width :], unit_one_ref, unit_two_ref, rstd_ref, low_ref, act_ref, slope_ref)
        hold_ref[:, span(step, TILE)] = low_ref[...]

    @pl.when(step >= tiles)
    def _():
        at = step - tiles
        pairs = width // pair
        attend_kernel(
            hold_ref,
            w_ref.at[:, span(at, pair)],
            w_ref.at[:, span(at + pairs, pair)],
            w_ref.at[:, span(at + 2 * pairs, pair)],
            w_ref.at[span(at, pair), 3 * width :],
            kmask_ref, qmask_ref, e_ref, ctx_out_ref, qkv_ref, stat_ref)


def first_half(layout, place, weights, mine, theirs, signal, ctx, w_first, kmask, qmask):
    width, tokens = signal.shape
    total = mine.shape[1]
    hidden = (total - width) // 2
    pair = 2 * HEAD_DIM
    pairs, heads = width // pair, width // HEAD_DIM
    tiles = tokens // TILE

    def at_tile(i):
        return jnp.minimum(i, tiles - 1)

    def at_pair(i):
        return jnp.maximum(i - tiles, 0)

    return pl.pallas_call(
        functools.partial(first_half_kernel, layout, tiles),
        name="first_half",
        grid=(tiles + pairs,),
        in_specs=[pl.BlockSpec(memory_space=pltpu.SMEM), once(weights.shape), once(mine.shape), once(theirs.shape),
                  tile(width, at_tile), tile(width, at_tile), once(w_first.shape), once(kmask.shape), once(qmask.shape)],
        out_specs=[whole((width, total)), tile(width, at_tile), tile(width, at_tile), tile(8, at_tile), tile(width, at_tile), tile(hidden, at_tile), tile(hidden, at_tile),
                   pl.BlockSpec((2, tokens, tokens), lambda i: (at_pair(i), 0, 0)),
                   pl.BlockSpec((pair, tokens), lambda i: (at_pair(i), 0)),
                   pl.BlockSpec((3, pair, tokens), lambda i: (0, at_pair(i), 0)),
                   pl.BlockSpec((2, 2, tokens), lambda i: (at_pair(i), 0, 0))],
        out_shape=[
            jax.ShapeDtypeStruct((width, total), BF),
            jax.ShapeDtypeStruct((width, tokens), F32),
            jax.ShapeDtypeStruct((width, tokens), F32),
            jax.ShapeDtypeStruct((8, tokens), F32),
            jax.ShapeDtypeStruct((width, tokens), BF),
            jax.ShapeDtypeStruct((hidden, tokens), BF),
            jax.ShapeDtypeStruct((hidden, tokens), BF),
            jax.ShapeDtypeStruct((heads, tokens, tokens), BF),
            jax.ShapeDtypeStruct((width, tokens), BF),
            jax.ShapeDtypeStruct((3, width, tokens), BF),
            jax.ShapeDtypeStruct((heads, 2, tokens), F32),
        ],
        scratch_shapes=[pltpu.VMEM((width, tokens), BF)],
        compiler_params=params(),
        cost_estimate=cost(2 * tokens * width * (width + 2 * hidden), 24 << 20, tokens * hidden),
    )(place, weights, mine, theirs, signal, ctx, w_first, kmask, qmask)


def second_dense_kernel(unit_ref, ctx_ref, cot_ref, stat_ref, rest_ref, col_ref,
                        out_ref, sums_ref, joined_ref, gctx_ref, inner_ref, mid_ref, act_ref, dz_ref, du_ref, dattn_ref, slope_ref):
    @pl.when(pl.program_id(0) == 0)
    def _():
        sums_ref[...] = jnp.zeros(sums_ref.shape, F32)

    ctx = ctx_ref[...]
    gain, shift = column(col_ref, 2), column(col_ref, 3)
    unit_one, rstd_one, low_middle, unit_two, rstd_two = dense_forward(
        unit_ref[...] * gain + shift, ctx, rest_ref, col_ref, act_ref, slope_ref)
    mid_ref[...] = low_middle
    out_ref[...] = (unit_two * gain + shift).astype(BF).T
    dense_back(cot_ref[...].astype(F32), unit_one, rstd_one, slope_ref, unit_two, rstd_two, ctx, stat_ref,
               rest_ref, col_ref, sums_ref, joined_ref, gctx_ref, inner_ref, dz_ref, du_ref, dattn_ref)


def second_half_kernel(tiles, unit_ref, ctx_ref, cot_ref, stat_ref, rest_ref, col_ref, e_ref, qkv_ref, pair_stat_ref,
                       out_ref, sums_ref, joined_ref, mid_ref, act_ref, dz_ref, du_ref, dattn_ref, dqkv_ref, slope_ref, gctx_ref, inner_ref, ds_ref):
    step = pl.program_id(0)

    @pl.when(step < tiles)
    def _():
        at = span(step, TILE)
        second_dense_kernel(unit_ref, ctx_ref, cot_ref, stat_ref, rest_ref, col_ref, out_ref, sums_ref, joined_ref,
                            gctx_ref.at[:, at], inner_ref.at[:, :, at], mid_ref, act_ref, dz_ref, du_ref, dattn_ref, slope_ref)

    @pl.when(step >= tiles)
    def _():
        pair = dqkv_ref.shape[1]
        attend_back_pair(e_ref, qkv_ref, pair_stat_ref, gctx_ref.at[span(step - tiles, pair)], inner_ref.at[pl.ds(2 * (step - tiles), 2)], dqkv_ref, ds_ref)


def second_half(unit, ctx, cot, stat, w_rest, w_first, e, qkv):
    width, tokens = unit.shape
    hidden = (w_rest.shape[1] - width) // 2
    heads = stat.shape[0]
    pair = 2 * HEAD_DIM
    pairs = width // pair
    tiles = tokens // TILE

    def at_tile(i):
        return jnp.minimum(i, tiles - 1)

    def at_pair(i):
        return jnp.maximum(i - tiles, 0)

    return pl.pallas_call(
        functools.partial(second_half_kernel, tiles),
        name="second_half",
        grid=(tiles + pairs,),
        in_specs=[tile(width, at_tile), tile(width, at_tile), tile(width, at_tile), heads_tile(heads, 2, at_tile), once(w_rest.shape), column_spec(width),
                  pl.BlockSpec((2, tokens, tokens), lambda i: (at_pair(i), 0, 0)),
                  pl.BlockSpec((3, pair, tokens), lambda i: (0, at_pair(i), 0)),
                  pl.BlockSpec((2, 2, tokens), lambda i: (at_pair(i), 0, 0))],
        out_specs=[pl.BlockSpec((TILE, width), lambda i: (at_tile(i), 0)), whole((12, width, LANES)), tile(width, at_tile),
                   tile(width, at_tile), tile(hidden, at_tile), tile(width, at_tile), tile(hidden, at_tile), tile(width, at_tile),
                   pl.BlockSpec((3, pair, tokens), lambda i: (0, at_pair(i), 0))],
        out_shape=[
            jax.ShapeDtypeStruct((tokens, width), BF),
            jax.ShapeDtypeStruct((12, width, LANES), F32),
            jax.ShapeDtypeStruct((width, tokens), F32),
            jax.ShapeDtypeStruct((width, tokens), BF),
            jax.ShapeDtypeStruct((hidden, tokens), BF),
            jax.ShapeDtypeStruct((width, tokens), BF),
            jax.ShapeDtypeStruct((hidden, tokens), BF),
            jax.ShapeDtypeStruct((width, tokens), BF),
            jax.ShapeDtypeStruct((3, width, tokens), BF),
        ],
        scratch_shapes=[pltpu.VMEM((hidden, TILE), F32), pltpu.VMEM((width, tokens), BF), pltpu.VMEM((heads, 1, tokens), F32), pltpu.VMEM((2, tokens, tokens), BF)],
        compiler_params=params(56),
        cost_estimate=cost(4 * tokens * width * (width + 2 * hidden), 28 << 20, tokens * hidden),
    )(unit, ctx, cot, stat, w_rest, w_first, e, qkv, stat)


def first_back_kernel(prior_ref, dqkv_ref, unit_one_ref, unit_two_ref, rstd_ref, slope_ref, ctx_ref, stat_ref,
                      wqkv_ref, rest_ref, col_ref,
                      vec_ref, joined_ref, gctx_ref, inner_ref, mid_ref, dz_ref, du_ref, dattn_ref, sums_ref, step, tiles):

    unit_one = unit_one_ref[...]
    mid_ref[...] = (unit_one * column(col_ref, 0) + column(col_ref, 1)).astype(BF)
    grad = prior_ref[...] + dg(wqkv_ref[...], dqkv_ref[...], 1, 0)
    dense_back(grad, unit_one, rstd_ref[0:1, :], slope_ref, unit_two_ref[...], rstd_ref[1:2, :], ctx_ref[...], stat_ref,
               rest_ref, col_ref, sums_ref, joined_ref, gctx_ref, inner_ref, dz_ref, du_ref, dattn_ref)

    @pl.when(step == tiles - 1)
    def _():
        lane = lax.broadcasted_iota(jnp.int32, vec_ref.shape, 1)
        out = jnp.zeros(vec_ref.shape, F32)
        for j in (0, 1, 2, 3, 6, 7, 8, 9, 10, 11):
            out = jnp.where(lane == j, jnp.sum(sums_ref[j], axis=1, keepdims=True), out)
        vec_ref[...] = out


class Layout:
    def __init__(self, mesh_batch, mesh_shard, width):
        self.batch = mesh_batch
        self.shards = mesh_shard
        self.parts = min(mesh_batch, width // mesh_shard // 16)
        self.planes = self.parts // 2
        self.rows = width // mesh_shard // self.parts

    def swap(self, value, axis, distance):
        size = self.batch if axis == "batch" else self.shards
        return lax.ppermute(value, axis, [(i, i ^ distance) for i in range(size)])

    def place(self):
        return jnp.stack([lax.axis_index("batch") % self.parts, lax.axis_index("shard")]).astype(jnp.int32)

    def row_of(self, place_ref, c, e, d):
        block = (place_ref[1] ^ d) * self.parts + (place_ref[0] ^ (2 * e + c))
        return pl.multiple_of(block * self.rows, self.rows)

    def along_shards(self, blocks):
        return [self.swap(blocks[d % len(blocks)], "shard", d) for d in range(1, self.shards)]

    def across_plane(self, blocks):
        return [self.swap(blocks[e % len(blocks)], "batch", 2 * e) for e in range(1, self.planes)]

    def across_cores(self, block):
        return self.swap(block, "batch", 1)

    def across_rest(self, own):
        distance = self.parts
        while distance < self.batch:
            own = add([own, self.swap(own, "batch", distance)])[0]
            distance *= 2
        return own


def tree(values):
    while len(values) > 1:
        values = [a + b for a, b in zip(values[::2], values[1::2], strict=True)]
    return values[0]


def whole_specs(values, tokens_in=()):
    return [whole(v.shape) for v in values] + [pl.BlockSpec(memory_space=pl.ANY)] * len(tokens_in)


def join_kernel(count, *refs):
    out_ref = refs[-1]
    at = 0
    for source in refs[:count]:
        out_ref[at : at + source.shape[0], :] = source[...]
        at += source.shape[0]


def join(blocks, tokens_in=()):
    rows, columns = sum(b.shape[0] for b in blocks), blocks[0].shape[1]
    return pl.pallas_call(
        functools.partial(join_kernel, len(blocks)),
        name="join",
        grid=(1,),
        in_specs=whole_specs(blocks, tokens_in),
        out_specs=whole((rows, columns)),
        out_shape=jax.ShapeDtypeStruct((rows, columns), BF),
        compiler_params=params(),
        cost_estimate=cost(0, 4 * rows * columns),
    )(*blocks, *tokens_in)


def add_kernel(count, outs, *refs):
    total = refs[0][...].astype(F32)
    for other in refs[1:count]:
        total = total + other[...].astype(F32)
    total = total.astype(BF)
    rows = refs[-1].shape[0]
    for i in range(outs):
        refs[i - outs][...] = total[i * rows : (i + 1) * rows]


def add(values, outs=1, tokens_in=()):
    rows, columns = values[0].shape
    part = jax.ShapeDtypeStruct((rows // outs, columns), BF)
    return pl.pallas_call(
        functools.partial(add_kernel, len(values), outs),
        name="add",
        grid=(1,),
        in_specs=whole_specs(values, tokens_in),
        out_specs=[whole(part.shape)] * outs,
        out_shape=[part] * outs,
        compiler_params=params(),
        cost_estimate=cost(len(values) * rows * columns, 2 * (len(values) + 1) * rows * columns),
    )(*values, *tokens_in)


def add_squares_kernel(count, others, *refs):
    out_ref = refs[-1]
    total = refs[0][...].astype(F32)
    for other in refs[1:count]:
        total = total + other[...].astype(F32)
    total = total.astype(BF)
    squares = jnp.sum(jnp.square(total.astype(F32)), keepdims=True)
    for other in refs[count : count + others]:
        squares = squares + jnp.sum(jnp.square(other[...].astype(F32)), keepdims=True)
    out_ref[...] = total
    high = squares.astype(BF)
    middle = (squares - high.astype(F32)).astype(BF)
    low = (squares - high.astype(F32) - middle.astype(F32)).astype(BF)
    used = total.shape[1] - LANES
    tail = total[:, used:]
    lane = lax.broadcasted_iota(jnp.int32, tail.shape, 1)
    for i, piece in enumerate((high, middle, low)):
        tail = jnp.where(lane == SQUARES_AT + i, piece.astype(F32), tail.astype(F32)).astype(BF)
    out_ref[:, used:] = tail


def add_squares(values, others):
    rows, columns = values[0].shape
    return pl.pallas_call(
        functools.partial(add_squares_kernel, len(values), len(others)),
        name="add_squares",
        grid=(1,),
        in_specs=whole_specs(list(values) + list(others)),
        out_specs=whole((rows, columns)),
        out_shape=jax.ShapeDtypeStruct((rows, columns), BF),
        compiler_params=params(),
        cost_estimate=cost(len(values) * rows * columns, 2 * (len(values) + 1) * rows * columns),
    )(*values, *others)


def shard_squares_kernel(layout, place_ref, mine_ref, theirs_ref, out_ref):
    used = mine_ref.shape[1] - LANES
    total = jnp.zeros((1, LANES), F32)
    lane = lax.broadcasted_iota(jnp.int32, (1, LANES), 1)
    riding = (lane >= SQUARES_AT) & (lane < SQUARES_AT + 3)
    for part in range(layout.parts):
        away = place_ref[0] ^ part
        at = pl.ds(pl.multiple_of((away >> 1) * layout.rows, layout.rows), layout.rows)
        mine = mine_ref[at, used:].astype(F32)[0:1]
        theirs = theirs_ref[at, used:].astype(F32)[0:1]
        total = total + jnp.where((away & 1) == 0, mine, theirs)
    total = jnp.sum(jnp.where(riding, total, 0.0), axis=1, keepdims=True)
    out_ref[...] = jnp.broadcast_to(total, out_ref.shape)


def shard_squares(layout, place, mine, theirs):
    return pl.pallas_call(
        functools.partial(shard_squares_kernel, layout),
        name="shard_squares",
        grid=(1,),
        in_specs=[pl.BlockSpec(memory_space=pltpu.SMEM)] + whole_specs((mine, theirs)),
        out_specs=whole((8, LANES)),
        out_shape=jax.ShapeDtypeStruct((8, LANES), F32),
        compiler_params=params(),
        cost_estimate=cost(0, 4 * mine.size),
    )(place, mine, theirs)


def pick_first_kernel(place_ref, w_ref, vec_ref, out_ref, columns_ref, hold_ref):
    hold_ref[...] = jnp.zeros(hold_ref.shape, F32)
    hold_ref[0 : vec_ref.shape[0], 0 : vec_ref.shape[1]] = vec_ref[...]
    hold_ref[...] = hold_ref[...].T
    columns_ref[...] = hold_ref[0 : columns_ref.shape[0], :].astype(BF)
    used = w_ref.shape[1]
    rows = out_ref.shape[0]
    out_ref[:, 0:used] = w_ref[...].astype(BF)
    out_ref[:, used:] = hold_ref[pl.ds(pl.multiple_of(place_ref[0] * rows, rows), rows), :].astype(BF)


def pick_first(layout, place, weights, vectors):
    shard_rows, columns = weights.shape
    used = columns // 4
    return pl.pallas_call(
        pick_first_kernel,
        name="pick_first",
        grid_spec=pltpu.PrefetchScalarGridSpec(
            num_scalar_prefetch=1,
            grid=(1,),
            in_specs=[pl.BlockSpec((layout.rows, used), lambda i, place: (place[0], 0)), pl.BlockSpec(vectors.shape, lambda i, place: (0, 0))],
            out_specs=[pl.BlockSpec((layout.rows, used + LANES), lambda i, place: (0, 0)), pl.BlockSpec((shard_rows, LANES), lambda i, place: (0, 0))],
            scratch_shapes=[pltpu.VMEM((LANES, LANES), F32)],
        ),
        out_shape=[jax.ShapeDtypeStruct((layout.rows, used + LANES), BF), jax.ShapeDtypeStruct((shard_rows, LANES), BF)],
        compiler_params=params(),
        cost_estimate=cost(0, 6 * layout.rows * columns),
    )(place, weights, vectors)


def pick_rest_kernel(place_ref, w_ref, *refs):
    out_ref = refs[-1]
    out_ref[...] = w_ref[:, w_ref.shape[1] - out_ref.shape[1] :].astype(BF)


def pick_rest(layout, place, weights, tokens_in):
    columns = weights.shape[1]
    return pl.pallas_call(
        pick_rest_kernel,
        name="pick_rest",
        grid_spec=pltpu.PrefetchScalarGridSpec(
            num_scalar_prefetch=1,
            grid=(1,),
            in_specs=[pl.BlockSpec((layout.rows, columns), lambda i, place: (place[0], 0))] + [pl.BlockSpec(memory_space=pl.ANY)] * len(tokens_in),
            out_specs=pl.BlockSpec((layout.rows, 3 * columns // 4), lambda i, place: (0, 0)),
        ),
        out_shape=jax.ShapeDtypeStruct((layout.rows, 3 * columns // 4), BF),
        compiler_params=params(),
        cost_estimate=cost(0, 6 * layout.rows * columns),
    )(place, weights, *tokens_in)


def put_blocks(layout, place_ref, sources, out_ref):
    for c, source in enumerate(sources):
        for e in range(layout.planes):
            for d in range(1, layout.shards):
                at = (e * (layout.shards - 1) + d - 1) * layout.rows
                out_ref[pl.ds(layout.row_of(place_ref, c, e, d), layout.rows), :] = source[at : at + layout.rows, :]


def own_rows(layout, place_ref):
    rows = layout.rows * layout.parts
    return pl.ds(pl.multiple_of(place_ref[1] * rows, rows), rows)


def collect_first_kernel(layout, place_ref, w_ref, columns_ref, mine_ref, theirs_ref, out_ref):
    put_blocks(layout, place_ref, (mine_ref, theirs_ref), out_ref)
    rows = own_rows(layout, place_ref)
    used = w_ref.shape[1]
    out_ref[rows, 0:used] = w_ref[...].astype(BF)
    out_ref[rows, used:] = columns_ref[...]


def collect_first(layout, place, weights, columns, mine, theirs):
    shard_rows, all_columns = weights.shape
    rows = shard_rows * layout.shards
    total = mine.shape[1]
    return pl.pallas_call(
        functools.partial(collect_first_kernel, layout),
        name="collect_first",
        grid=(1,),
        in_specs=[pl.BlockSpec(memory_space=pltpu.SMEM), pl.BlockSpec((shard_rows, all_columns // 4), lambda i: (0, 0))] + whole_specs((columns, mine, theirs)),
        out_specs=whole((rows, total)),
        out_shape=jax.ShapeDtypeStruct((rows, total), BF),
        compiler_params=params(),
        cost_estimate=cost(0, 4 * rows * total),
    )(place, weights, columns, mine, theirs)


def in_order(layout, place_ref, source_ref, target_ref):
    at = 0
    for c in range(2):
        for e in range(layout.planes):
            for d in range(layout.shards):
                target_ref[at : at + layout.rows] = source_ref[pl.ds(layout.row_of(place_ref, c, e, d), layout.rows), :]
                at += layout.rows


def weight_step(left_ref, ra_ref, rb_ref, keep_ref, send_ref):
    out = (dg(left_ref[0], ra_ref[...], 1, 1) + dg(left_ref[1], rb_ref[...], 1, 1)).astype(BF)
    half = out.shape[0] // 2
    keep_ref[...] = out[:half]
    send_ref[...] = out[half:]


def turn_kernel(layout, tiles, place_ref, prior_ref, dqkv_ref, unit_one_ref, unit_two_ref, rstd_ref, slope_ref, ctx_ref, stat_ref, sums_in_ref,
                wqkv_ref, rest_ref, col_ref, du_two_ref, hid_one_ref, hid_two_ref, mid_two_ref, dz_two_ref, ctx_one_ref, ctx_two_ref, dattn_two_ref,
                vec_ref, joined_ref, gctx_ref, inner_ref, keep_ref, send_ref,
                sums_ref, mid_ref, dz_ref, du_ref, dattn_ref, left_ref, far_ref, sem):
    step = pl.program_id(0)
    width = mid_ref.shape[0]
    count = du_ref.shape[0] // width
    copies = [
        pltpu.make_async_copy(source, far_ref.at[i], sem.at[i])
        for i, source in enumerate((mid_two_ref, dz_two_ref, ctx_one_ref, ctx_two_ref, dattn_two_ref))
    ]
    start = pltpu.make_async_copy(sums_in_ref, sums_ref, sem.at[len(copies)])

    @pl.when(step == 0)
    def _():
        start.start()
        start.wait()
        for copy in copies:
            copy.start()

    @pl.when(step < tiles)
    def _():
        at = span(step, WIDE_TILE)
        first_back_kernel(prior_ref, dqkv_ref, unit_one_ref, unit_two_ref, rstd_ref, slope_ref, ctx_ref, stat_ref,
                          wqkv_ref, rest_ref, col_ref, vec_ref, joined_ref, gctx_ref, inner_ref,
                          mid_ref.at[:, at], dz_ref.at[:, at], du_ref.at[:, at], dattn_ref.at[:, at], sums_ref, step, tiles)

    @pl.when(step == tiles)
    def _():
        for copy in copies:
            copy.wait()

    for at, first_ref, second_ref in ((0, mid_ref, far_ref.at[0]), (count, dz_ref, far_ref.at[1]), (2 * count, far_ref.at[2], far_ref.at[3])):
        @pl.when(step == tiles + at)
        def _(first_ref=first_ref, second_ref=second_ref):
            in_order(layout, place_ref, first_ref, left_ref.at[0])
            in_order(layout, place_ref, second_ref, left_ref.at[1])

    @pl.when((step >= tiles) & (step < tiles + count))
    def _():
        weight_step(left_ref, du_ref.at[span(step - tiles, width)], du_two_ref, keep_ref, send_ref)

    @pl.when((step >= tiles + count) & (step < tiles + 2 * count))
    def _():
        weight_step(left_ref, hid_one_ref, hid_two_ref, keep_ref, send_ref)

    @pl.when(step == tiles + 2 * count)
    def _():
        weight_step(left_ref, dattn_ref, far_ref.at[4], keep_ref, send_ref)


def turn(layout, place, prior, dqkv, unit_one, unit_two, rstd, slope, ctx_one, stat, sums, w_first, w_rest,
         du_two, hid_one, hid_two, mid_two, dz_two, ctx_two, dattn_two):
    width, tokens = prior.shape
    hidden = (w_rest.shape[1] - width) // 2
    heads = stat.shape[0]
    tiles = tokens // WIDE_TILE
    count = hidden // width
    half = jax.ShapeDtypeStruct((width // 2, 2 * hidden + width), BF)

    def at_tile(i):
        return jnp.minimum(i, tiles - 1)

    def rows_from(start):
        return pl.BlockSpec((width, tokens), lambda i: (jnp.clip(i - tiles - start, 0, count - 1), 0))

    columns = pl.BlockSpec((width // 2, width), lambda i: (0, jnp.clip(i - tiles, 0, 2 * count)))
    return pl.pallas_call(
        functools.partial(turn_kernel, layout, tiles),
        name="turn",
        grid=(tiles + 2 * count + 1,),
        in_specs=[pl.BlockSpec(memory_space=pltpu.SMEM), tile(width, at_tile, WIDE_TILE), tile(3 * width, at_tile, WIDE_TILE), tile(width, at_tile, WIDE_TILE), tile(width, at_tile, WIDE_TILE), tile(8, at_tile, WIDE_TILE),
                  tile(hidden, at_tile, WIDE_TILE), tile(width, at_tile, WIDE_TILE), heads_tile(heads, 2, at_tile, WIDE_TILE), pl.BlockSpec(memory_space=pl.ANY),
                  once((width, 3 * width)), once(w_rest.shape), column_spec(width), rows_from(0), rows_from(count), rows_from(count)]
        + [pl.BlockSpec(memory_space=pl.ANY)] * 5,
        out_specs=[whole((width, LANES)), tile(width, at_tile, WIDE_TILE), tile(width, at_tile, WIDE_TILE), heads_tile(heads, 1, at_tile, WIDE_TILE), columns, columns],
        out_shape=[
            jax.ShapeDtypeStruct((width, LANES), F32),
            jax.ShapeDtypeStruct((width, tokens), F32),
            jax.ShapeDtypeStruct((width, tokens), BF),
            jax.ShapeDtypeStruct((heads, 1, tokens), F32),
            half,
            half,
        ],
        scratch_shapes=[pltpu.VMEM((12, width, LANES), F32), pltpu.VMEM((width, tokens), BF), pltpu.VMEM((width, tokens), BF), pltpu.VMEM((hidden, tokens), BF),
                        pltpu.VMEM((width, tokens), BF), pltpu.VMEM((2, width, tokens), BF), pltpu.VMEM((5, width, tokens), BF), pltpu.SemaphoreType.DMA((6,))],
        compiler_params=params(60),
        cost_estimate=cost(2 * tokens * width * (4 * width + 2 * hidden), 28 << 20),
    )(place, prior, dqkv, unit_one, unit_two, rstd, slope, ctx_one, stat, sums, w_first, w_rest, w_first, du_two, hid_one, hid_two,
      mid_two, dz_two, ctx_one, ctx_two, dattn_two)


def last_kernel(layout, pairs, tiles, given, place_ref, e_ref, qkv_ref, stat_ref, grad_ref, inner_ref, done_ref, joined_ref, w_ref,
                la_ref, lb_ref, rb_ref, vec_in_ref, *refs):
    keep_ref, send_ref, input_ref, ds_ref, dqkv_ref, left_ref, vec_ref, order_ref = refs[given:]
    step = pl.program_id(0)
    pair = grad_ref.shape[0]
    rows = left_ref.shape[1]
    skipped = done_ref.shape[1]

    @pl.when(step == 0)
    def _():
        dqkv_ref[:, 0:skipped] = done_ref[...]
        in_order(layout, place_ref, la_ref, left_ref.at[0])
        in_order(layout, place_ref, lb_ref, left_ref.at[1])
        vec_ref[...] = vec_in_ref[...]

    @pl.when(step < pairs)
    def _():
        at = pl.ds(pl.multiple_of(skipped + step * pair, pair), pair)
        attend_back_pair(e_ref, qkv_ref, stat_ref, grad_ref, inner_ref, dqkv_ref.at[:, at], ds_ref)

    @pl.when((step >= pairs) & (step < pairs + tiles))
    def _():
        width = joined_ref.shape[1]
        at = pl.ds(pl.multiple_of((step - pairs) * width, width), width)
        total = joined_ref[...]
        for t in range(3):
            total = total + dg(w_ref[:, t * rows : (t + 1) * rows], dqkv_ref[t, :, at], 1, 0)
        input_ref[...] = total.T

    @pl.when(step >= pairs + tiles)
    def _():
        third = step - pairs - tiles
        ra, rb = dqkv_ref[third], rb_ref[0]
        out = (dg(left_ref[0], ra, 1, 1) + dg(left_ref[1], rb, 1, 1)).astype(BF)
        half = rows // 2
        columns = pl.ds(pl.multiple_of(third * rows, rows), rows)
        keep_ref[:, columns] = out[:half]
        send_ref[:, columns] = out[half:]
        sums = jnp.sum(lanes_sum(ra.astype(F32)) + lanes_sum(rb.astype(F32)), axis=1, keepdims=True)
        lane = lax.broadcasted_iota(jnp.int32, vec_ref.shape, 1)
        wanted = ((third == 0) & (lane == 4)) | ((third == 2) & (lane == 5))
        vec_ref[...] = jnp.where(wanted, sums, vec_ref[...])

    @pl.when(step == pl.num_programs(0) - 1)
    def _():
        in_order(layout, place_ref, vec_ref, order_ref)
        half = rows // 2
        used = keep_ref.shape[1] - LANES
        keep_ref[:, used:] = order_ref[0:half].astype(BF)
        send_ref[:, used:] = order_ref[half:].astype(BF)


def last(layout, place, e, qkv, stat, grad, inner, done, skipped, joined, w_first, left_one, left_two, dqkv_two, vec, tokens_in):
    rows, tokens = left_one.shape
    pair = 2 * HEAD_DIM
    pairs = rows // pair - skipped
    tiles = tokens // WIDE_TILE
    half = jax.ShapeDtypeStruct((rows // 2, 3 * rows + LANES), BF)

    def at_pair(i):
        return skipped + jnp.minimum(i, pairs - 1)

    def at_tile(i):
        return jnp.clip(i - pairs, 0, tiles - 1)

    return pl.pallas_call(
        functools.partial(last_kernel, layout, pairs, tiles, len(tokens_in)),
        name="last",
        grid=(pairs + tiles + 3,),
        in_specs=[
            pl.BlockSpec(memory_space=pltpu.SMEM),
            pl.BlockSpec((2, tokens, tokens), lambda i: (at_pair(i), 0, 0)),
            pl.BlockSpec((3, pair, tokens), lambda i: (0, at_pair(i), 0)),
            pl.BlockSpec((2, 2, tokens), lambda i: (at_pair(i), 0, 0)),
            pl.BlockSpec((pair, tokens), lambda i: (at_pair(i), 0)),
            pl.BlockSpec((2, 1, tokens), lambda i: (at_pair(i), 0, 0)),
            once((3, skipped * pair, tokens)),
            pl.BlockSpec((rows, WIDE_TILE), lambda i: (0, at_tile(i))),
            once((rows, 3 * rows)),
            once((rows, tokens)),
            once((rows, tokens)),
            pl.BlockSpec((1, rows, tokens), lambda i: (jnp.clip(i - pairs - tiles, 0, 2), 0, 0)),
            once(vec.shape),
        ] + [pl.BlockSpec(memory_space=pl.ANY)] * len(tokens_in),
        out_specs=[whole(half.shape)] * 2 + [pl.BlockSpec((WIDE_TILE, rows), lambda i: (at_tile(i), 0))],
        out_shape=[half, half, jax.ShapeDtypeStruct((tokens, rows), F32)],
        scratch_shapes=[pltpu.VMEM((2, tokens, tokens), BF), pltpu.VMEM((3, rows, tokens), BF), pltpu.VMEM((2, rows, tokens), BF),
                        pltpu.VMEM(vec.shape, F32), pltpu.VMEM(vec.shape, F32)],
        compiler_params=params(),
        cost_estimate=cost(12 * rows * rows * tokens, 12 * rows * tokens),
    )(place, e, qkv, stat, grad, inner, done, joined, w_first, left_one, left_two, dqkv_two, vec, *tokens_in)


def adam_kernel(layout, pieces, place_ref, *refs):
    grads = [refs[2 * i : 2 * i + 2] for i in range(len(pieces))]
    rest = refs[2 * len(pieces) :]
    shares, rest = rest[: layout.shards], rest[layout.shards :]
    w_ref, one_ref, two_ref, v_ref, vone_ref, vtwo_ref = rest[:6]
    gw_ref, nw_ref, none_ref, ntwo_ref, gv_ref, nv_ref, nvone_ref, nvtwo_ref, norm_ref = rest[6:15]
    holds, hold_ref = rest[15:-1], rest[-1]
    norm = jnp.sqrt(tree([share[0:1, 0:1] for share in shares]))
    clip_limit = math.sqrt(D * WCOLS)
    factor = clip_limit / jnp.maximum(norm, clip_limit)
    step = pl.program_id(0)
    rows = layout.rows

    @pl.when(step == 0)
    def _():
        norm_ref[...] = jnp.broadcast_to(norm, norm_ref.shape)
        for blocks, target in zip(grads, holds, strict=True):
            for c, block in enumerate(blocks):
                for e in range(layout.planes):
                    part = place_ref[0] ^ (2 * e + c)
                    target[pl.ds(pl.multiple_of(part * rows, rows), rows), :] = block[e * rows : (e + 1) * rows, :]
        hold_ref[0 : holds[-1].shape[0], :] = holds[-1][:, holds[-1].shape[1] - LANES :].astype(F32)
        grad = hold_ref[...].T[0 : gv_ref.shape[0], 0 : gv_ref.shape[1]]
        gv_ref[...] = grad
        nv_ref[...], nvone_ref[...], nvtwo_ref[...] = adam_update(v_ref[...], vone_ref[...], vtwo_ref[...], grad * factor)

    size = w_ref.shape[0]
    at = pl.ds(pl.multiple_of(step * size, size), size)
    for held, spans in zip(holds, pieces, strict=True):
        for source, target, width in spans:
            to = slice(target, target + width)
            grad = held[at, source : source + width].astype(F32)
            gw_ref[:, to] = grad
            nw_ref[:, to], none_ref[:, to], ntwo_ref[:, to] = adam_update(w_ref[:, to], one_ref[:, to], two_ref[:, to], grad * factor)


def adam(layout, place, shares, pieces, grads, weights, first, second, vectors, vector_first, vector_second):
    rows, columns = weights.shape
    block = 16
    natural = pl.BlockSpec((block, columns), lambda i: (i, 0))
    big = jax.ShapeDtypeStruct((rows, columns), F32)
    little = jax.ShapeDtypeStruct(vectors.shape, F32)
    flat = [t for blocks in grads for t in blocks] + list(shares)
    return pl.pallas_call(
        functools.partial(adam_kernel, layout, pieces),
        name="adam",
        grid=(rows // block,),
        in_specs=[pl.BlockSpec(memory_space=pltpu.SMEM)] + whole_specs(flat) + [natural] * 3 + [whole(vectors.shape)] * 3,
        out_specs=[natural] * 4 + [whole(vectors.shape)] * 4 + [whole((1, 1))],
        out_shape=[big] * 4 + [little] * 4 + [jax.ShapeDtypeStruct((1, 1), F32)],
        scratch_shapes=[pltpu.VMEM((rows, blocks[0].shape[1]), BF) for blocks in grads] + [pltpu.VMEM((LANES, LANES), F32)],
        compiler_params=params(32),
        cost_estimate=cost(20 * rows * columns, 30 * rows * columns, rows * columns),
    )(place, *flat, weights, first, second, vectors, vector_first, vector_second)


def masks(segments, tags, length):
    tokens = segments.shape[0]
    matches = segments[None, :] == jnp.arange(tags.shape[0], dtype=jnp.int32)[:, None]
    group = jnp.sum(jnp.where(matches, tags[:, None], 0), axis=0)
    live = jnp.arange(tokens, dtype=jnp.int32) < length
    kinds = jnp.arange(16, dtype=jnp.int32)[:, None]
    same = group[None, :] == kinds
    kmask = jnp.where(kinds < 4, (same & live[None, :]).astype(F32), jnp.where(kinds == 4, (~live)[None, :].astype(F32), 0.0))
    qmask = jnp.where(kinds < 4, jnp.where(same, 0.0, -FAR), jnp.where(kinds == 4, -FAR, 0.0))
    return kmask.astype(BF), jnp.broadcast_to(qmask, (16, tokens)).astype(BF)


def on_device(layout, inputs, cotangent, lengths, segment_ids, group_tags, weights, first_moments, second_moments, vectors, vector_first, vector_second):
    _, tokens, width = inputs.shape
    hidden = (weights.shape[1] - 4 * width) // 2
    pair = 2 * HEAD_DIM
    place = layout.place()
    kmask, qmask = masks(segment_ids[0], group_tags[0], lengths[0])
    act_one = inputs[0].T
    cot = cotangent[0].T

    first_part, own_columns = pick_first(layout, place, weights, vectors)
    first_z = join(layout.along_shards([first_part]))
    rest_part = pick_rest(layout, place, weights, (first_z,))
    first_mine = join([first_z] + layout.across_plane([first_z]))
    rest_z = join(layout.along_shards([rest_part]), (first_mine,))
    w_first = collect_first(layout, place, weights, own_columns, first_mine, layout.across_cores(first_mine))
    e_one, ctx_one, qkv_one, stat_one = attend(act_one, w_first, kmask, qmask)
    rest_mine = join([rest_z] + layout.across_plane([rest_z]), (ctx_one,))
    w_rest, unit_one, unit_two, rstd, act_two, hid_one, slope, e_two, ctx_two, qkv_two, stat_two = first_half(
        layout, place, weights, rest_mine, layout.across_cores(rest_mine), act_one, ctx_one, w_first, kmask, qmask)
    outputs, sums, joined_two, mid_two, hid_two, dz_two, du_two, dattn_two, dqkv_two = second_half(
        unit_two, ctx_two, cot, stat_two, w_rest, w_first, e_two, qkv_two)
    vec, joined_one, gctx_one, inner_one, keep, send = turn(
        layout, place, joined_two, dqkv_two.reshape(3 * width, tokens), unit_one, unit_two, rstd, slope, ctx_one, stat_one, sums, w_first, w_rest,
        du_two, hid_one, hid_two, mid_two, dz_two, ctx_two, dattn_two)
    operands = (e_one, qkv_one, stat_one, gctx_one, inner_one)
    done = attend_back(*operands, 0, 1)
    half = add((keep, layout.across_cores(send)), layout.planes, (done,))
    keep, send, input_grad = last(layout, place, *operands, done, 1, joined_one, w_first, act_one, act_two, dqkv_two, vec, (half[0],))
    plane = add([half[0]] + layout.across_plane(half), layout.shards, (keep,))
    half_qkv = add((keep, layout.across_cores(join([send], (plane[0],)))), layout.planes)
    plane_qkv = add([half_qkv[0]] + layout.across_plane(half_qkv), layout.shards)
    own_early = layout.across_rest(add([plane[0]] + layout.along_shards(plane), 1, (plane_qkv[0],))[0])
    own_qkv = [plane_qkv[0]] + layout.along_shards(plane_qkv)
    if layout.parts < layout.batch:
        own_qkv = [layout.across_rest(add(own_qkv)[0])]
    own_qkv = add_squares(own_qkv, (own_early,))
    all_early = join([own_early] + layout.across_plane([own_early]), (own_qkv,))
    all_qkv = join([own_qkv] + layout.across_plane([own_qkv]))
    grads = [(t, layout.across_cores(t)) for t in (all_early, all_qkv)]
    spans = [
        [(0, 4 * width, 2 * hidden), (2 * hidden, 3 * width, width)],
        [(0, 0, 3 * width)],
    ]
    share = shard_squares(layout, place, *grads[1])
    updated = adam(layout, place, [share] + layout.along_shards([share]), spans, grads, weights, first_moments, second_moments, vectors, vector_first, vector_second)
    grad_w, new_weights, new_first, new_second, grad_v, new_vectors, new_vector_first, new_vector_second, grad_norm = updated
    grad_norm = grad_norm.reshape(())
    return (
        outputs[None],
        input_grad[None],
        grad_w,
        grad_v,
        grad_norm,
        new_weights,
        new_first,
        new_second,
        new_vectors,
        new_vector_first,
        new_vector_second,
    )


def solution(mesh):
    rows = ("batch", "shard")
    placed = (
        P(rows, None, None),
        P(rows, None, None),
        P(rows),
        P(rows, None),
        P(rows, None),
        P("shard", None),
        P("shard", None),
        P("shard", None),
        P(None, "shard"),
        P(None, "shard"),
        P(None, "shard"),
    )
    return jax.shard_map(
        functools.partial(on_device, Layout(mesh.shape["batch"], mesh.shape["shard"], D)),
        mesh=mesh,
        in_specs=placed,
        out_specs=(
            P(rows, None, None),
            P(rows, None, None),
            P("shard", None),
            P(None, "shard"),
            P(),
            P("shard", None),
            P("shard", None),
            P("shard", None),
            P(None, "shard"),
            P(None, "shard"),
            P(None, "shard"),
        ),
        check_vma=False,
    )
```

```python
import functools
import math

import jax
import jax.numpy as jnp
from jax import lax
from jax.experimental import pallas as pl
from jax.experimental.pallas import tpu as pltpu
from jax.sharding import PartitionSpec as P

D = 512
FF = 2048
HEADS = 8
HEAD_DIM = 64
STEP = 10
WCOLS = 6144

NORM_EPS = 1e-05
BETA_ONE = 0.5
BETA_TWO = 0.5
ADAM_EPS = 1e-08
DECAY = 0.01
WARMUP = 4000.0
RATE_SCALE = 150000.0

BF = jnp.bfloat16
F32 = jnp.float32
FAR = 1e30
SAFE_SCORE = 60.0
TILE = 256
WIDE_TILE = 512
LANES = 128
SQUARES_AT = 12
COST_SCALE = 100


def params(mebibytes=50):
    return pltpu.CompilerParams(vmem_limit_bytes=mebibytes << 20)


def cost(flops, bytes_accessed, transcendentals=0):
    return pl.CostEstimate(flops=int(flops) // COST_SCALE, bytes_accessed=int(bytes_accessed) // COST_SCALE, transcendentals=int(transcendentals) // COST_SCALE)


def dg(left, right, left_dim, right_dim):
    return lax.dot_general(
        left, right, (((left_dim,), (right_dim,)), ((), ())), preferred_element_type=F32
    )


def whole(shape):
    return pl.BlockSpec(shape, lambda i: (0,) * len(shape))


def adam_update(master, moment_one, moment_two, gradient):
    moment_one = BETA_ONE * moment_one + (1.0 - BETA_ONE) * gradient
    moment_two = BETA_TWO * moment_two + (1.0 - BETA_TWO) * gradient * gradient
    step_rate = RATE_SCALE * D ** (-0.5) * min(STEP ** (-0.5), STEP * WARMUP ** (-1.5))
    fixed_first = moment_one / (1.0 - BETA_ONE**STEP)
    fixed_second = moment_two / (1.0 - BETA_TWO**STEP)
    master = master - step_rate * (
        fixed_first / (jnp.sqrt(fixed_second) + ADAM_EPS) + DECAY * master
    )
    return (master, moment_one, moment_two)


def attend_kernel(act_ref, wq_ref, wk_ref, wv_ref, col_ref, kmask_ref, qmask_ref, e_ref, ctx_ref, qkv_ref, stat_ref):
    act = act_ref[...]
    tokens = act.shape[1]
    q = (dg(wq_ref[...], act, 0, 0) + col_ref[:, 4:5].astype(F32)).astype(BF) * jnp.asarray(HEAD_DIM**-0.5, BF)
    k = dg(wk_ref[...], act, 0, 0).astype(BF)
    v = (dg(wv_ref[...], act, 0, 0) + col_ref[:, 5:6].astype(F32)).astype(BF)
    qkv_ref[0] = q
    qkv_ref[1] = k
    qkv_ref[2] = v
    dead = kmask_ref[4:5, :].astype(F32)
    bound = jnp.zeros((1, 1), F32)
    selves = []
    for h in range(2):
        rows = slice(h * HEAD_DIM, (h + 1) * HEAD_DIM)
        qf, kf = q[rows].astype(F32), k[rows].astype(F32)
        selves.append(jnp.sum(qf * kf, axis=0, keepdims=True))
        q_top = jnp.max(jnp.sum(qf * qf, axis=0, keepdims=True), axis=1, keepdims=True)
        k_top = jnp.max(jnp.sum(kf * kf, axis=0, keepdims=True), axis=1, keepdims=True)
        bound = jnp.maximum(bound, q_top * k_top)
    safe = bound[0, 0] <= SAFE_SCORE * SAFE_SCORE

    def scores(h):
        rows = slice(h * HEAD_DIM, (h + 1) * HEAD_DIM)
        keys = jnp.concatenate([k[rows], kmask_ref[...]], axis=0).T
        queries = jnp.concatenate([q[rows], qmask_ref[...]], axis=0)
        return dg(keys, queries, 1, 0)

    def finish(h, e, e_self):
        rows = slice(h * HEAD_DIM, (h + 1) * HEAD_DIM)
        low_e = e.astype(BF)
        e_ref[h] = low_e
        total = jnp.sum(e, axis=0, keepdims=True) + e_self
        scale = 1.0 / total
        values = v[rows]
        mixed = dg(values, low_e, 1, 0) + values.astype(F32) * e_self.astype(BF).astype(F32)
        ctx_ref[rows, :] = (mixed * scale).astype(BF)
        stat_ref[h, 0:1, :] = scale
        stat_ref[h, 1:2, :] = e_self

    @pl.when(safe)
    def _():
        for h in range(2):
            finish(h, jnp.exp(scores(h)), jnp.exp(selves[h]) * dead)

    @pl.when(jnp.logical_not(safe))
    def _():
        for h in range(2):
            s = scores(h)
            own = jnp.where(dead > 0, selves[h], -FAR)
            top = jnp.maximum(jnp.max(s, axis=0, keepdims=True), own)
            finish(h, jnp.exp(s - top), jnp.exp(own - top) * dead)


def attend(act, w_qkv, kmask, qmask):
    width, tokens = act.shape
    pairs = width // (2 * HEAD_DIM)
    pair = 2 * HEAD_DIM
    heads = width // HEAD_DIM
    return pl.pallas_call(
        attend_kernel,
        name="attend",
        grid=(pairs,),
        in_specs=[
            whole((width, tokens)),
            pl.BlockSpec((width, pair), lambda i: (0, i)),
            pl.BlockSpec((width, pair), lambda i: (0, pairs + i)),
            pl.BlockSpec((width, pair), lambda i: (0, 2 * pairs + i)),
            pl.BlockSpec((pair, pair), lambda i: (i, 3 * pairs)),
            whole((16, tokens)),
            whole((16, tokens)),
        ],
        out_specs=[
            pl.BlockSpec((2, tokens, tokens), lambda i: (i, 0, 0)),
            pl.BlockSpec((pair, tokens), lambda i: (i, 0)),
            pl.BlockSpec((3, pair, tokens), lambda i: (0, i, 0)),
            pl.BlockSpec((2, 2, tokens), lambda i: (i, 0, 0)),
        ],
        out_shape=[
            jax.ShapeDtypeStruct((heads, tokens, tokens), BF),
            jax.ShapeDtypeStruct((width, tokens), BF),
            jax.ShapeDtypeStruct((3, width, tokens), BF),
            jax.ShapeDtypeStruct((heads, 2, tokens), F32),
        ],
        compiler_params=params(),
        cost_estimate=cost(6 * width * width * tokens + 4 * width * tokens * tokens, 2 * heads * tokens * tokens, heads * tokens * tokens),
    )(act, w_qkv, w_qkv, w_qkv, w_qkv, kmask, qmask)


def attend_back_pair(e_ref, qkv_ref, stat_ref, grad_ref, inner_ref, out_ref, ds_ref):
    for h in range(2):
        rows = slice(h * HEAD_DIM, (h + 1) * HEAD_DIM)
        q, k, v = qkv_ref[0, rows], qkv_ref[1, rows], qkv_ref[2, rows]
        grad = grad_ref[rows]
        inner = inner_ref[h]
        e_self = stat_ref[h, 1:2, :]
        grad_f = grad.astype(F32)
        ds = (e_ref[h].astype(F32) * (dg(v.T, grad, 1, 0) - inner)).astype(BF)
        ds_ref[h] = ds
        own = (e_self * (jnp.sum(grad_f * v.astype(F32), axis=0, keepdims=True) - inner)).astype(BF).astype(F32)
        scale = HEAD_DIM**-0.5
        out_ref[0, rows] = ((dg(k, ds, 1, 0) + k.astype(F32) * own) * scale).astype(BF)
        out_ref[2, rows] = (dg(e_ref[h], grad, 1, 1).T + grad_f * e_self.astype(BF).astype(F32)).astype(BF)
        out_ref[1, rows] = (dg(ds_ref[h], q, 1, 1).T + q.astype(F32) * own).astype(BF)


def attend_back(e, qkv, stat, grad, inner, start=0, pairs=None):
    heads, tokens, _ = e.shape
    width = grad.shape[0]
    pair = 2 * HEAD_DIM
    pairs = pairs or heads // 2
    return pl.pallas_call(
        attend_back_pair,
        name="attend_back",
        grid=(pairs,),
        in_specs=[
            pl.BlockSpec((2, tokens, tokens), lambda i: (start + i, 0, 0)),
            pl.BlockSpec((3, pair, tokens), lambda i: (0, start + i, 0)),
            pl.BlockSpec((2, 2, tokens), lambda i: (start + i, 0, 0)),
            pl.BlockSpec((pair, tokens), lambda i: (start + i, 0)),
            pl.BlockSpec((2, 1, tokens), lambda i: (start + i, 0, 0)),
        ],
        out_specs=pl.BlockSpec((3, pair, tokens), lambda i: (0, i, 0)),
        out_shape=jax.ShapeDtypeStruct((3, pairs * pair, tokens), BF),
        scratch_shapes=[pltpu.VMEM((2, tokens, tokens), BF)],
        compiler_params=params(63),
        cost_estimate=cost(8 * pairs * pair * tokens * tokens, 4 * pairs * tokens * tokens),
    )(e, qkv, stat, grad, inner)


def normed(t):
    mean = jnp.mean(t, axis=0, keepdims=True)
    centred = t - mean
    rstd = lax.rsqrt(jnp.mean(centred * centred, axis=0, keepdims=True) + NORM_EPS)
    return centred * rstd, rstd


def normed_back(grad, unit, rstd, gain):
    scaled = grad * gain
    mean = jnp.mean(scaled, axis=0, keepdims=True)
    along = jnp.mean(scaled * unit, axis=0, keepdims=True)
    return rstd * (scaled - mean - unit * along)


def gelu_and_slope(t):
    square = t * t
    inside = jnp.tanh(t * (0.7978845608028654 + (0.7978845608028654 * 0.044715) * square))
    half = 0.5 + 0.5 * inside
    slope = half + (t * (0.5 - 0.5 * inside * inside)) * (
        0.7978845608028654 + (3.0 * 0.7978845608028654 * 0.044715) * square
    )
    return t * half, slope


def lanes_sum(t):
    out = t[:, 0:128]
    for j in range(128, t.shape[1], 128):
        out = out + t[:, j : j + 128]
    return out


def column(col_ref, j):
    return col_ref[:, j : j + 1].astype(F32)


def dense_forward(signal, ctx, rest_ref, col_ref, act_ref, slope_ref):
    wo_ref, win_ref, wback_ref = parts_of(rest_ref)
    joined = signal + dg(wo_ref[...], ctx, 0, 0) + column(col_ref, 6)
    unit_one, rstd_one = normed(joined)
    middle = unit_one * column(col_ref, 0) + column(col_ref, 1)
    low_middle = middle.astype(BF)
    width = middle.shape[0]
    summed = middle + column(col_ref, 7)
    for c in range(win_ref.shape[1] // width):
        rows = slice(c * width, (c + 1) * width)
        pre = dg(win_ref[:, rows], low_middle, 0, 0) + column(col_ref, 8 + c)
        gelu, slope = gelu_and_slope(pre)
        act = gelu.astype(BF)
        act_ref[rows, :] = act
        slope_ref[rows, :] = slope.astype(slope_ref.dtype)
        summed = summed + dg(wback_ref[:, rows], act, 1, 0)
    unit_two, rstd_two = normed(summed)
    return unit_one, rstd_one, low_middle, unit_two, rstd_two


def dense_back(grad, unit_one, rstd_one, slope_ref, unit_two, rstd_two, ctx, stat_ref, rest_ref, col_ref,
               sums_ref, joined_ref, gctx_ref, inner_ref, dz_ref, du_ref, dattn_ref):
    wo_ref, win_ref, wback_ref = parts_of(rest_ref)
    sums_ref[2] += lanes_sum(grad * unit_two)
    sums_ref[3] += lanes_sum(grad)
    grad_summed = normed_back(grad, unit_two, rstd_two, column(col_ref, 2))
    dz = grad_summed.astype(BF)
    dz_ref[...] = dz
    sums_ref[7] += lanes_sum(dz.astype(F32))
    width = dz.shape[0]
    grad_middle = grad_summed
    for c in range(win_ref.shape[1] // width):
        rows = slice(c * width, (c + 1) * width)
        du = (dg(wback_ref[:, rows], dz, 0, 0) * slope_ref[rows, :].astype(F32)).astype(BF)
        du_ref[rows, :] = du
        sums_ref[8 + c] += lanes_sum(du.astype(F32))
        grad_middle = grad_middle + dg(win_ref[:, rows], du, 1, 0)
    sums_ref[0] += lanes_sum(grad_middle * unit_one)
    sums_ref[1] += lanes_sum(grad_middle)
    grad_joined = normed_back(grad_middle, unit_one, rstd_one, column(col_ref, 0))
    joined_ref[...] = grad_joined
    dattn = grad_joined.astype(BF)
    dattn_ref[...] = dattn
    sums_ref[6] += lanes_sum(dattn.astype(F32))
    grad_ctx = dg(wo_ref[...], dattn, 1, 0)
    for h in range(stat_ref.shape[0]):
        rows = slice(h * HEAD_DIM, (h + 1) * HEAD_DIM)
        part = (grad_ctx[rows] * stat_ref[h, 0:1, :]).astype(BF)
        gctx_ref[rows, :] = part
        inner_ref[h] = jnp.sum(part.astype(F32) * ctx[rows].astype(F32), axis=0, keepdims=True)


def always(i):
    return i


def tile(rows, at=always, size=TILE):
    return pl.BlockSpec((rows, size), lambda i: (0, at(i)))


def heads_tile(heads, rows, at=always, size=TILE):
    return pl.BlockSpec((heads, rows, size), lambda i: (0, 0, at(i)))


def once(shape, *at):
    at = at or (0,) * len(shape)
    return pl.BlockSpec(shape, lambda i: at, pipeline_mode=pl.Buffered(1))


def span(step, size):
    return pl.ds(pl.multiple_of(step * size, size), size)


def rest_spec(w_rest):
    return pl.BlockSpec(w_rest.shape, lambda i: (0, 0), pipeline_mode=pl.Buffered(1))


def parts_of(rest_ref):
    width = rest_ref.shape[0]
    hidden = (rest_ref.shape[1] - width) // 2
    return rest_ref.at[:, 0:width], rest_ref.at[:, width : width + hidden], rest_ref.at[:, width + hidden :]


def column_spec(width):
    return pl.BlockSpec((width, LANES), lambda i: (0, 3 * width // LANES))


def first_dense_kernel(signal_ref, ctx_ref, rest_ref, col_ref,
                       unit_one_ref, unit_two_ref, rstd_ref, low_out_ref, act_ref, slope_ref):
    unit_one, rstd_one, _, unit_two, rstd_two = dense_forward(
        signal_ref[...].astype(F32), ctx_ref[...], rest_ref, col_ref, act_ref, slope_ref)
    unit_one_ref[...] = unit_one
    unit_two_ref[...] = unit_two
    rstd_ref[0:1, :] = rstd_one
    rstd_ref[1:2, :] = rstd_two
    low_out_ref[...] = (unit_two * column(col_ref, 2) + column(col_ref, 3)).astype(BF)


def first_half_kernel(layout, tiles, place_ref, own_ref, mine_ref, theirs_ref, signal_ref, ctx_ref, w_ref, kmask_ref, qmask_ref,
                      rest_ref, unit_one_ref, unit_two_ref, rstd_ref, low_ref, act_ref, slope_ref, e_ref, ctx_out_ref, qkv_ref, stat_ref, hold_ref):
    step = pl.program_id(0)
    width = ctx_ref.shape[0]
    pair = ctx_out_ref.shape[0]

    @pl.when(step == 0)
    def _():
        put_blocks(layout, place_ref, (mine_ref, theirs_ref), rest_ref)
        rest_ref[own_rows(layout, place_ref), :] = own_ref[:, own_ref.shape[1] - rest_ref.shape[1] :].astype(BF)

    @pl.when(step < tiles)
    def _():
        first_dense_kernel(signal_ref, ctx_ref, rest_ref, w_ref.at[:, 3 * width :], unit_one_ref, unit_two_ref, rstd_ref, low_ref, act_ref, slope_ref)
        hold_ref[:, span(step, TILE)] = low_ref[...]

    @pl.when(step >= tiles)
    def _():
        at = step - tiles
        pairs = width // pair
        attend_kernel(
            hold_ref,
            w_ref.at[:, span(at, pair)],
            w_ref.at[:, span(at + pairs, pair)],
            w_ref.at[:, span(at + 2 * pairs, pair)],
            w_ref.at[span(at, pair), 3 * width :],
            kmask_ref, qmask_ref, e_ref, ctx_out_ref, qkv_ref, stat_ref)


def first_half(layout, place, weights, mine, theirs, signal, ctx, w_first, kmask, qmask):
    width, tokens = signal.shape
    total = mine.shape[1]
    hidden = (total - width) // 2
    pair = 2 * HEAD_DIM
    pairs, heads = width // pair, width // HEAD_DIM
    tiles = tokens // TILE

    def at_tile(i):
        return jnp.minimum(i, tiles - 1)

    def at_pair(i):
        return jnp.maximum(i - tiles, 0)

    return pl.pallas_call(
        functools.partial(first_half_kernel, layout, tiles),
        name="first_half",
        grid=(tiles + pairs,),
        in_specs=[pl.BlockSpec(memory_space=pltpu.SMEM), once(weights.shape), once(mine.shape), once(theirs.shape),
                  tile(width, at_tile), tile(width, at_tile), once(w_first.shape), once(kmask.shape), once(qmask.shape)],
        out_specs=[whole((width, total)), tile(width, at_tile), tile(width, at_tile), tile(8, at_tile), tile(width, at_tile), tile(hidden, at_tile), tile(hidden, at_tile),
                   pl.BlockSpec((2, tokens, tokens), lambda i: (at_pair(i), 0, 0)),
                   pl.BlockSpec((pair, tokens), lambda i: (at_pair(i), 0)),
                   pl.BlockSpec((3, pair, tokens), lambda i: (0, at_pair(i), 0)),
                   pl.BlockSpec((2, 2, tokens), lambda i: (at_pair(i), 0, 0))],
        out_shape=[
            jax.ShapeDtypeStruct((width, total), BF),
            jax.ShapeDtypeStruct((width, tokens), F32),
            jax.ShapeDtypeStruct((width, tokens), F32),
            jax.ShapeDtypeStruct((8, tokens), F32),
            jax.ShapeDtypeStruct((width, tokens), BF),
            jax.ShapeDtypeStruct((hidden, tokens), BF),
            jax.ShapeDtypeStruct((hidden, tokens), BF),
            jax.ShapeDtypeStruct((heads, tokens, tokens), BF),
            jax.ShapeDtypeStruct((width, tokens), BF),
            jax.ShapeDtypeStruct((3, width, tokens), BF),
            jax.ShapeDtypeStruct((heads, 2, tokens), F32),
        ],
        scratch_shapes=[pltpu.VMEM((width, tokens), BF)],
        compiler_params=params(63),
        cost_estimate=cost(2 * tokens * width * (width + 2 * hidden), 24 << 20, tokens * hidden),
    )(place, weights, mine, theirs, signal, ctx, w_first, kmask, qmask)


def second_dense_kernel(unit_ref, ctx_ref, cot_ref, stat_ref, rest_ref, col_ref,
                        out_ref, sums_ref, joined_ref, gctx_ref, inner_ref, mid_ref, act_ref, dz_ref, du_ref, dattn_ref, slope_ref):
    @pl.when(pl.program_id(0) == 0)
    def _():
        sums_ref[...] = jnp.zeros(sums_ref.shape, F32)

    ctx = ctx_ref[...]
    gain, shift = column(col_ref, 2), column(col_ref, 3)
    unit_one, rstd_one, low_middle, unit_two, rstd_two = dense_forward(
        unit_ref[...] * gain + shift, ctx, rest_ref, col_ref, act_ref, slope_ref)
    mid_ref[...] = low_middle
    out_ref[...] = (unit_two * gain + shift).astype(BF).T
    dense_back(cot_ref[...].astype(F32), unit_one, rstd_one, slope_ref, unit_two, rstd_two, ctx, stat_ref,
               rest_ref, col_ref, sums_ref, joined_ref, gctx_ref, inner_ref, dz_ref, du_ref, dattn_ref)


def second_half_kernel(tiles, unit_ref, ctx_ref, cot_ref, stat_ref, rest_ref, col_ref, e_ref, qkv_ref, pair_stat_ref,
                       out_ref, sums_ref, joined_ref, mid_ref, act_ref, dz_ref, du_ref, dattn_ref, dqkv_ref, slope_ref, gctx_ref, inner_ref, ds_ref):
    step = pl.program_id(0)

    @pl.when(step < tiles)
    def _():
        at = span(step, WIDE_TILE)
        second_dense_kernel(unit_ref, ctx_ref, cot_ref, stat_ref, rest_ref, col_ref, out_ref, sums_ref, joined_ref,
                            gctx_ref.at[:, at], inner_ref.at[:, :, at], mid_ref, act_ref, dz_ref, du_ref, dattn_ref, slope_ref)

    @pl.when(step >= tiles)
    def _():
        pair = dqkv_ref.shape[1]
        attend_back_pair(e_ref, qkv_ref, pair_stat_ref, gctx_ref.at[span(step - tiles, pair)], inner_ref.at[pl.ds(2 * (step - tiles), 2)], dqkv_ref, ds_ref)


def second_half(unit, ctx, cot, stat, w_rest, w_first, e, qkv):
    width, tokens = unit.shape
    hidden = (w_rest.shape[1] - width) // 2
    heads = stat.shape[0]
    pair = 2 * HEAD_DIM
    pairs = width // pair
    tiles = tokens // WIDE_TILE

    def at_tile(i):
        return jnp.minimum(i, tiles - 1)

    def at_pair(i):
        return jnp.maximum(i - tiles, 0)

    return pl.pallas_call(
        functools.partial(second_half_kernel, tiles),
        name="second_half",
        grid=(tiles + pairs,),
        in_specs=[tile(width, at_tile, WIDE_TILE), tile(width, at_tile, WIDE_TILE), tile(width, at_tile, WIDE_TILE), heads_tile(heads, 2, at_tile, WIDE_TILE), once(w_rest.shape), column_spec(width),
                  pl.BlockSpec((2, tokens, tokens), lambda i: (at_pair(i), 0, 0)),
                  pl.BlockSpec((3, pair, tokens), lambda i: (0, at_pair(i), 0)),
                  pl.BlockSpec((2, 2, tokens), lambda i: (at_pair(i), 0, 0))],
        out_specs=[pl.BlockSpec((WIDE_TILE, width), lambda i: (at_tile(i), 0)), once((12, width, LANES)), tile(width, at_tile, WIDE_TILE),
                   tile(width, at_tile, WIDE_TILE), tile(hidden, at_tile, WIDE_TILE), tile(width, at_tile, WIDE_TILE), tile(hidden, at_tile, WIDE_TILE), tile(width, at_tile, WIDE_TILE),
                   pl.BlockSpec((3, pair, tokens), lambda i: (0, at_pair(i), 0))],
        out_shape=[
            jax.ShapeDtypeStruct((tokens, width), BF),
            jax.ShapeDtypeStruct((12, width, LANES), F32),
            jax.ShapeDtypeStruct((width, tokens), F32),
            jax.ShapeDtypeStruct((width, tokens), BF),
            jax.ShapeDtypeStruct((hidden, tokens), BF),
            jax.ShapeDtypeStruct((width, tokens), BF),
            jax.ShapeDtypeStruct((hidden, tokens), BF),
            jax.ShapeDtypeStruct((width, tokens), BF),
            jax.ShapeDtypeStruct((3, width, tokens), BF),
        ],
        scratch_shapes=[pltpu.VMEM((hidden, WIDE_TILE), F32), pltpu.VMEM((width, tokens), BF), pltpu.VMEM((heads, 1, tokens), F32), pltpu.VMEM((2, tokens, tokens), BF)],
        compiler_params=params(63),
        cost_estimate=cost(4 * tokens * width * (width + 2 * hidden), 28 << 20, tokens * hidden),
    )(unit, ctx, cot, stat, w_rest, w_first, e, qkv, stat)


def first_back_kernel(prior_ref, dqkv_ref, unit_one_ref, unit_two_ref, rstd_ref, slope_ref, ctx_ref, stat_ref,
                      wqkv_ref, rest_ref, col_ref,
                      vec_ref, joined_ref, gctx_ref, inner_ref, mid_ref, dz_ref, du_ref, dattn_ref, sums_ref, step, tiles):

    unit_one = unit_one_ref[...]
    mid_ref[...] = (unit_one * column(col_ref, 0) + column(col_ref, 1)).astype(BF)
    grad = prior_ref[...] + dg(wqkv_ref[...], dqkv_ref[...], 1, 0)
    dense_back(grad, unit_one, rstd_ref[0:1, :], slope_ref, unit_two_ref[...], rstd_ref[1:2, :], ctx_ref[...], stat_ref,
               rest_ref, col_ref, sums_ref, joined_ref, gctx_ref, inner_ref, dz_ref, du_ref, dattn_ref)

    @pl.when(step == tiles - 1)
    def _():
        lane = lax.broadcasted_iota(jnp.int32, vec_ref.shape, 1)
        out = jnp.zeros(vec_ref.shape, F32)
        for j in (0, 1, 2, 3, 6, 7, 8, 9, 10, 11):
            out = jnp.where(lane == j, jnp.sum(sums_ref[j], axis=1, keepdims=True), out)
        vec_ref[...] = out


class Layout:
    def __init__(self, mesh_batch, mesh_shard, width):
        self.batch = mesh_batch
        self.shards = mesh_shard
        self.parts = min(mesh_batch, width // mesh_shard // 16)
        self.planes = self.parts // 2
        self.rows = width // mesh_shard // self.parts

    def swap(self, value, axis, distance):
        size = self.batch if axis == "batch" else self.shards
        return lax.ppermute(value, axis, [(i, i ^ distance) for i in range(size)])

    def place(self):
        return jnp.stack([lax.axis_index("batch") % self.parts, lax.axis_index("shard")]).astype(jnp.int32)

    def row_of(self, place_ref, c, e, d):
        block = (place_ref[1] ^ d) * self.parts + (place_ref[0] ^ (2 * e + c))
        return pl.multiple_of(block * self.rows, self.rows)

    def along_shards(self, blocks):
        return [self.swap(blocks[d % len(blocks)], "shard", d) for d in range(1, self.shards)]

    def across_plane(self, blocks):
        return [self.swap(blocks[e % len(blocks)], "batch", 2 * e) for e in range(1, self.planes)]

    def across_cores(self, block):
        return self.swap(block, "batch", 1)

    def across_rest(self, own):
        distance = self.parts
        while distance < self.batch:
            own = add([own, self.swap(own, "batch", distance)])[0]
            distance *= 2
        return own


def tree(values):
    while len(values) > 1:
        values = [a + b for a, b in zip(values[::2], values[1::2], strict=True)]
    return values[0]


def whole_specs(values, tokens_in=()):
    return [whole(v.shape) for v in values] + [pl.BlockSpec(memory_space=pl.ANY)] * len(tokens_in)


def join_kernel(count, *refs):
    out_ref = refs[-1]
    at = 0
    for source in refs[:count]:
        out_ref[at : at + source.shape[0], :] = source[...]
        at += source.shape[0]


def join(blocks, tokens_in=()):
    rows, columns = sum(b.shape[0] for b in blocks), blocks[0].shape[1]
    return pl.pallas_call(
        functools.partial(join_kernel, len(blocks)),
        name="join",
        grid=(1,),
        in_specs=whole_specs(blocks, tokens_in),
        out_specs=whole((rows, columns)),
        out_shape=jax.ShapeDtypeStruct((rows, columns), BF),
        compiler_params=params(),
        cost_estimate=cost(0, 4 * rows * columns),
    )(*blocks, *tokens_in)


def add_kernel(count, outs, *refs):
    total = refs[0][...].astype(F32)
    for other in refs[1:count]:
        total = total + other[...].astype(F32)
    total = total.astype(BF)
    rows = refs[-1].shape[0]
    for i in range(outs):
        refs[i - outs][...] = total[i * rows : (i + 1) * rows]


def add(values, outs=1, tokens_in=()):
    rows, columns = values[0].shape
    part = jax.ShapeDtypeStruct((rows // outs, columns), BF)
    return pl.pallas_call(
        functools.partial(add_kernel, len(values), outs),
        name="add",
        grid=(1,),
        in_specs=whole_specs(values, tokens_in),
        out_specs=[whole(part.shape)] * outs,
        out_shape=[part] * outs,
        compiler_params=params(),
        cost_estimate=cost(len(values) * rows * columns, 2 * (len(values) + 1) * rows * columns),
    )(*values, *tokens_in)


def add_squares_kernel(count, others, *refs):
    out_ref = refs[-1]
    total = refs[0][...].astype(F32)
    for other in refs[1:count]:
        total = total + other[...].astype(F32)
    total = total.astype(BF)
    squares = jnp.sum(jnp.square(total.astype(F32)), keepdims=True)
    for other in refs[count : count + others]:
        squares = squares + jnp.sum(jnp.square(other[...].astype(F32)), keepdims=True)
    out_ref[...] = total
    high = squares.astype(BF)
    middle = (squares - high.astype(F32)).astype(BF)
    low = (squares - high.astype(F32) - middle.astype(F32)).astype(BF)
    used = total.shape[1] - LANES
    tail = total[:, used:]
    lane = lax.broadcasted_iota(jnp.int32, tail.shape, 1)
    for i, piece in enumerate((high, middle, low)):
        tail = jnp.where(lane == SQUARES_AT + i, piece.astype(F32), tail.astype(F32)).astype(BF)
    out_ref[:, used:] = tail


def add_squares(values, others):
    rows, columns = values[0].shape
    return pl.pallas_call(
        functools.partial(add_squares_kernel, len(values), len(others)),
        name="add_squares",
        grid=(1,),
        in_specs=whole_specs(list(values) + list(others)),
        out_specs=whole((rows, columns)),
        out_shape=jax.ShapeDtypeStruct((rows, columns), BF),
        compiler_params=params(),
        cost_estimate=cost(len(values) * rows * columns, 2 * (len(values) + 1) * rows * columns),
    )(*values, *others)


def shard_squares_kernel(layout, place_ref, mine_ref, theirs_ref, out_ref):
    used = mine_ref.shape[1] - LANES
    total = jnp.zeros((1, LANES), F32)
    lane = lax.broadcasted_iota(jnp.int32, (1, LANES), 1)
    riding = (lane >= SQUARES_AT) & (lane < SQUARES_AT + 3)
    for part in range(layout.parts):
        away = place_ref[0] ^ part
        at = pl.ds(pl.multiple_of((away >> 1) * layout.rows, layout.rows), layout.rows)
        mine = mine_ref[at, used:].astype(F32)[0:1]
        theirs = theirs_ref[at, used:].astype(F32)[0:1]
        total = total + jnp.where((away & 1) == 0, mine, theirs)
    total = jnp.sum(jnp.where(riding, total, 0.0), axis=1, keepdims=True)
    out_ref[...] = jnp.broadcast_to(total, out_ref.shape)


def shard_squares(layout, place, mine, theirs):
    return pl.pallas_call(
        functools.partial(shard_squares_kernel, layout),
        name="shard_squares",
        grid=(1,),
        in_specs=[pl.BlockSpec(memory_space=pltpu.SMEM)] + whole_specs((mine, theirs)),
        out_specs=whole((8, LANES)),
        out_shape=jax.ShapeDtypeStruct((8, LANES), F32),
        compiler_params=params(),
        cost_estimate=cost(0, 4 * mine.size),
    )(place, mine, theirs)


def pick_first_kernel(place_ref, w_ref, vec_ref, out_ref, columns_ref, hold_ref):
    hold_ref[...] = jnp.zeros(hold_ref.shape, F32)
    hold_ref[0 : vec_ref.shape[0], 0 : vec_ref.shape[1]] = vec_ref[...]
    hold_ref[...] = hold_ref[...].T
    columns_ref[...] = hold_ref[0 : columns_ref.shape[0], :].astype(BF)
    used = w_ref.shape[1]
    rows = out_ref.shape[0]
    out_ref[:, 0:used] = w_ref[...].astype(BF)
    out_ref[:, used:] = hold_ref[pl.ds(pl.multiple_of(place_ref[0] * rows, rows), rows), :].astype(BF)


def pick_first(layout, place, weights, vectors):
    shard_rows, columns = weights.shape
    used = columns // 4
    return pl.pallas_call(
        pick_first_kernel,
        name="pick_first",
        grid_spec=pltpu.PrefetchScalarGridSpec(
            num_scalar_prefetch=1,
            grid=(1,),
            in_specs=[pl.BlockSpec((layout.rows, used), lambda i, place: (place[0], 0)), pl.BlockSpec(vectors.shape, lambda i, place: (0, 0))],
            out_specs=[pl.BlockSpec((layout.rows, used + LANES), lambda i, place: (0, 0)), pl.BlockSpec((shard_rows, LANES), lambda i, place: (0, 0))],
            scratch_shapes=[pltpu.VMEM((LANES, LANES), F32)],
        ),
        out_shape=[jax.ShapeDtypeStruct((layout.rows, used + LANES), BF), jax.ShapeDtypeStruct((shard_rows, LANES), BF)],
        compiler_params=params(),
        cost_estimate=cost(0, 6 * layout.rows * columns),
    )(place, weights, vectors)


def pick_rest_kernel(place_ref, w_ref, *refs):
    out_ref = refs[-1]
    out_ref[...] = w_ref[:, w_ref.shape[1] - out_ref.shape[1] :].astype(BF)


def pick_rest(layout, place, weights, tokens_in):
    columns = weights.shape[1]
    return pl.pallas_call(
        pick_rest_kernel,
        name="pick_rest",
        grid_spec=pltpu.PrefetchScalarGridSpec(
            num_scalar_prefetch=1,
            grid=(1,),
            in_specs=[pl.BlockSpec((layout.rows, columns), lambda i, place: (place[0], 0))] + [pl.BlockSpec(memory_space=pl.ANY)] * len(tokens_in),
            out_specs=pl.BlockSpec((layout.rows, 3 * columns // 4), lambda i, place: (0, 0)),
        ),
        out_shape=jax.ShapeDtypeStruct((layout.rows, 3 * columns // 4), BF),
        compiler_params=params(),
        cost_estimate=cost(0, 6 * layout.rows * columns),
    )(place, weights, *tokens_in)


def put_blocks(layout, place_ref, sources, out_ref):
    for c, source in enumerate(sources):
        for e in range(layout.planes):
            for d in range(1, layout.shards):
                at = (e * (layout.shards - 1) + d - 1) * layout.rows
                out_ref[pl.ds(layout.row_of(place_ref, c, e, d), layout.rows), :] = source[at : at + layout.rows, :]


def own_rows(layout, place_ref):
    rows = layout.rows * layout.parts
    return pl.ds(pl.multiple_of(place_ref[1] * rows, rows), rows)


def collect_first_kernel(layout, place_ref, w_ref, columns_ref, mine_ref, theirs_ref, out_ref):
    put_blocks(layout, place_ref, (mine_ref, theirs_ref), out_ref)
    rows = own_rows(layout, place_ref)
    used = w_ref.shape[1]
    out_ref[rows, 0:used] = w_ref[...].astype(BF)
    out_ref[rows, used:] = columns_ref[...]


def collect_first(layout, place, weights, columns, mine, theirs):
    shard_rows, all_columns = weights.shape
    rows = shard_rows * layout.shards
    total = mine.shape[1]
    return pl.pallas_call(
        functools.partial(collect_first_kernel, layout),
        name="collect_first",
        grid=(1,),
        in_specs=[pl.BlockSpec(memory_space=pltpu.SMEM), pl.BlockSpec((shard_rows, all_columns // 4), lambda i: (0, 0))] + whole_specs((columns, mine, theirs)),
        out_specs=whole((rows, total)),
        out_shape=jax.ShapeDtypeStruct((rows, total), BF),
        compiler_params=params(),
        cost_estimate=cost(0, 4 * rows * total),
    )(place, weights, columns, mine, theirs)


def in_order(layout, place_ref, source_ref, target_ref):
    at = 0
    for c in range(2):
        for e in range(layout.planes):
            for d in range(layout.shards):
                target_ref[at : at + layout.rows] = source_ref[pl.ds(layout.row_of(place_ref, c, e, d), layout.rows), :]
                at += layout.rows


def weight_step(left_ref, ra_ref, rb_ref, keep_ref, send_ref):
    out = (dg(left_ref[0], ra_ref[...], 1, 1) + dg(left_ref[1], rb_ref[...], 1, 1)).astype(BF)
    half = out.shape[0] // 2
    keep_ref[...] = out[:half]
    send_ref[...] = out[half:]


def turn_kernel(layout, tiles, place_ref, prior_ref, dqkv_ref, unit_one_ref, unit_two_ref, rstd_ref, slope_ref, ctx_ref, stat_ref, sums_in_ref,
                wqkv_ref, rest_ref, col_ref, du_two_ref, hid_one_ref, hid_two_ref, mid_two_ref, dz_two_ref, ctx_one_ref, ctx_two_ref, dattn_two_ref,
                vec_ref, joined_ref, gctx_ref, inner_ref, keep_ref, send_ref,
                sums_ref, mid_ref, dz_ref, du_ref, dattn_ref, left_ref, far_ref, sem):
    step = pl.program_id(0)
    width = mid_ref.shape[0]
    count = du_ref.shape[0] // width
    copies = [
        pltpu.make_async_copy(source, far_ref.at[i], sem.at[i])
        for i, source in enumerate((mid_two_ref, dz_two_ref, ctx_one_ref, ctx_two_ref, dattn_two_ref))
    ]
    start = pltpu.make_async_copy(sums_in_ref, sums_ref, sem.at[len(copies)])

    @pl.when(step == 0)
    def _():
        start.start()
        start.wait()
        for copy in copies:
            copy.start()

    @pl.when(step < tiles)
    def _():
        at = span(step, WIDE_TILE)
        first_back_kernel(prior_ref, dqkv_ref, unit_one_ref, unit_two_ref, rstd_ref, slope_ref, ctx_ref, stat_ref,
                          wqkv_ref, rest_ref, col_ref, vec_ref, joined_ref, gctx_ref, inner_ref,
                          mid_ref.at[:, at], dz_ref.at[:, at], du_ref.at[:, at], dattn_ref.at[:, at], sums_ref, step, tiles)

    @pl.when(step == tiles)
    def _():
        for copy in copies:
            copy.wait()

    for at, first_ref, second_ref in ((0, mid_ref, far_ref.at[0]), (count, dz_ref, far_ref.at[1]), (2 * count, far_ref.at[2], far_ref.at[3])):
        @pl.when(step == tiles + at)
        def _(first_ref=first_ref, second_ref=second_ref):
            in_order(layout, place_ref, first_ref, left_ref.at[0])
            in_order(layout, place_ref, second_ref, left_ref.at[1])

    @pl.when((step >= tiles) & (step < tiles + count))
    def _():
        weight_step(left_ref, du_ref.at[span(step - tiles, width)], du_two_ref, keep_ref, send_ref)

    @pl.when((step >= tiles + count) & (step < tiles + 2 * count))
    def _():
        weight_step(left_ref, hid_one_ref, hid_two_ref, keep_ref, send_ref)

    @pl.when(step == tiles + 2 * count)
    def _():
        weight_step(left_ref, dattn_ref, far_ref.at[4], keep_ref, send_ref)


def turn(layout, place, prior, dqkv, unit_one, unit_two, rstd, slope, ctx_one, stat, sums, w_first, w_rest,
         du_two, hid_one, hid_two, mid_two, dz_two, ctx_two, dattn_two):
    width, tokens = prior.shape
    hidden = (w_rest.shape[1] - width) // 2
    heads = stat.shape[0]
    tiles = tokens // WIDE_TILE
    count = hidden // width
    half = jax.ShapeDtypeStruct((width // 2, 2 * hidden + width), BF)

    def at_tile(i):
        return jnp.minimum(i, tiles - 1)

    def rows_from(start):
        return pl.BlockSpec((width, tokens), lambda i: (jnp.clip(i - tiles - start, 0, count - 1), 0))

    columns = pl.BlockSpec((width // 2, width), lambda i: (0, jnp.clip(i - tiles, 0, 2 * count)))
    return pl.pallas_call(
        functools.partial(turn_kernel, layout, tiles),
        name="turn",
        grid=(tiles + 2 * count + 1,),
        in_specs=[pl.BlockSpec(memory_space=pltpu.SMEM), tile(width, at_tile, WIDE_TILE), tile(3 * width, at_tile, WIDE_TILE), tile(width, at_tile, WIDE_TILE), tile(width, at_tile, WIDE_TILE), tile(8, at_tile, WIDE_TILE),
                  tile(hidden, at_tile, WIDE_TILE), tile(width, at_tile, WIDE_TILE), heads_tile(heads, 2, at_tile, WIDE_TILE), pl.BlockSpec(memory_space=pl.ANY),
                  once((width, 3 * width)), once(w_rest.shape), column_spec(width), rows_from(0), rows_from(count), rows_from(count)]
        + [pl.BlockSpec(memory_space=pl.ANY)] * 5,
        out_specs=[whole((width, LANES)), tile(width, at_tile, WIDE_TILE), tile(width, at_tile, WIDE_TILE), heads_tile(heads, 1, at_tile, WIDE_TILE), columns, columns],
        out_shape=[
            jax.ShapeDtypeStruct((width, LANES), F32),
            jax.ShapeDtypeStruct((width, tokens), F32),
            jax.ShapeDtypeStruct((width, tokens), BF),
            jax.ShapeDtypeStruct((heads, 1, tokens), F32),
            half,
            half,
        ],
        scratch_shapes=[pltpu.VMEM((12, width, LANES), F32), pltpu.VMEM((width, tokens), BF), pltpu.VMEM((width, tokens), BF), pltpu.VMEM((hidden, tokens), BF),
                        pltpu.VMEM((width, tokens), BF), pltpu.VMEM((2, width, tokens), BF), pltpu.VMEM((5, width, tokens), BF), pltpu.SemaphoreType.DMA((6,))],
        compiler_params=params(63),
        cost_estimate=cost(2 * tokens * width * (4 * width + 2 * hidden), 28 << 20),
    )(place, prior, dqkv, unit_one, unit_two, rstd, slope, ctx_one, stat, sums, w_first, w_rest, w_first, du_two, hid_one, hid_two,
      mid_two, dz_two, ctx_one, ctx_two, dattn_two)


def last_kernel(layout, pairs, tiles, given, place_ref, e_ref, qkv_ref, stat_ref, grad_ref, inner_ref, done_ref, joined_ref, w_ref,
                la_ref, lb_ref, rb_ref, vec_in_ref, *refs):
    keep_ref, send_ref, input_ref, ds_ref, dqkv_ref, left_ref, vec_ref, order_ref = refs[given:]
    step = pl.program_id(0)
    pair = grad_ref.shape[0]
    rows = left_ref.shape[1]
    skipped = done_ref.shape[1]

    @pl.when(step == 0)
    def _():
        dqkv_ref[:, 0:skipped] = done_ref[...]
        in_order(layout, place_ref, la_ref, left_ref.at[0])
        in_order(layout, place_ref, lb_ref, left_ref.at[1])
        vec_ref[...] = vec_in_ref[...]

    @pl.when(step < pairs)
    def _():
        at = pl.ds(pl.multiple_of(skipped + step * pair, pair), pair)
        attend_back_pair(e_ref, qkv_ref, stat_ref, grad_ref, inner_ref, dqkv_ref.at[:, at], ds_ref)

    @pl.when((step >= pairs) & (step < pairs + tiles))
    def _():
        width = joined_ref.shape[1]
        at = pl.ds(pl.multiple_of((step - pairs) * width, width), width)
        total = joined_ref[...]
        for t in range(3):
            total = total + dg(w_ref[:, t * rows : (t + 1) * rows], dqkv_ref[t, :, at], 1, 0)
        input_ref[...] = total.T

    @pl.when(step >= pairs + tiles)
    def _():
        third = step - pairs - tiles
        ra, rb = dqkv_ref[third], rb_ref[0]
        out = (dg(left_ref[0], ra, 1, 1) + dg(left_ref[1], rb, 1, 1)).astype(BF)
        half = rows // 2
        columns = pl.ds(pl.multiple_of(third * rows, rows), rows)
        keep_ref[:, columns] = out[:half]
        send_ref[:, columns] = out[half:]
        sums = jnp.sum(lanes_sum(ra.astype(F32)) + lanes_sum(rb.astype(F32)), axis=1, keepdims=True)
        lane = lax.broadcasted_iota(jnp.int32, vec_ref.shape, 1)
        wanted = ((third == 0) & (lane == 4)) | ((third == 2) & (lane == 5))
        vec_ref[...] = jnp.where(wanted, sums, vec_ref[...])

    @pl.when(step == pl.num_programs(0) - 1)
    def _():
        in_order(layout, place_ref, vec_ref, order_ref)
        half = rows // 2
        used = keep_ref.shape[1] - LANES
        keep_ref[:, used:] = order_ref[0:half].astype(BF)
        send_ref[:, used:] = order_ref[half:].astype(BF)


def last(layout, place, e, qkv, stat, grad, inner, done, skipped, joined, w_first, left_one, left_two, dqkv_two, vec, tokens_in):
    rows, tokens = left_one.shape
    pair = 2 * HEAD_DIM
    pairs = rows // pair - skipped
    tiles = tokens // WIDE_TILE
    half = jax.ShapeDtypeStruct((rows // 2, 3 * rows + LANES), BF)

    def at_pair(i):
        return skipped + jnp.minimum(i, pairs - 1)

    def at_tile(i):
        return jnp.clip(i - pairs, 0, tiles - 1)

    return pl.pallas_call(
        functools.partial(last_kernel, layout, pairs, tiles, len(tokens_in)),
        name="last",
        grid=(pairs + tiles + 3,),
        in_specs=[
            pl.BlockSpec(memory_space=pltpu.SMEM),
            pl.BlockSpec((2, tokens, tokens), lambda i: (at_pair(i), 0, 0)),
            pl.BlockSpec((3, pair, tokens), lambda i: (0, at_pair(i), 0)),
            pl.BlockSpec((2, 2, tokens), lambda i: (at_pair(i), 0, 0)),
            pl.BlockSpec((pair, tokens), lambda i: (at_pair(i), 0)),
            pl.BlockSpec((2, 1, tokens), lambda i: (at_pair(i), 0, 0)),
            once((3, skipped * pair, tokens)),
            pl.BlockSpec((rows, WIDE_TILE), lambda i: (0, at_tile(i))),
            once((rows, 3 * rows)),
            once((rows, tokens)),
            once((rows, tokens)),
            pl.BlockSpec((1, rows, tokens), lambda i: (jnp.clip(i - pairs - tiles, 0, 2), 0, 0)),
            once(vec.shape),
        ] + [pl.BlockSpec(memory_space=pl.ANY)] * len(tokens_in),
        out_specs=[whole(half.shape)] * 2 + [pl.BlockSpec((WIDE_TILE, rows), lambda i: (at_tile(i), 0))],
        out_shape=[half, half, jax.ShapeDtypeStruct((tokens, rows), F32)],
        scratch_shapes=[pltpu.VMEM((2, tokens, tokens), BF), pltpu.VMEM((3, rows, tokens), BF), pltpu.VMEM((2, rows, tokens), BF),
                        pltpu.VMEM(vec.shape, F32), pltpu.VMEM(vec.shape, F32)],
        compiler_params=params(),
        cost_estimate=cost(12 * rows * rows * tokens, 12 * rows * tokens),
    )(place, e, qkv, stat, grad, inner, done, joined, w_first, left_one, left_two, dqkv_two, vec, *tokens_in)


def adam_kernel(layout, pieces, place_ref, *refs):
    grads = [refs[2 * i : 2 * i + 2] for i in range(len(pieces))]
    rest = refs[2 * len(pieces) :]
    shares, rest = rest[: layout.shards], rest[layout.shards :]
    w_ref, one_ref, two_ref, v_ref, vone_ref, vtwo_ref = rest[:6]
    gw_ref, nw_ref, none_ref, ntwo_ref, gv_ref, nv_ref, nvone_ref, nvtwo_ref, norm_ref = rest[6:15]
    holds, hold_ref = rest[15:-1], rest[-1]
    norm = jnp.sqrt(tree([share[0:1, 0:1] for share in shares]))
    clip_limit = math.sqrt(D * WCOLS)
    factor = clip_limit / jnp.maximum(norm, clip_limit)
    step = pl.program_id(0)
    rows = layout.rows

    @pl.when(step == 0)
    def _():
        norm_ref[...] = jnp.broadcast_to(norm, norm_ref.shape)
        for blocks, target in zip(grads, holds, strict=True):
            for c, block in enumerate(blocks):
                for e in range(layout.planes):
                    part = place_ref[0] ^ (2 * e + c)
                    target[pl.ds(pl.multiple_of(part * rows, rows), rows), :] = block[e * rows : (e + 1) * rows, :]
        hold_ref[0 : holds[-1].shape[0], :] = holds[-1][:, holds[-1].shape[1] - LANES :].astype(F32)
        grad = hold_ref[...].T[0 : gv_ref.shape[0], 0 : gv_ref.shape[1]]
        gv_ref[...] = grad
        nv_ref[...], nvone_ref[...], nvtwo_ref[...] = adam_update(v_ref[...], vone_ref[...], vtwo_ref[...], grad * factor)

    size = w_ref.shape[0]
    at = pl.ds(pl.multiple_of(step * size, size), size)
    for held, spans in zip(holds, pieces, strict=True):
        for source, target, width in spans:
            to = slice(target, target + width)
            grad = held[at, source : source + width].astype(F32)
            gw_ref[:, to] = grad
            nw_ref[:, to], none_ref[:, to], ntwo_ref[:, to] = adam_update(w_ref[:, to], one_ref[:, to], two_ref[:, to], grad * factor)


def adam(layout, place, shares, pieces, grads, weights, first, second, vectors, vector_first, vector_second):
    rows, columns = weights.shape
    block = 16
    natural = pl.BlockSpec((block, columns), lambda i: (i, 0))
    big = jax.ShapeDtypeStruct((rows, columns), F32)
    little = jax.ShapeDtypeStruct(vectors.shape, F32)
    flat = [t for blocks in grads for t in blocks] + list(shares)
    return pl.pallas_call(
        functools.partial(adam_kernel, layout, pieces),
        name="adam",
        grid=(rows // block,),
        in_specs=[pl.BlockSpec(memory_space=pltpu.SMEM)] + whole_specs(flat) + [natural] * 3 + [whole(vectors.shape)] * 3,
        out_specs=[natural] * 4 + [whole(vectors.shape)] * 4 + [whole((1, 1))],
        out_shape=[big] * 4 + [little] * 4 + [jax.ShapeDtypeStruct((1, 1), F32)],
        scratch_shapes=[pltpu.VMEM((rows, blocks[0].shape[1]), BF) for blocks in grads] + [pltpu.VMEM((LANES, LANES), F32)],
        compiler_params=params(32),
        cost_estimate=cost(20 * rows * columns, 30 * rows * columns, rows * columns),
    )(place, *flat, weights, first, second, vectors, vector_first, vector_second)


def masks(segments, tags, length):
    tokens = segments.shape[0]
    matches = segments[None, :] == jnp.arange(tags.shape[0], dtype=jnp.int32)[:, None]
    group = jnp.sum(jnp.where(matches, tags[:, None], 0), axis=0)
    live = jnp.arange(tokens, dtype=jnp.int32) < length
    kinds = jnp.arange(16, dtype=jnp.int32)[:, None]
    same = group[None, :] == kinds
    kmask = jnp.where(kinds < 4, (same & live[None, :]).astype(F32), jnp.where(kinds == 4, (~live)[None, :].astype(F32), 0.0))
    qmask = jnp.where(kinds < 4, jnp.where(same, 0.0, -FAR), jnp.where(kinds == 4, -FAR, 0.0))
    return kmask.astype(BF), jnp.broadcast_to(qmask, (16, tokens)).astype(BF)


def on_device(layout, inputs, cotangent, lengths, segment_ids, group_tags, weights, first_moments, second_moments, vectors, vector_first, vector_second):
    _, tokens, width = inputs.shape
    hidden = (weights.shape[1] - 4 * width) // 2
    pair = 2 * HEAD_DIM
    place = layout.place()
    kmask, qmask = masks(segment_ids[0], group_tags[0], lengths[0])
    act_one = inputs[0].T
    cot = cotangent[0].T

    first_part, own_columns = pick_first(layout, place, weights, vectors)
    first_z = join(layout.along_shards([first_part]))
    rest_part = pick_rest(layout, place, weights, (first_z,))
    first_mine = join([first_z] + layout.across_plane([first_z]))
    rest_z = join(layout.along_shards([rest_part]), (first_mine,))
    w_first = collect_first(layout, place, weights, own_columns, first_mine, layout.across_cores(first_mine))
    e_one, ctx_one, qkv_one, stat_one = attend(act_one, w_first, kmask, qmask)
    rest_mine = join([rest_z] + layout.across_plane([rest_z]), (ctx_one,))
    w_rest, unit_one, unit_two, rstd, act_two, hid_one, slope, e_two, ctx_two, qkv_two, stat_two = first_half(
        layout, place, weights, rest_mine, layout.across_cores(rest_mine), act_one, ctx_one, w_first, kmask, qmask)
    outputs, sums, joined_two, mid_two, hid_two, dz_two, du_two, dattn_two, dqkv_two = second_half(
        unit_two, ctx_two, cot, stat_two, w_rest, w_first, e_two, qkv_two)
    vec, joined_one, gctx_one, inner_one, keep, send = turn(
        layout, place, joined_two, dqkv_two.reshape(3 * width, tokens), unit_one, unit_two, rstd, slope, ctx_one, stat_one, sums, w_first, w_rest,
        du_two, hid_one, hid_two, mid_two, dz_two, ctx_two, dattn_two)
    operands = (e_one, qkv_one, stat_one, gctx_one, inner_one)
    done = attend_back(*operands, 0, 1)
    half = add((keep, layout.across_cores(send)), layout.planes, (done,))
    keep, send, input_grad = last(layout, place, *operands, done, 1, joined_one, w_first, act_one, act_two, dqkv_two, vec, (half[0],))
    plane = add([half[0]] + layout.across_plane(half), layout.shards, (keep,))
    half_qkv = add((keep, layout.across_cores(join([send], (plane[0],)))), layout.planes)
    plane_qkv = add([half_qkv[0]] + layout.across_plane(half_qkv), layout.shards)
    own_early = layout.across_rest(add([plane[0]] + layout.along_shards(plane), 1, (plane_qkv[0],))[0])
    own_qkv = [plane_qkv[0]] + layout.along_shards(plane_qkv)
    if layout.parts < layout.batch:
        own_qkv = [layout.across_rest(add(own_qkv)[0])]
    own_qkv = add_squares(own_qkv, (own_early,))
    all_early = join([own_early] + layout.across_plane([own_early]), (own_qkv,))
    all_qkv = join([own_qkv] + layout.across_plane([own_qkv]))
    grads = [(t, layout.across_cores(t)) for t in (all_early, all_qkv)]
    spans = [
        [(0, 4 * width, 2 * hidden), (2 * hidden, 3 * width, width)],
        [(0, 0, 3 * width)],
    ]
    share = shard_squares(layout, place, *grads[1])
    updated = adam(layout, place, [share] + layout.along_shards([share]), spans, grads, weights, first_moments, second_moments, vectors, vector_first, vector_second)
    grad_w, new_weights, new_first, new_second, grad_v, new_vectors, new_vector_first, new_vector_second, grad_norm = updated
    grad_norm = grad_norm.reshape(())
    return (
        outputs[None],
        input_grad[None],
        grad_w,
        grad_v,
        grad_norm,
        new_weights,
        new_first,
        new_second,
        new_vectors,
        new_vector_first,
        new_vector_second,
    )


def solution(mesh):
    rows = ("batch", "shard")
    placed = (
        P(rows, None, None),
        P(rows, None, None),
        P(rows),
        P(rows, None),
        P(rows, None),
        P("shard", None),
        P("shard", None),
        P("shard", None),
        P(None, "shard"),
        P(None, "shard"),
        P(None, "shard"),
    )
    return jax.shard_map(
        functools.partial(on_device, Layout(mesh.shape["batch"], mesh.shape["shard"], D)),
        mesh=mesh,
        in_specs=placed,
        out_specs=(
            P(rows, None, None),
            P(rows, None, None),
            P("shard", None),
            P(None, "shard"),
            P(),
            P("shard", None),
            P("shard", None),
            P("shard", None),
            P(None, "shard"),
            P(None, "shard"),
            P(None, "shard"),
        ),
        check_vma=False,
    )
```

```python
import functools
import math

import jax
import jax.numpy as jnp
from jax import lax
from jax.experimental import pallas as pl
from jax.experimental.pallas import tpu as pltpu
from jax.sharding import PartitionSpec as P

D = 512
FF = 2048
HEADS = 8
HEAD_DIM = 64
STEP = 10
WCOLS = 6144

NORM_EPS = 1e-05
BETA_ONE = 0.5
BETA_TWO = 0.5
ADAM_EPS = 1e-08
DECAY = 0.01
WARMUP = 4000.0
RATE_SCALE = 150000.0

BF = jnp.bfloat16
F32 = jnp.float32
FAR = 1e30
SAFE_SCORE = 60.0
TILE = 256
WIDE_TILE = 512
LANES = 128
SQUARES_AT = 12
COST_SCALE = 100


def params(mebibytes=50):
    return pltpu.CompilerParams(vmem_limit_bytes=mebibytes << 20)


def cost(flops, bytes_accessed, transcendentals=0):
    return pl.CostEstimate(flops=int(flops) // COST_SCALE, bytes_accessed=int(bytes_accessed) // COST_SCALE, transcendentals=int(transcendentals) // COST_SCALE)


def dg(left, right, left_dim, right_dim):
    return lax.dot_general(
        left, right, (((left_dim,), (right_dim,)), ((), ())), preferred_element_type=F32
    )


def whole(shape):
    return pl.BlockSpec(shape, lambda i: (0,) * len(shape))


def adam_update(master, moment_one, moment_two, gradient):
    moment_one = BETA_ONE * moment_one + (1.0 - BETA_ONE) * gradient
    moment_two = BETA_TWO * moment_two + (1.0 - BETA_TWO) * gradient * gradient
    step_rate = RATE_SCALE * D ** (-0.5) * min(STEP ** (-0.5), STEP * WARMUP ** (-1.5))
    fixed_first = moment_one / (1.0 - BETA_ONE**STEP)
    fixed_second = moment_two / (1.0 - BETA_TWO**STEP)
    master = master - step_rate * (
        fixed_first / (jnp.sqrt(fixed_second) + ADAM_EPS) + DECAY * master
    )
    return (master, moment_one, moment_two)


def attend_kernel(act_ref, wq_ref, wk_ref, wv_ref, col_ref, kmask_ref, qmask_ref, e_ref, ctx_ref, qkv_ref, stat_ref):
    act = act_ref[...]
    tokens = act.shape[1]
    q = (dg(wq_ref[...], act, 0, 0) + col_ref[:, 4:5].astype(F32)).astype(BF) * jnp.asarray(HEAD_DIM**-0.5, BF)
    k = dg(wk_ref[...], act, 0, 0).astype(BF)
    v = (dg(wv_ref[...], act, 0, 0) + col_ref[:, 5:6].astype(F32)).astype(BF)
    qkv_ref[0] = q
    qkv_ref[1] = k
    qkv_ref[2] = v
    dead = kmask_ref[4:5, :].astype(F32)
    bound = jnp.zeros((1, 1), F32)
    selves = []
    for h in range(2):
        rows = slice(h * HEAD_DIM, (h + 1) * HEAD_DIM)
        qf, kf = q[rows].astype(F32), k[rows].astype(F32)
        selves.append(jnp.sum(qf * kf, axis=0, keepdims=True))
        q_top = jnp.max(jnp.sum(qf * qf, axis=0, keepdims=True), axis=1, keepdims=True)
        k_top = jnp.max(jnp.sum(kf * kf, axis=0, keepdims=True), axis=1, keepdims=True)
        bound = jnp.maximum(bound, q_top * k_top)
    safe = bound[0, 0] <= SAFE_SCORE * SAFE_SCORE

    def scores(h):
        rows = slice(h * HEAD_DIM, (h + 1) * HEAD_DIM)
        keys = jnp.concatenate([k[rows], kmask_ref[...]], axis=0).T
        queries = jnp.concatenate([q[rows], qmask_ref[...]], axis=0)
        return dg(keys, queries, 1, 0)

    def finish(h, e, e_self):
        rows = slice(h * HEAD_DIM, (h + 1) * HEAD_DIM)
        low_e = e.astype(BF)
        e_ref[h] = low_e
        total = jnp.sum(e, axis=0, keepdims=True) + e_self
        scale = 1.0 / total
        values = v[rows]
        mixed = dg(values, low_e, 1, 0) + values.astype(F32) * e_self.astype(BF).astype(F32)
        ctx_ref[rows, :] = (mixed * scale).astype(BF)
        stat_ref[h, 0:1, :] = scale
        stat_ref[h, 1:2, :] = e_self

    @pl.when(safe)
    def _():
        for h in range(2):
            finish(h, jnp.exp(scores(h)), jnp.exp(selves[h]) * dead)

    @pl.when(jnp.logical_not(safe))
    def _():
        for h in range(2):
            s = scores(h)
            own = jnp.where(dead > 0, selves[h], -FAR)
            top = jnp.maximum(jnp.max(s, axis=0, keepdims=True), own)
            finish(h, jnp.exp(s - top), jnp.exp(own - top) * dead)


def attend(act, w_qkv, kmask, qmask):
    width, tokens = act.shape
    pairs = width // (2 * HEAD_DIM)
    pair = 2 * HEAD_DIM
    heads = width // HEAD_DIM
    return pl.pallas_call(
        attend_kernel,
        name="attend",
        grid=(pairs,),
        in_specs=[
            whole((width, tokens)),
            pl.BlockSpec((width, pair), lambda i: (0, i)),
            pl.BlockSpec((width, pair), lambda i: (0, pairs + i)),
            pl.BlockSpec((width, pair), lambda i: (0, 2 * pairs + i)),
            pl.BlockSpec((pair, pair), lambda i: (i, 3 * pairs)),
            whole((16, tokens)),
            whole((16, tokens)),
        ],
        out_specs=[
            pl.BlockSpec((2, tokens, tokens), lambda i: (i, 0, 0)),
            pl.BlockSpec((pair, tokens), lambda i: (i, 0)),
            pl.BlockSpec((3, pair, tokens), lambda i: (0, i, 0)),
            pl.BlockSpec((2, 2, tokens), lambda i: (i, 0, 0)),
        ],
        out_shape=[
            jax.ShapeDtypeStruct((heads, tokens, tokens), BF),
            jax.ShapeDtypeStruct((width, tokens), BF),
            jax.ShapeDtypeStruct((3, width, tokens), BF),
            jax.ShapeDtypeStruct((heads, 2, tokens), F32),
        ],
        compiler_params=params(),
        cost_estimate=cost(6 * width * width * tokens + 4 * width * tokens * tokens, 2 * heads * tokens * tokens, heads * tokens * tokens),
    )(act, w_qkv, w_qkv, w_qkv, w_qkv, kmask, qmask)


def attend_back_pair(e_ref, qkv_ref, stat_ref, grad_ref, inner_ref, out_ref, ds_ref):
    for h in range(2):
        rows = slice(h * HEAD_DIM, (h + 1) * HEAD_DIM)
        q, k, v = qkv_ref[0, rows], qkv_ref[1, rows], qkv_ref[2, rows]
        grad = grad_ref[rows]
        inner = inner_ref[h]
        e_self = stat_ref[h, 1:2, :]
        grad_f = grad.astype(F32)
        ds = (e_ref[h].astype(F32) * (dg(v.T, grad, 1, 0) - inner)).astype(BF)
        ds_ref[h] = ds
        own = (e_self * (jnp.sum(grad_f * v.astype(F32), axis=0, keepdims=True) - inner)).astype(BF).astype(F32)
        scale = HEAD_DIM**-0.5
        out_ref[0, rows] = ((dg(k, ds, 1, 0) + k.astype(F32) * own) * scale).astype(BF)
        out_ref[2, rows] = (dg(e_ref[h], grad, 1, 1).T + grad_f * e_self.astype(BF).astype(F32)).astype(BF)
        out_ref[1, rows] = (dg(ds_ref[h], q, 1, 1).T + q.astype(F32) * own).astype(BF)


def attend_back(e, qkv, stat, grad, inner, start=0, pairs=None):
    heads, tokens, _ = e.shape
    width = grad.shape[0]
    pair = 2 * HEAD_DIM
    pairs = pairs or heads // 2
    return pl.pallas_call(
        attend_back_pair,
        name="attend_back",
        grid=(pairs,),
        in_specs=[
            pl.BlockSpec((2, tokens, tokens), lambda i: (start + i, 0, 0)),
            pl.BlockSpec((3, pair, tokens), lambda i: (0, start + i, 0)),
            pl.BlockSpec((2, 2, tokens), lambda i: (start + i, 0, 0)),
            pl.BlockSpec((pair, tokens), lambda i: (start + i, 0)),
            pl.BlockSpec((2, 1, tokens), lambda i: (start + i, 0, 0)),
        ],
        out_specs=pl.BlockSpec((3, pair, tokens), lambda i: (0, i, 0)),
        out_shape=jax.ShapeDtypeStruct((3, pairs * pair, tokens), BF),
        scratch_shapes=[pltpu.VMEM((2, tokens, tokens), BF)],
        compiler_params=params(63),
        cost_estimate=cost(8 * pairs * pair * tokens * tokens, 4 * pairs * tokens * tokens),
    )(e, qkv, stat, grad, inner)


def normed(t):
    mean = jnp.mean(t, axis=0, keepdims=True)
    centred = t - mean
    rstd = lax.rsqrt(jnp.mean(centred * centred, axis=0, keepdims=True) + NORM_EPS)
    return centred * rstd, rstd


def normed_back(grad, unit, rstd, gain):
    scaled = grad * gain
    mean = jnp.mean(scaled, axis=0, keepdims=True)
    along = jnp.mean(scaled * unit, axis=0, keepdims=True)
    return rstd * (scaled - mean - unit * along)


def gelu_and_slope(t):
    square = t * t
    inside = jnp.tanh(t * (0.7978845608028654 + (0.7978845608028654 * 0.044715) * square))
    half = 0.5 + 0.5 * inside
    slope = half + (t * (0.5 - 0.5 * inside * inside)) * (
        0.7978845608028654 + (3.0 * 0.7978845608028654 * 0.044715) * square
    )
    return t * half, slope


def lanes_sum(t):
    out = t[:, 0:128]
    for j in range(128, t.shape[1], 128):
        out = out + t[:, j : j + 128]
    return out


def column(col_ref, j):
    return col_ref[:, j : j + 1].astype(F32)


def dense_forward(signal, ctx, rest_ref, col_ref, act_ref, slope_ref):
    wo_ref, win_ref, wback_ref = parts_of(rest_ref)
    joined = signal + dg(wo_ref[...], ctx, 0, 0) + column(col_ref, 6)
    unit_one, rstd_one = normed(joined)
    middle = unit_one * column(col_ref, 0) + column(col_ref, 1)
    low_middle = middle.astype(BF)
    width = middle.shape[0]
    summed = middle + column(col_ref, 7)
    for c in range(win_ref.shape[1] // width):
        rows = slice(c * width, (c + 1) * width)
        pre = dg(win_ref[:, rows], low_middle, 0, 0) + column(col_ref, 8 + c)
        gelu, slope = gelu_and_slope(pre)
        act = gelu.astype(BF)
        act_ref[rows, :] = act
        slope_ref[rows, :] = slope.astype(slope_ref.dtype)
        summed = summed + dg(wback_ref[:, rows], act, 1, 0)
    unit_two, rstd_two = normed(summed)
    return unit_one, rstd_one, low_middle, unit_two, rstd_two


def dense_back(grad, unit_one, rstd_one, slope_ref, unit_two, rstd_two, ctx, stat_ref, rest_ref, col_ref,
               sums_ref, joined_ref, gctx_ref, inner_ref, dz_ref, du_ref, dattn_ref):
    wo_ref, win_ref, wback_ref = parts_of(rest_ref)
    sums_ref[2] += lanes_sum(grad * unit_two)
    sums_ref[3] += lanes_sum(grad)
    grad_summed = normed_back(grad, unit_two, rstd_two, column(col_ref, 2))
    dz = grad_summed.astype(BF)
    dz_ref[...] = dz
    sums_ref[7] += lanes_sum(dz.astype(F32))
    width = dz.shape[0]
    grad_middle = grad_summed
    for c in range(win_ref.shape[1] // width):
        rows = slice(c * width, (c + 1) * width)
        du = (dg(wback_ref[:, rows], dz, 0, 0) * slope_ref[rows, :].astype(F32)).astype(BF)
        du_ref[rows, :] = du
        sums_ref[8 + c] += lanes_sum(du.astype(F32))
        grad_middle = grad_middle + dg(win_ref[:, rows], du, 1, 0)
    sums_ref[0] += lanes_sum(grad_middle * unit_one)
    sums_ref[1] += lanes_sum(grad_middle)
    grad_joined = normed_back(grad_middle, unit_one, rstd_one, column(col_ref, 0))
    joined_ref[...] = grad_joined
    dattn = grad_joined.astype(BF)
    dattn_ref[...] = dattn
    sums_ref[6] += lanes_sum(dattn.astype(F32))
    grad_ctx = dg(wo_ref[...], dattn, 1, 0)
    for h in range(stat_ref.shape[0]):
        rows = slice(h * HEAD_DIM, (h + 1) * HEAD_DIM)
        part = (grad_ctx[rows] * stat_ref[h, 0:1, :]).astype(BF)
        gctx_ref[rows, :] = part
        inner_ref[h] = jnp.sum(part.astype(F32) * ctx[rows].astype(F32), axis=0, keepdims=True)


def always(i):
    return i


def tile(rows, at=always, size=TILE):
    return pl.BlockSpec((rows, size), lambda i: (0, at(i)))


def heads_tile(heads, rows, at=always, size=TILE):
    return pl.BlockSpec((heads, rows, size), lambda i: (0, 0, at(i)))


def once(shape, *at):
    at = at or (0,) * len(shape)
    return pl.BlockSpec(shape, lambda i: at, pipeline_mode=pl.Buffered(1))


def span(step, size):
    return pl.ds(pl.multiple_of(step * size, size), size)


def rest_spec(w_rest):
    return pl.BlockSpec(w_rest.shape, lambda i: (0, 0), pipeline_mode=pl.Buffered(1))


def parts_of(rest_ref):
    width = rest_ref.shape[0]
    hidden = (rest_ref.shape[1] - width) // 2
    return rest_ref.at[:, 0:width], rest_ref.at[:, width : width + hidden], rest_ref.at[:, width + hidden :]


def column_spec(width):
    return pl.BlockSpec((width, LANES), lambda i: (0, 3 * width // LANES))


def first_dense_kernel(signal_ref, ctx_ref, rest_ref, col_ref,
                       unit_one_ref, unit_two_ref, rstd_ref, low_out_ref, act_ref, slope_ref):
    unit_one, rstd_one, _, unit_two, rstd_two = dense_forward(
        signal_ref[...].astype(F32), ctx_ref[...], rest_ref, col_ref, act_ref, slope_ref)
    unit_one_ref[...] = unit_one
    unit_two_ref[...] = unit_two
    rstd_ref[0:1, :] = rstd_one
    rstd_ref[1:2, :] = rstd_two
    low_out_ref[...] = (unit_two * column(col_ref, 2) + column(col_ref, 3)).astype(BF)


def first_half_kernel(layout, tiles, place_ref, own_ref, mine_ref, theirs_ref, signal_ref, ctx_ref, w_ref, kmask_ref, qmask_ref,
                      rest_ref, unit_one_ref, unit_two_ref, rstd_ref, low_ref, act_ref, slope_ref, e_ref, ctx_out_ref, qkv_ref, stat_ref, hold_ref):
    step = pl.program_id(0)
    width = ctx_ref.shape[0]
    pair = ctx_out_ref.shape[0]

    @pl.when(step == 0)
    def _():
        put_blocks(layout, place_ref, (mine_ref, theirs_ref), rest_ref)
        rest_ref[own_rows(layout, place_ref), :] = own_ref[:, own_ref.shape[1] - rest_ref.shape[1] :].astype(BF)

    @pl.when(step < tiles)
    def _():
        first_dense_kernel(signal_ref, ctx_ref, rest_ref, w_ref.at[:, 3 * width :], unit_one_ref, unit_two_ref, rstd_ref, low_ref, act_ref, slope_ref)
        hold_ref[:, span(step, TILE)] = low_ref[...]

    @pl.when(step >= tiles)
    def _():
        at = step - tiles
        pairs = width // pair
        attend_kernel(
            hold_ref,
            w_ref.at[:, span(at, pair)],
            w_ref.at[:, span(at + pairs, pair)],
            w_ref.at[:, span(at + 2 * pairs, pair)],
            w_ref.at[span(at, pair), 3 * width :],
            kmask_ref, qmask_ref, e_ref, ctx_out_ref, qkv_ref, stat_ref)


def first_half(layout, place, weights, mine, theirs, signal, ctx, w_first, kmask, qmask):
    width, tokens = signal.shape
    total = mine.shape[1]
    hidden = (total - width) // 2
    pair = 2 * HEAD_DIM
    pairs, heads = width // pair, width // HEAD_DIM
    tiles = tokens // TILE

    def at_tile(i):
        return jnp.minimum(i, tiles - 1)

    def at_pair(i):
        return jnp.maximum(i - tiles, 0)

    return pl.pallas_call(
        functools.partial(first_half_kernel, layout, tiles),
        name="first_half",
        grid=(tiles + pairs,),
        in_specs=[pl.BlockSpec(memory_space=pltpu.SMEM), once(weights.shape), once(mine.shape), once(theirs.shape),
                  tile(width, at_tile), tile(width, at_tile), once(w_first.shape), once(kmask.shape), once(qmask.shape)],
        out_specs=[whole((width, total)), tile(width, at_tile), tile(width, at_tile), tile(8, at_tile), tile(width, at_tile), tile(hidden, at_tile), tile(hidden, at_tile),
                   pl.BlockSpec((2, tokens, tokens), lambda i: (at_pair(i), 0, 0)),
                   pl.BlockSpec((pair, tokens), lambda i: (at_pair(i), 0)),
                   pl.BlockSpec((3, pair, tokens), lambda i: (0, at_pair(i), 0)),
                   pl.BlockSpec((2, 2, tokens), lambda i: (at_pair(i), 0, 0))],
        out_shape=[
            jax.ShapeDtypeStruct((width, total), BF),
            jax.ShapeDtypeStruct((width, tokens), F32),
            jax.ShapeDtypeStruct((width, tokens), F32),
            jax.ShapeDtypeStruct((8, tokens), F32),
            jax.ShapeDtypeStruct((width, tokens), BF),
            jax.ShapeDtypeStruct((hidden, tokens), BF),
            jax.ShapeDtypeStruct((hidden, tokens), BF),
            jax.ShapeDtypeStruct((heads, tokens, tokens), BF),
            jax.ShapeDtypeStruct((width, tokens), BF),
            jax.ShapeDtypeStruct((3, width, tokens), BF),
            jax.ShapeDtypeStruct((heads, 2, tokens), F32),
        ],
        scratch_shapes=[pltpu.VMEM((width, tokens), BF)],
        compiler_params=params(63),
        cost_estimate=cost(2 * tokens * width * (width + 2 * hidden), 24 << 20, tokens * hidden),
    )(place, weights, mine, theirs, signal, ctx, w_first, kmask, qmask)


def second_dense_kernel(unit_ref, ctx_ref, cot_ref, stat_ref, rest_ref, col_ref,
                        out_ref, sums_ref, joined_ref, gctx_ref, inner_ref, mid_ref, act_ref, dz_ref, du_ref, dattn_ref, slope_ref):
    @pl.when(pl.program_id(0) == 0)
    def _():
        sums_ref[...] = jnp.zeros(sums_ref.shape, F32)

    ctx = ctx_ref[...]
    gain, shift = column(col_ref, 2), column(col_ref, 3)
    unit_one, rstd_one, low_middle, unit_two, rstd_two = dense_forward(
        unit_ref[...] * gain + shift, ctx, rest_ref, col_ref, act_ref, slope_ref)
    mid_ref[...] = low_middle
    out_ref[...] = (unit_two * gain + shift).astype(BF).T
    dense_back(cot_ref[...].astype(F32), unit_one, rstd_one, slope_ref, unit_two, rstd_two, ctx, stat_ref,
               rest_ref, col_ref, sums_ref, joined_ref, gctx_ref, inner_ref, dz_ref, du_ref, dattn_ref)


def second_half_kernel(tiles, unit_ref, ctx_ref, cot_ref, stat_ref, rest_ref, col_ref, e_ref, qkv_ref, pair_stat_ref,
                       out_ref, sums_ref, joined_ref, mid_ref, act_ref, dz_ref, du_ref, dattn_ref, dqkv_ref, slope_ref, gctx_ref, inner_ref, ds_ref):
    step = pl.program_id(0)

    @pl.when(step < tiles)
    def _():
        at = span(step, WIDE_TILE)
        second_dense_kernel(unit_ref, ctx_ref, cot_ref, stat_ref, rest_ref, col_ref, out_ref, sums_ref, joined_ref,
                            gctx_ref.at[:, at], inner_ref.at[:, :, at], mid_ref, act_ref, dz_ref, du_ref, dattn_ref, slope_ref)

    @pl.when(step >= tiles)
    def _():
        pair = dqkv_ref.shape[1]
        attend_back_pair(e_ref, qkv_ref, pair_stat_ref, gctx_ref.at[span(step - tiles, pair)], inner_ref.at[pl.ds(2 * (step - tiles), 2)], dqkv_ref, ds_ref)


def second_half(unit, ctx, cot, stat, w_rest, w_first, e, qkv):
    width, tokens = unit.shape
    hidden = (w_rest.shape[1] - width) // 2
    heads = stat.shape[0]
    pair = 2 * HEAD_DIM
    pairs = width // pair
    tiles = tokens // WIDE_TILE

    def at_tile(i):
        return jnp.minimum(i, tiles - 1)

    def at_pair(i):
        return jnp.maximum(i - tiles, 0)

    return pl.pallas_call(
        functools.partial(second_half_kernel, tiles),
        name="second_half",
        grid=(tiles + pairs,),
        in_specs=[tile(width, at_tile, WIDE_TILE), tile(width, at_tile, WIDE_TILE), tile(width, at_tile, WIDE_TILE), heads_tile(heads, 2, at_tile, WIDE_TILE), once(w_rest.shape), column_spec(width),
                  pl.BlockSpec((2, tokens, tokens), lambda i: (at_pair(i), 0, 0)),
                  pl.BlockSpec((3, pair, tokens), lambda i: (0, at_pair(i), 0)),
                  pl.BlockSpec((2, 2, tokens), lambda i: (at_pair(i), 0, 0))],
        out_specs=[pl.BlockSpec((WIDE_TILE, width), lambda i: (at_tile(i), 0)), once((12, width, LANES)), tile(width, at_tile, WIDE_TILE),
                   tile(width, at_tile, WIDE_TILE), tile(hidden, at_tile, WIDE_TILE), tile(width, at_tile, WIDE_TILE), tile(hidden, at_tile, WIDE_TILE), tile(width, at_tile, WIDE_TILE),
                   pl.BlockSpec((3, pair, tokens), lambda i: (0, at_pair(i), 0))],
        out_shape=[
            jax.ShapeDtypeStruct((tokens, width), BF),
            jax.ShapeDtypeStruct((12, width, LANES), F32),
            jax.ShapeDtypeStruct((width, tokens), F32),
            jax.ShapeDtypeStruct((width, tokens), BF),
            jax.ShapeDtypeStruct((hidden, tokens), BF),
            jax.ShapeDtypeStruct((width, tokens), BF),
            jax.ShapeDtypeStruct((hidden, tokens), BF),
            jax.ShapeDtypeStruct((width, tokens), BF),
            jax.ShapeDtypeStruct((3, width, tokens), BF),
        ],
        scratch_shapes=[pltpu.VMEM((hidden, WIDE_TILE), F32), pltpu.VMEM((width, tokens), BF), pltpu.VMEM((heads, 1, tokens), F32), pltpu.VMEM((2, tokens, tokens), BF)],
        compiler_params=params(63),
        cost_estimate=cost(4 * tokens * width * (width + 2 * hidden), 28 << 20, tokens * hidden),
    )(unit, ctx, cot, stat, w_rest, w_first, e, qkv, stat)


def first_back_kernel(prior_ref, dqkv_ref, unit_one_ref, unit_two_ref, rstd_ref, slope_ref, ctx_ref, stat_ref,
                      wqkv_ref, rest_ref, col_ref,
                      vec_ref, joined_ref, gctx_ref, inner_ref, mid_ref, dz_ref, du_ref, dattn_ref, sums_ref, step, tiles):

    unit_one = unit_one_ref[...]
    mid_ref[...] = (unit_one * column(col_ref, 0) + column(col_ref, 1)).astype(BF)
    grad = prior_ref[...] + dg(wqkv_ref[...], dqkv_ref[...], 1, 0)
    dense_back(grad, unit_one, rstd_ref[0:1, :], slope_ref, unit_two_ref[...], rstd_ref[1:2, :], ctx_ref[...], stat_ref,
               rest_ref, col_ref, sums_ref, joined_ref, gctx_ref, inner_ref, dz_ref, du_ref, dattn_ref)

    @pl.when(step == tiles - 1)
    def _():
        lane = lax.broadcasted_iota(jnp.int32, vec_ref.shape, 1)
        out = jnp.zeros(vec_ref.shape, F32)
        for j in (0, 1, 2, 3, 6, 7, 8, 9, 10, 11):
            out = jnp.where(lane == j, jnp.sum(sums_ref[j], axis=1, keepdims=True), out)
        vec_ref[...] = out


class Layout:
    def __init__(self, mesh_batch, mesh_shard, width):
        self.batch = mesh_batch
        self.shards = mesh_shard
        self.parts = min(mesh_batch, width // mesh_shard // 16)
        self.planes = self.parts // 2
        self.rows = width // mesh_shard // self.parts

    def swap(self, value, axis, distance):
        size = self.batch if axis == "batch" else self.shards
        return lax.ppermute(value, axis, [(i, i ^ distance) for i in range(size)])

    def place(self):
        return jnp.stack([lax.axis_index("batch") % self.parts, lax.axis_index("shard")]).astype(jnp.int32)

    def row_of(self, place_ref, c, e, d):
        block = (place_ref[1] ^ d) * self.parts + (place_ref[0] ^ (2 * e + c))
        return pl.multiple_of(block * self.rows, self.rows)

    def along_shards(self, blocks):
        return [self.swap(blocks[d % len(blocks)], "shard", d) for d in range(1, self.shards)]

    def across_plane(self, blocks):
        return [self.swap(blocks[e % len(blocks)], "batch", 2 * e) for e in range(1, self.planes)]

    def across_cores(self, block):
        return self.swap(block, "batch", 1)

    def across_rest(self, own):
        distance = self.parts
        while distance < self.batch:
            own = add([own, self.swap(own, "batch", distance)])[0]
            distance *= 2
        return own


def tree(values):
    while len(values) > 1:
        values = [a + b for a, b in zip(values[::2], values[1::2], strict=True)]
    return values[0]


def whole_specs(values, tokens_in=()):
    return [whole(v.shape) for v in values] + [pl.BlockSpec(memory_space=pl.ANY)] * len(tokens_in)


def join_kernel(count, *refs):
    out_ref = refs[-1]
    at = 0
    for source in refs[:count]:
        out_ref[at : at + source.shape[0], :] = source[...]
        at += source.shape[0]


def join(blocks, tokens_in=()):
    rows, columns = sum(b.shape[0] for b in blocks), blocks[0].shape[1]
    return pl.pallas_call(
        functools.partial(join_kernel, len(blocks)),
        name="join",
        grid=(1,),
        in_specs=whole_specs(blocks, tokens_in),
        out_specs=whole((rows, columns)),
        out_shape=jax.ShapeDtypeStruct((rows, columns), BF),
        compiler_params=params(),
        cost_estimate=cost(0, 4 * rows * columns),
    )(*blocks, *tokens_in)


def add_kernel(count, outs, *refs):
    total = refs[0][...].astype(F32)
    for other in refs[1:count]:
        total = total + other[...].astype(F32)
    total = total.astype(BF)
    rows = refs[-1].shape[0]
    for i in range(outs):
        refs[i - outs][...] = total[i * rows : (i + 1) * rows]


def add(values, outs=1, tokens_in=()):
    rows, columns = values[0].shape
    part = jax.ShapeDtypeStruct((rows // outs, columns), BF)
    return pl.pallas_call(
        functools.partial(add_kernel, len(values), outs),
        name="add",
        grid=(1,),
        in_specs=whole_specs(values, tokens_in),
        out_specs=[whole(part.shape)] * outs,
        out_shape=[part] * outs,
        compiler_params=params(),
        cost_estimate=cost(len(values) * rows * columns, 2 * (len(values) + 1) * rows * columns),
    )(*values, *tokens_in)


def add_squares_kernel(count, others, *refs):
    out_ref = refs[-1]
    total = refs[0][...].astype(F32)
    for other in refs[1:count]:
        total = total + other[...].astype(F32)
    total = total.astype(BF)
    squares = jnp.sum(jnp.square(total.astype(F32)), keepdims=True)
    for other in refs[count : count + others]:
        squares = squares + jnp.sum(jnp.square(other[...].astype(F32)), keepdims=True)
    out_ref[...] = total
    high = squares.astype(BF)
    middle = (squares - high.astype(F32)).astype(BF)
    low = (squares - high.astype(F32) - middle.astype(F32)).astype(BF)
    used = total.shape[1] - LANES
    tail = total[:, used:]
    lane = lax.broadcasted_iota(jnp.int32, tail.shape, 1)
    for i, piece in enumerate((high, middle, low)):
        tail = jnp.where(lane == SQUARES_AT + i, piece.astype(F32), tail.astype(F32)).astype(BF)
    out_ref[:, used:] = tail


def add_squares(values, others):
    rows, columns = values[0].shape
    return pl.pallas_call(
        functools.partial(add_squares_kernel, len(values), len(others)),
        name="add_squares",
        grid=(1,),
        in_specs=whole_specs(list(values) + list(others)),
        out_specs=whole((rows, columns)),
        out_shape=jax.ShapeDtypeStruct((rows, columns), BF),
        compiler_params=params(),
        cost_estimate=cost(len(values) * rows * columns, 2 * (len(values) + 1) * rows * columns),
    )(*values, *others)


def shard_squares_kernel(layout, place_ref, mine_ref, theirs_ref, out_ref):
    used = mine_ref.shape[1] - LANES
    total = jnp.zeros((1, LANES), F32)
    lane = lax.broadcasted_iota(jnp.int32, (1, LANES), 1)
    riding = (lane >= SQUARES_AT) & (lane < SQUARES_AT + 3)
    for part in range(layout.parts):
        away = place_ref[0] ^ part
        at = pl.ds(pl.multiple_of((away >> 1) * layout.rows, layout.rows), layout.rows)
        mine = mine_ref[at, used:].astype(F32)[0:1]
        theirs = theirs_ref[at, used:].astype(F32)[0:1]
        total = total + jnp.where((away & 1) == 0, mine, theirs)
    total = jnp.sum(jnp.where(riding, total, 0.0), axis=1, keepdims=True)
    out_ref[...] = jnp.broadcast_to(total, out_ref.shape)


def shard_squares(layout, place, mine, theirs):
    return pl.pallas_call(
        functools.partial(shard_squares_kernel, layout),
        name="shard_squares",
        grid=(1,),
        in_specs=[pl.BlockSpec(memory_space=pltpu.SMEM)] + whole_specs((mine, theirs)),
        out_specs=whole((8, LANES)),
        out_shape=jax.ShapeDtypeStruct((8, LANES), F32),
        compiler_params=params(),
        cost_estimate=cost(0, 4 * mine.size),
    )(place, mine, theirs)


def pick_first_kernel(place_ref, w_ref, vec_ref, out_ref, columns_ref, hold_ref):
    hold_ref[...] = jnp.zeros(hold_ref.shape, F32)
    hold_ref[0 : vec_ref.shape[0], 0 : vec_ref.shape[1]] = vec_ref[...]
    hold_ref[...] = hold_ref[...].T
    columns_ref[...] = hold_ref[0 : columns_ref.shape[0], :].astype(BF)
    used = w_ref.shape[1]
    rows = out_ref.shape[0]
    out_ref[:, 0:used] = w_ref[...].astype(BF)
    out_ref[:, used:] = hold_ref[pl.ds(pl.multiple_of(place_ref[0] * rows, rows), rows), :].astype(BF)


def pick_first(layout, place, weights, vectors):
    shard_rows, columns = weights.shape
    used = columns // 4
    return pl.pallas_call(
        pick_first_kernel,
        name="pick_first",
        grid_spec=pltpu.PrefetchScalarGridSpec(
            num_scalar_prefetch=1,
            grid=(1,),
            in_specs=[pl.BlockSpec((layout.rows, used), lambda i, place: (place[0], 0)), pl.BlockSpec(vectors.shape, lambda i, place: (0, 0))],
            out_specs=[pl.BlockSpec((layout.rows, used + LANES), lambda i, place: (0, 0)), pl.BlockSpec((shard_rows, LANES), lambda i, place: (0, 0))],
            scratch_shapes=[pltpu.VMEM((LANES, LANES), F32)],
        ),
        out_shape=[jax.ShapeDtypeStruct((layout.rows, used + LANES), BF), jax.ShapeDtypeStruct((shard_rows, LANES), BF)],
        compiler_params=params(),
        cost_estimate=cost(0, 6 * layout.rows * columns),
    )(place, weights, vectors)


def pick_rest_kernel(place_ref, w_ref, *refs):
    out_ref = refs[-1]
    out_ref[...] = w_ref[:, w_ref.shape[1] - out_ref.shape[1] :].astype(BF)


def pick_rest(layout, place, weights, tokens_in):
    columns = weights.shape[1]
    return pl.pallas_call(
        pick_rest_kernel,
        name="pick_rest",
        grid_spec=pltpu.PrefetchScalarGridSpec(
            num_scalar_prefetch=1,
            grid=(1,),
            in_specs=[pl.BlockSpec((layout.rows, columns), lambda i, place: (place[0], 0))] + [pl.BlockSpec(memory_space=pl.ANY)] * len(tokens_in),
            out_specs=pl.BlockSpec((layout.rows, 3 * columns // 4), lambda i, place: (0, 0)),
        ),
        out_shape=jax.ShapeDtypeStruct((layout.rows, 3 * columns // 4), BF),
        compiler_params=params(),
        cost_estimate=cost(0, 6 * layout.rows * columns),
    )(place, weights, *tokens_in)


def put_blocks(layout, place_ref, sources, out_ref):
    for c, source in enumerate(sources):
        for e in range(layout.planes):
            for d in range(1, layout.shards):
                at = (e * (layout.shards - 1) + d - 1) * layout.rows
                out_ref[pl.ds(layout.row_of(place_ref, c, e, d), layout.rows), :] = source[at : at + layout.rows, :]


def own_rows(layout, place_ref):
    rows = layout.rows * layout.parts
    return pl.ds(pl.multiple_of(place_ref[1] * rows, rows), rows)


def collect_first_kernel(layout, place_ref, w_ref, columns_ref, mine_ref, theirs_ref, out_ref):
    put_blocks(layout, place_ref, (mine_ref, theirs_ref), out_ref)
    rows = own_rows(layout, place_ref)
    used = w_ref.shape[1]
    out_ref[rows, 0:used] = w_ref[...].astype(BF)
    out_ref[rows, used:] = columns_ref[...]


def collect_first(layout, place, weights, columns, mine, theirs):
    shard_rows, all_columns = weights.shape
    rows = shard_rows * layout.shards
    total = mine.shape[1]
    return pl.pallas_call(
        functools.partial(collect_first_kernel, layout),
        name="collect_first",
        grid=(1,),
        in_specs=[pl.BlockSpec(memory_space=pltpu.SMEM), pl.BlockSpec((shard_rows, all_columns // 4), lambda i: (0, 0))] + whole_specs((columns, mine, theirs)),
        out_specs=whole((rows, total)),
        out_shape=jax.ShapeDtypeStruct((rows, total), BF),
        compiler_params=params(),
        cost_estimate=cost(0, 4 * rows * total),
    )(place, weights, columns, mine, theirs)


def in_order(layout, place_ref, source_ref, target_ref):
    at = 0
    for c in range(2):
        for e in range(layout.planes):
            for d in range(layout.shards):
                target_ref[at : at + layout.rows] = source_ref[pl.ds(layout.row_of(place_ref, c, e, d), layout.rows), :]
                at += layout.rows


def weight_step(left_ref, ra_ref, rb_ref, keep_ref, send_ref):
    out = (dg(left_ref[0], ra_ref[...], 1, 1) + dg(left_ref[1], rb_ref[...], 1, 1)).astype(BF)
    half = out.shape[0] // 2
    keep_ref[...] = out[:half]
    send_ref[...] = out[half:]


def turn_kernel(layout, tiles, place_ref, prior_ref, dqkv_ref, unit_one_ref, unit_two_ref, rstd_ref, slope_ref, ctx_ref, stat_ref, sums_in_ref,
                wqkv_ref, rest_ref, col_ref, du_two_ref, hid_one_ref, hid_two_ref, mid_two_ref, dz_two_ref, ctx_one_ref, ctx_two_ref, dattn_two_ref,
                vec_ref, joined_ref, gctx_ref, inner_ref, keep_ref, send_ref,
                sums_ref, mid_ref, dz_ref, du_ref, dattn_ref, left_ref, far_ref, sem):
    step = pl.program_id(0)
    width = mid_ref.shape[0]
    count = du_ref.shape[0] // width
    copies = [
        pltpu.make_async_copy(source, far_ref.at[i], sem.at[i])
        for i, source in enumerate((mid_two_ref, dz_two_ref, ctx_one_ref, ctx_two_ref, dattn_two_ref))
    ]
    start = pltpu.make_async_copy(sums_in_ref, sums_ref, sem.at[len(copies)])

    @pl.when(step == 0)
    def _():
        start.start()
        start.wait()
        for copy in copies:
            copy.start()

    @pl.when(step < tiles)
    def _():
        at = span(step, WIDE_TILE)
        first_back_kernel(prior_ref, dqkv_ref, unit_one_ref, unit_two_ref, rstd_ref, slope_ref, ctx_ref, stat_ref,
                          wqkv_ref, rest_ref, col_ref, vec_ref, joined_ref, gctx_ref, inner_ref,
                          mid_ref.at[:, at], dz_ref.at[:, at], du_ref.at[:, at], dattn_ref.at[:, at], sums_ref, step, tiles)

    @pl.when(step == tiles)
    def _():
        for copy in copies:
            copy.wait()

    for at, first_ref, second_ref in ((0, mid_ref, far_ref.at[0]), (count, dz_ref, far_ref.at[1]), (2 * count, far_ref.at[2], far_ref.at[3])):
        @pl.when(step == tiles + at)
        def _(first_ref=first_ref, second_ref=second_ref):
            in_order(layout, place_ref, first_ref, left_ref.at[0])
            in_order(layout, place_ref, second_ref, left_ref.at[1])

    @pl.when((step >= tiles) & (step < tiles + count))
    def _():
        weight_step(left_ref, du_ref.at[span(step - tiles, width)], du_two_ref, keep_ref, send_ref)

    @pl.when((step >= tiles + count) & (step < tiles + 2 * count))
    def _():
        weight_step(left_ref, hid_one_ref, hid_two_ref, keep_ref, send_ref)

    @pl.when(step == tiles + 2 * count)
    def _():
        weight_step(left_ref, dattn_ref, far_ref.at[4], keep_ref, send_ref)


def turn(layout, place, prior, dqkv, unit_one, unit_two, rstd, slope, ctx_one, stat, sums, w_first, w_rest,
         du_two, hid_one, hid_two, mid_two, dz_two, ctx_two, dattn_two):
    width, tokens = prior.shape
    hidden = (w_rest.shape[1] - width) // 2
    heads = stat.shape[0]
    tiles = tokens // WIDE_TILE
    count = hidden // width
    half = jax.ShapeDtypeStruct((width // 2, 2 * hidden + width), BF)

    def at_tile(i):
        return jnp.minimum(i, tiles - 1)

    def rows_from(start):
        return pl.BlockSpec((width, tokens), lambda i: (jnp.clip(i - tiles - start, 0, count - 1), 0))

    columns = pl.BlockSpec((width // 2, width), lambda i: (0, jnp.clip(i - tiles, 0, 2 * count)))
    return pl.pallas_call(
        functools.partial(turn_kernel, layout, tiles),
        name="turn",
        grid=(tiles + 2 * count + 1,),
        in_specs=[pl.BlockSpec(memory_space=pltpu.SMEM), tile(width, at_tile, WIDE_TILE), tile(3 * width, at_tile, WIDE_TILE), tile(width, at_tile, WIDE_TILE), tile(width, at_tile, WIDE_TILE), tile(8, at_tile, WIDE_TILE),
                  tile(hidden, at_tile, WIDE_TILE), tile(width, at_tile, WIDE_TILE), heads_tile(heads, 2, at_tile, WIDE_TILE), pl.BlockSpec(memory_space=pl.ANY),
                  once((width, 3 * width)), once(w_rest.shape), column_spec(width), rows_from(0), rows_from(count), rows_from(count)]
        + [pl.BlockSpec(memory_space=pl.ANY)] * 5,
        out_specs=[whole((width, LANES)), tile(width, at_tile, WIDE_TILE), tile(width, at_tile, WIDE_TILE), heads_tile(heads, 1, at_tile, WIDE_TILE), columns, columns],
        out_shape=[
            jax.ShapeDtypeStruct((width, LANES), F32),
            jax.ShapeDtypeStruct((width, tokens), F32),
            jax.ShapeDtypeStruct((width, tokens), BF),
            jax.ShapeDtypeStruct((heads, 1, tokens), F32),
            half,
            half,
        ],
        scratch_shapes=[pltpu.VMEM((12, width, LANES), F32), pltpu.VMEM((width, tokens), BF), pltpu.VMEM((width, tokens), BF), pltpu.VMEM((hidden, tokens), BF),
                        pltpu.VMEM((width, tokens), BF), pltpu.VMEM((2, width, tokens), BF), pltpu.VMEM((5, width, tokens), BF), pltpu.SemaphoreType.DMA((6,))],
        compiler_params=params(63),
        cost_estimate=cost(2 * tokens * width * (4 * width + 2 * hidden), 28 << 20),
    )(place, prior, dqkv, unit_one, unit_two, rstd, slope, ctx_one, stat, sums, w_first, w_rest, w_first, du_two, hid_one, hid_two,
      mid_two, dz_two, ctx_one, ctx_two, dattn_two)


def last_kernel(layout, pairs, tiles, given, place_ref, e_ref, qkv_ref, stat_ref, grad_ref, inner_ref, done_ref, joined_ref, w_ref,
                la_ref, lb_ref, rb_ref, vec_in_ref, *refs):
    keep_ref, send_ref, input_ref, ds_ref, dqkv_ref, left_ref, vec_ref, order_ref = refs[given:]
    step = pl.program_id(0)
    pair = grad_ref.shape[0]
    rows = left_ref.shape[1]
    skipped = done_ref.shape[1]

    @pl.when(step == 0)
    def _():
        dqkv_ref[:, 0:skipped] = done_ref[...]
        in_order(layout, place_ref, la_ref, left_ref.at[0])
        in_order(layout, place_ref, lb_ref, left_ref.at[1])
        vec_ref[...] = vec_in_ref[...]

    @pl.when(step < pairs)
    def _():
        at = pl.ds(pl.multiple_of(skipped + step * pair, pair), pair)
        attend_back_pair(e_ref, qkv_ref, stat_ref, grad_ref, inner_ref, dqkv_ref.at[:, at], ds_ref)

    @pl.when((step >= pairs) & (step < pairs + tiles))
    def _():
        width = joined_ref.shape[1]
        at = pl.ds(pl.multiple_of((step - pairs) * width, width), width)
        total = joined_ref[...]
        for t in range(3):
            total = total + dg(w_ref[:, t * rows : (t + 1) * rows], dqkv_ref[t, :, at], 1, 0)
        input_ref[...] = total.T

    @pl.when(step >= pairs + tiles)
    def _():
        third = step - pairs - tiles
        ra, rb = dqkv_ref[third], rb_ref[0]
        out = (dg(left_ref[0], ra, 1, 1) + dg(left_ref[1], rb, 1, 1)).astype(BF)
        half = rows // 2
        columns = pl.ds(pl.multiple_of(third * rows, rows), rows)
        keep_ref[:, columns] = out[:half]
        send_ref[:, columns] = out[half:]
        sums = jnp.sum(lanes_sum(ra.astype(F32)) + lanes_sum(rb.astype(F32)), axis=1, keepdims=True)
        lane = lax.broadcasted_iota(jnp.int32, vec_ref.shape, 1)
        wanted = ((third == 0) & (lane == 4)) | ((third == 2) & (lane == 5))
        vec_ref[...] = jnp.where(wanted, sums, vec_ref[...])

    @pl.when(step == pl.num_programs(0) - 1)
    def _():
        in_order(layout, place_ref, vec_ref, order_ref)
        half = rows // 2
        used = keep_ref.shape[1] - LANES
        keep_ref[:, used:] = order_ref[0:half].astype(BF)
        send_ref[:, used:] = order_ref[half:].astype(BF)


def last(layout, place, e, qkv, stat, grad, inner, done, skipped, joined, w_first, left_one, left_two, dqkv_two, vec, tokens_in):
    rows, tokens = left_one.shape
    pair = 2 * HEAD_DIM
    pairs = rows // pair - skipped
    tiles = tokens // WIDE_TILE
    half = jax.ShapeDtypeStruct((rows // 2, 3 * rows + LANES), BF)

    def at_pair(i):
        return skipped + jnp.minimum(i, pairs - 1)

    def at_tile(i):
        return jnp.clip(i - pairs, 0, tiles - 1)

    return pl.pallas_call(
        functools.partial(last_kernel, layout, pairs, tiles, len(tokens_in)),
        name="last",
        grid=(pairs + tiles + 3,),
        in_specs=[
            pl.BlockSpec(memory_space=pltpu.SMEM),
            pl.BlockSpec((2, tokens, tokens), lambda i: (at_pair(i), 0, 0)),
            pl.BlockSpec((3, pair, tokens), lambda i: (0, at_pair(i), 0)),
            pl.BlockSpec((2, 2, tokens), lambda i: (at_pair(i), 0, 0)),
            pl.BlockSpec((pair, tokens), lambda i: (at_pair(i), 0)),
            pl.BlockSpec((2, 1, tokens), lambda i: (at_pair(i), 0, 0)),
            once((3, skipped * pair, tokens)),
            pl.BlockSpec((rows, WIDE_TILE), lambda i: (0, at_tile(i))),
            once((rows, 3 * rows)),
            once((rows, tokens)),
            once((rows, tokens)),
            pl.BlockSpec((1, rows, tokens), lambda i: (jnp.clip(i - pairs - tiles, 0, 2), 0, 0)),
            once(vec.shape),
        ] + [pl.BlockSpec(memory_space=pl.ANY)] * len(tokens_in),
        out_specs=[whole(half.shape)] * 2 + [pl.BlockSpec((WIDE_TILE, rows), lambda i: (at_tile(i), 0))],
        out_shape=[half, half, jax.ShapeDtypeStruct((tokens, rows), F32)],
        scratch_shapes=[pltpu.VMEM((2, tokens, tokens), BF), pltpu.VMEM((3, rows, tokens), BF), pltpu.VMEM((2, rows, tokens), BF),
                        pltpu.VMEM(vec.shape, F32), pltpu.VMEM(vec.shape, F32)],
        compiler_params=params(),
        cost_estimate=cost(12 * rows * rows * tokens, 12 * rows * tokens),
    )(place, e, qkv, stat, grad, inner, done, joined, w_first, left_one, left_two, dqkv_two, vec, *tokens_in)


def adam_kernel(layout, pieces, place_ref, *refs):
    grads = [refs[2 * i : 2 * i + 2] for i in range(len(pieces))]
    rest = refs[2 * len(pieces) :]
    shares, rest = rest[: layout.shards], rest[layout.shards :]
    w_ref, one_ref, two_ref, v_ref, vone_ref, vtwo_ref = rest[:6]
    gw_ref, nw_ref, none_ref, ntwo_ref, gv_ref, nv_ref, nvone_ref, nvtwo_ref, norm_ref = rest[6:15]
    holds, hold_ref = rest[15:-1], rest[-1]
    norm = jnp.sqrt(tree([share[0:1, 0:1] for share in shares]))
    clip_limit = math.sqrt(D * WCOLS)
    factor = clip_limit / jnp.maximum(norm, clip_limit)
    step = pl.program_id(0)
    rows = layout.rows

    @pl.when(step == 0)
    def _():
        norm_ref[...] = jnp.broadcast_to(norm, norm_ref.shape)
        for blocks, target in zip(grads, holds, strict=True):
            for c, block in enumerate(blocks):
                for e in range(layout.planes):
                    part = place_ref[0] ^ (2 * e + c)
                    target[pl.ds(pl.multiple_of(part * rows, rows), rows), :] = block[e * rows : (e + 1) * rows, :]
        hold_ref[0 : holds[-1].shape[0], :] = holds[-1][:, holds[-1].shape[1] - LANES :].astype(F32)
        grad = hold_ref[...].T[0 : gv_ref.shape[0], 0 : gv_ref.shape[1]]
        gv_ref[...] = grad
        nv_ref[...], nvone_ref[...], nvtwo_ref[...] = adam_update(v_ref[...], vone_ref[...], vtwo_ref[...], grad * factor)

    size = w_ref.shape[0]
    at = pl.ds(pl.multiple_of(step * size, size), size)
    for held, spans in zip(holds, pieces, strict=True):
        for source, target, width in spans:
            to = slice(target, target + width)
            grad = held[at, source : source + width].astype(F32)
            gw_ref[:, to] = grad
            nw_ref[:, to], none_ref[:, to], ntwo_ref[:, to] = adam_update(w_ref[:, to], one_ref[:, to], two_ref[:, to], grad * factor)


def adam(layout, place, shares, pieces, grads, weights, first, second, vectors, vector_first, vector_second):
    rows, columns = weights.shape
    block = 16
    natural = pl.BlockSpec((block, columns), lambda i: (i, 0))
    big = jax.ShapeDtypeStruct((rows, columns), F32)
    little = jax.ShapeDtypeStruct(vectors.shape, F32)
    flat = [t for blocks in grads for t in blocks] + list(shares)
    return pl.pallas_call(
        functools.partial(adam_kernel, layout, pieces),
        name="adam",
        grid=(rows // block,),
        in_specs=[pl.BlockSpec(memory_space=pltpu.SMEM)] + whole_specs(flat) + [natural] * 3 + [whole(vectors.shape)] * 3,
        out_specs=[natural] * 4 + [whole(vectors.shape)] * 4 + [whole((1, 1))],
        out_shape=[big] * 4 + [little] * 4 + [jax.ShapeDtypeStruct((1, 1), F32)],
        scratch_shapes=[pltpu.VMEM((rows, blocks[0].shape[1]), BF) for blocks in grads] + [pltpu.VMEM((LANES, LANES), F32)],
        compiler_params=params(32),
        cost_estimate=cost(20 * rows * columns, 30 * rows * columns, rows * columns),
    )(place, *flat, weights, first, second, vectors, vector_first, vector_second)


def masks(segments, tags, length):
    tokens = segments.shape[0]
    matches = segments[None, :] == jnp.arange(tags.shape[0], dtype=jnp.int32)[:, None]
    group = jnp.sum(jnp.where(matches, tags[:, None], 0), axis=0)
    live = jnp.arange(tokens, dtype=jnp.int32) < length
    kinds = jnp.arange(16, dtype=jnp.int32)[:, None]
    same = group[None, :] == kinds
    kmask = jnp.where(kinds < 4, (same & live[None, :]).astype(F32), jnp.where(kinds == 4, (~live)[None, :].astype(F32), 0.0))
    qmask = jnp.where(kinds < 4, jnp.where(same, 0.0, -FAR), jnp.where(kinds == 4, -FAR, 0.0))
    return kmask.astype(BF), jnp.broadcast_to(qmask, (16, tokens)).astype(BF)


def on_device(layout, inputs, cotangent, lengths, segment_ids, group_tags, weights, first_moments, second_moments, vectors, vector_first, vector_second):
    _, tokens, width = inputs.shape
    hidden = (weights.shape[1] - 4 * width) // 2
    pair = 2 * HEAD_DIM
    place = layout.place()
    kmask, qmask = masks(segment_ids[0], group_tags[0], lengths[0])
    act_one = inputs[0].T
    cot = cotangent[0].T

    first_part, own_columns = pick_first(layout, place, weights, vectors)
    first_z = join(layout.along_shards([first_part]))
    rest_part = pick_rest(layout, place, weights, (first_z,))
    first_mine = join([first_z] + layout.across_plane([first_z]))
    rest_z = join(layout.along_shards([rest_part]), (first_mine,))
    w_first = collect_first(layout, place, weights, own_columns, first_mine, layout.across_cores(first_mine))
    e_one, ctx_one, qkv_one, stat_one = attend(act_one, w_first, kmask, qmask)
    rest_mine = join([rest_z] + layout.across_plane([rest_z]), (ctx_one,))
    w_rest, unit_one, unit_two, rstd, act_two, hid_one, slope, e_two, ctx_two, qkv_two, stat_two = first_half(
        layout, place, weights, rest_mine, layout.across_cores(rest_mine), act_one, ctx_one, w_first, kmask, qmask)
    outputs, sums, joined_two, mid_two, hid_two, dz_two, du_two, dattn_two, dqkv_two = second_half(
        unit_two, ctx_two, cot, stat_two, w_rest, w_first, e_two, qkv_two)
    vec, joined_one, gctx_one, inner_one, keep, send = turn(
        layout, place, joined_two, dqkv_two.reshape(3 * width, tokens), unit_one, unit_two, rstd, slope, ctx_one, stat_one, sums, w_first, w_rest,
        du_two, hid_one, hid_two, mid_two, dz_two, ctx_two, dattn_two)
    operands = (e_one, qkv_one, stat_one, gctx_one, inner_one)
    done = attend_back(*operands, 0, 1)
    half = add((keep, layout.across_cores(send)), layout.planes, (done,))
    keep, send, input_grad = last(layout, place, *operands, done, 1, joined_one, w_first, act_one, act_two, dqkv_two, vec, (half[0],))
    plane = add([half[0]] + layout.across_plane(half), layout.shards, (keep,))
    half_qkv = add((keep, layout.across_cores(join([send], (plane[0],)))), layout.planes)
    plane_qkv = add([half_qkv[0]] + layout.across_plane(half_qkv), layout.shards)
    far_qkv = layout.along_shards(plane_qkv)
    own_early = layout.across_rest(add([plane[0]] + layout.along_shards(plane), 1, (far_qkv[0],))[0])
    own_qkv = [plane_qkv[0]] + far_qkv
    if layout.parts < layout.batch:
        own_qkv = [layout.across_rest(add(own_qkv)[0])]
    own_qkv = add_squares(own_qkv, (own_early,))
    all_early = join([own_early] + layout.across_plane([own_early]), (own_qkv,))
    all_qkv = join([own_qkv] + layout.across_plane([own_qkv]))
    grads = [(t, layout.across_cores(t)) for t in (all_early, all_qkv)]
    spans = [
        [(0, 4 * width, 2 * hidden), (2 * hidden, 3 * width, width)],
        [(0, 0, 3 * width)],
    ]
    share = shard_squares(layout, place, *grads[1])
    updated = adam(layout, place, [share] + layout.along_shards([share]), spans, grads, weights, first_moments, second_moments, vectors, vector_first, vector_second)
    grad_w, new_weights, new_first, new_second, grad_v, new_vectors, new_vector_first, new_vector_second, grad_norm = updated
    grad_norm = grad_norm.reshape(())
    return (
        outputs[None],
        input_grad[None],
        grad_w,
        grad_v,
        grad_norm,
        new_weights,
        new_first,
        new_second,
        new_vectors,
        new_vector_first,
        new_vector_second,
    )


def solution(mesh):
    rows = ("batch", "shard")
    placed = (
        P(rows, None, None),
        P(rows, None, None),
        P(rows),
        P(rows, None),
        P(rows, None),
        P("shard", None),
        P("shard", None),
        P("shard", None),
        P(None, "shard"),
        P(None, "shard"),
        P(None, "shard"),
    )
    return jax.shard_map(
        functools.partial(on_device, Layout(mesh.shape["batch"], mesh.shape["shard"], D)),
        mesh=mesh,
        in_specs=placed,
        out_specs=(
            P(rows, None, None),
            P(rows, None, None),
            P("shard", None),
            P(None, "shard"),
            P(),
            P("shard", None),
            P("shard", None),
            P("shard", None),
            P(None, "shard"),
            P(None, "shard"),
            P(None, "shard"),
        ),
        check_vma=False,
    )
```

```python
import functools
import math

import jax
import jax.numpy as jnp
from jax import lax
from jax.experimental import pallas as pl
from jax.experimental.pallas import tpu as pltpu
from jax.sharding import PartitionSpec as P

D = 512
FF = 2048
HEADS = 8
HEAD_DIM = 64
STEP = 10
WCOLS = 6144

NORM_EPS = 1e-05
BETA_ONE = 0.5
BETA_TWO = 0.5
ADAM_EPS = 1e-08
DECAY = 0.01
WARMUP = 4000.0
RATE_SCALE = 150000.0

BF = jnp.bfloat16
F32 = jnp.float32
FAR = 1e30
SAFE_SCORE = 60.0
TILE = 256
WIDE_TILE = 512
LANES = 128
SQUARES_AT = 12
COST_SCALE = 100


def params(mebibytes=50):
    return pltpu.CompilerParams(vmem_limit_bytes=mebibytes << 20)


def cost(flops, bytes_accessed, transcendentals=0):
    return pl.CostEstimate(flops=int(flops) // COST_SCALE, bytes_accessed=int(bytes_accessed) // COST_SCALE, transcendentals=int(transcendentals) // COST_SCALE)


def dg(left, right, left_dim, right_dim):
    return lax.dot_general(
        left, right, (((left_dim,), (right_dim,)), ((), ())), preferred_element_type=F32
    )


def whole(shape):
    return pl.BlockSpec(shape, lambda i: (0,) * len(shape))


def adam_update(master, moment_one, moment_two, gradient):
    moment_one = BETA_ONE * moment_one + (1.0 - BETA_ONE) * gradient
    moment_two = BETA_TWO * moment_two + (1.0 - BETA_TWO) * gradient * gradient
    step_rate = RATE_SCALE * D ** (-0.5) * min(STEP ** (-0.5), STEP * WARMUP ** (-1.5))
    fixed_first = moment_one / (1.0 - BETA_ONE**STEP)
    fixed_second = moment_two / (1.0 - BETA_TWO**STEP)
    master = master - step_rate * (
        fixed_first / (jnp.sqrt(fixed_second) + ADAM_EPS) + DECAY * master
    )
    return (master, moment_one, moment_two)


def attend_kernel(act_ref, wq_ref, wk_ref, wv_ref, col_ref, kmask_ref, qmask_ref, e_ref, ctx_ref, qkv_ref, stat_ref):
    act = act_ref[...]
    tokens = act.shape[1]
    q = (dg(wq_ref[...], act, 0, 0) + col_ref[:, 4:5].astype(F32)).astype(BF) * jnp.asarray(HEAD_DIM**-0.5, BF)
    k = dg(wk_ref[...], act, 0, 0).astype(BF)
    v = (dg(wv_ref[...], act, 0, 0) + col_ref[:, 5:6].astype(F32)).astype(BF)
    qkv_ref[0] = q
    qkv_ref[1] = k
    qkv_ref[2] = v
    dead = kmask_ref[4:5, :].astype(F32)
    bound = jnp.zeros((1, 1), F32)
    selves = []
    for h in range(2):
        rows = slice(h * HEAD_DIM, (h + 1) * HEAD_DIM)
        qf, kf = q[rows].astype(F32), k[rows].astype(F32)
        selves.append(jnp.sum(qf * kf, axis=0, keepdims=True))
        q_top = jnp.max(jnp.sum(qf * qf, axis=0, keepdims=True), axis=1, keepdims=True)
        k_top = jnp.max(jnp.sum(kf * kf, axis=0, keepdims=True), axis=1, keepdims=True)
        bound = jnp.maximum(bound, q_top * k_top)
    safe = bound[0, 0] <= SAFE_SCORE * SAFE_SCORE

    def scores(h):
        rows = slice(h * HEAD_DIM, (h + 1) * HEAD_DIM)
        keys = jnp.concatenate([k[rows], kmask_ref[...]], axis=0).T
        queries = jnp.concatenate([q[rows], qmask_ref[...]], axis=0)
        return dg(keys, queries, 1, 0)

    def finish(h, e, e_self):
        rows = slice(h * HEAD_DIM, (h + 1) * HEAD_DIM)
        low_e = e.astype(BF)
        e_ref[h] = low_e
        total = jnp.sum(e, axis=0, keepdims=True) + e_self
        scale = 1.0 / total
        values = v[rows]
        mixed = dg(values, low_e, 1, 0) + values.astype(F32) * e_self.astype(BF).astype(F32)
        ctx_ref[rows, :] = (mixed * scale).astype(BF)
        stat_ref[h, 0:1, :] = scale
        stat_ref[h, 1:2, :] = e_self

    @pl.when(safe)
    def _():
        for h in range(2):
            finish(h, jnp.exp(scores(h)), jnp.exp(selves[h]) * dead)

    @pl.when(jnp.logical_not(safe))
    def _():
        for h in range(2):
            s = scores(h)
            own = jnp.where(dead > 0, selves[h], -FAR)
            top = jnp.maximum(jnp.max(s, axis=0, keepdims=True), own)
            finish(h, jnp.exp(s - top), jnp.exp(own - top) * dead)


def attend(act, w_qkv, kmask, qmask):
    width, tokens = act.shape
    pairs = width // (2 * HEAD_DIM)
    pair = 2 * HEAD_DIM
    heads = width // HEAD_DIM
    return pl.pallas_call(
        attend_kernel,
        name="attend",
        grid=(pairs,),
        in_specs=[
            whole((width, tokens)),
            pl.BlockSpec((width, pair), lambda i: (0, i)),
            pl.BlockSpec((width, pair), lambda i: (0, pairs + i)),
            pl.BlockSpec((width, pair), lambda i: (0, 2 * pairs + i)),
            pl.BlockSpec((pair, pair), lambda i: (i, 3 * pairs)),
            whole((16, tokens)),
            whole((16, tokens)),
        ],
        out_specs=[
            pl.BlockSpec((2, tokens, tokens), lambda i: (i, 0, 0)),
            pl.BlockSpec((pair, tokens), lambda i: (i, 0)),
            pl.BlockSpec((3, pair, tokens), lambda i: (0, i, 0)),
            pl.BlockSpec((2, 2, tokens), lambda i: (i, 0, 0)),
        ],
        out_shape=[
            jax.ShapeDtypeStruct((heads, tokens, tokens), BF),
            jax.ShapeDtypeStruct((width, tokens), BF),
            jax.ShapeDtypeStruct((3, width, tokens), BF),
            jax.ShapeDtypeStruct((heads, 2, tokens), F32),
        ],
        compiler_params=params(),
        cost_estimate=cost(6 * width * width * tokens + 4 * width * tokens * tokens, 2 * heads * tokens * tokens, heads * tokens * tokens),
    )(act, w_qkv, w_qkv, w_qkv, w_qkv, kmask, qmask)


def attend_back_pair(e_ref, qkv_ref, stat_ref, grad_ref, inner_ref, out_ref, ds_ref):
    for h in range(2):
        rows = slice(h * HEAD_DIM, (h + 1) * HEAD_DIM)
        q, k, v = qkv_ref[0, rows], qkv_ref[1, rows], qkv_ref[2, rows]
        grad = grad_ref[rows]
        inner = inner_ref[h]
        e_self = stat_ref[h, 1:2, :]
        grad_f = grad.astype(F32)
        ds = (e_ref[h].astype(F32) * (dg(v.T, grad, 1, 0) - inner)).astype(BF)
        ds_ref[h] = ds
        own = (e_self * (jnp.sum(grad_f * v.astype(F32), axis=0, keepdims=True) - inner)).astype(BF).astype(F32)
        scale = HEAD_DIM**-0.5
        out_ref[0, rows] = ((dg(k, ds, 1, 0) + k.astype(F32) * own) * scale).astype(BF)
        out_ref[2, rows] = (dg(e_ref[h], grad, 1, 1).T + grad_f * e_self.astype(BF).astype(F32)).astype(BF)
        out_ref[1, rows] = (dg(ds_ref[h], q, 1, 1).T + q.astype(F32) * own).astype(BF)


def attend_back(e, qkv, stat, grad, inner, start=0, pairs=None):
    heads, tokens, _ = e.shape
    width = grad.shape[0]
    pair = 2 * HEAD_DIM
    pairs = pairs or heads // 2
    return pl.pallas_call(
        attend_back_pair,
        name="attend_back",
        grid=(pairs,),
        in_specs=[
            pl.BlockSpec((2, tokens, tokens), lambda i: (start + i, 0, 0)),
            pl.BlockSpec((3, pair, tokens), lambda i: (0, start + i, 0)),
            pl.BlockSpec((2, 2, tokens), lambda i: (start + i, 0, 0)),
            pl.BlockSpec((pair, tokens), lambda i: (start + i, 0)),
            pl.BlockSpec((2, 1, tokens), lambda i: (start + i, 0, 0)),
        ],
        out_specs=pl.BlockSpec((3, pair, tokens), lambda i: (0, i, 0)),
        out_shape=jax.ShapeDtypeStruct((3, pairs * pair, tokens), BF),
        scratch_shapes=[pltpu.VMEM((2, tokens, tokens), BF)],
        compiler_params=params(63),
        cost_estimate=cost(8 * pairs * pair * tokens * tokens, 4 * pairs * tokens * tokens),
    )(e, qkv, stat, grad, inner)


def normed(t):
    mean = jnp.mean(t, axis=0, keepdims=True)
    centred = t - mean
    rstd = lax.rsqrt(jnp.mean(centred * centred, axis=0, keepdims=True) + NORM_EPS)
    return centred * rstd, rstd


def normed_back(grad, unit, rstd, gain):
    scaled = grad * gain
    mean = jnp.mean(scaled, axis=0, keepdims=True)
    along = jnp.mean(scaled * unit, axis=0, keepdims=True)
    return rstd * (scaled - mean - unit * along)


def gelu_and_slope(t):
    square = t * t
    inside = jnp.tanh(t * (0.7978845608028654 + (0.7978845608028654 * 0.044715) * square))
    half = 0.5 + 0.5 * inside
    slope = half + (t * (0.5 - 0.5 * inside * inside)) * (
        0.7978845608028654 + (3.0 * 0.7978845608028654 * 0.044715) * square
    )
    return t * half, slope


def lanes_sum(t):
    out = t[:, 0:128]
    for j in range(128, t.shape[1], 128):
        out = out + t[:, j : j + 128]
    return out


def column(col_ref, j):
    return col_ref[:, j : j + 1].astype(F32)


def dense_forward(signal, ctx, rest_ref, col_ref, act_ref, slope_ref):
    wo_ref, win_ref, wback_ref = parts_of(rest_ref)
    joined = signal + dg(wo_ref[...], ctx, 0, 0) + column(col_ref, 6)
    unit_one, rstd_one = normed(joined)
    middle = unit_one * column(col_ref, 0) + column(col_ref, 1)
    low_middle = middle.astype(BF)
    width = middle.shape[0]
    summed = middle + column(col_ref, 7)
    count = win_ref.shape[1] // width

    def before(c):
        return dg(win_ref[:, c * width : (c + 1) * width], low_middle, 0, 0) + column(col_ref, 8 + c)

    following = before(0)
    for c in range(count):
        rows = slice(c * width, (c + 1) * width)
        pre = following
        if c + 1 < count:
            following = before(c + 1)
        gelu, slope = gelu_and_slope(pre)
        act = gelu.astype(BF)
        act_ref[rows, :] = act
        slope_ref[rows, :] = slope.astype(slope_ref.dtype)
        summed = summed + dg(wback_ref[:, rows], act, 1, 0)
    unit_two, rstd_two = normed(summed)
    return unit_one, rstd_one, low_middle, unit_two, rstd_two


def dense_back(grad, unit_one, rstd_one, slope_ref, unit_two, rstd_two, ctx, stat_ref, rest_ref, col_ref,
               sums_ref, joined_ref, gctx_ref, inner_ref, dz_ref, du_ref, dattn_ref):
    wo_ref, win_ref, wback_ref = parts_of(rest_ref)
    sums_ref[2] += lanes_sum(grad * unit_two)
    sums_ref[3] += lanes_sum(grad)
    grad_summed = normed_back(grad, unit_two, rstd_two, column(col_ref, 2))
    dz = grad_summed.astype(BF)
    dz_ref[...] = dz
    sums_ref[7] += lanes_sum(dz.astype(F32))
    width = dz.shape[0]
    grad_middle = grad_summed
    for c in range(win_ref.shape[1] // width):
        rows = slice(c * width, (c + 1) * width)
        du = (dg(wback_ref[:, rows], dz, 0, 0) * slope_ref[rows, :].astype(F32)).astype(BF)
        du_ref[rows, :] = du
        sums_ref[8 + c] += lanes_sum(du.astype(F32))
        grad_middle = grad_middle + dg(win_ref[:, rows], du, 1, 0)
    sums_ref[0] += lanes_sum(grad_middle * unit_one)
    sums_ref[1] += lanes_sum(grad_middle)
    grad_joined = normed_back(grad_middle, unit_one, rstd_one, column(col_ref, 0))
    joined_ref[...] = grad_joined
    dattn = grad_joined.astype(BF)
    dattn_ref[...] = dattn
    sums_ref[6] += lanes_sum(dattn.astype(F32))
    grad_ctx = dg(wo_ref[...], dattn, 1, 0)
    for h in range(stat_ref.shape[0]):
        rows = slice(h * HEAD_DIM, (h + 1) * HEAD_DIM)
        part = (grad_ctx[rows] * stat_ref[h, 0:1, :]).astype(BF)
        gctx_ref[rows, :] = part
        inner_ref[h] = jnp.sum(part.astype(F32) * ctx[rows].astype(F32), axis=0, keepdims=True)


def always(i):
    return i


def tile(rows, at=always, size=TILE):
    return pl.BlockSpec((rows, size), lambda i: (0, at(i)))


def heads_tile(heads, rows, at=always, size=TILE):
    return pl.BlockSpec((heads, rows, size), lambda i: (0, 0, at(i)))


def once(shape, *at):
    at = at or (0,) * len(shape)
    return pl.BlockSpec(shape, lambda i: at, pipeline_mode=pl.Buffered(1))


def span(step, size):
    return pl.ds(pl.multiple_of(step * size, size), size)


def rest_spec(w_rest):
    return pl.BlockSpec(w_rest.shape, lambda i: (0, 0), pipeline_mode=pl.Buffered(1))


def parts_of(rest_ref):
    width = rest_ref.shape[0]
    hidden = (rest_ref.shape[1] - width) // 2
    return rest_ref.at[:, 0:width], rest_ref.at[:, width : width + hidden], rest_ref.at[:, width + hidden :]


def column_spec(width):
    return pl.BlockSpec((width, LANES), lambda i: (0, 3 * width // LANES))


def first_dense_kernel(signal_ref, ctx_ref, rest_ref, col_ref,
                       unit_one_ref, unit_two_ref, rstd_ref, low_out_ref, act_ref, slope_ref):
    unit_one, rstd_one, _, unit_two, rstd_two = dense_forward(
        signal_ref[...].astype(F32), ctx_ref[...], rest_ref, col_ref, act_ref, slope_ref)
    unit_one_ref[...] = unit_one
    unit_two_ref[...] = unit_two
    rstd_ref[0:1, :] = rstd_one
    rstd_ref[1:2, :] = rstd_two
    low_out_ref[...] = (unit_two * column(col_ref, 2) + column(col_ref, 3)).astype(BF)


def first_half_kernel(layout, tiles, place_ref, own_ref, mine_ref, theirs_ref, signal_ref, ctx_ref, w_ref, kmask_ref, qmask_ref,
                      rest_ref, unit_one_ref, unit_two_ref, rstd_ref, low_ref, act_ref, slope_ref, e_ref, ctx_out_ref, qkv_ref, stat_ref, hold_ref):
    step = pl.program_id(0)
    width = ctx_ref.shape[0]
    pair = ctx_out_ref.shape[0]

    @pl.when(step == 0)
    def _():
        put_blocks(layout, place_ref, (mine_ref, theirs_ref), rest_ref)
        rest_ref[own_rows(layout, place_ref), :] = own_ref[:, own_ref.shape[1] - rest_ref.shape[1] :].astype(BF)

    @pl.when(step < tiles)
    def _():
        first_dense_kernel(signal_ref, ctx_ref, rest_ref, w_ref.at[:, 3 * width :], unit_one_ref, unit_two_ref, rstd_ref, low_ref, act_ref, slope_ref)
        hold_ref[:, span(step, WIDE_TILE)] = low_ref[...]

    @pl.when(step >= tiles)
    def _():
        at = step - tiles
        pairs = width // pair
        attend_kernel(
            hold_ref,
            w_ref.at[:, span(at, pair)],
            w_ref.at[:, span(at + pairs, pair)],
            w_ref.at[:, span(at + 2 * pairs, pair)],
            w_ref.at[span(at, pair), 3 * width :],
            kmask_ref, qmask_ref, e_ref, ctx_out_ref, qkv_ref, stat_ref)


def first_half(layout, place, weights, mine, theirs, signal, ctx, w_first, kmask, qmask):
    width, tokens = signal.shape
    total = mine.shape[1]
    hidden = (total - width) // 2
    pair = 2 * HEAD_DIM
    pairs, heads = width // pair, width // HEAD_DIM
    tiles = tokens // WIDE_TILE

    def at_tile(i):
        return jnp.minimum(i, tiles - 1)

    def at_pair(i):
        return jnp.maximum(i - tiles, 0)

    return pl.pallas_call(
        functools.partial(first_half_kernel, layout, tiles),
        name="first_half",
        grid=(tiles + pairs,),
        in_specs=[pl.BlockSpec(memory_space=pltpu.SMEM), once(weights.shape), once(mine.shape), once(theirs.shape),
                  tile(width, at_tile, WIDE_TILE), tile(width, at_tile, WIDE_TILE), once(w_first.shape), once(kmask.shape), once(qmask.shape)],
        out_specs=[whole((width, total)), tile(width, at_tile, WIDE_TILE), tile(width, at_tile, WIDE_TILE), tile(8, at_tile, WIDE_TILE), tile(width, at_tile, WIDE_TILE), tile(hidden, at_tile, WIDE_TILE), tile(hidden, at_tile, WIDE_TILE),
                   pl.BlockSpec((2, tokens, tokens), lambda i: (at_pair(i), 0, 0)),
                   pl.BlockSpec((pair, tokens), lambda i: (at_pair(i), 0)),
                   pl.BlockSpec((3, pair, tokens), lambda i: (0, at_pair(i), 0)),
                   pl.BlockSpec((2, 2, tokens), lambda i: (at_pair(i), 0, 0))],
        out_shape=[
            jax.ShapeDtypeStruct((width, total), BF),
            jax.ShapeDtypeStruct((width, tokens), F32),
            jax.ShapeDtypeStruct((width, tokens), F32),
            jax.ShapeDtypeStruct((8, tokens), F32),
            jax.ShapeDtypeStruct((width, tokens), BF),
            jax.ShapeDtypeStruct((hidden, tokens), BF),
            jax.ShapeDtypeStruct((hidden, tokens), BF),
            jax.ShapeDtypeStruct((heads, tokens, tokens), BF),
            jax.ShapeDtypeStruct((width, tokens), BF),
            jax.ShapeDtypeStruct((3, width, tokens), BF),
            jax.ShapeDtypeStruct((heads, 2, tokens), F32),
        ],
        scratch_shapes=[pltpu.VMEM((width, tokens), BF)],
        compiler_params=params(63),
        cost_estimate=cost(2 * tokens * width * (width + 2 * hidden), 24 << 20, tokens * hidden),
    )(place, weights, mine, theirs, signal, ctx, w_first, kmask, qmask)


def second_dense_kernel(unit_ref, ctx_ref, cot_ref, stat_ref, rest_ref, col_ref,
                        out_ref, sums_ref, joined_ref, gctx_ref, inner_ref, mid_ref, act_ref, dz_ref, du_ref, dattn_ref, slope_ref):
    @pl.when(pl.program_id(0) == 0)
    def _():
        sums_ref[...] = jnp.zeros(sums_ref.shape, F32)

    ctx = ctx_ref[...]
    gain, shift = column(col_ref, 2), column(col_ref, 3)
    unit_one, rstd_one, low_middle, unit_two, rstd_two = dense_forward(
        unit_ref[...] * gain + shift, ctx, rest_ref, col_ref, act_ref, slope_ref)
    mid_ref[...] = low_middle
    out_ref[...] = (unit_two * gain + shift).astype(BF).T
    dense_back(cot_ref[...].astype(F32), unit_one, rstd_one, slope_ref, unit_two, rstd_two, ctx, stat_ref,
               rest_ref, col_ref, sums_ref, joined_ref, gctx_ref, inner_ref, dz_ref, du_ref, dattn_ref)


def second_half_kernel(tiles, unit_ref, ctx_ref, cot_ref, stat_ref, rest_ref, col_ref, e_ref, qkv_ref, pair_stat_ref,
                       out_ref, sums_ref, joined_ref, mid_ref, act_ref, dz_ref, du_ref, dattn_ref, dqkv_ref, slope_ref, gctx_ref, inner_ref, ds_ref):
    step = pl.program_id(0)

    @pl.when(step < tiles)
    def _():
        at = span(step, WIDE_TILE)
        second_dense_kernel(unit_ref, ctx_ref, cot_ref, stat_ref, rest_ref, col_ref, out_ref, sums_ref, joined_ref,
                            gctx_ref.at[:, at], inner_ref.at[:, :, at], mid_ref, act_ref, dz_ref, du_ref, dattn_ref, slope_ref)

    @pl.when(step >= tiles)
    def _():
        pair = dqkv_ref.shape[1]
        attend_back_pair(e_ref, qkv_ref, pair_stat_ref, gctx_ref.at[span(step - tiles, pair)], inner_ref.at[pl.ds(2 * (step - tiles), 2)], dqkv_ref, ds_ref)


def second_half(unit, ctx, cot, stat, w_rest, w_first, e, qkv):
    width, tokens = unit.shape
    hidden = (w_rest.shape[1] - width) // 2
    heads = stat.shape[0]
    pair = 2 * HEAD_DIM
    pairs = width // pair
    tiles = tokens // WIDE_TILE

    def at_tile(i):
        return jnp.minimum(i, tiles - 1)

    def at_pair(i):
        return jnp.maximum(i - tiles, 0)

    return pl.pallas_call(
        functools.partial(second_half_kernel, tiles),
        name="second_half",
        grid=(tiles + pairs,),
        in_specs=[tile(width, at_tile, WIDE_TILE), tile(width, at_tile, WIDE_TILE), tile(width, at_tile, WIDE_TILE), heads_tile(heads, 2, at_tile, WIDE_TILE), once(w_rest.shape), column_spec(width),
                  pl.BlockSpec((2, tokens, tokens), lambda i: (at_pair(i), 0, 0)),
                  pl.BlockSpec((3, pair, tokens), lambda i: (0, at_pair(i), 0)),
                  pl.BlockSpec((2, 2, tokens), lambda i: (at_pair(i), 0, 0))],
        out_specs=[pl.BlockSpec((WIDE_TILE, width), lambda i: (at_tile(i), 0)), once((12, width, LANES)), tile(width, at_tile, WIDE_TILE),
                   tile(width, at_tile, WIDE_TILE), tile(hidden, at_tile, WIDE_TILE), tile(width, at_tile, WIDE_TILE), tile(hidden, at_tile, WIDE_TILE), tile(width, at_tile, WIDE_TILE),
                   pl.BlockSpec((3, pair, tokens), lambda i: (0, at_pair(i), 0))],
        out_shape=[
            jax.ShapeDtypeStruct((tokens, width), BF),
            jax.ShapeDtypeStruct((12, width, LANES), F32),
            jax.ShapeDtypeStruct((width, tokens), F32),
            jax.ShapeDtypeStruct((width, tokens), BF),
            jax.ShapeDtypeStruct((hidden, tokens), BF),
            jax.ShapeDtypeStruct((width, tokens), BF),
            jax.ShapeDtypeStruct((hidden, tokens), BF),
            jax.ShapeDtypeStruct((width, tokens), BF),
            jax.ShapeDtypeStruct((3, width, tokens), BF),
        ],
        scratch_shapes=[pltpu.VMEM((hidden, WIDE_TILE), F32), pltpu.VMEM((width, tokens), BF), pltpu.VMEM((heads, 1, tokens), F32), pltpu.VMEM((2, tokens, tokens), BF)],
        compiler_params=params(63),
        cost_estimate=cost(4 * tokens * width * (width + 2 * hidden), 28 << 20, tokens * hidden),
    )(unit, ctx, cot, stat, w_rest, w_first, e, qkv, stat)


def first_back_kernel(prior_ref, dqkv_ref, unit_one_ref, unit_two_ref, rstd_ref, slope_ref, ctx_ref, stat_ref,
                      wqkv_ref, rest_ref, col_ref,
                      vec_ref, joined_ref, gctx_ref, inner_ref, mid_ref, dz_ref, du_ref, dattn_ref, sums_ref, step, tiles):

    unit_one = unit_one_ref[...]
    mid_ref[...] = (unit_one * column(col_ref, 0) + column(col_ref, 1)).astype(BF)
    grad = prior_ref[...] + dg(wqkv_ref[...], dqkv_ref[...], 1, 0)
    dense_back(grad, unit_one, rstd_ref[0:1, :], slope_ref, unit_two_ref[...], rstd_ref[1:2, :], ctx_ref[...], stat_ref,
               rest_ref, col_ref, sums_ref, joined_ref, gctx_ref, inner_ref, dz_ref, du_ref, dattn_ref)

    @pl.when(step == tiles - 1)
    def _():
        lane = lax.broadcasted_iota(jnp.int32, vec_ref.shape, 1)
        out = jnp.zeros(vec_ref.shape, F32)
        for j in (0, 1, 2, 3, 6, 7, 8, 9, 10, 11):
            out = jnp.where(lane == j, jnp.sum(sums_ref[j], axis=1, keepdims=True), out)
        vec_ref[...] = out


class Layout:
    def __init__(self, mesh_batch, mesh_shard, width):
        self.batch = mesh_batch
        self.shards = mesh_shard
        self.parts = min(mesh_batch, width // mesh_shard // 16)
        self.planes = self.parts // 2
        self.rows = width // mesh_shard // self.parts

    def swap(self, value, axis, distance):
        size = self.batch if axis == "batch" else self.shards
        return lax.ppermute(value, axis, [(i, i ^ distance) for i in range(size)])

    def place(self):
        return jnp.stack([lax.axis_index("batch") % self.parts, lax.axis_index("shard")]).astype(jnp.int32)

    def row_of(self, place_ref, c, e, d):
        block = (place_ref[1] ^ d) * self.parts + (place_ref[0] ^ (2 * e + c))
        return pl.multiple_of(block * self.rows, self.rows)

    def along_shards(self, blocks):
        return [self.swap(blocks[d % len(blocks)], "shard", d) for d in range(1, self.shards)]

    def across_plane(self, blocks):
        return [self.swap(blocks[e % len(blocks)], "batch", 2 * e) for e in range(1, self.planes)]

    def across_cores(self, block):
        return self.swap(block, "batch", 1)

    def across_rest(self, own):
        distance = self.parts
        while distance < self.batch:
            own = add([own, self.swap(own, "batch", distance)])[0]
            distance *= 2
        return own


def tree(values):
    while len(values) > 1:
        values = [a + b for a, b in zip(values[::2], values[1::2], strict=True)]
    return values[0]


def whole_specs(values, tokens_in=()):
    return [whole(v.shape) for v in values] + [pl.BlockSpec(memory_space=pl.ANY)] * len(tokens_in)


def join_kernel(count, *refs):
    out_ref = refs[-1]
    at = 0
    for source in refs[:count]:
        out_ref[at : at + source.shape[0], :] = source[...]
        at += source.shape[0]


def join(blocks, tokens_in=()):
    rows, columns = sum(b.shape[0] for b in blocks), blocks[0].shape[1]
    return pl.pallas_call(
        functools.partial(join_kernel, len(blocks)),
        name="join",
        grid=(1,),
        in_specs=whole_specs(blocks, tokens_in),
        out_specs=whole((rows, columns)),
        out_shape=jax.ShapeDtypeStruct((rows, columns), BF),
        compiler_params=params(),
        cost_estimate=cost(0, 4 * rows * columns),
    )(*blocks, *tokens_in)


def add_kernel(count, outs, *refs):
    total = refs[0][...].astype(F32)
    for other in refs[1:count]:
        total = total + other[...].astype(F32)
    total = total.astype(BF)
    rows = refs[-1].shape[0]
    for i in range(outs):
        refs[i - outs][...] = total[i * rows : (i + 1) * rows]


def add(values, outs=1, tokens_in=()):
    rows, columns = values[0].shape
    part = jax.ShapeDtypeStruct((rows // outs, columns), BF)
    return pl.pallas_call(
        functools.partial(add_kernel, len(values), outs),
        name="add",
        grid=(1,),
        in_specs=whole_specs(values, tokens_in),
        out_specs=[whole(part.shape)] * outs,
        out_shape=[part] * outs,
        compiler_params=params(),
        cost_estimate=cost(len(values) * rows * columns, 2 * (len(values) + 1) * rows * columns),
    )(*values, *tokens_in)


def add_squares_kernel(count, others, *refs):
    out_ref = refs[-1]
    total = refs[0][...].astype(F32)
    for other in refs[1:count]:
        total = total + other[...].astype(F32)
    total = total.astype(BF)
    squares = jnp.sum(jnp.square(total.astype(F32)), keepdims=True)
    for other in refs[count : count + others]:
        squares = squares + jnp.sum(jnp.square(other[...].astype(F32)), keepdims=True)
    out_ref[...] = total
    high = squares.astype(BF)
    middle = (squares - high.astype(F32)).astype(BF)
    low = (squares - high.astype(F32) - middle.astype(F32)).astype(BF)
    used = total.shape[1] - LANES
    tail = total[:, used:]
    lane = lax.broadcasted_iota(jnp.int32, tail.shape, 1)
    for i, piece in enumerate((high, middle, low)):
        tail = jnp.where(lane == SQUARES_AT + i, piece.astype(F32), tail.astype(F32)).astype(BF)
    out_ref[:, used:] = tail


def add_squares(values, others):
    rows, columns = values[0].shape
    return pl.pallas_call(
        functools.partial(add_squares_kernel, len(values), len(others)),
        name="add_squares",
        grid=(1,),
        in_specs=whole_specs(list(values) + list(others)),
        out_specs=whole((rows, columns)),
        out_shape=jax.ShapeDtypeStruct((rows, columns), BF),
        compiler_params=params(),
        cost_estimate=cost(len(values) * rows * columns, 2 * (len(values) + 1) * rows * columns),
    )(*values, *others)


def shard_squares_kernel(layout, place_ref, mine_ref, theirs_ref, out_ref):
    used = mine_ref.shape[1] - LANES
    total = jnp.zeros((1, LANES), F32)
    lane = lax.broadcasted_iota(jnp.int32, (1, LANES), 1)
    riding = (lane >= SQUARES_AT) & (lane < SQUARES_AT + 3)
    for part in range(layout.parts):
        away = place_ref[0] ^ part
        at = pl.ds(pl.multiple_of((away >> 1) * layout.rows, layout.rows), layout.rows)
        mine = mine_ref[at, used:].astype(F32)[0:1]
        theirs = theirs_ref[at, used:].astype(F32)[0:1]
        total = total + jnp.where((away & 1) == 0, mine, theirs)
    total = jnp.sum(jnp.where(riding, total, 0.0), axis=1, keepdims=True)
    out_ref[...] = jnp.broadcast_to(total, out_ref.shape)


def shard_squares(layout, place, mine, theirs):
    return pl.pallas_call(
        functools.partial(shard_squares_kernel, layout),
        name="shard_squares",
        grid=(1,),
        in_specs=[pl.BlockSpec(memory_space=pltpu.SMEM)] + whole_specs((mine, theirs)),
        out_specs=whole((8, LANES)),
        out_shape=jax.ShapeDtypeStruct((8, LANES), F32),
        compiler_params=params(),
        cost_estimate=cost(0, 4 * mine.size),
    )(place, mine, theirs)


def pick_first_kernel(place_ref, w_ref, vec_ref, out_ref, columns_ref, hold_ref):
    hold_ref[...] = jnp.zeros(hold_ref.shape, F32)
    hold_ref[0 : vec_ref.shape[0], 0 : vec_ref.shape[1]] = vec_ref[...]
    hold_ref[...] = hold_ref[...].T
    columns_ref[...] = hold_ref[0 : columns_ref.shape[0], :].astype(BF)
    used = w_ref.shape[1]
    rows = out_ref.shape[0]
    out_ref[:, 0:used] = w_ref[...].astype(BF)
    out_ref[:, used:] = hold_ref[pl.ds(pl.multiple_of(place_ref[0] * rows, rows), rows), :].astype(BF)


def pick_first(layout, place, weights, vectors):
    shard_rows, columns = weights.shape
    used = columns // 4
    return pl.pallas_call(
        pick_first_kernel,
        name="pick_first",
        grid_spec=pltpu.PrefetchScalarGridSpec(
            num_scalar_prefetch=1,
            grid=(1,),
            in_specs=[pl.BlockSpec((layout.rows, used), lambda i, place: (place[0], 0)), pl.BlockSpec(vectors.shape, lambda i, place: (0, 0))],
            out_specs=[pl.BlockSpec((layout.rows, used + LANES), lambda i, place: (0, 0)), pl.BlockSpec((shard_rows, LANES), lambda i, place: (0, 0))],
            scratch_shapes=[pltpu.VMEM((LANES, LANES), F32)],
        ),
        out_shape=[jax.ShapeDtypeStruct((layout.rows, used + LANES), BF), jax.ShapeDtypeStruct((shard_rows, LANES), BF)],
        compiler_params=params(),
        cost_estimate=cost(0, 6 * layout.rows * columns),
    )(place, weights, vectors)


def pick_rest_kernel(place_ref, w_ref, *refs):
    out_ref = refs[-1]
    out_ref[...] = w_ref[:, w_ref.shape[1] - out_ref.shape[1] :].astype(BF)


def pick_rest(layout, place, weights, tokens_in):
    columns = weights.shape[1]
    return pl.pallas_call(
        pick_rest_kernel,
        name="pick_rest",
        grid_spec=pltpu.PrefetchScalarGridSpec(
            num_scalar_prefetch=1,
            grid=(1,),
            in_specs=[pl.BlockSpec((layout.rows, columns), lambda i, place: (place[0], 0))] + [pl.BlockSpec(memory_space=pl.ANY)] * len(tokens_in),
            out_specs=pl.BlockSpec((layout.rows, 3 * columns // 4), lambda i, place: (0, 0)),
        ),
        out_shape=jax.ShapeDtypeStruct((layout.rows, 3 * columns // 4), BF),
        compiler_params=params(),
        cost_estimate=cost(0, 6 * layout.rows * columns),
    )(place, weights, *tokens_in)


def put_blocks(layout, place_ref, sources, out_ref):
    for c, source in enumerate(sources):
        for e in range(layout.planes):
            for d in range(1, layout.shards):
                at = (e * (layout.shards - 1) + d - 1) * layout.rows
                out_ref[pl.ds(layout.row_of(place_ref, c, e, d), layout.rows), :] = source[at : at + layout.rows, :]


def own_rows(layout, place_ref):
    rows = layout.rows * layout.parts
    return pl.ds(pl.multiple_of(place_ref[1] * rows, rows), rows)


def collect_first_kernel(layout, place_ref, w_ref, columns_ref, mine_ref, theirs_ref, out_ref):
    put_blocks(layout, place_ref, (mine_ref, theirs_ref), out_ref)
    rows = own_rows(layout, place_ref)
    used = w_ref.shape[1]
    out_ref[rows, 0:used] = w_ref[...].astype(BF)
    out_ref[rows, used:] = columns_ref[...]


def collect_first(layout, place, weights, columns, mine, theirs):
    shard_rows, all_columns = weights.shape
    rows = shard_rows * layout.shards
    total = mine.shape[1]
    return pl.pallas_call(
        functools.partial(collect_first_kernel, layout),
        name="collect_first",
        grid=(1,),
        in_specs=[pl.BlockSpec(memory_space=pltpu.SMEM), pl.BlockSpec((shard_rows, all_columns // 4), lambda i: (0, 0))] + whole_specs((columns, mine, theirs)),
        out_specs=whole((rows, total)),
        out_shape=jax.ShapeDtypeStruct((rows, total), BF),
        compiler_params=params(),
        cost_estimate=cost(0, 4 * rows * total),
    )(place, weights, columns, mine, theirs)


def in_order(layout, place_ref, source_ref, target_ref):
    at = 0
    for c in range(2):
        for e in range(layout.planes):
            for d in range(layout.shards):
                target_ref[at : at + layout.rows] = source_ref[pl.ds(layout.row_of(place_ref, c, e, d), layout.rows), :]
                at += layout.rows


def weight_step(left_ref, ra_ref, rb_ref, keep_ref, send_ref):
    out = (dg(left_ref[0], ra_ref[...], 1, 1) + dg(left_ref[1], rb_ref[...], 1, 1)).astype(BF)
    half = out.shape[0] // 2
    keep_ref[...] = out[:half]
    send_ref[...] = out[half:]


def turn_kernel(layout, tiles, place_ref, prior_ref, dqkv_ref, unit_one_ref, unit_two_ref, rstd_ref, slope_ref, ctx_ref, stat_ref, sums_in_ref,
                wqkv_ref, rest_ref, col_ref, du_two_ref, hid_one_ref, hid_two_ref, mid_two_ref, dz_two_ref, ctx_one_ref, ctx_two_ref, dattn_two_ref,
                vec_ref, joined_ref, gctx_ref, inner_ref, keep_ref, send_ref,
                sums_ref, mid_ref, dz_ref, du_ref, dattn_ref, left_ref, far_ref, sem):
    step = pl.program_id(0)
    width = mid_ref.shape[0]
    count = du_ref.shape[0] // width
    copies = [
        pltpu.make_async_copy(source, far_ref.at[i], sem.at[i])
        for i, source in enumerate((mid_two_ref, dz_two_ref, ctx_one_ref, ctx_two_ref, dattn_two_ref))
    ]
    start = pltpu.make_async_copy(sums_in_ref, sums_ref, sem.at[len(copies)])

    @pl.when(step == 0)
    def _():
        start.start()
        start.wait()
        for copy in copies:
            copy.start()

    @pl.when(step < tiles)
    def _():
        at = span(step, WIDE_TILE)
        first_back_kernel(prior_ref, dqkv_ref, unit_one_ref, unit_two_ref, rstd_ref, slope_ref, ctx_ref, stat_ref,
                          wqkv_ref, rest_ref, col_ref, vec_ref, joined_ref, gctx_ref, inner_ref,
                          mid_ref.at[:, at], dz_ref.at[:, at], du_ref.at[:, at], dattn_ref.at[:, at], sums_ref, step, tiles)

    @pl.when(step == tiles)
    def _():
        for copy in copies:
            copy.wait()

    for at, first_ref, second_ref in ((0, mid_ref, far_ref.at[0]), (count, dz_ref, far_ref.at[1]), (2 * count, far_ref.at[2], far_ref.at[3])):
        @pl.when(step == tiles + at)
        def _(first_ref=first_ref, second_ref=second_ref):
            in_order(layout, place_ref, first_ref, left_ref.at[0])
            in_order(layout, place_ref, second_ref, left_ref.at[1])

    @pl.when((step >= tiles) & (step < tiles + count))
    def _():
        weight_step(left_ref, du_ref.at[span(step - tiles, width)], du_two_ref, keep_ref, send_ref)

    @pl.when((step >= tiles + count) & (step < tiles + 2 * count))
    def _():
        weight_step(left_ref, hid_one_ref, hid_two_ref, keep_ref, send_ref)

    @pl.when(step == tiles + 2 * count)
    def _():
        weight_step(left_ref, dattn_ref, far_ref.at[4], keep_ref, send_ref)


def turn(layout, place, prior, dqkv, unit_one, unit_two, rstd, slope, ctx_one, stat, sums, w_first, w_rest,
         du_two, hid_one, hid_two, mid_two, dz_two, ctx_two, dattn_two):
    width, tokens = prior.shape
    hidden = (w_rest.shape[1] - width) // 2
    heads = stat.shape[0]
    tiles = tokens // WIDE_TILE
    count = hidden // width
    half = jax.ShapeDtypeStruct((width // 2, 2 * hidden + width), BF)

    def at_tile(i):
        return jnp.minimum(i, tiles - 1)

    def rows_from(start):
        return pl.BlockSpec((width, tokens), lambda i: (jnp.clip(i - tiles - start, 0, count - 1), 0))

    columns = pl.BlockSpec((width // 2, width), lambda i: (0, jnp.clip(i - tiles, 0, 2 * count)))
    return pl.pallas_call(
        functools.partial(turn_kernel, layout, tiles),
        name="turn",
        grid=(tiles + 2 * count + 1,),
        in_specs=[pl.BlockSpec(memory_space=pltpu.SMEM), tile(width, at_tile, WIDE_TILE), tile(3 * width, at_tile, WIDE_TILE), tile(width, at_tile, WIDE_TILE), tile(width, at_tile, WIDE_TILE), tile(8, at_tile, WIDE_TILE),
                  tile(hidden, at_tile, WIDE_TILE), tile(width, at_tile, WIDE_TILE), heads_tile(heads, 2, at_tile, WIDE_TILE), pl.BlockSpec(memory_space=pl.ANY),
                  once((width, 3 * width)), once(w_rest.shape), column_spec(width), rows_from(0), rows_from(count), rows_from(count)]
        + [pl.BlockSpec(memory_space=pl.ANY)] * 5,
        out_specs=[whole((width, LANES)), tile(width, at_tile, WIDE_TILE), tile(width, at_tile, WIDE_TILE), heads_tile(heads, 1, at_tile, WIDE_TILE), columns, columns],
        out_shape=[
            jax.ShapeDtypeStruct((width, LANES), F32),
            jax.ShapeDtypeStruct((width, tokens), F32),
            jax.ShapeDtypeStruct((width, tokens), BF),
            jax.ShapeDtypeStruct((heads, 1, tokens), F32),
            half,
            half,
        ],
        scratch_shapes=[pltpu.VMEM((12, width, LANES), F32), pltpu.VMEM((width, tokens), BF), pltpu.VMEM((width, tokens), BF), pltpu.VMEM((hidden, tokens), BF),
                        pltpu.VMEM((width, tokens), BF), pltpu.VMEM((2, width, tokens), BF), pltpu.VMEM((5, width, tokens), BF), pltpu.SemaphoreType.DMA((6,))],
        compiler_params=params(63),
        cost_estimate=cost(2 * tokens * width * (4 * width + 2 * hidden), 28 << 20),
    )(place, prior, dqkv, unit_one, unit_two, rstd, slope, ctx_one, stat, sums, w_first, w_rest, w_first, du_two, hid_one, hid_two,
      mid_two, dz_two, ctx_one, ctx_two, dattn_two)


def last_kernel(layout, pairs, tiles, given, place_ref, e_ref, qkv_ref, stat_ref, grad_ref, inner_ref, done_ref, joined_ref, w_ref,
                la_ref, lb_ref, rb_ref, vec_in_ref, *refs):
    keep_ref, send_ref, input_ref, ds_ref, dqkv_ref, left_ref, vec_ref, order_ref = refs[given:]
    step = pl.program_id(0)
    pair = grad_ref.shape[0]
    rows = left_ref.shape[1]
    skipped = done_ref.shape[1]

    @pl.when(step == 0)
    def _():
        dqkv_ref[:, 0:skipped] = done_ref[...]
        in_order(layout, place_ref, la_ref, left_ref.at[0])
        in_order(layout, place_ref, lb_ref, left_ref.at[1])
        vec_ref[...] = vec_in_ref[...]

    @pl.when(step < pairs)
    def _():
        at = pl.ds(pl.multiple_of(skipped + step * pair, pair), pair)
        attend_back_pair(e_ref, qkv_ref, stat_ref, grad_ref, inner_ref, dqkv_ref.at[:, at], ds_ref)

    @pl.when((step >= pairs) & (step < pairs + tiles))
    def _():
        width = joined_ref.shape[1]
        at = pl.ds(pl.multiple_of((step - pairs) * width, width), width)
        total = joined_ref[...]
        for t in range(3):
            total = total + dg(w_ref[:, t * rows : (t + 1) * rows], dqkv_ref[t, :, at], 1, 0)
        input_ref[...] = total.T

    @pl.when(step >= pairs + tiles)
    def _():
        third = step - pairs - tiles
        ra, rb = dqkv_ref[third], rb_ref[0]
        out = (dg(left_ref[0], ra, 1, 1) + dg(left_ref[1], rb, 1, 1)).astype(BF)
        half = rows // 2
        columns = pl.ds(pl.multiple_of(third * rows, rows), rows)
        keep_ref[:, columns] = out[:half]
        send_ref[:, columns] = out[half:]
        sums = jnp.sum(lanes_sum(ra.astype(F32)) + lanes_sum(rb.astype(F32)), axis=1, keepdims=True)
        lane = lax.broadcasted_iota(jnp.int32, vec_ref.shape, 1)
        wanted = ((third == 0) & (lane == 4)) | ((third == 2) & (lane == 5))
        vec_ref[...] = jnp.where(wanted, sums, vec_ref[...])

    @pl.when(step == pl.num_programs(0) - 1)
    def _():
        in_order(layout, place_ref, vec_ref, order_ref)
        half = rows // 2
        used = keep_ref.shape[1] - LANES
        keep_ref[:, used:] = order_ref[0:half].astype(BF)
        send_ref[:, used:] = order_ref[half:].astype(BF)


def last(layout, place, e, qkv, stat, grad, inner, done, skipped, joined, w_first, left_one, left_two, dqkv_two, vec, tokens_in):
    rows, tokens = left_one.shape
    pair = 2 * HEAD_DIM
    pairs = rows // pair - skipped
    tiles = tokens // WIDE_TILE
    half = jax.ShapeDtypeStruct((rows // 2, 3 * rows + LANES), BF)

    def at_pair(i):
        return skipped + jnp.minimum(i, pairs - 1)

    def at_tile(i):
        return jnp.clip(i - pairs, 0, tiles - 1)

    return pl.pallas_call(
        functools.partial(last_kernel, layout, pairs, tiles, len(tokens_in)),
        name="last",
        grid=(pairs + tiles + 3,),
        in_specs=[
            pl.BlockSpec(memory_space=pltpu.SMEM),
            pl.BlockSpec((2, tokens, tokens), lambda i: (at_pair(i), 0, 0)),
            pl.BlockSpec((3, pair, tokens), lambda i: (0, at_pair(i), 0)),
            pl.BlockSpec((2, 2, tokens), lambda i: (at_pair(i), 0, 0)),
            pl.BlockSpec((pair, tokens), lambda i: (at_pair(i), 0)),
            pl.BlockSpec((2, 1, tokens), lambda i: (at_pair(i), 0, 0)),
            once((3, skipped * pair, tokens)),
            pl.BlockSpec((rows, WIDE_TILE), lambda i: (0, at_tile(i))),
            once((rows, 3 * rows)),
            once((rows, tokens)),
            once((rows, tokens)),
            pl.BlockSpec((1, rows, tokens), lambda i: (jnp.clip(i - pairs - tiles, 0, 2), 0, 0)),
            once(vec.shape),
        ] + [pl.BlockSpec(memory_space=pl.ANY)] * len(tokens_in),
        out_specs=[whole(half.shape)] * 2 + [pl.BlockSpec((WIDE_TILE, rows), lambda i: (at_tile(i), 0))],
        out_shape=[half, half, jax.ShapeDtypeStruct((tokens, rows), F32)],
        scratch_shapes=[pltpu.VMEM((2, tokens, tokens), BF), pltpu.VMEM((3, rows, tokens), BF), pltpu.VMEM((2, rows, tokens), BF),
                        pltpu.VMEM(vec.shape, F32), pltpu.VMEM(vec.shape, F32)],
        compiler_params=params(),
        cost_estimate=cost(12 * rows * rows * tokens, 12 * rows * tokens),
    )(place, e, qkv, stat, grad, inner, done, joined, w_first, left_one, left_two, dqkv_two, vec, *tokens_in)


def adam_kernel(layout, pieces, place_ref, *refs):
    grads = [refs[2 * i : 2 * i + 2] for i in range(len(pieces))]
    rest = refs[2 * len(pieces) :]
    shares, rest = rest[: layout.shards], rest[layout.shards :]
    w_ref, one_ref, two_ref, v_ref, vone_ref, vtwo_ref = rest[:6]
    gw_ref, nw_ref, none_ref, ntwo_ref, gv_ref, nv_ref, nvone_ref, nvtwo_ref, norm_ref = rest[6:15]
    holds, hold_ref = rest[15:-1], rest[-1]
    norm = jnp.sqrt(tree([share[0:1, 0:1] for share in shares]))
    clip_limit = math.sqrt(D * WCOLS)
    factor = clip_limit / jnp.maximum(norm, clip_limit)
    step = pl.program_id(0)
    rows = layout.rows

    @pl.when(step == 0)
    def _():
        norm_ref[...] = jnp.broadcast_to(norm, norm_ref.shape)
        for blocks, target in zip(grads, holds, strict=True):
            for c, block in enumerate(blocks):
                for e in range(layout.planes):
                    part = place_ref[0] ^ (2 * e + c)
                    target[pl.ds(pl.multiple_of(part * rows, rows), rows), :] = block[e * rows : (e + 1) * rows, :]
        hold_ref[0 : holds[-1].shape[0], :] = holds[-1][:, holds[-1].shape[1] - LANES :].astype(F32)
        grad = hold_ref[...].T[0 : gv_ref.shape[0], 0 : gv_ref.shape[1]]
        gv_ref[...] = grad
        nv_ref[...], nvone_ref[...], nvtwo_ref[...] = adam_update(v_ref[...], vone_ref[...], vtwo_ref[...], grad * factor)

    size = w_ref.shape[0]
    at = pl.ds(pl.multiple_of(step * size, size), size)
    for held, spans in zip(holds, pieces, strict=True):
        for source, target, width in spans:
            to = slice(target, target + width)
            grad = held[at, source : source + width].astype(F32)
            gw_ref[:, to] = grad
            nw_ref[:, to], none_ref[:, to], ntwo_ref[:, to] = adam_update(w_ref[:, to], one_ref[:, to], two_ref[:, to], grad * factor)


def adam(layout, place, shares, pieces, grads, weights, first, second, vectors, vector_first, vector_second):
    rows, columns = weights.shape
    block = 16
    natural = pl.BlockSpec((block, columns), lambda i: (i, 0))
    big = jax.ShapeDtypeStruct((rows, columns), F32)
    little = jax.ShapeDtypeStruct(vectors.shape, F32)
    flat = [t for blocks in grads for t in blocks] + list(shares)
    return pl.pallas_call(
        functools.partial(adam_kernel, layout, pieces),
        name="adam",
        grid=(rows // block,),
        in_specs=[pl.BlockSpec(memory_space=pltpu.SMEM)] + whole_specs(flat) + [natural] * 3 + [whole(vectors.shape)] * 3,
        out_specs=[natural] * 4 + [whole(vectors.shape)] * 4 + [whole((1, 1))],
        out_shape=[big] * 4 + [little] * 4 + [jax.ShapeDtypeStruct((1, 1), F32)],
        scratch_shapes=[pltpu.VMEM((rows, blocks[0].shape[1]), BF) for blocks in grads] + [pltpu.VMEM((LANES, LANES), F32)],
        compiler_params=params(32),
        cost_estimate=cost(20 * rows * columns, 30 * rows * columns, rows * columns),
    )(place, *flat, weights, first, second, vectors, vector_first, vector_second)


def masks(segments, tags, length):
    tokens = segments.shape[0]
    matches = segments[None, :] == jnp.arange(tags.shape[0], dtype=jnp.int32)[:, None]
    group = jnp.sum(jnp.where(matches, tags[:, None], 0), axis=0)
    live = jnp.arange(tokens, dtype=jnp.int32) < length
    kinds = jnp.arange(16, dtype=jnp.int32)[:, None]
    same = group[None, :] == kinds
    kmask = jnp.where(kinds < 4, (same & live[None, :]).astype(F32), jnp.where(kinds == 4, (~live)[None, :].astype(F32), 0.0))
    qmask = jnp.where(kinds < 4, jnp.where(same, 0.0, -FAR), jnp.where(kinds == 4, -FAR, 0.0))
    return kmask.astype(BF), jnp.broadcast_to(qmask, (16, tokens)).astype(BF)


def on_device(layout, inputs, cotangent, lengths, segment_ids, group_tags, weights, first_moments, second_moments, vectors, vector_first, vector_second):
    _, tokens, width = inputs.shape
    hidden = (weights.shape[1] - 4 * width) // 2
    pair = 2 * HEAD_DIM
    place = layout.place()
    kmask, qmask = masks(segment_ids[0], group_tags[0], lengths[0])
    act_one = inputs[0].T
    cot = cotangent[0].T

    first_part, own_columns = pick_first(layout, place, weights, vectors)
    first_z = join(layout.along_shards([first_part]))
    rest_part = pick_rest(layout, place, weights, (first_z,))
    first_mine = join([first_z] + layout.across_plane([first_z]))
    rest_z = join(layout.along_shards([rest_part]), (first_mine,))
    w_first = collect_first(layout, place, weights, own_columns, first_mine, layout.across_cores(first_mine))
    e_one, ctx_one, qkv_one, stat_one = attend(act_one, w_first, kmask, qmask)
    rest_mine = join([rest_z] + layout.across_plane([rest_z]), (ctx_one,))
    w_rest, unit_one, unit_two, rstd, act_two, hid_one, slope, e_two, ctx_two, qkv_two, stat_two = first_half(
        layout, place, weights, rest_mine, layout.across_cores(rest_mine), act_one, ctx_one, w_first, kmask, qmask)
    outputs, sums, joined_two, mid_two, hid_two, dz_two, du_two, dattn_two, dqkv_two = second_half(
        unit_two, ctx_two, cot, stat_two, w_rest, w_first, e_two, qkv_two)
    vec, joined_one, gctx_one, inner_one, keep, send = turn(
        layout, place, joined_two, dqkv_two.reshape(3 * width, tokens), unit_one, unit_two, rstd, slope, ctx_one, stat_one, sums, w_first, w_rest,
        du_two, hid_one, hid_two, mid_two, dz_two, ctx_two, dattn_two)
    operands = (e_one, qkv_one, stat_one, gctx_one, inner_one)
    done = attend_back(*operands, 0, 1)
    half = add((keep, layout.across_cores(send)), layout.planes, (done,))
    keep, send, input_grad = last(layout, place, *operands, done, 1, joined_one, w_first, act_one, act_two, dqkv_two, vec, (half[0],))
    plane = add([half[0]] + layout.across_plane(half), layout.shards, (keep,))
    half_qkv = add((keep, layout.across_cores(join([send], (plane[0],)))), layout.planes)
    plane_qkv = add([half_qkv[0]] + layout.across_plane(half_qkv), layout.shards)
    far_qkv = layout.along_shards(plane_qkv)
    own_early = layout.across_rest(add([plane[0]] + layout.along_shards(plane), 1, (far_qkv[0],))[0])
    own_qkv = [plane_qkv[0]] + far_qkv
    if layout.parts < layout.batch:
        own_qkv = [layout.across_rest(add(own_qkv)[0])]
    own_qkv = add_squares(own_qkv, (own_early,))
    all_early = join([own_early] + layout.across_plane([own_early]), (own_qkv,))
    all_qkv = join([own_qkv] + layout.across_plane([own_qkv]))
    grads = [(t, layout.across_cores(t)) for t in (all_early, all_qkv)]
    spans = [
        [(0, 4 * width, 2 * hidden), (2 * hidden, 3 * width, width)],
        [(0, 0, 3 * width)],
    ]
    share = shard_squares(layout, place, *grads[1])
    updated = adam(layout, place, [share] + layout.along_shards([share]), spans, grads, weights, first_moments, second_moments, vectors, vector_first, vector_second)
    grad_w, new_weights, new_first, new_second, grad_v, new_vectors, new_vector_first, new_vector_second, grad_norm = updated
    grad_norm = grad_norm.reshape(())
    return (
        outputs[None],
        input_grad[None],
        grad_w,
        grad_v,
        grad_norm,
        new_weights,
        new_first,
        new_second,
        new_vectors,
        new_vector_first,
        new_vector_second,
    )


def solution(mesh):
    rows = ("batch", "shard")
    placed = (
        P(rows, None, None),
        P(rows, None, None),
        P(rows),
        P(rows, None),
        P(rows, None),
        P("shard", None),
        P("shard", None),
        P("shard", None),
        P(None, "shard"),
        P(None, "shard"),
        P(None, "shard"),
    )
    return jax.shard_map(
        functools.partial(on_device, Layout(mesh.shape["batch"], mesh.shape["shard"], D)),
        mesh=mesh,
        in_specs=placed,
        out_specs=(
            P(rows, None, None),
            P(rows, None, None),
            P("shard", None),
            P(None, "shard"),
            P(),
            P("shard", None),
            P("shard", None),
            P("shard", None),
            P(None, "shard"),
            P(None, "shard"),
            P(None, "shard"),
        ),
        check_vma=False,
    )
```
